32 devices in a mesh: section: 4 (over y, core), video: 2 (over x), dp: 4 (over z).
Axes of the slice: x: 2, y: 2, z: 4, core: 2. Of those that a mesh axis runs over, the one named last changes fastest.
Arguments:
- grad_latent: bfloat16 [4, 2, 64, 64, 128], P('dp', 'video', 'section'), may hold values from -6 to 6
- input_one: bfloat16 [4, 2, 64, 64, 128], P('dp', 'video', 'section'), may hold values from -6 to 6
- preact_one: bfloat16 [4, 2, 64, 64, 128], P('dp', 'video', 'section'), may hold values from -8 to 8
- input_two: bfloat16 [4, 2, 64, 64, 128], P('dp', 'video', 'section'), may hold values from -6 to 6
- preact_two: bfloat16 [4, 2, 64, 64, 128], P('dp', 'video', 'section'), may hold values from -8 to 8
- spatial_one: bfloat16 [3, 3, 128, 128], replicated, may hold values from -0.1875 to 0.1875
- temporal_one: bfloat16 [3, 128, 128], replicated, may hold values from -0.3125 to 0.3125
- spatial_two: bfloat16 [3, 3, 128, 128], replicated, may hold values from -0.1875 to 0.1875
- temporal_two: bfloat16 [3, 128, 128], replicated, may hold values from -0.3125 to 0.3125
Outputs:
- grad_input: bfloat16 [4, 2, 64, 64, 128], P('dp', 'video', 'section')
- grad_spatial_one: float32 [3, 3, 128, 128], replicated
- grad_temporal_one: float32 [3, 128, 128], replicated
- grad_spatial_two: float32 [3, 3, 128, 128], replicated
- grad_temporal_two: float32 [3, 128, 128], replicated
The draws below stay inside these ranges and needn't reach their ends.
All inputs are finite; a program needn't handle non-finite values.
Results may differ from the reference program's by a relative error of at most 0.0061.
Values may be sent and summed in bfloat16 or wider, within the bound.
No kernel may reach another device: no remote copies, remote signals or barrier semaphores. Data moves between devices by JAX's collectives and lax.ppermute only.
A program may use at most 64 MiB of HBM per device.

```python
import jax
import jax.numpy as jnp
from jax import lax

CH = 128
COLS = 64
FRAMES = 2
ROWS = 64
CLIPS = 4


def levels(key, extent, cuts, smallest, largest):
    def one(position, blocks):
        steps = jax.random.uniform(jax.random.fold_in(jax.random.fold_in(key, 6), position), (blocks,), jnp.float32, smallest / len(cuts), largest / len(cuts))
        return jnp.repeat(jnp.exp(steps), extent[position] // blocks).reshape((-1,) + (1,) * (len(extent) - position - 1))

    gain = one(*cuts[0])
    for cut in cuts[1:]:
        gain = gain * one(*cut)
    return gain


def centred(key, shape, spread, most, shards=(), held_as=jnp.bfloat16):
    entries = jax.random.normal(key, shape, jnp.float32) * spread
    if len(shards) > 0:
        entries = levels(key, shape, shards, -0.22, 0.18) * entries
    return jnp.clip(entries, min=-most, max=most).astype(held_as)


def setup_inputs(seed: int = 0) -> dict:
    key_of = jax.random.split(jax.random.key(seed), 10)
    return {
        "grad_latent": centred(key_of[0], (CLIPS, FRAMES, ROWS, COLS, CH), 1.0, 6.0, ((0, 4), (1, 2), (2, 4))),
        "input_one": centred(key_of[1], (CLIPS, FRAMES, ROWS, COLS, CH), 1.0, 6.0, ((0, 4), (1, 2), (2, 4))),
        "preact_one": centred(key_of[2], (CLIPS, FRAMES, ROWS, COLS, CH), 2.0, 8.0, ((0, 4), (1, 2), (2, 4))),
        "input_two": centred(key_of[3], (CLIPS, FRAMES, ROWS, COLS, CH), 1.0, 6.0, ((0, 4), (1, 2), (2, 4))),
        "preact_two": centred(key_of[4], (CLIPS, FRAMES, ROWS, COLS, CH), 2.0, 8.0, ((0, 4), (1, 2), (2, 4))),
        "spatial_one": centred(key_of[5], (3, 3, CH, CH), (9 * CH) ** -0.5, 0.1875),
        "temporal_one": centred(key_of[6], (3, CH, CH), (3 * CH) ** -0.5, 0.3125),
        "spatial_two": centred(key_of[7], (3, 3, CH, CH), (9 * CH) ** -0.5, 0.1875),
        "temporal_two": centred(key_of[8], (3, CH, CH), (3 * CH) ** -0.5, 0.3125),
    }


def spatial_conv(field, kernel):
    return lax.conv_general_dilated(field, kernel, (1, 1), 'SAME', dimension_numbers=('NHWC', 'HWIO', 'NHWC'), precision=lax.Precision.HIGHEST)

def temporal_back(grad_out, act, kernel):
    frames = grad_out.shape[0]
    gz = grad_out.astype(jnp.float32)
    av = act.astype(jnp.float32)
    kf = kernel.astype(jnp.float32)
    gpad = jnp.pad(gz, ((0, 2), (0, 0), (0, 0), (0, 0)))
    apad = jnp.pad(av, ((2, 0), (0, 0), (0, 0), (0, 0)))
    gact = jnp.zeros(gz.shape, jnp.float32)
    kgrads = []
    for k in range(3):
        gact = gact + jnp.einsum('thwo,io->thwi', gpad[2 - k:2 - k + frames], kf[k], precision=lax.Precision.HIGHEST)
        kgrads.append(jnp.einsum('thwi,thwo->io', apad[k:k + frames], gz, precision=lax.Precision.HIGHEST))
    return (gact.astype(jnp.bfloat16), jnp.stack(kgrads))

def block_back(grad_out, saved_in, preact, spatial, temporal):
    hval = preact.astype(jnp.float32)
    sig = jax.nn.sigmoid(hval)
    act = (hval * sig).astype(jnp.bfloat16)
    gact, kgrad_t = temporal_back(grad_out, act, temporal)
    gpre = (gact.astype(jnp.float32) * sig * (1.0 + hval * (1.0 - sig))).astype(jnp.bfloat16)
    _, pullback = jax.vjp(spatial_conv, saved_in.astype(jnp.float32), spatial.astype(jnp.float32))
    gin, kgrad_s = pullback(gpre.astype(jnp.float32))
    grad_in = (grad_out.astype(jnp.float32) + gin).astype(jnp.bfloat16)
    return (grad_in, kgrad_s, kgrad_t)

def one_clip(items, spatial_one, temporal_one, spatial_two, temporal_two):
    grad_latent, input_one, preact_one, input_two, preact_two = items
    grad_mid, gs2, gt2 = block_back(grad_latent, input_two, preact_two, spatial_two, temporal_two)
    grad_in, gs1, gt1 = block_back(grad_mid, input_one, preact_one, spatial_one, temporal_one)
    return (grad_in, gs1, gt1, gs2, gt2)

def reference(grad_latent, input_one, preact_one, input_two, preact_two, spatial_one, temporal_one, spatial_two, temporal_two):

    def step(items):
        return one_clip(items, spatial_one, temporal_one, spatial_two, temporal_two)
    grad_in, gs1, gt1, gs2, gt2 = lax.map(step, (grad_latent, input_one, preact_one, input_two, preact_two))
    scale = 1.0 / jnp.sqrt(jnp.float32(CLIPS * FRAMES * ROWS * COLS))
    return (grad_in, scale * lax.optimization_barrier(jnp.sum(gs1, axis=0)), scale * lax.optimization_barrier(jnp.sum(gt1, axis=0)), scale * lax.optimization_barrier(jnp.sum(gs2, axis=0)), scale * lax.optimization_barrier(jnp.sum(gt2, axis=0)))
```

```python
import functools
import math

import jax
import jax.numpy as jnp
from jax import lax
from jax.experimental import pallas as pl
from jax.experimental.pallas import tpu as pltpu
from jax.sharding import PartitionSpec as P

AXES = ("section", "video", "dp")
VMEM_LIMIT = 24 * 1024 * 1024


def sigmoid(value):
    return 1.0 / (1.0 + jnp.exp(-value))


def from_ahead(block, band_step, frame_step):
    bands, frames = lax.axis_size("section"), lax.axis_size("video")
    pairs = [
        ((band + band_step) * frames + frame + frame_step, band * frames + frame)
        for band in range(bands)
        for frame in range(frames)
        if 0 <= band + band_step < bands and frame + frame_step < frames
    ]
    return lax.ppermute(block, ("section", "video"), pairs)


def beside(gpre, views_ref, start):
    count, cols, ch = gpre.shape
    at = lax.broadcasted_iota(jnp.int32, gpre.shape, 1)
    right = jnp.where(at == cols - 1, 0.0, pltpu.roll(gpre, cols - 1, 1))
    left = jnp.where(at == 0, 0.0, pltpu.roll(gpre, 1, 1))
    here = pl.ds(start, count)
    views_ref[here, :, 0:ch] = right.astype(jnp.bfloat16)
    views_ref[here, :, ch : 2 * ch] = gpre.astype(jnp.bfloat16)
    views_ref[here, :, 2 * ch : 3 * ch] = left.astype(jnp.bfloat16)


def pre_gradient(grads, preact, temporal_ref):
    count, cols, ch = preact.shape
    flat = jnp.concatenate([grad.reshape(count * cols, ch) for grad in grads], axis=1)
    kernel = jnp.concatenate([temporal_ref[2 - step] for step in range(len(grads))], axis=1)
    gact = lax.dot_general(
        flat, kernel, (((1,), (1,)), ((), ())), preferred_element_type=jnp.float32
    )
    gact = gact.astype(jnp.bfloat16).astype(jnp.float32).reshape(preact.shape)
    hval = preact.astype(jnp.float32)
    sig = sigmoid(hval)
    return gact * sig * (1.0 + hval * (1.0 - sig))


def convolved(views_ref, spatial_ref, base, start, count, first):
    cols, width = views_ref.shape[1], views_ref.shape[2]
    total = first
    for ky in range(3):
        view = views_ref[pl.ds(start + base - ky, count)].reshape(count * cols, width)
        kernel = jnp.concatenate([spatial_ref[ky, kx] for kx in range(3)], axis=1)
        total = total + lax.dot_general(
            view, kernel, (((1,), (1,)), ((), ())), preferred_element_type=jnp.float32
        )
    return total


def spatial_sums(saved_t, views_ref, base, rows, out_ref):
    cols, width = views_ref.shape[1], views_ref.shape[2]
    ch = width // 3
    for ky in range(3):
        view = views_ref[base - ky : base - ky + rows].reshape(rows * cols, width)
        sums = jnp.dot(saved_t, view, preferred_element_type=jnp.float32).astype(jnp.bfloat16)
        for kx in range(3):
            out_ref[pl.ds((3 * ky + kx) * ch, ch), :] = sums[:, kx * ch : (kx + 1) * ch]


def temporal_sums(act_t, grads, out_ref):
    pixels, ch = grads[0].shape
    sums = jnp.dot(
        act_t, jnp.concatenate(grads, axis=1), preferred_element_type=jnp.float32
    ).astype(jnp.bfloat16)
    for k in range(3):
        step = 2 - k
        here = pl.ds((9 + k) * ch, ch)
        if step < len(grads):
            out_ref[here, :] = sums[:, step * ch : (step + 1) * ch]
        else:
            out_ref[here, :] = jnp.zeros((ch, ch), jnp.bfloat16)


def mid_kernel(later, *refs):
    grad_ref, preact_ref, low_ref, high_ref = refs[:4]
    later_refs = refs[4 : 4 + 3 * later]
    temporal_ref, spatial_ref, mid_ref, gpre_ref, views_ref = refs[4 + 3 * later :]
    rows, cols, ch = grad_ref.shape

    def part(first, preact, grads):
        gpre = pre_gradient(grads, preact, temporal_ref)
        gpre_ref[pl.ds(first, preact.shape[0])] = gpre.astype(jnp.bfloat16)
        beside(gpre, views_ref, first)

    part(0, low_ref[2:4], [low_ref[0:2]] + [later_refs[3 * n + 1][...] for n in range(later)])
    part(
        rows + 2,
        high_ref[2:4],
        [high_ref[0:2]] + [later_refs[3 * n + 2][...] for n in range(later)],
    )

    step = 4

    @pl.loop(0, rows // step)
    def _(n):
        here = pl.ds(n * step, step)
        part(
            n * step + 2,
            preact_ref[here],
            [grad_ref[here]] + [later_refs[3 * m][here] for m in range(later)],
        )

    def mid(first, start, count):
        total = convolved(
            views_ref,
            spatial_ref,
            2,
            start,
            count,
            first.astype(jnp.float32).reshape(count * cols, ch),
        )
        mid_ref[pl.ds(start, count)] = total.astype(jnp.bfloat16).reshape(count, cols, ch)

    mid(low_ref[1:2], 0, 1)
    mid(high_ref[0:1], rows + 1, 1)

    @pl.loop(0, rows // step)
    def _(n):
        mid(grad_ref[pl.ds(n * step, step)], n * step + 1, step)


def sums_kernel(later, *refs):
    saved_ref, preact_ref, gpre_ref, grad_ref = refs[:4]
    later_refs = refs[4 : 4 + later]
    out_ref, views_ref, act_ref = refs[4 + later :]
    rows, cols, ch = saved_ref.shape
    step = 4

    @pl.loop(0, gpre_ref.shape[0] // step)
    def _(n):
        beside(gpre_ref[pl.ds(n * step, step)].astype(jnp.float32), views_ref, n * step)

    @pl.loop(0, rows // step)
    def _(n):
        here = pl.ds(n * step, step)
        hval = preact_ref[here].astype(jnp.float32)
        act_ref[here] = (hval * sigmoid(hval)).astype(jnp.bfloat16)

    flat = (rows * cols, ch)
    spatial_sums(saved_ref[...].reshape(flat).T, views_ref, 3, rows, out_ref)
    grads = [grad_ref[...].reshape(flat)] + [ref[...].reshape(flat) for ref in later_refs]
    temporal_sums(act_ref[...].reshape(flat).T, grads, out_ref)


def first_kernel(later, bands, *refs):
    saved_ref, preact_ref, low_ref, high_ref, mid_ref = refs[:5]
    later_refs = refs[5 : 5 + later]
    temporal_ref, gpre_ref, out_ref, views_ref, act_ref = refs[5 + later :]
    rows, cols, ch = saved_ref.shape
    band = lax.axis_index("section")
    mids = [mid_ref] + list(later_refs)

    def part(first, preact, inside):
        here = pl.ds(first, preact.shape[0])
        gpre = pre_gradient([ref[here] for ref in mids], preact, temporal_ref)
        if inside is not None:
            gpre = jnp.where(inside, gpre, 0.0)
        gpre_ref[here] = gpre.astype(jnp.bfloat16)
        beside(gpre, views_ref, first)

    part(0, low_ref[4:5], band > 0)
    part(rows + 1, high_ref[4:5], band < bands - 1)
    step = 4

    @pl.loop(0, rows // step)
    def _(n):
        here = pl.ds(n * step, step)
        part(n * step + 1, preact_ref[here], None)
        hval = preact_ref[here].astype(jnp.float32)
        act_ref[here] = (hval * sigmoid(hval)).astype(jnp.bfloat16)

    flat = (rows * cols, ch)
    spatial_sums(saved_ref[...].reshape(flat).T, views_ref, 2, rows, out_ref)
    grads = [ref[1 : rows + 1].reshape(flat) for ref in mids]
    temporal_sums(act_ref[...].reshape(flat).T, grads, out_ref)


def input_kernel(mid_ref, gpre_ref, spatial_ref, out_ref, views_ref):
    rows, cols, ch = out_ref.shape
    step = 6 if gpre_ref.shape[0] % 6 == 0 else 1

    @pl.loop(0, gpre_ref.shape[0] // step)
    def _(n):
        beside(gpre_ref[pl.ds(n * step, step)].astype(jnp.float32), views_ref, n * step)

    step = 4

    @pl.loop(0, rows // step)
    def _(n):
        first = mid_ref[pl.ds(n * step + 1, step)].astype(jnp.float32)
        total = convolved(
            views_ref, spatial_ref, 2, n * step, step, first.reshape(step * cols, ch)
        )
        out_ref[pl.ds(n * step, step)] = total.astype(jnp.bfloat16).reshape(step, cols, ch)


def total_kernel(factor, parts_ref, out_ref):
    total = parts_ref[0].astype(jnp.float32)
    for n in range(1, parts_ref.shape[0]):
        total = total + parts_ref[n].astype(jnp.float32)
    total = (total * factor).astype(jnp.bfloat16)
    for n in range(out_ref.shape[0]):
        out_ref[n] = total


def call(kernel, outs, scratch, flops, *operands):
    single = len(outs) == 1
    moved = sum(math.prod(x.shape) * x.dtype.itemsize for x in (*operands, *outs))
    return pl.pallas_call(
        kernel,
        out_shape=outs[0] if single else tuple(outs),
        in_specs=[pl.BlockSpec(memory_space=pltpu.VMEM)] * len(operands),
        out_specs=pl.BlockSpec(memory_space=pltpu.VMEM)
        if single
        else tuple(pl.BlockSpec(memory_space=pltpu.VMEM) for _ in outs),
        scratch_shapes=scratch,
        compiler_params=pltpu.CompilerParams(vmem_limit_bytes=VMEM_LIMIT),
        cost_estimate=pl.CostEstimate(
            flops=int(flops), bytes_accessed=int(moved), transcendentals=0
        ),
    )(*operands)


def bf16(*shape):
    return jax.ShapeDtypeStruct(shape, jnp.bfloat16)


def summed(parts, factor):
    height, width = parts.shape
    axes, count = [], 1
    for axis in AXES:
        if height % (16 * count * lax.axis_size(axis)) == 0:
            axes.append(axis)
            count *= lax.axis_size(axis)
    rest = tuple(axis for axis in AXES if axis not in axes)
    axes = tuple(axes)
    mine = lax.all_to_all(parts, axes, split_axis=0, concat_axis=0, tiled=True)
    mine = mine.reshape(count, height // count, width)
    if rest:
        total = lax.psum(jnp.sum(mine.astype(jnp.float32), axis=0), rest)
        total = (total * factor).astype(jnp.bfloat16)
        return lax.all_gather(total, axes, axis=0, tiled=True)
    spread = call(
        functools.partial(total_kernel, factor), [bf16(*mine.shape)], [], parts.size, mine
    )
    spread = spread.reshape(height, width)
    return lax.all_to_all(spread, axes, split_axis=0, concat_axis=0, tiled=True)


def on_device(
    grad_latent,
    input_one,
    preact_one,
    input_two,
    preact_two,
    spatial_one,
    temporal_one,
    spatial_two,
    temporal_two,
):
    shape = grad_latent.shape
    rows, cols, ch = shape[2:]
    bands, frames = lax.axis_size("section"), lax.axis_size("video")
    later = min(2, frames - 1)
    pixels = lax.axis_size("dp") * frames * bands * rows * cols
    factor = 1.0 / math.sqrt(pixels)
    grad, saved_one, pre_one, saved_two, pre_two = (
        x.reshape(rows, cols, ch)
        for x in (grad_latent, input_one, preact_one, input_two, preact_two)
    )

    tail, head = grad[rows - 2 :], grad[:2]
    ahead = [[from_ahead(grad, 0, n + 1)] for n in range(later)]
    low = from_ahead(jnp.concatenate([tail, pre_two[rows - 2 :], pre_one[rows - 1 :]]), -1, 0)
    high = from_ahead(jnp.concatenate([head, pre_two[:2], pre_one[:1]]), 1, 0)
    for n in range(later):
        ahead[n].append(from_ahead(tail, -1, n + 1))
        ahead[n].append(from_ahead(head, 1, n + 1))

    area = rows * cols
    conv = 2 * area * 9 * ch * ch
    mid, gpre_two = call(
        functools.partial(mid_kernel, later),
        [bf16(rows + 2, cols, ch), bf16(rows + 4, cols, ch)],
        [pltpu.VMEM((rows + 4, cols, 3 * ch), jnp.bfloat16)],
        2 * conv,
        grad,
        pre_two,
        low,
        high,
        *[x for group in ahead for x in group],
        temporal_two,
        spatial_two,
    )
    mids = [from_ahead(mid, 0, n + 1) for n in range(later)]
    parts_two = call(
        functools.partial(sums_kernel, later),
        [bf16(12 * ch, ch)],
        [
            pltpu.VMEM((rows + 4, cols, 3 * ch), jnp.bfloat16),
            pltpu.VMEM((rows, cols, ch), jnp.bfloat16),
        ],
        2 * conv,
        saved_two,
        pre_two,
        gpre_two,
        grad,
        *[group[0] for group in ahead],
    )
    sums_two = summed(parts_two, factor)
    gpre_one, parts_one = call(
        functools.partial(first_kernel, later, bands),
        [bf16(rows + 2, cols, ch), bf16(12 * ch, ch)],
        [
            pltpu.VMEM((rows + 2, cols, 3 * ch), jnp.bfloat16),
            pltpu.VMEM((rows, cols, ch), jnp.bfloat16),
        ],
        3 * conv,
        saved_one,
        pre_one,
        low,
        high,
        mid,
        *mids,
        temporal_one,
    )
    sums_one = summed(parts_one, factor)
    grad_in = call(
        input_kernel,
        [bf16(rows, cols, ch)],
        [pltpu.VMEM((rows + 2, cols, 3 * ch), jnp.bfloat16)],
        2 * conv,
        mid,
        gpre_one,
        spatial_one,
    )

    def split(sums):
        sums = sums.astype(jnp.float32).reshape(12, ch, ch)
        return sums[:9].reshape(3, 3, ch, ch), sums[9:]

    gs_one, gt_one = split(sums_one)
    gs_two, gt_two = split(sums_two)
    return (grad_in.reshape(shape), gs_one, gt_one, gs_two, gt_two)


def solution(mesh):
    whole = P("dp", "video", "section", None, None)
    return jax.shard_map(
        on_device,
        mesh=mesh,
        in_specs=(whole,) * 5 + (P(),) * 4,
        out_specs=(whole, P(), P(), P(), P()),
        check_vma=False,
    )
```

```python
import functools
import math

import jax
import jax.numpy as jnp
from jax import lax
from jax.experimental import pallas as pl
from jax.experimental.pallas import tpu as pltpu
from jax.sharding import PartitionSpec as P

AXES = ("section", "video", "dp")
VMEM_LIMIT = 24 * 1024 * 1024


def sigmoid(value):
    return 1.0 / (1.0 + jnp.exp(-value))


def from_ahead(block, band_step, frame_step):
    bands, frames = lax.axis_size("section"), lax.axis_size("video")
    pairs = [
        ((band + band_step) * frames + frame + frame_step, band * frames + frame)
        for band in range(bands)
        for frame in range(frames)
        if 0 <= band + band_step < bands and frame + frame_step < frames
    ]
    return lax.ppermute(block, ("section", "video"), pairs)


def beside(gpre, views_ref, start):
    count, cols, ch = gpre.shape
    at = lax.broadcasted_iota(jnp.int32, gpre.shape, 1)
    right = jnp.where(at == cols - 1, 0.0, pltpu.roll(gpre, cols - 1, 1))
    left = jnp.where(at == 0, 0.0, pltpu.roll(gpre, 1, 1))
    here = pl.ds(start, count)
    views_ref[here, :, 0:ch] = right.astype(jnp.bfloat16)
    views_ref[here, :, ch : 2 * ch] = gpre.astype(jnp.bfloat16)
    views_ref[here, :, 2 * ch : 3 * ch] = left.astype(jnp.bfloat16)


def pre_gradient(grads, preact, temporal_ref):
    count, cols, ch = preact.shape
    flat = jnp.concatenate([grad.reshape(count * cols, ch) for grad in grads], axis=1)
    kernel = jnp.concatenate([temporal_ref[2 - step] for step in range(len(grads))], axis=1)
    gact = lax.dot_general(
        flat, kernel, (((1,), (1,)), ((), ())), preferred_element_type=jnp.float32
    )
    gact = gact.astype(jnp.bfloat16).astype(jnp.float32).reshape(preact.shape)
    hval = preact.astype(jnp.float32)
    sig = sigmoid(hval)
    return gact * sig * (1.0 + hval * (1.0 - sig))


def convolved(views_ref, spatial_ref, base, start, count, first):
    cols, width = views_ref.shape[1], views_ref.shape[2]
    total = first
    for ky in range(3):
        view = views_ref[pl.ds(start + base - ky, count)].reshape(count * cols, width)
        kernel = jnp.concatenate([spatial_ref[ky, kx] for kx in range(3)], axis=1)
        total = total + lax.dot_general(
            view, kernel, (((1,), (1,)), ((), ())), preferred_element_type=jnp.float32
        )
    return total


def spatial_sums(saved_t, views_ref, base, rows, out_ref):
    cols, width = views_ref.shape[1], views_ref.shape[2]
    ch = width // 3
    for ky in range(3):
        view = views_ref[base - ky : base - ky + rows].reshape(rows * cols, width)
        sums = jnp.dot(saved_t, view, preferred_element_type=jnp.float32).astype(jnp.bfloat16)
        for kx in range(3):
            out_ref[pl.ds((3 * ky + kx) * ch, ch), :] = sums[:, kx * ch : (kx + 1) * ch]


def temporal_sums(act_t, grads, out_ref):
    pixels, ch = grads[0].shape
    sums = jnp.dot(
        act_t, jnp.concatenate(grads, axis=1), preferred_element_type=jnp.float32
    ).astype(jnp.bfloat16)
    for k in range(3):
        step = 2 - k
        here = pl.ds((9 + k) * ch, ch)
        if step < len(grads):
            out_ref[here, :] = sums[:, step * ch : (step + 1) * ch]
        else:
            out_ref[here, :] = jnp.zeros((ch, ch), jnp.bfloat16)


def middle(refs, laters, temporal_ref, spatial_ref, mid_ref, gpre_ref, views_ref):
    grad_ref, preact_ref, low_ref, high_ref = refs
    rows, cols, ch = grad_ref.shape

    def part(first, preact, grads):
        gpre = pre_gradient(grads, preact, temporal_ref)
        gpre_ref[pl.ds(first, preact.shape[0])] = gpre.astype(jnp.bfloat16)
        beside(gpre, views_ref, first)

    part(0, low_ref[2:4], [low_ref[0:2]] + [edge[0:2] for _, edge in laters])
    part(rows + 2, high_ref[2:4], [high_ref[0:2]] + [edge[2:4] for _, edge in laters])

    step = 4

    @pl.loop(0, rows // step)
    def _(n):
        here = pl.ds(n * step, step)
        grads = [grad_ref[here]] + [whole[here] for whole, _ in laters]
        part(n * step + 2, preact_ref[here], grads)

    def mid(first, start, count):
        total = convolved(
            views_ref,
            spatial_ref,
            2,
            start,
            count,
            first.astype(jnp.float32).reshape(count * cols, ch),
        )
        mid_ref[pl.ds(start, count)] = total.astype(jnp.bfloat16).reshape(count, cols, ch)

    mid(low_ref[1:2], 0, 1)
    mid(high_ref[0:1], rows + 1, 1)

    @pl.loop(0, rows // step)
    def _(n):
        mid(grad_ref[pl.ds(n * step, step)], n * step + 1, step)


def pack_kernel(*refs):
    parts, (up_ref, down_ref) = refs[:6], refs[6:]
    up_ref[0:2], up_ref[2:4], up_ref[4:5] = (part[...] for part in parts[:3])
    down_ref[0:2], down_ref[2:4], down_ref[4:5] = (part[...] for part in parts[3:])


def last_kernel(*refs):
    inputs, kernels, outs = refs[:4], refs[4:6], refs[6:]
    mid_ref, gpre_ref, edge_ref, views_ref = outs

    @pl.when(lax.axis_index("video") == lax.axis_size("video") - 1)
    def _():
        edge_ref[0:2] = inputs[2][0:2]
        edge_ref[2:4] = inputs[3][0:2]
        middle(inputs, [], *kernels, mid_ref, gpre_ref, views_ref)


def mid_kernel(later, *refs):
    inputs, refs = refs[:4], refs[4:]
    laters, refs = [refs[2 * n : 2 * n + 2] for n in range(later)], refs[2 * later :]
    kernels, refs = refs[:2], refs[2:]
    if len(refs) == 3:
        middle(inputs, laters, *kernels, *refs)
        return
    known, (mid_ref, gpre_ref, views_ref) = refs[:2], refs[2:]
    last = lax.axis_index("video") == lax.axis_size("video") - 1

    @pl.when(last)
    def _():
        mid_ref[...] = known[0][...]
        gpre_ref[...] = known[1][...]

    @pl.when(jnp.logical_not(last))
    def _():
        middle(inputs, laters, *kernels, mid_ref, gpre_ref, views_ref)


def sums_kernel(later, *refs):
    saved_ref, preact_ref, gpre_ref, grad_ref = refs[:4]
    later_refs = refs[4 : 4 + later]
    out_ref, views_ref, act_ref = refs[4 + later :]
    rows, cols, ch = saved_ref.shape
    step = 4

    @pl.loop(0, gpre_ref.shape[0] // step)
    def _(n):
        beside(gpre_ref[pl.ds(n * step, step)].astype(jnp.float32), views_ref, n * step)

    @pl.loop(0, rows // step)
    def _(n):
        here = pl.ds(n * step, step)
        hval = preact_ref[here].astype(jnp.float32)
        act_ref[here] = (hval * sigmoid(hval)).astype(jnp.bfloat16)

    flat = (rows * cols, ch)
    spatial_sums(saved_ref[...].reshape(flat).T, views_ref, 3, rows, out_ref)
    grads = [grad_ref[...].reshape(flat)] + [ref[...].reshape(flat) for ref in later_refs]
    temporal_sums(act_ref[...].reshape(flat).T, grads, out_ref)


def first_kernel(later, bands, *refs):
    saved_ref, preact_ref, low_ref, high_ref, mid_ref = refs[:5]
    later_refs = refs[5 : 5 + later]
    temporal_ref, gpre_ref, out_ref, views_ref, act_ref = refs[5 + later :]
    rows, cols, ch = saved_ref.shape
    band = lax.axis_index("section")
    mids = [mid_ref] + list(later_refs)

    def part(first, preact, inside):
        here = pl.ds(first, preact.shape[0])
        gpre = pre_gradient([ref[here] for ref in mids], preact, temporal_ref)
        if inside is not None:
            gpre = jnp.where(inside, gpre, 0.0)
        gpre_ref[here] = gpre.astype(jnp.bfloat16)
        beside(gpre, views_ref, first)

    part(0, low_ref[4:5], band > 0)
    part(rows + 1, high_ref[4:5], band < bands - 1)
    step = 4

    @pl.loop(0, rows // step)
    def _(n):
        here = pl.ds(n * step, step)
        part(n * step + 1, preact_ref[here], None)
        hval = preact_ref[here].astype(jnp.float32)
        act_ref[here] = (hval * sigmoid(hval)).astype(jnp.bfloat16)

    flat = (rows * cols, ch)
    spatial_sums(saved_ref[...].reshape(flat).T, views_ref, 2, rows, out_ref)
    grads = [ref[1 : rows + 1].reshape(flat) for ref in mids]
    temporal_sums(act_ref[...].reshape(flat).T, grads, out_ref)


def input_kernel(mid_ref, gpre_ref, spatial_ref, out_ref, views_ref):
    rows, cols, ch = out_ref.shape
    step = 6 if gpre_ref.shape[0] % 6 == 0 else 1

    @pl.loop(0, gpre_ref.shape[0] // step)
    def _(n):
        beside(gpre_ref[pl.ds(n * step, step)].astype(jnp.float32), views_ref, n * step)

    step = 4

    @pl.loop(0, rows // step)
    def _(n):
        first = mid_ref[pl.ds(n * step + 1, step)].astype(jnp.float32)
        total = convolved(
            views_ref, spatial_ref, 2, n * step, step, first.reshape(step * cols, ch)
        )
        out_ref[pl.ds(n * step, step)] = total.astype(jnp.bfloat16).reshape(step, cols, ch)


def pair_kernel(one_ref, two_ref, out_ref):
    height = out_ref.shape[2]

    @pl.loop(0, out_ref.shape[0])
    def _(n):
        here = pl.ds(pl.multiple_of(n * height, height), height)
        for block, ref in enumerate((one_ref, two_ref)):
            total = ref[0, here].astype(jnp.float32)
            for part in range(1, ref.shape[0]):
                total = total + ref[part, here].astype(jnp.float32)
            out_ref[n, block] = total.astype(jnp.bfloat16)


def total_kernel(factor, parts_ref, out_ref):
    total = parts_ref[0].astype(jnp.float32)
    for n in range(1, parts_ref.shape[0]):
        total = total + parts_ref[n].astype(jnp.float32)
    total = (total * factor).astype(jnp.bfloat16)
    for n in range(out_ref.shape[0]):
        out_ref[n] = total


def place_kernel(*refs):
    shares, outs = refs[:4], refs[4:]
    band = lax.axis_index("section")
    height = shares[0].shape[2]
    for flip, share in enumerate(shares):
        place = jnp.bitwise_xor(band, flip)
        for block in range(2):
            spatial_ref, temporal_ref = outs[2 * block : 2 * block + 2]

            @pl.when(place < 3)
            def _():
                for n in range(share.shape[0]):
                    value = share[n, block].astype(jnp.float32)
                    spatial_ref[place, n * height : (n + 1) * height] = value

            @pl.when(place == 3)
            def _():
                for n in range(share.shape[0]):
                    value = share[n, block].astype(jnp.float32)
                    temporal_ref[n * height : (n + 1) * height] = value


def call(kernel, outs, scratch, flops, *operands, grid=(), in_specs=None):
    single = len(outs) == 1
    moved = sum(math.prod(x.shape) * x.dtype.itemsize for x in (*operands, *outs))
    vmem = pl.BlockSpec(memory_space=pltpu.VMEM)
    return pl.pallas_call(
        kernel,
        out_shape=outs[0] if single else tuple(outs),
        grid=grid,
        in_specs=in_specs or [vmem] * len(operands),
        out_specs=vmem if single else (vmem,) * len(outs),
        scratch_shapes=scratch,
        compiler_params=pltpu.CompilerParams(vmem_limit_bytes=VMEM_LIMIT),
        cost_estimate=pl.CostEstimate(
            flops=int(flops), bytes_accessed=int(moved), transcendentals=0
        ),
    )(*operands)


def bf16(*shape):
    return jax.ShapeDtypeStruct(shape, jnp.bfloat16)


def f32(*shape):
    return jax.ShapeDtypeStruct(shape, jnp.float32)


def split(sums, ch):
    sums = sums.astype(jnp.float32).reshape(12, ch, ch)
    return sums[:9].reshape(3, 3, ch, ch), sums[9:]


def band_sums(parts):
    bands = lax.axis_size("section")
    height, ch = parts.shape
    mine = lax.all_to_all(parts, "section", split_axis=0, concat_axis=0, tiled=True)
    return mine.reshape(bands, height // bands, ch)


def totals(one, two, factor):
    bands, height, ch = one.shape
    axes, count = [], 1
    for axis in ("video", "dp"):
        if height % (16 * count * lax.axis_size(axis)) == 0:
            axes.append(axis)
            count *= lax.axis_size(axis)
    rest = tuple(axis for axis in ("video", "dp") if axis not in axes)
    axes = tuple(axes)
    cut = (count, 2, height // count, ch)

    def exchanged(x):
        x = x.reshape(2 * height, ch)
        x = lax.all_to_all(x, axes, split_axis=0, concat_axis=0, tiled=True)
        return x.reshape(cut)

    mine = exchanged(call(pair_kernel, [bf16(*cut)], [], one.size, one, two))
    if rest:
        total = lax.psum(jnp.sum(mine.astype(jnp.float32), axis=0), rest)
        total = (total * factor).astype(jnp.bfloat16)
        spread = jnp.broadcast_to(total, cut)
    else:
        spread = call(functools.partial(total_kernel, factor), [bf16(*cut)], [], one.size, mine)
    share = exchanged(spread)

    def flipped(x, flip):
        pairs = [(band ^ flip, band) for band in range(bands)]
        return lax.ppermute(x, "section", pairs)

    across = flipped(share, 2)
    outs = call(
        place_kernel,
        [f32(3, height, ch), f32(height, ch)] * 2,
        [],
        share.size,
        share,
        flipped(share, 1),
        across,
        flipped(across, 1),
    )
    return [x.reshape(3, 3, ch, ch) if x.ndim == 3 else x.reshape(3, ch, ch) for x in outs]


def on_device(
    grad_latent,
    input_one,
    preact_one,
    input_two,
    preact_two,
    spatial_one,
    temporal_one,
    spatial_two,
    temporal_two,
):
    shape = grad_latent.shape
    rows, cols, ch = shape[2:]
    bands, frames = lax.axis_size("section"), lax.axis_size("video")
    later = min(2, frames - 1)
    pixels = lax.axis_size("dp") * frames * bands * rows * cols
    factor = 1.0 / math.sqrt(pixels)
    grad, saved_one, pre_one, saved_two, pre_two = (
        x.reshape(rows, cols, ch)
        for x in (grad_latent, input_one, preact_one, input_two, preact_two)
    )
    area = rows * cols
    conv = 2 * area * 9 * ch * ch
    views_four = pltpu.VMEM((rows + 4, cols, 3 * ch), jnp.bfloat16)
    views_two = pltpu.VMEM((rows + 2, cols, 3 * ch), jnp.bfloat16)
    acts = pltpu.VMEM((rows, cols, ch), jnp.bfloat16)

    wholes = [from_ahead(grad, 0, n + 1) for n in range(later)]

    def edge_spec(count, last):
        return pl.BlockSpec((count, cols, ch), lambda _: (rows // count - 1 if last else 0, 0, 0))

    counts = (2, 2, 1)
    up, down = call(
        pack_kernel,
        [bf16(5, cols, ch)] * 2,
        [],
        1,
        *(grad, pre_two, pre_one) * 2,
        grid=(1,),
        in_specs=[edge_spec(n, False) for n in counts] + [edge_spec(n, True) for n in counts],
    )
    low = from_ahead(down, -1, 0)
    high = from_ahead(up, 1, 0)
    inputs = (grad, pre_two, low, high)
    kernels = (temporal_two, spatial_two)
    field = [bf16(rows + 2, cols, ch), bf16(rows + 4, cols, ch)]
    known = ()
    if frames == 2:
        *known, edge = call(
            last_kernel,
            field + [bf16(4, cols, ch)],
            [views_four],
            2 * conv,
            *inputs,
            *kernels,
        )
    else:
        edge = jnp.concatenate([low[:2], high[:2]])
    edges = [from_ahead(edge, 0, n + 1) for n in range(later)]
    mids = [from_ahead(known[0], 0, 1)] if known else None
    laters = [x for pair in zip(wholes, edges) for x in pair]
    mid, gpre_two = call(
        functools.partial(mid_kernel, later),
        field,
        [views_four],
        2 * conv,
        *inputs,
        *laters,
        *kernels,
        *known,
    )
    if mids is None:
        mids = [from_ahead(mid, 0, n + 1) for n in range(later)]
    parts_two = call(
        functools.partial(sums_kernel, later),
        [bf16(12 * ch, ch)],
        [views_four, acts],
        2 * conv,
        saved_two,
        pre_two,
        gpre_two,
        grad,
        *wholes,
    )
    shares_two = band_sums(parts_two) if bands == 4 else None
    gpre_one, parts_one = call(
        functools.partial(first_kernel, later, bands),
        [bf16(rows + 2, cols, ch), bf16(12 * ch, ch)],
        [views_two, acts],
        3 * conv,
        saved_one,
        pre_one,
        low,
        high,
        mid,
        *mids,
        temporal_one,
    )
    if bands == 4:
        sums = totals(band_sums(parts_one), shares_two, factor)
    else:
        whole = lax.psum((parts_one.astype(jnp.float32), parts_two.astype(jnp.float32)), AXES)
        sums = [x for total in whole for x in split(factor * total, ch)]
    grad_in = call(
        input_kernel,
        [bf16(rows, cols, ch)],
        [views_two],
        2 * conv,
        mid,
        gpre_one,
        spatial_one,
    )
    return (grad_in.reshape(shape), *sums)


def solution(mesh):
    whole = P("dp", "video", "section", None, None)
    return jax.shard_map(
        on_device,
        mesh=mesh,
        in_specs=(whole,) * 5 + (P(),) * 4,
        out_specs=(whole, P(), P(), P(), P()),
        check_vma=False,
    )
```

```python
import functools
import math

import jax
import jax.numpy as jnp
from jax import lax
from jax.experimental import pallas as pl
from jax.experimental.pallas import tpu as pltpu
from jax.sharding import PartitionSpec as P

MIB = 1024 * 1024


def sigmoid(value):
    return 1.0 / (1.0 + jnp.exp(-value))


def bf16(*shape):
    return jax.ShapeDtypeStruct(shape, jnp.bfloat16)


def f32(*shape):
    return jax.ShapeDtypeStruct(shape, jnp.float32)


def call(kernel, outs, scratch, flops, *operands, grid=(), in_specs=None, limit=24):
    single = len(outs) == 1
    moved = sum(math.prod(x.shape) * x.dtype.itemsize for x in (*operands, *outs))
    vmem = pl.BlockSpec(memory_space=pltpu.VMEM)
    return pl.pallas_call(
        kernel,
        out_shape=outs[0] if single else tuple(outs),
        grid=grid,
        in_specs=in_specs or [vmem] * len(operands),
        out_specs=vmem if single else (vmem,) * len(outs),
        scratch_shapes=scratch,
        compiler_params=pltpu.CompilerParams(vmem_limit_bytes=limit * MIB),
        cost_estimate=pl.CostEstimate(
            flops=int(flops), bytes_accessed=int(moved), transcendentals=0
        ),
    )(*operands)


def from_ahead(block, band_step, frame_step):
    bands, frames = lax.axis_size("section"), lax.axis_size("video")
    pairs = [
        ((band + band_step) * frames + frame + frame_step, band * frames + frame)
        for band in range(bands)
        for frame in range(frames)
        if 0 <= band + band_step < bands and frame + frame_step < frames
    ]
    return lax.ppermute(block, ("section", "video"), pairs)


def flipped(block, axis, flip):
    count = lax.axis_size(axis)
    return lax.ppermute(block, axis, [(place ^ flip, place) for place in range(count)])


def beside(gpre, views_ref, start):
    count, cols, ch = gpre.shape
    at = lax.broadcasted_iota(jnp.int32, gpre.shape, 1)
    right = jnp.where(at == cols - 1, 0.0, pltpu.roll(gpre, cols - 1, 1))
    left = jnp.where(at == 0, 0.0, pltpu.roll(gpre, 1, 1))
    here = pl.ds(start, count)
    views_ref[here, :, 0:ch] = right.astype(jnp.bfloat16)
    views_ref[here, :, ch : 2 * ch] = gpre.astype(jnp.bfloat16)
    views_ref[here, :, 2 * ch : 3 * ch] = left.astype(jnp.bfloat16)


def pre_gradient(grads, preact, temporal_ref):
    count, cols, ch = preact.shape
    flat = jnp.concatenate([grad.reshape(count * cols, ch) for grad in grads], axis=1)
    kernel = jnp.concatenate([temporal_ref[2 - step] for step in range(len(grads))], axis=1)
    gact = lax.dot_general(
        flat, kernel, (((1,), (1,)), ((), ())), preferred_element_type=jnp.float32
    )
    gact = gact.astype(jnp.bfloat16).astype(jnp.float32).reshape(preact.shape)
    hval = preact.astype(jnp.float32)
    sig = sigmoid(hval)
    return gact * sig * (1.0 + hval * (1.0 - sig))


def convolved(views_ref, spatial_ref, start, first):
    count, cols, ch = first.shape
    total = first.astype(jnp.float32).reshape(count * cols, ch)
    for ky in range(3):
        view = views_ref[pl.ds(start + 2 - ky, count)].reshape(count * cols, 3 * ch)
        kernel = jnp.concatenate([spatial_ref[ky, kx] for kx in range(3)], axis=1)
        total = total + lax.dot_general(
            view, kernel, (((1,), (1,)), ((), ())), preferred_element_type=jnp.float32
        )
    return total.astype(jnp.bfloat16).reshape(first.shape)


def kernel_sums(saved_ref, above, below, act, grads, views, sums_ref):
    rows, cols, ch = saved_ref.shape
    flat = (rows * cols, ch)
    saved = [
        jnp.concatenate([above, saved_ref[: rows - 1]], axis=0),
        saved_ref[...],
        jnp.concatenate([saved_ref[1:], below], axis=0),
    ]
    for ky in range(3):
        sums = jnp.dot(saved[ky].reshape(flat).T, views, preferred_element_type=jnp.float32)
        for kx in range(3):
            sums_ref[ky, kx * ch : (kx + 1) * ch] = sums[:, kx * ch : (kx + 1) * ch]
    sums = jnp.dot(
        act.reshape(flat).T,
        jnp.concatenate([grad.reshape(flat) for grad in grads], axis=1),
        preferred_element_type=jnp.float32,
    )
    for k in range(3):
        step = 2 - k
        here = slice(k * ch, (k + 1) * ch)
        if step < len(grads):
            sums_ref[3, here] = sums[:, step * ch : (step + 1) * ch]
        else:
            sums_ref[3, here] = jnp.zeros((ch, ch), jnp.float32)


def hand_out(sums_ref, outs):
    band = lax.axis_index("section")
    outs[0][...] = sums_ref[band]
    for flip in range(1, 4):
        outs[flip][...] = sums_ref[jnp.bitwise_xor(band, flip)].astype(jnp.bfloat16)


def pack_kernel(*refs):
    parts, (up_ref, down_ref) = refs[:8], refs[8:]
    for n in range(4):
        up_ref[n : n + 1] = parts[n][...]
        down_ref[n : n + 1] = parts[n + 4][...]


def interior(grad_ref, preact_ref, wholes, temporal_ref, spatial_ref, inner_ref, gpre_ref, views_ref):
    rows, cols, ch = grad_ref.shape
    step = 4

    @pl.loop(0, rows // step)
    def _(n):
        here = pl.ds(n * step, step)
        grads = [ref[here] for ref in (grad_ref, *wholes)]
        gpre = pre_gradient(grads, preact_ref[here], temporal_ref)
        gpre_ref[here] = gpre.astype(jnp.bfloat16)
        beside(gpre, views_ref, n * step)

    half = rows // 2 - 1

    @pl.loop(0, 2)
    def _(n):
        first = grad_ref[pl.ds(n * half + 1, half)]
        inner_ref[pl.ds(n * half, half)] = convolved(views_ref, spatial_ref, n * half, first)


def edge_rows(grad_ref, low_ref, high_ref, afters, gpre_ref, temporal_ref, spatial_ref, views_ref):
    rows, cols, ch = grad_ref.shape
    above = [low_ref[0:1]] + [ref[2:3] for ref in afters]
    below = [high_ref[0:1]] + [ref[3:4] for ref in afters]
    beside(pre_gradient(above, low_ref[1:2], temporal_ref), views_ref, 0)
    beside(gpre_ref[0:2].astype(jnp.float32), views_ref, 1)
    beside(gpre_ref[rows - 2 : rows].astype(jnp.float32), views_ref, 3)
    beside(pre_gradient(below, high_ref[1:2], temporal_ref), views_ref, 5)
    return (
        convolved(views_ref, spatial_ref, 0, grad_ref[0:1]),
        convolved(views_ref, spatial_ref, 3, grad_ref[rows - 1 : rows]),
    )


def on_last(body):
    pl.when(lax.axis_index("video") == lax.axis_size("video") - 1)(body)


def last_inner_kernel(grad_ref, preact_ref, temporal_ref, spatial_ref, inner_ref, gpre_ref, views_ref):
    on_last(
        lambda: interior(
            grad_ref, preact_ref, [], temporal_ref, spatial_ref, inner_ref, gpre_ref, views_ref
        )
    )


def last_edge_kernel(grad_ref, low_ref, high_ref, gpre_ref, temporal_ref, spatial_ref, edge_ref, views_ref):
    def body():
        edge_ref[0:1], edge_ref[1:2] = edge_rows(
            grad_ref, low_ref, high_ref, [], gpre_ref, temporal_ref, spatial_ref, views_ref
        )
        edge_ref[2:3] = low_ref[0:1]
        edge_ref[3:4] = high_ref[0:1]

    on_last(body)


def inner_kernel(later, *refs):
    inputs, wholes, kernels = refs[:2], refs[2 : 2 + later], refs[2 + later : 4 + later]
    known, outs = refs[4 + later : -3], refs[-3:]
    if not known:
        interior(*inputs, wholes, *kernels, *outs)
        return

    def copied():
        outs[0][...] = known[0][...]
        outs[1][...] = known[1][...]

    on_last(copied)

    @pl.when(lax.axis_index("video") < lax.axis_size("video") - 1)
    def _():
        interior(*inputs, wholes, *kernels, *outs)


def mid_kernel(later, *refs):
    grad_ref, low_ref, high_ref, inner_ref, gpre_ref = refs[:5]
    afters, (temporal_ref, spatial_ref, mid_ref, views_ref) = refs[5 : 5 + later], refs[5 + later :]
    rows = grad_ref.shape[0]
    first, last = edge_rows(
        grad_ref, low_ref, high_ref, afters, gpre_ref, temporal_ref, spatial_ref, views_ref
    )
    mid_ref[0:1], mid_ref[rows - 1 : rows] = first, last
    mid_ref[1 : rows - 1] = inner_ref[...]


def two_kernel(later, *refs):
    saved_ref, preact_ref, gpre_ref, low_ref, high_ref, grad_ref = refs[:6]
    wholes, outs = refs[6 : 6 + later], refs[6 + later : 10 + later]
    views_ref, act_ref, sums_ref = refs[10 + later :]
    rows, cols, ch = saved_ref.shape
    step = 4

    @pl.loop(0, rows // step)
    def _(n):
        here = pl.ds(n * step, step)
        beside(gpre_ref[here].astype(jnp.float32), views_ref, n * step)
        hval = preact_ref[here].astype(jnp.float32)
        act_ref[here] = (hval * sigmoid(hval)).astype(jnp.bfloat16)

    views = views_ref[...].reshape(rows * cols, 3 * ch)
    grads = [ref[...] for ref in (grad_ref, *wholes)]
    kernel_sums(saved_ref, low_ref[2:3], high_ref[2:3], act_ref[...], grads, views, sums_ref)
    hand_out(sums_ref, outs)


def block_one(saved_ref, preact_ref, low_ref, high_ref, mids, temporal_ref, outs, scratch):
    gpre_ref, first_ref, last_ref = outs[:3]
    views_ref, act_ref, sums_ref = scratch
    rows, cols, ch = saved_ref.shape
    step = 4

    @pl.loop(0, rows // step)
    def _(n):
        here = pl.ds(n * step, step)
        gpre = pre_gradient([ref[here] for ref in mids], preact_ref[here], temporal_ref)
        gpre_ref[here] = gpre.astype(jnp.bfloat16)
        beside(gpre, views_ref, n * step)
        hval = preact_ref[here].astype(jnp.float32)
        act_ref[here] = (hval * sigmoid(hval)).astype(jnp.bfloat16)

    first_ref[...] = gpre_ref[0:1]
    last_ref[...] = gpre_ref[rows - 1 : rows]
    views = views_ref[...].reshape(rows * cols, 3 * ch)
    grads = [ref[...] for ref in mids]
    kernel_sums(saved_ref, low_ref[3:4], high_ref[3:4], act_ref[...], grads, views, sums_ref)
    hand_out(sums_ref, outs[3:])


def one_kernel(later, *refs):
    saved_ref, preact_ref, low_ref, high_ref, mid_ref = refs[:5]
    nexts, temporal_ref = refs[5 : 5 + later], refs[5 + later]
    outs, scratch = refs[6 + later : 13 + later], refs[13 + later :]
    block_one(
        saved_ref, preact_ref, low_ref, high_ref, [mid_ref, *nexts], temporal_ref, outs, scratch
    )


def mid_one_kernel(*refs):
    grad_ref, low_ref, high_ref, inner_ref, gpre_two_ref, after_inner_ref, after_edge_ref = refs[:7]
    temporal_two_ref, spatial_two_ref, saved_ref, preact_ref, temporal_ref = refs[7:12]
    mid_ref, outs, scratch = refs[12], refs[13:20], refs[20:23]
    next_ref, edge_views_ref = refs[23:]
    rows = grad_ref.shape[0]
    mid_kernel(
        1,
        grad_ref,
        low_ref,
        high_ref,
        inner_ref,
        gpre_two_ref,
        after_edge_ref,
        temporal_two_ref,
        spatial_two_ref,
        mid_ref,
        edge_views_ref,
    )
    next_ref[0:1] = after_edge_ref[0:1]
    next_ref[1 : rows - 1] = after_inner_ref[...]
    next_ref[rows - 1 : rows] = after_edge_ref[1:2]
    block_one(
        saved_ref, preact_ref, low_ref, high_ref, [mid_ref, next_ref], temporal_ref, outs, scratch
    )


def input_kernel(mid_ref, gpre_ref, above_ref, below_ref, spatial_ref, out_ref, views_ref):
    rows, cols, ch = out_ref.shape
    step = 4
    beside(above_ref[...].astype(jnp.float32), views_ref, 0)
    beside(below_ref[...].astype(jnp.float32), views_ref, rows + 1)

    @pl.loop(0, rows // step)
    def _(n):
        gpre = gpre_ref[pl.ds(n * step, step)].astype(jnp.float32)
        beside(gpre, views_ref, n * step + 1)

    @pl.loop(0, rows // step)
    def _(n):
        here = pl.ds(n * step, step)
        out_ref[here] = convolved(views_ref, spatial_ref, n * step, mid_ref[here])


def added(refs, rows):
    total = refs[0][rows].astype(jnp.float32)
    for ref in refs[1:]:
        total = total + ref[rows].astype(jnp.float32)
    return total


def band_kernel(own_ref, *refs):
    parts, (keep_ref, send_ref) = refs[:3], refs[3:]
    half = keep_ref.shape[0]
    frame = lax.axis_index("video")
    mine = pl.ds(pl.multiple_of(frame * half, half), half)
    other = pl.ds(pl.multiple_of((1 - frame) * half, half), half)
    keep_ref[...] = added((own_ref, *parts), mine)
    send_ref[...] = added((own_ref, *parts), other).astype(jnp.bfloat16)


def frame_kernel(keep_ref, part_ref, out_ref):
    out_ref[...] = (keep_ref[...] + part_ref[...].astype(jnp.float32)).astype(jnp.bfloat16)


def clip_kernel(factor, *refs):
    out_ref = refs[-1]
    for block in range(2):
        a, b, c, d = (ref[...].astype(jnp.float32) for ref in refs[4 * block : 4 * block + 4])
        out_ref[block] = (((a + b) + (c + d)) * factor).astype(jnp.bfloat16)


def join_kernel(own_ref, other_ref, out_ref):
    frame = lax.axis_index("video")
    out_ref[frame] = own_ref[...]
    out_ref[1 - frame] = other_ref[...]


def place_kernel(*refs):
    shares, outs = refs[:4], refs[4:]
    band = lax.axis_index("section")
    parts, _, height, _ = shares[0].shape
    for flip, share in enumerate(shares):
        place = jnp.bitwise_xor(band, flip)

        @pl.when(place < 3)
        def _():
            for block in range(2):
                for n in range(parts):
                    here = slice(n * height, (n + 1) * height)
                    outs[2 * block][place, here] = share[n, block].astype(jnp.float32)

        @pl.when(place == 3)
        def _():
            for block in range(2):
                for n in range(parts):
                    here = slice(n * height, (n + 1) * height)
                    outs[2 * block + 1][here] = share[n, block].astype(jnp.float32)


def frames_summed(own, *parts):
    height, ch = own.shape
    half = height // 2
    keep, send = call(band_kernel, [f32(half, ch), bf16(half, ch)], [], own.size, own, *parts)
    other = flipped(send, "video", 1)
    return call(frame_kernel, [bf16(half, ch)], [], half * ch, keep, other)


def totals(one, two, factor):
    height, ch = one[0].shape
    one, two = (
        [own] + [flipped(part, "section", flip + 1) for flip, part in enumerate(parts)]
        for own, *parts in (one, two)
    )
    if lax.axis_size("video") == 2 and lax.axis_size("dp") == 4:
        two, one = frames_summed(*two), frames_summed(*one)
        parts = [
            x
            for own in (one, two)
            for x in [own] + [flipped(own, "dp", flip) for flip in range(1, 4)]
        ]
        half = height // 2
        own = call(
            functools.partial(clip_kernel, factor), [bf16(2, half, ch)], [], 8 * height * ch, *parts
        )
        other = flipped(own, "video", 1)
        share = call(join_kernel, [bf16(2, 2, half, ch)], [], 1, own, other)
    else:
        own = [sum(x.astype(jnp.float32) for x in parts) for parts in (one, two)]
        share = lax.psum(jnp.stack(own), ("video", "dp")) * factor
        share = share.astype(jnp.bfloat16)[None]
    across = flipped(share, "section", 2)
    outs = call(
        place_kernel,
        [f32(3, height, ch), f32(height, ch)] * 2,
        [],
        share.size,
        share,
        flipped(share, "section", 1),
        across,
        flipped(across, "section", 1),
    )
    return [x.reshape(3, 3, ch, ch) if x.ndim == 3 else x.reshape(3, ch, ch) for x in outs]


def on_device(
    grad_latent,
    input_one,
    preact_one,
    input_two,
    preact_two,
    spatial_one,
    temporal_one,
    spatial_two,
    temporal_two,
):
    shape = grad_latent.shape
    rows, cols, ch = shape[2:]
    bands, frames = lax.axis_size("section"), lax.axis_size("video")
    later = min(2, frames - 1)
    pixels = lax.axis_size("dp") * frames * bands * rows * cols
    factor = 1.0 / math.sqrt(pixels)
    grad, saved_one, pre_one, saved_two, pre_two = (
        x.reshape(rows, cols, ch)
        for x in (grad_latent, input_one, preact_one, input_two, preact_two)
    )
    conv = 2 * rows * cols * 9 * ch * ch
    views = pltpu.VMEM((rows, cols, 3 * ch), jnp.bfloat16)
    edge_views = pltpu.VMEM((6, cols, 3 * ch), jnp.bfloat16)
    act = pltpu.VMEM((rows, cols, ch), jnp.bfloat16)
    sums = pltpu.VMEM((4, 3 * ch, ch), jnp.float32)
    handed = [f32(3 * ch, ch)] + [bf16(3 * ch, ch)] * 3
    inner_outs = [bf16(rows - 2, cols, ch), bf16(rows, cols, ch)]
    kernels = (temporal_two, spatial_two)

    wholes = [from_ahead(grad, 0, n + 1) for n in range(later)]
    edges = [pl.BlockSpec((1, cols, ch), lambda _, at=at: (at, 0, 0)) for at in (0, rows - 1)]
    up, down = call(
        pack_kernel,
        [bf16(4, cols, ch)] * 2,
        [],
        1,
        *(grad, pre_two, saved_two, saved_one) * 2,
        grid=(1,),
        in_specs=[edges[0]] * 4 + [edges[1]] * 4,
        limit=56,
    )
    low = from_ahead(down, -1, 0)
    high = from_ahead(up, 1, 0)

    known = ()
    if frames == 2:
        known = call(last_inner_kernel, inner_outs, [views], 1.2 * conv, grad, pre_two, *kernels)
        after_inner = from_ahead(known[0], 0, 1)
        edge = call(
            last_edge_kernel,
            [bf16(4, cols, ch)],
            [edge_views],
            conv // 8,
            grad,
            low,
            high,
            known[1],
            *kernels,
        )
    else:
        edge = jnp.concatenate([grad[:1], grad[rows - 1 :], low[:1], high[:1]])
    after_edges = [from_ahead(edge, 0, n + 1) for n in range(later)]
    inner, gpre_two = call(
        functools.partial(inner_kernel, later),
        inner_outs,
        [views],
        1.2 * conv,
        grad,
        pre_two,
        *wholes,
        *kernels,
        *known,
    )
    parts_two = call(
        functools.partial(two_kernel, later),
        handed,
        [views, act, sums],
        1.2 * conv,
        saved_two,
        pre_two,
        gpre_two,
        low,
        high,
        grad,
        *wholes,
    )
    mid_inputs = (grad, low, high, inner, gpre_two)
    one_inputs = (saved_one, pre_one)
    mid_outs = [bf16(rows, cols, ch)]
    one_outs = [bf16(rows, cols, ch)] + [bf16(1, cols, ch)] * 2 + handed
    if frames == 2:
        mid, gpre_one, first, last, *parts_one = call(
            mid_one_kernel,
            mid_outs + one_outs,
            [views, act, sums, act, edge_views],
            1.5 * conv,
            *mid_inputs,
            after_inner,
            *after_edges,
            *kernels,
            *one_inputs,
            temporal_one,
        )
    else:
        mid = call(
            functools.partial(mid_kernel, later),
            mid_outs,
            [edge_views],
            conv // 8,
            *mid_inputs,
            *after_edges,
            *kernels,
        )
        gpre_one, first, last, *parts_one = call(
            functools.partial(one_kernel, later),
            one_outs,
            [views, act, sums],
            1.2 * conv,
            *one_inputs,
            low,
            high,
            mid,
            *[from_ahead(mid, 0, n + 1) for n in range(later)],
            temporal_one,
        )
    sums = totals(parts_one, parts_two, factor)
    grad_in = call(
        input_kernel,
        [bf16(rows, cols, ch)],
        [pltpu.VMEM((rows + 2, cols, 3 * ch), jnp.bfloat16)],
        conv,
        mid,
        gpre_one,
        from_ahead(last, -1, 0),
        from_ahead(first, 1, 0),
        spatial_one,
    )
    return (grad_in.reshape(shape), *sums)


def solution(mesh):
    whole = P("dp", "video", "section", None, None)
    return jax.shard_map(
        on_device,
        mesh=mesh,
        in_specs=(whole,) * 5 + (P(),) * 4,
        out_specs=(whole, P(), P(), P(), P()),
        check_vma=False,
    )
```

```python
import functools
import math

import jax
import jax.numpy as jnp
from jax import lax
from jax.experimental import pallas as pl
from jax.experimental.pallas import tpu as pltpu
from jax.sharding import PartitionSpec as P

MIB = 1024 * 1024


def sigmoid(value):
    return 1.0 / (1.0 + jnp.exp(-value))


def bf16(*shape):
    return jax.ShapeDtypeStruct(shape, jnp.bfloat16)


def f32(*shape):
    return jax.ShapeDtypeStruct(shape, jnp.float32)


def call(kernel, outs, scratch, flops, *operands, after=(), whole=False, limit=24):
    single = len(outs) == 1
    moved = sum(math.prod(x.shape) * x.dtype.itemsize for x in (*operands, *outs))
    vmem = pl.BlockSpec(memory_space=pltpu.VMEM)
    spare = pl.BlockSpec(memory_space=pl.ANY)
    spec = spare if whole else vmem
    count = len(operands)
    operands = (*operands, *after)

    def body(*refs):
        kernel(*refs[:count], *refs[len(operands) :])

    return pl.pallas_call(
        body,
        out_shape=outs[0] if single else tuple(outs),
        in_specs=[spec] * count + [spare] * len(after),
        out_specs=spec if single else (spec,) * len(outs),
        scratch_shapes=scratch,
        compiler_params=pltpu.CompilerParams(vmem_limit_bytes=limit * MIB),
        cost_estimate=pl.CostEstimate(
            flops=int(flops), bytes_accessed=int(moved), transcendentals=0
        ),
    )(*operands)


def from_ahead(block, band_step, frame_step):
    bands, frames = lax.axis_size("section"), lax.axis_size("video")
    pairs = [
        ((band + band_step) * frames + frame + frame_step, band * frames + frame)
        for band in range(bands)
        for frame in range(frames)
        if 0 <= band + band_step < bands and frame + frame_step < frames
    ]
    return lax.ppermute(block, ("section", "video"), pairs)


def paired(block, start):
    bands = lax.axis_size("section")
    pairs = [(band, band + 1) for band in range(start, bands - 1, 2)]
    return lax.ppermute(block, "section", pairs + [(right, left) for left, right in pairs])


def beside_band(pair_refs, row):
    odd = lax.rem(lax.axis_index("section"), 2) == 1
    first, second = (ref[row : row + 1] for ref in pair_refs)
    return jnp.where(odd, first, second), jnp.where(odd, second, first)


def flipped(block, axis, flip):
    count = lax.axis_size(axis)
    return lax.ppermute(block, axis, [(place ^ flip, place) for place in range(count)])


def beside(gpre, views_ref, start):
    count, cols, ch = gpre.shape
    at = lax.broadcasted_iota(jnp.int32, gpre.shape, 1)
    right = jnp.where(at == cols - 1, 0.0, pltpu.roll(gpre, cols - 1, 1))
    left = jnp.where(at == 0, 0.0, pltpu.roll(gpre, 1, 1))
    here = pl.ds(start, count)
    views_ref[here, :, 0:ch] = right.astype(jnp.bfloat16)
    views_ref[here, :, ch : 2 * ch] = gpre.astype(jnp.bfloat16)
    views_ref[here, :, 2 * ch : 3 * ch] = left.astype(jnp.bfloat16)


def pre_gradient(grads, preact, temporal_ref):
    count, cols, ch = preact.shape
    flat = jnp.concatenate([grad.reshape(count * cols, ch) for grad in grads], axis=1)
    kernel = jnp.concatenate([temporal_ref[2 - step] for step in range(len(grads))], axis=1)
    gact = lax.dot_general(
        flat, kernel, (((1,), (1,)), ((), ())), preferred_element_type=jnp.float32
    )
    gact = gact.astype(jnp.bfloat16).astype(jnp.float32).reshape(preact.shape)
    hval = preact.astype(jnp.float32)
    sig = sigmoid(hval)
    return gact * sig * (1.0 + hval * (1.0 - sig))


def convolved(views_ref, spatial_ref, start, first):
    count, cols, ch = first.shape
    total = first.astype(jnp.float32).reshape(count * cols, ch)
    for ky in range(3):
        view = views_ref[pl.ds(start + 2 - ky, count)].reshape(count * cols, 3 * ch)
        kernel = jnp.concatenate([spatial_ref[ky, kx] for kx in range(3)], axis=1)
        total = total + lax.dot_general(
            view, kernel, (((1,), (1,)), ((), ())), preferred_element_type=jnp.float32
        )
    return total.astype(jnp.bfloat16).reshape(first.shape)


def kernel_sums(saved_ref, above, below, act, grads, views, sums_ref):
    rows, cols, ch = saved_ref.shape
    flat = (rows * cols, ch)
    saved = [
        jnp.concatenate([above, saved_ref[: rows - 1]], axis=0),
        saved_ref[...],
        jnp.concatenate([saved_ref[1:], below], axis=0),
    ]
    for ky in range(3):
        sums = jnp.dot(saved[ky].reshape(flat).T, views, preferred_element_type=jnp.float32)
        for kx in range(3):
            sums_ref[ky, kx * ch : (kx + 1) * ch] = sums[:, kx * ch : (kx + 1) * ch]
    sums = jnp.dot(
        act.reshape(flat).T,
        jnp.concatenate([grad.reshape(flat) for grad in grads], axis=1),
        preferred_element_type=jnp.float32,
    )
    for k in range(3):
        step = 2 - k
        here = slice(k * ch, (k + 1) * ch)
        if step < len(grads):
            sums_ref[3, here] = sums[:, step * ch : (step + 1) * ch]
        else:
            sums_ref[3, here] = jnp.zeros((ch, ch), jnp.float32)


def hand_out(sums_ref, outs):
    band = lax.axis_index("section")
    outs[0][...] = sums_ref[band]
    for flip in range(1, 4):
        outs[flip][...] = sums_ref[jnp.bitwise_xor(band, flip)].astype(jnp.bfloat16)


def pack_kernel(*refs):
    parts, outs, sems = refs[:4], refs[4:6], refs[6]
    last = parts[0].shape[0] - 1
    odd = lax.rem(lax.axis_index("section"), 2)
    copies = []
    for n, part in enumerate(parts):
        for out, row in zip(outs, ((1 - odd) * last, odd * last)):
            sem = sems.at[len(copies)]
            copies.append(
                pltpu.make_async_copy(part.at[pl.ds(row, 1)], out.at[pl.ds(n, 1)], sem)
            )
    for copy in copies:
        copy.start()
    for copy in copies:
        copy.wait()


def interior(grad_ref, preact_ref, wholes, temporal_ref, spatial_ref, inner_ref, gpre_ref, views_ref):
    rows, cols, ch = grad_ref.shape
    step = 4

    @pl.loop(0, rows // step)
    def _(n):
        here = pl.ds(n * step, step)
        grads = [ref[here] for ref in (grad_ref, *wholes)]
        gpre = pre_gradient(grads, preact_ref[here], temporal_ref)
        gpre_ref[here] = gpre.astype(jnp.bfloat16)
        beside(gpre, views_ref, n * step)

    half = rows // 2 - 1

    @pl.loop(0, 2)
    def _(n):
        first = grad_ref[pl.ds(n * half + 1, half)]
        inner_ref[pl.ds(n * half, half)] = convolved(views_ref, spatial_ref, n * half, first)


def edge_rows(grad_ref, pair_refs, afters, gpre_ref, temporal_ref, spatial_ref, views_ref):
    rows, cols, ch = grad_ref.shape
    (grad_above, grad_below), (above_pre, below_pre) = (beside_band(pair_refs, n) for n in (0, 1))
    above = [grad_above] + [ref[2:3] for ref in afters]
    below = [grad_below] + [ref[3:4] for ref in afters]
    beside(pre_gradient(above, above_pre, temporal_ref), views_ref, 0)
    beside(gpre_ref[0:2].astype(jnp.float32), views_ref, 1)
    beside(gpre_ref[rows - 2 : rows].astype(jnp.float32), views_ref, 3)
    beside(pre_gradient(below, below_pre, temporal_ref), views_ref, 5)
    return (
        convolved(views_ref, spatial_ref, 0, grad_ref[0:1]),
        convolved(views_ref, spatial_ref, 3, grad_ref[rows - 1 : rows]),
    )


def on_last(body):
    pl.when(lax.axis_index("video") == lax.axis_size("video") - 1)(body)


def last_inner_kernel(grad_ref, preact_ref, temporal_ref, spatial_ref, inner_ref, gpre_ref, views_ref):
    on_last(
        lambda: interior(
            grad_ref, preact_ref, [], temporal_ref, spatial_ref, inner_ref, gpre_ref, views_ref
        )
    )


def last_edge_kernel(grad_ref, one_ref, two_ref, gpre_ref, temporal_ref, spatial_ref, edge_ref, views_ref):
    def body():
        edge_ref[0:1], edge_ref[1:2] = edge_rows(
            grad_ref, (one_ref, two_ref), [], gpre_ref, temporal_ref, spatial_ref, views_ref
        )
        edge_ref[2:3], edge_ref[3:4] = beside_band((one_ref, two_ref), 0)

    on_last(body)


def inner_kernel(later, *refs):
    inputs, wholes, kernels = refs[:2], refs[2 : 2 + later], refs[2 + later : 4 + later]
    known, outs = refs[4 + later : -3], refs[-3:]
    if not known:
        interior(*inputs, wholes, *kernels, *outs)
        return

    def copied():
        outs[0][...] = known[0][...]
        outs[1][...] = known[1][...]

    on_last(copied)

    @pl.when(lax.axis_index("video") < lax.axis_size("video") - 1)
    def _():
        interior(*inputs, wholes, *kernels, *outs)


def mid_kernel(later, *refs):
    grad_ref, inner_ref, gpre_ref = refs[0], refs[3], refs[4]
    afters, (temporal_ref, spatial_ref, mid_ref, views_ref) = refs[5 : 5 + later], refs[5 + later :]
    rows = grad_ref.shape[0]
    first, last = edge_rows(
        grad_ref, refs[1:3], afters, gpre_ref, temporal_ref, spatial_ref, views_ref
    )
    mid_ref[0:1], mid_ref[rows - 1 : rows] = first, last
    mid_ref[1 : rows - 1] = inner_ref[...]


def two_kernel(later, *refs):
    saved_ref, preact_ref, gpre_ref = refs[:3]
    pair_refs, grad_ref = refs[3:5], refs[5]
    wholes, outs = refs[6 : 6 + later], refs[6 + later : 10 + later]
    views_ref, act_ref, sums_ref = refs[10 + later :]
    rows, cols, ch = saved_ref.shape
    step = 4

    @pl.loop(0, rows // step)
    def _(n):
        here = pl.ds(n * step, step)
        beside(gpre_ref[here].astype(jnp.float32), views_ref, n * step)
        hval = preact_ref[here].astype(jnp.float32)
        act_ref[here] = (hval * sigmoid(hval)).astype(jnp.bfloat16)

    views = views_ref[...].reshape(rows * cols, 3 * ch)
    grads = [ref[...] for ref in (grad_ref, *wholes)]
    above, below = beside_band(pair_refs, 2)
    kernel_sums(saved_ref, above, below, act_ref[...], grads, views, sums_ref)
    hand_out(sums_ref, outs)


def block_one(saved_ref, preact_ref, pair_refs, mids, temporal_ref, outs, scratch):
    gpre_ref, edge_refs = outs[0], outs[1:3]
    views_ref, act_ref, sums_ref = scratch
    rows, cols, ch = saved_ref.shape
    step = 4

    @pl.loop(0, rows // step)
    def _(n):
        here = pl.ds(n * step, step)
        gpre = pre_gradient([ref[here] for ref in mids], preact_ref[here], temporal_ref)
        gpre_ref[here] = gpre.astype(jnp.bfloat16)
        beside(gpre, views_ref, n * step)
        hval = preact_ref[here].astype(jnp.float32)
        act_ref[here] = (hval * sigmoid(hval)).astype(jnp.bfloat16)

    odd = lax.rem(lax.axis_index("section"), 2)
    edge_refs[0][...] = gpre_ref[pl.ds((1 - odd) * (rows - 1), 1)]
    edge_refs[1][...] = gpre_ref[pl.ds(odd * (rows - 1), 1)]
    views = views_ref[...].reshape(rows * cols, 3 * ch)
    grads = [ref[...] for ref in mids]
    above, below = beside_band(pair_refs, 3)
    kernel_sums(saved_ref, above, below, act_ref[...], grads, views, sums_ref)
    hand_out(sums_ref, outs[3:])


def one_kernel(later, *refs):
    saved_ref, preact_ref, mid_ref = refs[0], refs[1], refs[4]
    nexts, temporal_ref = refs[5 : 5 + later], refs[5 + later]
    outs, scratch = refs[6 + later : 13 + later], refs[13 + later :]
    block_one(saved_ref, preact_ref, refs[2:4], [mid_ref, *nexts], temporal_ref, outs, scratch)


def mid_one_kernel(*refs):
    grad_ref, pair_refs, (after_inner_ref, after_edge_ref) = refs[0], refs[1:3], refs[5:7]
    temporal_two_ref, spatial_two_ref, saved_ref, preact_ref, temporal_ref = refs[7:12]
    mid_ref, outs, scratch = refs[12], refs[13:20], refs[20:23]
    next_ref, edge_views_ref = refs[23:]
    rows = grad_ref.shape[0]
    mid_kernel(
        1,
        *refs[:5],
        after_edge_ref,
        temporal_two_ref,
        spatial_two_ref,
        mid_ref,
        edge_views_ref,
    )
    next_ref[0:1] = after_edge_ref[0:1]
    next_ref[1 : rows - 1] = after_inner_ref[...]
    next_ref[rows - 1 : rows] = after_edge_ref[1:2]
    block_one(saved_ref, preact_ref, pair_refs, [mid_ref, next_ref], temporal_ref, outs, scratch)


def input_kernel(mid_ref, gpre_ref, one_ref, two_ref, spatial_ref, out_ref, views_ref):
    rows, cols, ch = out_ref.shape
    step = 4
    above, below = beside_band((one_ref, two_ref), 0)
    beside(above.astype(jnp.float32), views_ref, 0)
    beside(below.astype(jnp.float32), views_ref, rows + 1)

    @pl.loop(0, rows // step)
    def _(n):
        gpre = gpre_ref[pl.ds(n * step, step)].astype(jnp.float32)
        beside(gpre, views_ref, n * step + 1)

    @pl.loop(0, rows // step)
    def _(n):
        here = pl.ds(n * step, step)
        out_ref[here] = convolved(views_ref, spatial_ref, n * step, mid_ref[here])


def added(refs, rows):
    total = refs[0][rows].astype(jnp.float32)
    for ref in refs[1:]:
        total = total + ref[rows].astype(jnp.float32)
    return total


def band_kernel(own_ref, *refs):
    parts, (keep_ref, send_ref) = refs[:3], refs[3:]
    half = keep_ref.shape[0]
    frame = lax.axis_index("video")
    mine = pl.ds(pl.multiple_of(frame * half, half), half)
    other = pl.ds(pl.multiple_of((1 - frame) * half, half), half)
    keep_ref[...] = added((own_ref, *parts), mine)
    send_ref[...] = added((own_ref, *parts), other).astype(jnp.bfloat16)


def frame_kernel(keep_ref, part_ref, out_ref):
    out_ref[...] = (keep_ref[...] + part_ref[...].astype(jnp.float32)).astype(jnp.bfloat16)


def clip_kernel(factor, *refs):
    out_ref = refs[-1]
    for block in range(2):
        a, b, c, d = (ref[...].astype(jnp.float32) for ref in refs[4 * block : 4 * block + 4])
        out_ref[block] = (((a + b) + (c + d)) * factor).astype(jnp.bfloat16)


def join_kernel(own_ref, other_ref, out_ref):
    frame = lax.axis_index("video")
    out_ref[frame] = own_ref[...]
    out_ref[1 - frame] = other_ref[...]


def place_kernel(*refs):
    shares, outs = refs[:4], refs[4:]
    band = lax.axis_index("section")
    parts, _, height, _ = shares[0].shape
    for flip, share in enumerate(shares):
        place = jnp.bitwise_xor(band, flip)

        @pl.when(place < 3)
        def _():
            for block in range(2):
                for n in range(parts):
                    here = slice(n * height, (n + 1) * height)
                    outs[2 * block][place, here] = share[n, block].astype(jnp.float32)

        @pl.when(place == 3)
        def _():
            for block in range(2):
                for n in range(parts):
                    here = slice(n * height, (n + 1) * height)
                    outs[2 * block + 1][here] = share[n, block].astype(jnp.float32)


def frames_summed(own, *parts, after=()):
    height, ch = own.shape
    half = height // 2
    outs = [f32(half, ch), bf16(half, ch)]
    keep, send = call(band_kernel, outs, [], own.size, own, *parts, after=after)
    other = flipped(send, "video", 1)
    return call(frame_kernel, [bf16(half, ch)], [], half * ch, keep, other)


def totals(one, two, factor, meanwhile):
    height, ch = one[0].shape
    one, two = (
        [own] + [flipped(part, "section", flip + 1) for flip, part in enumerate(parts)]
        for own, *parts in (one, two)
    )
    if lax.axis_size("video") == 2 and lax.axis_size("dp") == 4:
        two = frames_summed(*two)
        one = frames_summed(*one, after=(two,))
        done = meanwhile((one,))
        parts = [
            x
            for own in (one, two)
            for x in [own] + [flipped(own, "dp", flip) for flip in range(1, 4)]
        ]
        half = height // 2
        own = call(
            functools.partial(clip_kernel, factor),
            [bf16(2, half, ch)],
            [],
            8 * height * ch,
            *parts,
            after=(done,),
        )
        other = flipped(own, "video", 1)
        share = call(join_kernel, [bf16(2, 2, half, ch)], [], 1, own, other)
    else:
        done = meanwhile(())
        own = [sum(x.astype(jnp.float32) for x in parts) for parts in (one, two)]
        share = lax.psum(jnp.stack(own), ("video", "dp")) * factor
        share = share.astype(jnp.bfloat16)[None]
    across = flipped(share, "section", 2)
    outs = call(
        place_kernel,
        [f32(3, height, ch), f32(height, ch)] * 2,
        [],
        share.size,
        share,
        flipped(share, "section", 1),
        across,
        flipped(across, "section", 1),
    )
    outs = [x.reshape(3, 3, ch, ch) if x.ndim == 3 else x.reshape(3, ch, ch) for x in outs]
    return done, outs


def on_device(
    grad_latent,
    input_one,
    preact_one,
    input_two,
    preact_two,
    spatial_one,
    temporal_one,
    spatial_two,
    temporal_two,
):
    shape = grad_latent.shape
    rows, cols, ch = shape[2:]
    bands, frames = lax.axis_size("section"), lax.axis_size("video")
    later = min(2, frames - 1)
    pixels = lax.axis_size("dp") * frames * bands * rows * cols
    factor = 1.0 / math.sqrt(pixels)
    grad, saved_one, pre_one, saved_two, pre_two = (
        x.reshape(rows, cols, ch)
        for x in (grad_latent, input_one, preact_one, input_two, preact_two)
    )
    conv = 2 * rows * cols * 9 * ch * ch
    views = pltpu.VMEM((rows, cols, 3 * ch), jnp.bfloat16)
    edge_views = pltpu.VMEM((6, cols, 3 * ch), jnp.bfloat16)
    act = pltpu.VMEM((rows, cols, ch), jnp.bfloat16)
    sums = pltpu.VMEM((4, 3 * ch, ch), jnp.float32)
    handed = [f32(3 * ch, ch)] + [bf16(3 * ch, ch)] * 3
    inner_outs = [bf16(rows - 2, cols, ch), bf16(rows, cols, ch)]
    kernels = (temporal_two, spatial_two)

    wholes = [from_ahead(grad, 0, n + 1) for n in range(later)]
    packs = call(
        pack_kernel,
        [bf16(4, cols, ch)] * 2,
        [pltpu.SemaphoreType.DMA((8,))],
        1,
        grad,
        pre_two,
        saved_two,
        saved_one,
        whole=True,
        limit=58,
    )
    pairs = [paired(pack, start) for start, pack in enumerate(packs)]

    known = ()
    if frames == 2:
        known = call(
            last_inner_kernel,
            inner_outs,
            [views],
            1.2 * conv,
            grad,
            pre_two,
            *kernels,
            after=pairs[:1],
        )
        after_inner = from_ahead(known[0], 0, 1)
        edge = call(
            last_edge_kernel,
            [bf16(4, cols, ch)],
            [edge_views],
            conv // 8,
            grad,
            *pairs,
            known[1],
            *kernels,
        )
    else:
        odd = lax.rem(lax.axis_index("section"), 2) == 1
        one, two = (pair[:1] for pair in pairs)
        above, below = jnp.where(odd, one, two), jnp.where(odd, two, one)
        edge = jnp.concatenate([grad[:1], grad[rows - 1 :], above, below])
    after_edges = [from_ahead(edge, 0, n + 1) for n in range(later)]
    inner, gpre_two = call(
        functools.partial(inner_kernel, later),
        inner_outs,
        [views],
        1.2 * conv,
        grad,
        pre_two,
        *wholes,
        *kernels,
        *known,
    )
    parts_two = call(
        functools.partial(two_kernel, later),
        handed,
        [views, act, sums],
        1.2 * conv,
        saved_two,
        pre_two,
        gpre_two,
        *pairs,
        grad,
        *wholes,
    )
    mid_inputs = (grad, *pairs, inner, gpre_two)
    one_inputs = (saved_one, pre_one)
    mid_outs = [bf16(rows, cols, ch)]
    one_outs = [bf16(rows, cols, ch)] + [bf16(1, cols, ch)] * 2 + handed
    if frames == 2:
        mid, gpre_one, *tail = call(
            mid_one_kernel,
            mid_outs + one_outs,
            [views, act, sums, act, edge_views],
            1.5 * conv,
            *mid_inputs,
            after_inner,
            *after_edges,
            *kernels,
            *one_inputs,
            temporal_one,
        )
    else:
        mid = call(
            functools.partial(mid_kernel, later),
            mid_outs,
            [edge_views],
            conv // 8,
            *mid_inputs,
            *after_edges,
            *kernels,
        )
        gpre_one, *tail = call(
            functools.partial(one_kernel, later),
            one_outs,
            [views, act, sums],
            1.2 * conv,
            *one_inputs,
            *pairs,
            mid,
            *[from_ahead(mid, 0, n + 1) for n in range(later)],
            temporal_one,
        )
    edges_one, parts_one = tail[:2], tail[2:]

    def input_gradient(after):
        return call(
            input_kernel,
            [bf16(rows, cols, ch)],
            [pltpu.VMEM((rows + 2, cols, 3 * ch), jnp.bfloat16)],
            conv,
            mid,
            gpre_one,
            *[paired(edge, start) for start, edge in enumerate(edges_one)],
            spatial_one,
            after=after,
        )

    grad_in, sums = totals(parts_one, parts_two, factor, input_gradient)
    return (grad_in.reshape(shape), *sums)


def solution(mesh):
    whole = P("dp", "video", "section", None, None)
    return jax.shard_map(
        on_device,
        mesh=mesh,
        in_specs=(whole,) * 5 + (P(),) * 4,
        out_specs=(whole, P(), P(), P(), P()),
        check_vma=False,
    )
```

```python
import functools
import math

import jax
import jax.numpy as jnp
from jax import lax
from jax.experimental import pallas as pl
from jax.experimental.pallas import tpu as pltpu
from jax.sharding import PartitionSpec as P

MIB = 1024 * 1024


def sigmoid(value):
    return 1.0 / (1.0 + jnp.exp(-value))


def bf16(*shape):
    return jax.ShapeDtypeStruct(shape, jnp.bfloat16)


def f32(*shape):
    return jax.ShapeDtypeStruct(shape, jnp.float32)


def call(kernel, outs, scratch, flops, *operands, after=(), spare_inputs=False, limit=24):
    single = len(outs) == 1
    moved = sum(math.prod(x.shape) * x.dtype.itemsize for x in (*operands, *outs))
    vmem = pl.BlockSpec(memory_space=pltpu.VMEM)
    spare = pl.BlockSpec(memory_space=pl.ANY)
    spec = spare if spare_inputs else vmem
    count = len(operands)
    operands = (*operands, *after)

    def body(*refs):
        kernel(*refs[:count], *refs[len(operands) :])

    return pl.pallas_call(
        body,
        out_shape=outs[0] if single else tuple(outs),
        in_specs=[spec] * count + [spare] * len(after),
        out_specs=vmem if single else (vmem,) * len(outs),
        scratch_shapes=scratch,
        compiler_params=pltpu.CompilerParams(vmem_limit_bytes=limit * MIB),
        cost_estimate=pl.CostEstimate(
            flops=int(flops), bytes_accessed=int(moved), transcendentals=0
        ),
    )(*operands)


def from_ahead(block, band_step, frame_step):
    bands, frames = lax.axis_size("section"), lax.axis_size("video")
    pairs = [
        ((band + band_step) * frames + frame + frame_step, band * frames + frame)
        for band in range(bands)
        for frame in range(frames)
        if 0 <= band + band_step < bands and frame + frame_step < frames
    ]
    return lax.ppermute(block, ("section", "video"), pairs)


def paired(block, start):
    bands = lax.axis_size("section")
    pairs = [(band, band + 1) for band in range(start, bands - 1, 2)]
    return lax.ppermute(block, "section", pairs + [(right, left) for left, right in pairs])


def beside_band(pair_refs, row):
    odd = lax.rem(lax.axis_index("section"), 2) == 1
    first, second = (ref[row : row + 1] for ref in pair_refs)
    return jnp.where(odd, first, second), jnp.where(odd, second, first)


def flipped(block, axis, flip):
    count = lax.axis_size(axis)
    return lax.ppermute(block, axis, [(place ^ flip, place) for place in range(count)])


def beside(gpre, views_ref, start):
    count, cols, ch = gpre.shape
    at = lax.broadcasted_iota(jnp.int32, gpre.shape, 1)
    right = jnp.where(at == cols - 1, 0.0, pltpu.roll(gpre, cols - 1, 1))
    left = jnp.where(at == 0, 0.0, pltpu.roll(gpre, 1, 1))
    here = pl.ds(start, count)
    views_ref[here, :, 0:ch] = right.astype(jnp.bfloat16)
    views_ref[here, :, ch : 2 * ch] = gpre.astype(jnp.bfloat16)
    views_ref[here, :, 2 * ch : 3 * ch] = left.astype(jnp.bfloat16)


def pre_gradient(grads, preact, temporal_ref):
    count, cols, ch = preact.shape
    flat = jnp.concatenate([grad.reshape(count * cols, ch) for grad in grads], axis=1)
    kernel = jnp.concatenate([temporal_ref[2 - step] for step in range(len(grads))], axis=1)
    gact = lax.dot_general(
        flat, kernel, (((1,), (1,)), ((), ())), preferred_element_type=jnp.float32
    )
    gact = gact.astype(jnp.bfloat16).astype(jnp.float32).reshape(preact.shape)
    hval = preact.astype(jnp.float32)
    sig = sigmoid(hval)
    return gact * sig * (1.0 + hval * (1.0 - sig))


def convolved(views_ref, spatial_ref, start, first):
    count, cols, ch = first.shape
    total = first.astype(jnp.float32).reshape(count * cols, ch)
    for ky in range(3):
        view = views_ref[pl.ds(start + 2 - ky, count)].reshape(count * cols, 3 * ch)
        kernel = jnp.concatenate([spatial_ref[ky, kx] for kx in range(3)], axis=1)
        total = total + lax.dot_general(
            view, kernel, (((1,), (1,)), ((), ())), preferred_element_type=jnp.float32
        )
    return total.astype(jnp.bfloat16).reshape(first.shape)


def is_last():
    return lax.axis_index("video") == lax.axis_size("video") - 1


def kernel_sums(saved_ref, above, below, act, grads, views, sums_ref):
    rows, cols, ch = saved_ref.shape
    flat = (rows * cols, ch)
    saved = [
        jnp.concatenate([above, saved_ref[: rows - 1]], axis=0),
        saved_ref[...],
        jnp.concatenate([saved_ref[1:], below], axis=0),
    ]
    for ky in range(3):
        sums = jnp.dot(saved[ky].reshape(flat).T, views, preferred_element_type=jnp.float32)
        for kx in range(3):
            sums_ref[ky, kx * ch : (kx + 1) * ch] = sums[:, kx * ch : (kx + 1) * ch]
    sums = jnp.dot(
        act.reshape(flat).T,
        jnp.concatenate([grad.reshape(flat) for grad in grads], axis=1),
        preferred_element_type=jnp.float32,
    )
    zeros = jnp.zeros((ch, ch), jnp.float32)
    for k in range(3):
        step = 2 - k
        value = sums[:, step * ch : (step + 1) * ch] if step < len(grads) else zeros
        sums_ref[3, k * ch : (k + 1) * ch] = jnp.where(is_last(), zeros, value) if step else value


def hand_out(sums_ref, keep_ref, send_ref):
    odd = lax.rem(lax.axis_index("section"), 2)
    for n in range(2):
        keep_ref[n] = sums_ref[2 * n + odd]
        send_ref[n] = sums_ref[2 * n + 1 - odd].astype(jnp.bfloat16)


def pack_kernel(*refs):
    parts, outs, sems = refs[:4], refs[4:6], refs[6]
    last = parts[0].shape[0] - 1
    odd = lax.rem(lax.axis_index("section"), 2)
    copies = []
    for n, part in enumerate(parts):
        for out, row in zip(outs, ((1 - odd) * last, odd * last)):
            sem = sems.at[len(copies)]
            copies.append(
                pltpu.make_async_copy(part.at[pl.ds(row, 1)], out.at[pl.ds(n, 1)], sem)
            )
    for copy in copies:
        copy.start()
    for copy in copies:
        copy.wait()


def interior(grad_ref, preact_ref, wholes, temporal_ref, spatial_ref, inner_ref, gpre_ref, views_ref):
    rows, cols, ch = grad_ref.shape
    step = 4

    @pl.loop(0, rows // step)
    def _(n):
        here = pl.ds(n * step, step)
        grads = [ref[here] for ref in (grad_ref, *wholes)]
        gpre = pre_gradient(grads, preact_ref[here], temporal_ref)
        gpre_ref[here] = gpre.astype(jnp.bfloat16)
        beside(gpre, views_ref, n * step)

    half = rows // 2 - 1

    @pl.loop(0, 2)
    def _(n):
        first = grad_ref[pl.ds(n * half + 1, half)]
        inner_ref[pl.ds(n * half, half)] = convolved(views_ref, spatial_ref, n * half, first)


def edge_rows(grad_ref, pair_refs, afters, gpre_ref, temporal_ref, spatial_ref, views_ref):
    rows, cols, ch = grad_ref.shape
    (grad_above, grad_below), (above_pre, below_pre) = (beside_band(pair_refs, n) for n in (0, 1))
    above = [grad_above] + [ref[2:3] for ref in afters]
    below = [grad_below] + [ref[3:4] for ref in afters]
    beside(pre_gradient(above, above_pre, temporal_ref), views_ref, 0)
    beside(gpre_ref[0:2].astype(jnp.float32), views_ref, 1)
    beside(gpre_ref[rows - 2 : rows].astype(jnp.float32), views_ref, 3)
    beside(pre_gradient(below, below_pre, temporal_ref), views_ref, 5)
    return (
        convolved(views_ref, spatial_ref, 0, grad_ref[0:1]),
        convolved(views_ref, spatial_ref, 3, grad_ref[rows - 1 : rows]),
    )


def last_inner_kernel(grad_ref, preact_ref, temporal_ref, spatial_ref, inner_ref, gpre_ref, views_ref):
    @pl.when(is_last())
    def _():
        interior(
            grad_ref, preact_ref, [], temporal_ref, spatial_ref, inner_ref, gpre_ref, views_ref
        )


def last_edge_kernel(grad_ref, one_ref, two_ref, gpre_ref, temporal_ref, spatial_ref, edge_ref, views_ref):
    @pl.when(is_last())
    def _():
        edge_ref[0:1], edge_ref[1:2] = edge_rows(
            grad_ref, (one_ref, two_ref), [], gpre_ref, temporal_ref, spatial_ref, views_ref
        )
        edge_ref[2:3], edge_ref[3:4] = beside_band((one_ref, two_ref), 0)


def inner_kernel(later, *refs):
    inputs, wholes, kernels = refs[:2], refs[2 : 2 + later], refs[2 + later : 4 + later]
    known, outs = refs[4 + later : -3], refs[-3:]
    if not known:
        interior(*inputs, wholes, *kernels, *outs)
        return

    @pl.when(is_last())
    def _():
        outs[0][...] = known[0][...]
        outs[1][...] = known[1][...]

    @pl.when(jnp.logical_not(is_last()))
    def _():
        interior(*inputs, wholes, *kernels, *outs)


def mid_kernel(later, *refs):
    grad_ref, inner_ref, gpre_ref = refs[0], refs[3], refs[4]
    afters, (temporal_ref, spatial_ref, mid_ref, views_ref) = refs[5 : 5 + later], refs[5 + later :]
    rows = grad_ref.shape[0]
    first, last = edge_rows(
        grad_ref, refs[1:3], afters, gpre_ref, temporal_ref, spatial_ref, views_ref
    )
    mid_ref[0:1], mid_ref[rows - 1 : rows] = first, last
    mid_ref[1 : rows - 1] = inner_ref[...]


def two_kernel(later, *refs):
    saved_ref, preact_ref, gpre_ref = refs[:3]
    pair_refs, grad_ref = refs[3:5], refs[5]
    wholes, outs = refs[6 : 6 + later], refs[6 + later : 8 + later]
    views_ref, act_ref, sums_ref = refs[8 + later :]
    rows, cols, ch = saved_ref.shape
    step = 4

    @pl.loop(0, rows // step)
    def _(n):
        here = pl.ds(n * step, step)
        beside(gpre_ref[here].astype(jnp.float32), views_ref, n * step)
        hval = preact_ref[here].astype(jnp.float32)
        act_ref[here] = (hval * sigmoid(hval)).astype(jnp.bfloat16)

    views = views_ref[...].reshape(rows * cols, 3 * ch)
    grads = [ref[...] for ref in (grad_ref, *wholes)]
    above, below = beside_band(pair_refs, 2)
    kernel_sums(saved_ref, above, below, act_ref[...], grads, views, sums_ref)
    hand_out(sums_ref, *outs)


def block_one(saved_ref, preact_ref, pair_refs, mids, temporal_ref, outs, scratch):
    gpre_ref, edge_refs = outs[0], outs[1:3]
    views_ref, act_ref, sums_ref = scratch
    rows, cols, ch = saved_ref.shape
    step = 4

    @pl.loop(0, rows // step)
    def _(n):
        here = pl.ds(n * step, step)
        gpre = pre_gradient([ref[here] for ref in mids], preact_ref[here], temporal_ref)
        gpre_ref[here] = gpre.astype(jnp.bfloat16)
        beside(gpre, views_ref, n * step)
        hval = preact_ref[here].astype(jnp.float32)
        act_ref[here] = (hval * sigmoid(hval)).astype(jnp.bfloat16)

    odd = lax.rem(lax.axis_index("section"), 2)
    edge_refs[0][...] = gpre_ref[pl.ds((1 - odd) * (rows - 1), 1)]
    edge_refs[1][...] = gpre_ref[pl.ds(odd * (rows - 1), 1)]
    views = views_ref[...].reshape(rows * cols, 3 * ch)
    grads = [ref[...] for ref in mids]
    above, below = beside_band(pair_refs, 3)
    kernel_sums(saved_ref, above, below, act_ref[...], grads, views, sums_ref)
    hand_out(sums_ref, *outs[3:])


def one_kernel(later, *refs):
    saved_ref, preact_ref, mid_ref = refs[0], refs[1], refs[4]
    nexts, temporal_ref = refs[5 : 5 + later], refs[5 + later]
    outs, scratch = refs[6 + later : 11 + later], refs[11 + later :]
    block_one(saved_ref, preact_ref, refs[2:4], [mid_ref, *nexts], temporal_ref, outs, scratch)


def mid_one_kernel(*refs):
    grad_ref, pair_refs, (after_inner_ref, after_edge_ref) = refs[0], refs[1:3], refs[5:7]
    temporal_two_ref, spatial_two_ref, saved_ref, preact_ref, temporal_ref = refs[7:12]
    mid_ref, outs, scratch = refs[12], refs[13:18], refs[18:21]
    next_ref, edge_ref, edge_views_ref = refs[21:]
    rows = grad_ref.shape[0]

    @pl.when(is_last())
    def _():
        edge_ref[...] = jnp.zeros(edge_ref.shape, edge_ref.dtype)
        next_ref[...] = jnp.zeros(next_ref.shape, next_ref.dtype)

    @pl.when(jnp.logical_not(is_last()))
    def _():
        edge_ref[...] = after_edge_ref[...]
        next_ref[0:1] = after_edge_ref[0:1]
        next_ref[1 : rows - 1] = after_inner_ref[...]
        next_ref[rows - 1 : rows] = after_edge_ref[1:2]

    mid_kernel(
        1, *refs[:5], edge_ref, temporal_two_ref, spatial_two_ref, mid_ref, edge_views_ref
    )
    block_one(saved_ref, preact_ref, pair_refs, [mid_ref, next_ref], temporal_ref, outs, scratch)


def input_kernel(mid_ref, gpre_ref, one_ref, two_ref, spatial_ref, out_ref, token_ref, views_ref):
    rows, cols, ch = out_ref.shape
    token_ref[...] = jnp.zeros(token_ref.shape, token_ref.dtype)
    step = 4
    above, below = beside_band((one_ref, two_ref), 0)
    beside(above.astype(jnp.float32), views_ref, 0)
    beside(below.astype(jnp.float32), views_ref, rows + 1)

    @pl.loop(0, rows // step)
    def _(n):
        gpre = gpre_ref[pl.ds(n * step, step)].astype(jnp.float32)
        beside(gpre, views_ref, n * step + 1)

    @pl.loop(0, rows // step)
    def _(n):
        here = pl.ds(n * step, step)
        out_ref[here] = convolved(views_ref, spatial_ref, n * step, mid_ref[here])


def pair_kernel(keep_ref, part_ref, own_ref, send_ref):
    across = lax.axis_index("section") // 2
    own_ref[...] = keep_ref[across] + part_ref[across].astype(jnp.float32)
    other = keep_ref[1 - across] + part_ref[1 - across].astype(jnp.float32)
    send_ref[...] = other.astype(jnp.bfloat16)


def band_kernel(one_ref, one_part_ref, two_ref, two_part_ref, keep_ref, send_ref):
    half = keep_ref.shape[1]
    frame = lax.axis_index("video")
    mine = pl.ds(pl.multiple_of(frame * half, half), half)
    other = pl.ds(pl.multiple_of((1 - frame) * half, half), half)
    for block, (own, part) in enumerate(((one_ref, one_part_ref), (two_ref, two_part_ref))):
        keep_ref[block] = own[mine] + part[mine].astype(jnp.float32)
        send_ref[block] = (own[other] + part[other].astype(jnp.float32)).astype(jnp.bfloat16)


def add_kernel(one_ref, two_ref, out_ref):
    total = one_ref[...].astype(jnp.float32) + two_ref[...].astype(jnp.float32)
    out_ref[...] = total.astype(jnp.bfloat16)


def scaled_kernel(factor, one_ref, two_ref, out_ref):
    total = one_ref[...].astype(jnp.float32) + two_ref[...].astype(jnp.float32)
    out_ref[...] = (total * factor).astype(jnp.bfloat16)


def join_kernel(own_ref, other_ref, out_ref):
    frame = lax.axis_index("video")
    out_ref[frame] = own_ref[...]
    out_ref[1 - frame] = other_ref[...]


def place_kernel(*refs):
    shares, outs = refs[:4], refs[4:]
    band = lax.axis_index("section")
    parts, _, height, _ = shares[0].shape
    for flip, share in enumerate(shares):
        place = jnp.bitwise_xor(band, flip)

        @pl.when(place < 3)
        def _():
            for block in range(2):
                for n in range(parts):
                    here = slice(n * height, (n + 1) * height)
                    outs[2 * block][place, here] = share[n, block].astype(jnp.float32)

        @pl.when(place == 3)
        def _():
            for block in range(2):
                for n in range(parts):
                    here = slice(n * height, (n + 1) * height)
                    outs[2 * block + 1][here] = share[n, block].astype(jnp.float32)


def bands_summed(keep, send):
    _, height, ch = keep.shape
    part = flipped(send, "section", 1)
    outs = [f32(height, ch), bf16(height, ch)]
    own, across = call(pair_kernel, outs, [], keep.size, keep, part)
    return own, flipped(across, "section", 2)


def totals(one, two, factor, meanwhile):
    height, ch = one[0].shape
    if lax.axis_size("video") == 2 and lax.axis_size("dp") == 4:
        cut = (2, height // 2, ch)
        size = height * ch
        keep, send = call(band_kernel, [f32(*cut), bf16(*cut)], [], 2 * size, *one, *two)
        own = call(add_kernel, [bf16(*cut)], [], size, keep, flipped(send, "video", 1))
        done, token = meanwhile((own,))
        own = call(add_kernel, [bf16(*cut)], [], size, own, flipped(own, "dp", 1))
        own = call(
            functools.partial(scaled_kernel, factor),
            [bf16(*cut)],
            [],
            size,
            own,
            flipped(own, "dp", 2),
            after=(token,),
        )
        other = flipped(own, "video", 1)
        share = call(join_kernel, [bf16(2, *cut)], [], 1, own, other)
    else:
        done, _ = meanwhile(())
        own = [sum(x.astype(jnp.float32) for x in parts) for parts in (one, two)]
        share = lax.psum(jnp.stack(own), ("video", "dp")) * factor
        share = share.astype(jnp.bfloat16)[None]
    across = flipped(share, "section", 2)
    outs = call(
        place_kernel,
        [f32(3, height, ch), f32(height, ch)] * 2,
        [],
        share.size,
        share,
        flipped(share, "section", 1),
        across,
        flipped(across, "section", 1),
    )
    outs = [x.reshape(3, 3, ch, ch) if x.ndim == 3 else x.reshape(3, ch, ch) for x in outs]
    return done, outs


def on_device(
    grad_latent,
    input_one,
    preact_one,
    input_two,
    preact_two,
    spatial_one,
    temporal_one,
    spatial_two,
    temporal_two,
):
    shape = grad_latent.shape
    rows, cols, ch = shape[2:]
    bands, frames = lax.axis_size("section"), lax.axis_size("video")
    later = min(2, frames - 1)
    pixels = lax.axis_size("dp") * frames * bands * rows * cols
    factor = 1.0 / math.sqrt(pixels)
    grad, saved_one, pre_one, saved_two, pre_two = (
        x.reshape(rows, cols, ch)
        for x in (grad_latent, input_one, preact_one, input_two, preact_two)
    )
    conv = 2 * rows * cols * 9 * ch * ch
    views = pltpu.VMEM((rows, cols, 3 * ch), jnp.bfloat16)
    edge_views = pltpu.VMEM((6, cols, 3 * ch), jnp.bfloat16)
    act = pltpu.VMEM((rows, cols, ch), jnp.bfloat16)
    sums = pltpu.VMEM((4, 3 * ch, ch), jnp.float32)
    handed = [f32(2, 3 * ch, ch), bf16(2, 3 * ch, ch)]
    inner_outs = [bf16(rows - 2, cols, ch), bf16(rows, cols, ch)]
    kernels = (temporal_two, spatial_two)

    def from_later(x):
        if frames == 2:
            return [flipped(x, "video", 1)]
        return [from_ahead(x, 0, n + 1) for n in range(later)]

    wholes = from_later(grad)
    packs = call(
        pack_kernel,
        [bf16(4, cols, ch)] * 2,
        [pltpu.SemaphoreType.DMA((8,))],
        1,
        grad,
        pre_two,
        saved_two,
        saved_one,
        spare_inputs=True,
        limit=58,
    )
    pairs = [paired(pack, start) for start, pack in enumerate(packs)]

    known = ()
    if frames == 2:
        known = call(
            last_inner_kernel,
            inner_outs,
            [views],
            1.2 * conv,
            grad,
            pre_two,
            *kernels,
            after=pairs[:1],
        )
        (after_inner,) = from_later(known[0])
        edge = call(
            last_edge_kernel,
            [bf16(4, cols, ch)],
            [edge_views],
            conv // 8,
            grad,
            *pairs,
            known[1],
            *kernels,
        )
    else:
        odd = lax.rem(lax.axis_index("section"), 2) == 1
        one, two = (pair[:1] for pair in pairs)
        above, below = jnp.where(odd, one, two), jnp.where(odd, two, one)
        edge = jnp.concatenate([grad[:1], grad[rows - 1 :], above, below])
    after_edges = from_later(edge)
    inner, gpre_two = call(
        functools.partial(inner_kernel, later),
        inner_outs,
        [views],
        1.2 * conv,
        grad,
        pre_two,
        *wholes,
        *kernels,
        *known,
    )
    parts_two = call(
        functools.partial(two_kernel, later),
        handed,
        [views, act, sums],
        1.2 * conv,
        saved_two,
        pre_two,
        gpre_two,
        *pairs,
        grad,
        *wholes,
    )
    sums_two = bands_summed(*parts_two)
    mid_inputs = (grad, *pairs, inner, gpre_two)
    one_inputs = (saved_one, pre_one)
    mid_outs = [bf16(rows, cols, ch)]
    one_outs = [bf16(rows, cols, ch)] + [bf16(1, cols, ch)] * 2 + handed
    if frames == 2:
        mid, gpre_one, *tail = call(
            mid_one_kernel,
            mid_outs + one_outs,
            [views, act, sums, act, pltpu.VMEM((4, cols, ch), jnp.bfloat16), edge_views],
            1.5 * conv,
            *mid_inputs,
            after_inner,
            *after_edges,
            *kernels,
            *one_inputs,
            temporal_one,
            after=sums_two[:1],
        )
    else:
        mid = call(
            functools.partial(mid_kernel, later),
            mid_outs,
            [edge_views],
            conv // 8,
            *mid_inputs,
            *after_edges,
            *kernels,
        )
        gpre_one, *tail = call(
            functools.partial(one_kernel, later),
            one_outs,
            [views, act, sums],
            1.2 * conv,
            *one_inputs,
            *pairs,
            mid,
            *from_later(mid),
            temporal_one,
        )
    edges_one, parts_one = tail[:2], tail[2:]

    def input_gradient(after):
        return call(
            input_kernel,
            [bf16(rows, cols, ch), f32(8, 128)],
            [pltpu.VMEM((rows + 2, cols, 3 * ch), jnp.bfloat16)],
            conv,
            mid,
            gpre_one,
            *[paired(edge, start) for start, edge in enumerate(edges_one)],
            spatial_one,
            after=after,
        )

    grad_in, sums = totals(bands_summed(*parts_one), sums_two, factor, input_gradient)
    return (grad_in.reshape(shape), *sums)


def solution(mesh):
    whole = P("dp", "video", "section", None, None)
    return jax.shard_map(
        on_device,
        mesh=mesh,
        in_specs=(whole,) * 5 + (P(),) * 4,
        out_specs=(whole, P(), P(), P(), P()),
        check_vma=False,
    )
```

```python
import functools
import math

import jax
import jax.numpy as jnp
from jax import lax
from jax.experimental import pallas as pl
from jax.experimental.pallas import tpu as pltpu
from jax.sharding import PartitionSpec as P

MIB = 1024 * 1024


def sigmoid(value):
    return 1.0 / (1.0 + jnp.exp(-value))


def bf16(*shape):
    return jax.ShapeDtypeStruct(shape, jnp.bfloat16)


def f32(*shape):
    return jax.ShapeDtypeStruct(shape, jnp.float32)


def call(kernel, outs, scratch, flops, *operands, after=(), spare_inputs=False, limit=24):
    single = len(outs) == 1
    moved = sum(math.prod(x.shape) * x.dtype.itemsize for x in (*operands, *outs))
    vmem = pl.BlockSpec(memory_space=pltpu.VMEM)
    spare = pl.BlockSpec(memory_space=pl.ANY)
    spec = spare if spare_inputs else vmem
    count = len(operands)
    operands = (*operands, *after)

    def body(*refs):
        kernel(*refs[:count], *refs[len(operands) :])

    return pl.pallas_call(
        body,
        out_shape=outs[0] if single else tuple(outs),
        in_specs=[spec] * count + [spare] * len(after),
        out_specs=vmem if single else (vmem,) * len(outs),
        scratch_shapes=scratch,
        compiler_params=pltpu.CompilerParams(vmem_limit_bytes=limit * MIB),
        cost_estimate=pl.CostEstimate(
            flops=int(flops), bytes_accessed=int(moved), transcendentals=0
        ),
    )(*operands)


def from_ahead(block, band_step, frame_step):
    bands, frames = lax.axis_size("section"), lax.axis_size("video")
    pairs = [
        ((band + band_step) * frames + frame + frame_step, band * frames + frame)
        for band in range(bands)
        for frame in range(frames)
        if 0 <= band + band_step < bands and frame + frame_step < frames
    ]
    return lax.ppermute(block, ("section", "video"), pairs)


def paired(block, start):
    bands = lax.axis_size("section")
    pairs = [(band, band + 1) for band in range(start, bands - 1, 2)]
    return lax.ppermute(block, "section", pairs + [(right, left) for left, right in pairs])


def beside_band(pair_refs, row):
    odd = lax.rem(lax.axis_index("section"), 2) == 1
    first, second = (ref[row : row + 1] for ref in pair_refs)
    return jnp.where(odd, first, second), jnp.where(odd, second, first)


def flipped(block, axis, flip):
    count = lax.axis_size(axis)
    return lax.ppermute(block, axis, [(place ^ flip, place) for place in range(count)])


def beside(gpre, views_ref, start):
    count, cols, ch = gpre.shape
    at = lax.broadcasted_iota(jnp.int32, gpre.shape, 1)
    right = jnp.where(at == cols - 1, 0.0, pltpu.roll(gpre, cols - 1, 1))
    left = jnp.where(at == 0, 0.0, pltpu.roll(gpre, 1, 1))
    here = pl.ds(start, count)
    views_ref[here, :, 0:ch] = right.astype(jnp.bfloat16)
    views_ref[here, :, ch : 2 * ch] = gpre.astype(jnp.bfloat16)
    views_ref[here, :, 2 * ch : 3 * ch] = left.astype(jnp.bfloat16)


def pre_gradient(grads, preact, temporal_ref):
    count, cols, ch = preact.shape
    flat = jnp.concatenate([grad.reshape(count * cols, ch) for grad in grads], axis=1)
    kernel = jnp.concatenate([temporal_ref[2 - step] for step in range(len(grads))], axis=1)
    gact = lax.dot_general(
        flat, kernel, (((1,), (1,)), ((), ())), preferred_element_type=jnp.float32
    )
    gact = gact.astype(jnp.bfloat16).astype(jnp.float32).reshape(preact.shape)
    hval = preact.astype(jnp.float32)
    sig = sigmoid(hval)
    return gact * sig * (1.0 + hval * (1.0 - sig))


def convolved(views_ref, spatial_ref, start, first):
    count, cols, ch = first.shape
    total = first.astype(jnp.float32).reshape(count * cols, ch)
    for ky in range(3):
        view = views_ref[pl.ds(start + 2 - ky, count)].reshape(count * cols, 3 * ch)
        kernel = jnp.concatenate([spatial_ref[ky, kx] for kx in range(3)], axis=1)
        total = total + lax.dot_general(
            view, kernel, (((1,), (1,)), ((), ())), preferred_element_type=jnp.float32
        )
    return total.astype(jnp.bfloat16).reshape(first.shape)


def is_last():
    return lax.axis_index("video") == lax.axis_size("video") - 1


def kernel_sums(saved_ref, above, below, act, grads, views, sums_ref):
    rows, cols, ch = saved_ref.shape
    flat = (rows * cols, ch)
    saved = [
        jnp.concatenate([above, saved_ref[: rows - 1]], axis=0),
        saved_ref[...],
        jnp.concatenate([saved_ref[1:], below], axis=0),
    ]
    for ky in range(3):
        sums = jnp.dot(saved[ky].reshape(flat).T, views, preferred_element_type=jnp.float32)
        for kx in range(3):
            sums_ref[ky, kx * ch : (kx + 1) * ch] = sums[:, kx * ch : (kx + 1) * ch]
    sums = jnp.dot(
        act.reshape(flat).T,
        jnp.concatenate([grad.reshape(flat) for grad in grads], axis=1),
        preferred_element_type=jnp.float32,
    )
    zeros = jnp.zeros((ch, ch), jnp.float32)
    for k in range(3):
        step = 2 - k
        value = sums[:, step * ch : (step + 1) * ch] if step < len(grads) else zeros
        sums_ref[3, k * ch : (k + 1) * ch] = jnp.where(is_last(), zeros, value) if step else value


def hand_out(sums_ref, keep_ref, send_ref):
    odd = lax.rem(lax.axis_index("section"), 2)
    height = sums_ref.shape[1]
    for n in range(2):
        keep_ref[n] = sums_ref[2 * n + odd]
        send_ref[n * height : (n + 1) * height] = sums_ref[2 * n + 1 - odd].astype(jnp.bfloat16)


def pack_kernel(*refs):
    parts, outs, sems = refs[:4], refs[4:6], refs[6]
    last = parts[0].shape[0] - 1
    odd = lax.rem(lax.axis_index("section"), 2)
    copies = []
    for n, part in enumerate(parts):
        for out, row in zip(outs, ((1 - odd) * last, odd * last)):
            sem = sems.at[len(copies)]
            copies.append(
                pltpu.make_async_copy(part.at[pl.ds(row, 1)], out.at[pl.ds(n, 1)], sem)
            )
    for copy in copies:
        copy.start()
    for copy in copies:
        copy.wait()


def interior(grad_ref, preact_ref, wholes, temporal_ref, spatial_ref, inner_ref, gpre_ref, views_ref):
    rows, cols, ch = grad_ref.shape
    step = 4

    @pl.loop(0, rows // step)
    def _(n):
        here = pl.ds(n * step, step)
        grads = [ref[here] for ref in (grad_ref, *wholes)]
        gpre = pre_gradient(grads, preact_ref[here], temporal_ref)
        gpre_ref[here] = gpre.astype(jnp.bfloat16)
        beside(gpre, views_ref, n * step)

    half = rows // 2 - 1

    @pl.loop(0, 2)
    def _(n):
        first = grad_ref[pl.ds(n * half + 1, half)]
        inner_ref[pl.ds(n * half, half)] = convolved(views_ref, spatial_ref, n * half, first)


def edge_rows(grad_ref, pair_refs, afters, gpre_ref, temporal_ref, spatial_ref, views_ref):
    rows, cols, ch = grad_ref.shape
    (grad_above, grad_below), (above_pre, below_pre) = (beside_band(pair_refs, n) for n in (0, 1))
    above = [grad_above] + [ref[0:1] for ref in afters]
    below = [grad_below] + [ref[1:2] for ref in afters]
    beside(pre_gradient(above, above_pre, temporal_ref), views_ref, 0)
    beside(gpre_ref[0:2].astype(jnp.float32), views_ref, 1)
    beside(gpre_ref[rows - 2 : rows].astype(jnp.float32), views_ref, 3)
    beside(pre_gradient(below, below_pre, temporal_ref), views_ref, 5)
    return (
        convolved(views_ref, spatial_ref, 0, grad_ref[0:1]),
        convolved(views_ref, spatial_ref, 3, grad_ref[rows - 1 : rows]),
    )


def last_inner_kernel(grad_ref, preact_ref, temporal_ref, spatial_ref, inner_ref, gpre_ref, views_ref):
    @pl.when(is_last())
    def _():
        interior(
            grad_ref, preact_ref, [], temporal_ref, spatial_ref, inner_ref, gpre_ref, views_ref
        )


def last_mid_kernel(grad_ref, one_ref, two_ref, inner_ref, gpre_ref, temporal_ref, spatial_ref, sent_ref, views_ref):
    rows = grad_ref.shape[0]

    @pl.when(is_last())
    def _():
        sent_ref[0:1], sent_ref[rows - 1 : rows] = edge_rows(
            grad_ref, (one_ref, two_ref), [], gpre_ref, temporal_ref, spatial_ref, views_ref
        )
        sent_ref[1 : rows - 1] = inner_ref[...]
        sent_ref[rows : rows + 1], sent_ref[rows + 1 : rows + 2] = beside_band(
            (one_ref, two_ref), 0
        )


def inner_kernel(later, *refs):
    inputs, wholes, kernels = refs[:2], refs[2 : 2 + later], refs[2 + later : 4 + later]
    known, outs = refs[4 + later : -3], refs[-3:]
    if not known:
        interior(*inputs, wholes, *kernels, *outs)
        return

    @pl.when(is_last())
    def _():
        outs[0][...] = known[0][...]
        outs[1][...] = known[1][...]

    @pl.when(jnp.logical_not(is_last()))
    def _():
        interior(*inputs, wholes, *kernels, *outs)


def mid_kernel(later, *refs):
    grad_ref, inner_ref, gpre_ref = refs[0], refs[3], refs[4]
    afters, (temporal_ref, spatial_ref, mid_ref, views_ref) = refs[5 : 5 + later], refs[5 + later :]
    rows = grad_ref.shape[0]
    first, last = edge_rows(
        grad_ref, refs[1:3], afters, gpre_ref, temporal_ref, spatial_ref, views_ref
    )
    mid_ref[0:1], mid_ref[rows - 1 : rows] = first, last
    mid_ref[1 : rows - 1] = inner_ref[...]


def two_kernel(later, *refs):
    saved_ref, preact_ref, gpre_ref = refs[:3]
    pair_refs, grad_ref = refs[3:5], refs[5]
    wholes, outs = refs[6 : 6 + later], refs[6 + later : 8 + later]
    views_ref, act_ref, sums_ref = refs[8 + later :]
    rows, cols, ch = saved_ref.shape
    step = 4

    @pl.loop(0, rows // step)
    def _(n):
        here = pl.ds(n * step, step)
        beside(gpre_ref[here].astype(jnp.float32), views_ref, n * step)
        hval = preact_ref[here].astype(jnp.float32)
        act_ref[here] = (hval * sigmoid(hval)).astype(jnp.bfloat16)

    views = views_ref[...].reshape(rows * cols, 3 * ch)
    grads = [ref[...] for ref in (grad_ref, *wholes)]
    above, below = beside_band(pair_refs, 2)
    kernel_sums(saved_ref, above, below, act_ref[...], grads, views, sums_ref)
    hand_out(sums_ref, *outs)


def block_one(saved_ref, preact_ref, pair_refs, mids, temporal_ref, outs, scratch):
    gpre_ref, keep_ref, send_ref = outs
    views_ref, act_ref, sums_ref = scratch
    rows, cols, ch = saved_ref.shape
    step = 4

    @pl.loop(0, rows // step)
    def _(n):
        here = pl.ds(n * step, step)
        gpre = pre_gradient([ref[here] for ref in mids], preact_ref[here], temporal_ref)
        gpre_ref[here] = gpre.astype(jnp.bfloat16)
        beside(gpre, views_ref, n * step)
        hval = preact_ref[here].astype(jnp.float32)
        act_ref[here] = (hval * sigmoid(hval)).astype(jnp.bfloat16)

    odd = lax.rem(lax.axis_index("section"), 2)
    size = send_ref.shape[0] - 2 * cols
    send_ref[size : size + cols] = gpre_ref[(1 - odd) * (rows - 1)]
    send_ref[size + cols : size + 2 * cols] = gpre_ref[odd * (rows - 1)]
    views = views_ref[...].reshape(rows * cols, 3 * ch)
    grads = [ref[...] for ref in mids]
    above, below = beside_band(pair_refs, 3)
    kernel_sums(saved_ref, above, below, act_ref[...], grads, views, sums_ref)
    hand_out(sums_ref, keep_ref, send_ref)


def one_kernel(later, *refs):
    saved_ref, preact_ref, mid_ref = refs[0], refs[1], refs[4]
    nexts, temporal_ref = refs[5 : 5 + later], refs[5 + later]
    outs, scratch = refs[6 + later : 9 + later], refs[9 + later :]
    block_one(saved_ref, preact_ref, refs[2:4], [mid_ref, *nexts], temporal_ref, outs, scratch)


def mid_one_kernel(*refs):
    pair_refs, after_ref = refs[1:3], refs[5]
    temporal_two_ref, spatial_two_ref, saved_ref, preact_ref, temporal_ref = refs[6:11]
    mid_ref, outs, scratch = refs[11], refs[12:15], refs[15:18]
    next_ref, edge_ref, edge_views_ref = refs[18:]
    rows = next_ref.shape[0]

    @pl.when(is_last())
    def _():
        edge_ref[...] = jnp.zeros(edge_ref.shape, edge_ref.dtype)
        next_ref[...] = jnp.zeros(next_ref.shape, next_ref.dtype)

    @pl.when(jnp.logical_not(is_last()))
    def _():
        next_ref[...] = after_ref[:rows]
        edge_ref[...] = after_ref[rows:]

    mid_kernel(
        1, *refs[:5], edge_ref, temporal_two_ref, spatial_two_ref, mid_ref, edge_views_ref
    )
    block_one(saved_ref, preact_ref, pair_refs, [mid_ref, next_ref], temporal_ref, outs, scratch)


def input_kernel(mid_ref, gpre_ref, pair_ref, across_ref, spatial_ref, out_ref, token_ref, views_ref):
    rows, cols, ch = out_ref.shape
    band, bands = lax.axis_index("section"), lax.axis_size("section")
    first = pair_ref[pair_ref.shape[0] - 2 * cols : pair_ref.shape[0] - cols]
    second = across_ref[across_ref.shape[0] - cols :]
    second = jnp.where((band > 0) & (band < bands - 1), second, jnp.zeros_like(second))
    odd = lax.rem(band, 2) == 1
    above, below = jnp.where(odd, first, second), jnp.where(odd, second, first)
    token_ref[...] = jnp.zeros(token_ref.shape, token_ref.dtype)
    step = 4
    beside(above.astype(jnp.float32)[None], views_ref, 0)
    beside(below.astype(jnp.float32)[None], views_ref, rows + 1)

    @pl.loop(0, rows // step)
    def _(n):
        gpre = gpre_ref[pl.ds(n * step, step)].astype(jnp.float32)
        beside(gpre, views_ref, n * step + 1)

    @pl.loop(0, rows // step)
    def _(n):
        here = pl.ds(n * step, step)
        out_ref[here] = convolved(views_ref, spatial_ref, n * step, mid_ref[here])


def pair_kernel(keep_ref, part_ref, own_ref, send_ref):
    _, height, _ = keep_ref.shape
    across = lax.axis_index("section") // 2
    other = 1 - across
    part = part_ref[pl.ds(pl.multiple_of(across * height, height), height)]
    own_ref[...] = keep_ref[across] + part.astype(jnp.float32)
    part = part_ref[pl.ds(pl.multiple_of(other * height, height), height)]
    send_ref[:height] = (keep_ref[other] + part.astype(jnp.float32)).astype(jnp.bfloat16)
    rest = send_ref.shape[0] - height
    if rest:
        send_ref[height:] = part_ref[2 * height + rest :]


def band_kernel(one_ref, one_part_ref, two_ref, two_part_ref, keep_ref, send_ref):
    half = keep_ref.shape[1]
    frame = lax.axis_index("video")
    mine = pl.ds(pl.multiple_of(frame * half, half), half)
    other = pl.ds(pl.multiple_of((1 - frame) * half, half), half)
    for block, (own, part) in enumerate(((one_ref, one_part_ref), (two_ref, two_part_ref))):
        keep_ref[block] = own[mine] + part[mine].astype(jnp.float32)
        send_ref[block] = (own[other] + part[other].astype(jnp.float32)).astype(jnp.bfloat16)


def add_kernel(one_ref, two_ref, out_ref):
    total = one_ref[...].astype(jnp.float32) + two_ref[...].astype(jnp.float32)
    out_ref[...] = total.astype(jnp.bfloat16)


def scaled_kernel(factor, one_ref, two_ref, out_ref):
    total = one_ref[...].astype(jnp.float32) + two_ref[...].astype(jnp.float32)
    out_ref[...] = (total * factor).astype(jnp.bfloat16)


def place_kernel(*refs):
    shares, outs = refs[:-4], refs[-4:]
    band, frame = lax.axis_index("section"), lax.axis_index("video")
    halves = len(shares) // 4
    height = shares[0].shape[1]
    for n, share in enumerate(shares):
        place = jnp.bitwise_xor(band, n // halves)
        half = jnp.bitwise_xor(frame, n % halves) if halves == 2 else 0
        here = pl.ds(pl.multiple_of(half * height, height), height)

        @pl.when(place < 3)
        def _():
            for block in range(2):
                outs[2 * block][place, here] = share[block].astype(jnp.float32)

        @pl.when(place == 3)
        def _():
            for block in range(2):
                outs[2 * block + 1][here] = share[block].astype(jnp.float32)


def bands_summed(keep, send, after=()):
    _, height, ch = keep.shape
    rest = (send.shape[0] - 2 * height) // 2
    pair = flipped(send, "section", 1)
    outs = [f32(height, ch), bf16(height + rest, ch)]
    own, across = call(pair_kernel, outs, [], keep.size, keep, pair, after=after)
    return own, flipped(across, "section", 2), pair


def totals(one, two, factor, meanwhile):
    height, ch = one[0].shape
    if lax.axis_size("video") == 2 and lax.axis_size("dp") == 4:
        cut = (2, height // 2, ch)
        size = height * ch
        operands = (*one[:2], *two[:2])
        keep, send = call(band_kernel, [f32(*cut), bf16(*cut)], [], 2 * size, *operands)
        own = call(add_kernel, [bf16(*cut)], [], size, keep, flipped(send, "video", 1))
        done, token = meanwhile((own,))
        own = call(add_kernel, [bf16(*cut)], [], size, own, flipped(own, "dp", 1))
        own = call(
            functools.partial(scaled_kernel, factor),
            [bf16(*cut)],
            [],
            size,
            own,
            flipped(own, "dp", 2),
            after=(token,),
        )
        shares = [own, flipped(own, "video", 1)]
    else:
        done, _ = meanwhile(())
        own = [x[0] + x[1][:height].astype(jnp.float32) for x in (one, two)]
        share = lax.psum(jnp.stack(own), ("video", "dp")) * factor
        shares = [share.astype(jnp.bfloat16)]
    across = [flipped(share, "section", 2) for share in shares]
    outs = call(
        place_kernel,
        [f32(3, height, ch), f32(height, ch)] * 2,
        [],
        4 * height * ch,
        *shares,
        *[flipped(share, "section", 1) for share in shares],
        *across,
        *[flipped(share, "section", 1) for share in across],
    )
    outs = [x.reshape(3, 3, ch, ch) if x.ndim == 3 else x.reshape(3, ch, ch) for x in outs]
    return done, outs


def on_device(
    grad_latent,
    input_one,
    preact_one,
    input_two,
    preact_two,
    spatial_one,
    temporal_one,
    spatial_two,
    temporal_two,
):
    shape = grad_latent.shape
    rows, cols, ch = shape[2:]
    bands, frames = lax.axis_size("section"), lax.axis_size("video")
    later = min(2, frames - 1)
    pixels = lax.axis_size("dp") * frames * bands * rows * cols
    factor = 1.0 / math.sqrt(pixels)
    grad, saved_one, pre_one, saved_two, pre_two = (
        x.reshape(rows, cols, ch)
        for x in (grad_latent, input_one, preact_one, input_two, preact_two)
    )
    conv = 2 * rows * cols * 9 * ch * ch
    views = pltpu.VMEM((rows, cols, 3 * ch), jnp.bfloat16)
    edge_views = pltpu.VMEM((6, cols, 3 * ch), jnp.bfloat16)
    act = pltpu.VMEM((rows, cols, ch), jnp.bfloat16)
    sums = pltpu.VMEM((4, 3 * ch, ch), jnp.float32)
    handed = [f32(2, 3 * ch, ch), bf16(6 * ch, ch)]
    inner_outs = [bf16(rows - 2, cols, ch), bf16(rows, cols, ch)]
    kernels = (temporal_two, spatial_two)

    def from_later(x):
        if frames == 2:
            return [flipped(x, "video", 1)]
        return [from_ahead(x, 0, n + 1) for n in range(later)]

    wholes = from_later(grad)
    packs = call(
        pack_kernel,
        [bf16(4, cols, ch)] * 2,
        [pltpu.SemaphoreType.DMA((8,))],
        1,
        grad,
        pre_two,
        saved_two,
        saved_one,
        spare_inputs=True,
        limit=58,
    )
    pairs = [paired(pack, start) for start, pack in enumerate(packs)]

    known = ()
    if frames == 2:
        known = call(
            last_inner_kernel,
            inner_outs,
            [views],
            1.2 * conv,
            grad,
            pre_two,
            *kernels,
            after=pairs[:1],
        )
        sent = call(
            last_mid_kernel,
            [bf16(rows + 2, cols, ch)],
            [edge_views],
            conv // 8,
            grad,
            *pairs,
            *known,
            *kernels,
        )
        afters = from_later(sent)
    else:
        odd = lax.rem(lax.axis_index("section"), 2) == 1
        one, two = (pair[:1] for pair in pairs)
        above, below = jnp.where(odd, one, two), jnp.where(odd, two, one)
        afters = from_later(jnp.concatenate([above, below]))
    inner, gpre_two = call(
        functools.partial(inner_kernel, later),
        inner_outs,
        [views],
        1.2 * conv,
        grad,
        pre_two,
        *wholes,
        *kernels,
        *known,
        after=(sent,) if frames == 2 else (),
    )
    parts_two = call(
        functools.partial(two_kernel, later),
        handed,
        [views, act, sums],
        1.2 * conv,
        saved_two,
        pre_two,
        gpre_two,
        *pairs,
        grad,
        *wholes,
    )
    sums_two = bands_summed(*parts_two)
    mid_inputs = (grad, *pairs, inner, gpre_two)
    one_inputs = (saved_one, pre_one)
    mid_outs = [bf16(rows, cols, ch)]
    one_outs = [bf16(rows, cols, ch), f32(2, 3 * ch, ch), bf16(6 * ch + 2 * cols, ch)]
    if frames == 2:
        mid, gpre_one, *parts_one = call(
            mid_one_kernel,
            mid_outs + one_outs,
            [views, act, sums, act, pltpu.VMEM((2, cols, ch), jnp.bfloat16), edge_views],
            1.5 * conv,
            *mid_inputs,
            *afters,
            *kernels,
            *one_inputs,
            temporal_one,
            after=sums_two[:1],
        )
    else:
        mid = call(
            functools.partial(mid_kernel, later),
            mid_outs,
            [edge_views],
            conv // 8,
            *mid_inputs,
            *afters,
            *kernels,
        )
        gpre_one, *parts_one = call(
            functools.partial(one_kernel, later),
            one_outs,
            [views, act, sums],
            1.2 * conv,
            *one_inputs,
            *pairs,
            mid,
            *from_later(mid),
            temporal_one,
        )
    keep, send = parts_one
    send, across = lax.optimization_barrier((send, sums_two[1]))
    sums_two = (sums_two[0], across)
    sums_one = bands_summed(keep, send)

    def input_gradient(after):
        return call(
            input_kernel,
            [bf16(rows, cols, ch), f32(8, 128)],
            [pltpu.VMEM((rows + 2, cols, 3 * ch), jnp.bfloat16)],
            conv,
            mid,
            gpre_one,
            sums_one[2],
            sums_one[1],
            spatial_one,
            after=after,
        )

    grad_in, sums = totals(sums_one, sums_two, factor, input_gradient)
    return (grad_in.reshape(shape), *sums)


def solution(mesh):
    whole = P("dp", "video", "section", None, None)
    return jax.shard_map(
        on_device,
        mesh=mesh,
        in_specs=(whole,) * 5 + (P(),) * 4,
        out_specs=(whole, P(), P(), P(), P()),
        check_vma=False,
    )
```

```python
import functools
import math

import jax
import jax.numpy as jnp
from jax import lax
from jax.experimental import pallas as pl
from jax.experimental.pallas import tpu as pltpu
from jax.sharding import PartitionSpec as P

MIB = 1024 * 1024


def sigmoid(value):
    return 1.0 / (1.0 + jnp.exp(-value))


def bf16(*shape):
    return jax.ShapeDtypeStruct(shape, jnp.bfloat16)


def f32(*shape):
    return jax.ShapeDtypeStruct(shape, jnp.float32)


def call(kernel, outs, scratch, flops, *operands, after=(), spare_inputs=False, limit=24):
    single = len(outs) == 1
    moved = sum(math.prod(x.shape) * x.dtype.itemsize for x in (*operands, *outs))
    vmem = pl.BlockSpec(memory_space=pltpu.VMEM)
    spare = pl.BlockSpec(memory_space=pl.ANY)
    spec = spare if spare_inputs else vmem
    count = len(operands)
    operands = (*operands, *after)

    def body(*refs):
        kernel(*refs[:count], *refs[len(operands) :])

    return pl.pallas_call(
        body,
        out_shape=outs[0] if single else tuple(outs),
        in_specs=[spec] * count + [spare] * len(after),
        out_specs=vmem if single else (vmem,) * len(outs),
        scratch_shapes=scratch,
        compiler_params=pltpu.CompilerParams(vmem_limit_bytes=limit * MIB),
        cost_estimate=pl.CostEstimate(
            flops=int(flops), bytes_accessed=int(moved), transcendentals=0
        ),
    )(*operands)


def from_ahead(block, band_step, frame_step):
    bands, frames = lax.axis_size("section"), lax.axis_size("video")
    pairs = [
        ((band + band_step) * frames + frame + frame_step, band * frames + frame)
        for band in range(bands)
        for frame in range(frames)
        if 0 <= band + band_step < bands and frame + frame_step < frames
    ]
    return lax.ppermute(block, ("section", "video"), pairs)


def beside_band(pair_refs, row):
    band = lax.axis_index("section")
    odd = lax.rem(band, 2) == 1
    inside = (band > 0) & (band < lax.axis_size("section") - 1)
    first, second = (ref[row : row + 1] for ref in pair_refs)
    second = jnp.where(inside, second, jnp.zeros_like(second))
    return jnp.where(odd, first, second), jnp.where(odd, second, first)


def flipped(block, axis, flip):
    count = lax.axis_size(axis)
    return lax.ppermute(block, axis, [(place ^ flip, place) for place in range(count)])


def flipped_both(block):
    bands = lax.axis_size("section")
    pairs = [
        (2 * (band ^ 2) + 1 - frame, 2 * band + frame) for band in range(bands) for frame in range(2)
    ]
    return lax.ppermute(block, ("section", "video"), pairs)


def later_than(block, *others):
    return lax.optimization_barrier((block, *others))[0]


def beside(gpre, views_ref, start):
    count, cols, ch = gpre.shape
    at = lax.broadcasted_iota(jnp.int32, gpre.shape, 1)
    right = jnp.where(at == cols - 1, 0.0, pltpu.roll(gpre, cols - 1, 1))
    left = jnp.where(at == 0, 0.0, pltpu.roll(gpre, 1, 1))
    here = pl.ds(start, count)
    views_ref[here, :, 0:ch] = right.astype(jnp.bfloat16)
    views_ref[here, :, ch : 2 * ch] = gpre.astype(jnp.bfloat16)
    views_ref[here, :, 2 * ch : 3 * ch] = left.astype(jnp.bfloat16)


def pre_gradient(grads, preact, temporal_ref):
    count, cols, ch = preact.shape
    flat = jnp.concatenate([grad.reshape(count * cols, ch) for grad in grads], axis=1)
    kernel = jnp.concatenate([temporal_ref[2 - step] for step in range(len(grads))], axis=1)
    gact = lax.dot_general(
        flat, kernel, (((1,), (1,)), ((), ())), preferred_element_type=jnp.float32
    )
    gact = gact.astype(jnp.bfloat16).astype(jnp.float32).reshape(preact.shape)
    hval = preact.astype(jnp.float32)
    sig = sigmoid(hval)
    return gact * sig * (1.0 + hval * (1.0 - sig))


def convolved(views_ref, spatial_ref, start, first):
    count, cols, ch = first.shape
    total = first.astype(jnp.float32).reshape(count * cols, ch)
    for ky in range(3):
        view = views_ref[pl.ds(start + 2 - ky, count)].reshape(count * cols, 3 * ch)
        kernel = jnp.concatenate([spatial_ref[ky, kx] for kx in range(3)], axis=1)
        total = total + lax.dot_general(
            view, kernel, (((1,), (1,)), ((), ())), preferred_element_type=jnp.float32
        )
    return total.astype(jnp.bfloat16).reshape(first.shape)


def is_last():
    return lax.axis_index("video") == lax.axis_size("video") - 1


def kernel_sums(saved_ref, above, below, act, grads, views, sums_ref):
    rows, cols, ch = saved_ref.shape
    flat = (rows * cols, ch)
    saved = [
        jnp.concatenate([above, saved_ref[: rows - 1]], axis=0),
        saved_ref[...],
        jnp.concatenate([saved_ref[1:], below], axis=0),
    ]
    for ky in range(3):
        sums = jnp.dot(saved[ky].reshape(flat).T, views, preferred_element_type=jnp.float32)
        for kx in range(3):
            sums_ref[ky, kx * ch : (kx + 1) * ch] = sums[:, kx * ch : (kx + 1) * ch]
    sums = jnp.dot(
        act.reshape(flat).T,
        jnp.concatenate([grad.reshape(flat) for grad in grads], axis=1),
        preferred_element_type=jnp.float32,
    )
    zeros = jnp.zeros((ch, ch), jnp.float32)
    for k in range(3):
        step = 2 - k
        value = sums[:, step * ch : (step + 1) * ch] if step < len(grads) else zeros
        sums_ref[3, k * ch : (k + 1) * ch] = jnp.where(is_last(), zeros, value) if step else value


def hand_out(sums_ref, keep_ref, send_ref):
    odd = lax.rem(lax.axis_index("section"), 2)
    height = sums_ref.shape[1]
    for n in range(2):
        keep_ref[n] = sums_ref[2 * n + odd]
        send_ref[n * height : (n + 1) * height] = sums_ref[2 * n + 1 - odd].astype(jnp.bfloat16)


def pack_kernel(*refs):
    parts, outs, sems = refs[:4], refs[4:6], refs[6]
    last = parts[0].shape[0] - 1
    odd = lax.rem(lax.axis_index("section"), 2)
    copies = []
    for n, part in enumerate(parts):
        for out, row in zip(outs, ((1 - odd) * last, odd * last)):
            sem = sems.at[len(copies)]
            copies.append(
                pltpu.make_async_copy(part.at[pl.ds(row, 1)], out.at[pl.ds(n, 1)], sem)
            )
    for copy in copies:
        copy.start()
    for copy in copies:
        copy.wait()


def interior(grad_ref, preact_ref, wholes, temporal_ref, spatial_ref, inner_ref, gpre_ref, views_ref):
    rows, cols, ch = grad_ref.shape
    step = 4

    @pl.loop(0, rows // step)
    def _(n):
        here = pl.ds(n * step, step)
        grads = [ref[here] for ref in (grad_ref, *wholes)]
        gpre = pre_gradient(grads, preact_ref[here], temporal_ref)
        gpre_ref[here] = gpre.astype(jnp.bfloat16)
        beside(gpre, views_ref, n * step)

    half = rows // 2 - 1

    @pl.loop(0, 2)
    def _(n):
        first = grad_ref[pl.ds(n * half + 1, half)]
        inner_ref[pl.ds(n * half, half)] = convolved(views_ref, spatial_ref, n * half, first)


def edge_rows(grad_ref, pair_refs, afters, gpre_ref, temporal_ref, spatial_ref, views_ref):
    rows, cols, ch = grad_ref.shape
    (grad_above, grad_below), (above_pre, below_pre) = (beside_band(pair_refs, n) for n in (0, 1))
    above = [grad_above] + [ref[0:1] for ref in afters]
    below = [grad_below] + [ref[1:2] for ref in afters]
    beside(pre_gradient(above, above_pre, temporal_ref), views_ref, 0)
    beside(gpre_ref[0:2].astype(jnp.float32), views_ref, 1)
    beside(gpre_ref[rows - 2 : rows].astype(jnp.float32), views_ref, 3)
    beside(pre_gradient(below, below_pre, temporal_ref), views_ref, 5)
    return (
        convolved(views_ref, spatial_ref, 0, grad_ref[0:1]),
        convolved(views_ref, spatial_ref, 3, grad_ref[rows - 1 : rows]),
    )


def last_inner_kernel(grad_ref, preact_ref, temporal_ref, spatial_ref, inner_ref, gpre_ref, views_ref):
    @pl.when(is_last())
    def _():
        interior(
            grad_ref, preact_ref, [], temporal_ref, spatial_ref, inner_ref, gpre_ref, views_ref
        )


def last_mid_kernel(grad_ref, one_ref, two_ref, inner_ref, gpre_ref, temporal_ref, spatial_ref, sent_ref, views_ref):
    rows = grad_ref.shape[0]

    @pl.when(is_last())
    def _():
        sent_ref[0:1], sent_ref[rows - 1 : rows] = edge_rows(
            grad_ref, (one_ref, two_ref), [], gpre_ref, temporal_ref, spatial_ref, views_ref
        )
        sent_ref[1 : rows - 1] = inner_ref[...]
        sent_ref[rows : rows + 1], sent_ref[rows + 1 : rows + 2] = beside_band(
            (one_ref, two_ref), 0
        )


def inner_kernel(later, *refs):
    inputs, wholes, kernels = refs[:2], refs[2 : 2 + later], refs[2 + later : 4 + later]
    known, outs = refs[4 + later : -3], refs[-3:]
    if not known:
        interior(*inputs, wholes, *kernels, *outs)
        return

    @pl.when(is_last())
    def _():
        outs[0][...] = known[0][...]
        outs[1][...] = known[1][...]

    @pl.when(jnp.logical_not(is_last()))
    def _():
        interior(*inputs, wholes, *kernels, *outs)


def mid_kernel(later, *refs):
    grad_ref, inner_ref, gpre_ref = refs[0], refs[3], refs[4]
    afters, (temporal_ref, spatial_ref, mid_ref, views_ref) = refs[5 : 5 + later], refs[5 + later :]
    rows = grad_ref.shape[0]
    first, last = edge_rows(
        grad_ref, refs[1:3], afters, gpre_ref, temporal_ref, spatial_ref, views_ref
    )
    mid_ref[0:1], mid_ref[rows - 1 : rows] = first, last
    mid_ref[1 : rows - 1] = inner_ref[...]


def two_kernel(later, *refs):
    saved_ref, preact_ref, gpre_ref = refs[:3]
    pair_refs, grad_ref = refs[3:5], refs[5]
    wholes, outs = refs[6 : 6 + later], refs[6 + later : 8 + later]
    views_ref, act_ref, sums_ref = refs[8 + later :]
    rows, cols, ch = saved_ref.shape
    step = 4

    @pl.loop(0, rows // step)
    def _(n):
        here = pl.ds(n * step, step)
        beside(gpre_ref[here].astype(jnp.float32), views_ref, n * step)
        hval = preact_ref[here].astype(jnp.float32)
        act_ref[here] = (hval * sigmoid(hval)).astype(jnp.bfloat16)

    views = views_ref[...].reshape(rows * cols, 3 * ch)
    grads = [ref[...] for ref in (grad_ref, *wholes)]
    above, below = beside_band(pair_refs, 2)
    kernel_sums(saved_ref, above, below, act_ref[...], grads, views, sums_ref)
    hand_out(sums_ref, *outs)


def block_one(saved_ref, preact_ref, pair_refs, mids, temporal_ref, outs, scratch):
    gpre_ref, keep_ref, send_ref = outs
    views_ref, act_ref, sums_ref = scratch
    rows, cols, ch = saved_ref.shape
    step = 4

    @pl.loop(0, rows // step)
    def _(n):
        here = pl.ds(n * step, step)
        gpre = pre_gradient([ref[here] for ref in mids], preact_ref[here], temporal_ref)
        gpre_ref[here] = gpre.astype(jnp.bfloat16)
        beside(gpre, views_ref, n * step)
        hval = preact_ref[here].astype(jnp.float32)
        act_ref[here] = (hval * sigmoid(hval)).astype(jnp.bfloat16)

    odd = lax.rem(lax.axis_index("section"), 2)
    size = send_ref.shape[0] - 2 * cols
    send_ref[size : size + cols] = gpre_ref[(1 - odd) * (rows - 1)]
    send_ref[size + cols : size + 2 * cols] = gpre_ref[odd * (rows - 1)]
    views = views_ref[...].reshape(rows * cols, 3 * ch)
    grads = [ref[...] for ref in mids]
    above, below = beside_band(pair_refs, 3)
    kernel_sums(saved_ref, above, below, act_ref[...], grads, views, sums_ref)
    hand_out(sums_ref, keep_ref, send_ref)


def one_kernel(later, *refs):
    saved_ref, preact_ref, mid_ref = refs[0], refs[1], refs[4]
    nexts, temporal_ref = refs[5 : 5 + later], refs[5 + later]
    outs, scratch = refs[6 + later : 9 + later], refs[9 + later :]
    block_one(saved_ref, preact_ref, refs[2:4], [mid_ref, *nexts], temporal_ref, outs, scratch)


def mid_one_kernel(*refs):
    pair_refs, after_ref = refs[1:3], refs[5]
    temporal_two_ref, spatial_two_ref, saved_ref, preact_ref, temporal_ref = refs[6:11]
    mid_ref, outs, scratch = refs[11], refs[12:15], refs[15:18]
    next_ref, edge_ref, edge_views_ref = refs[18:]
    rows = next_ref.shape[0]

    @pl.when(is_last())
    def _():
        edge_ref[...] = jnp.zeros(edge_ref.shape, edge_ref.dtype)
        next_ref[...] = jnp.zeros(next_ref.shape, next_ref.dtype)

    @pl.when(jnp.logical_not(is_last()))
    def _():
        next_ref[...] = after_ref[:rows]
        edge_ref[...] = after_ref[rows:]

    mid_kernel(
        1, *refs[:5], edge_ref, temporal_two_ref, spatial_two_ref, mid_ref, edge_views_ref
    )
    block_one(saved_ref, preact_ref, pair_refs, [mid_ref, next_ref], temporal_ref, outs, scratch)


def input_kernel(mid_ref, gpre_ref, pair_ref, across_ref, spatial_ref, out_ref, token_ref, views_ref):
    rows, cols, ch = out_ref.shape
    pair = pair_ref[pair_ref.shape[0] - 2 * cols : pair_ref.shape[0] - cols]
    above, below = beside_band((pair[None], across_ref[across_ref.shape[0] - cols :][None]), 0)
    token_ref[...] = jnp.zeros(token_ref.shape, token_ref.dtype)
    step = 4
    beside(above.astype(jnp.float32), views_ref, 0)
    beside(below.astype(jnp.float32), views_ref, rows + 1)

    @pl.loop(0, rows // step)
    def _(n):
        gpre = gpre_ref[pl.ds(n * step, step)].astype(jnp.float32)
        beside(gpre, views_ref, n * step + 1)

    @pl.loop(0, rows // step)
    def _(n):
        here = pl.ds(n * step, step)
        out_ref[here] = convolved(views_ref, spatial_ref, n * step, mid_ref[here])


def halves(count, index):
    return [pl.ds(pl.multiple_of(n * count, count), count) for n in (index, 1 - index)]


def pair_kernel(keep_ref, part_ref, own_ref, send_ref):
    across = lax.axis_index("section") // 2
    mine, other = halves(own_ref.shape[0], across)
    own_ref[...] = keep_ref[across] + part_ref[mine].astype(jnp.float32)
    total = keep_ref[1 - across] + part_ref[other].astype(jnp.float32)
    send_ref[...] = total.astype(jnp.bfloat16)


def band_kernel(own_ref, part_ref, keep_ref, send_ref):
    mine, other = halves(keep_ref.shape[0], lax.axis_index("video"))
    keep_ref[...] = own_ref[mine] + part_ref[mine].astype(jnp.float32)
    send_ref[...] = (own_ref[other] + part_ref[other].astype(jnp.float32)).astype(jnp.bfloat16)


def pair_quarter_kernel(keep_ref, part_ref, own_ref, across_ref, frame_ref, both_ref):
    _, height, _ = keep_ref.shape
    half = own_ref.shape[0]
    band = lax.axis_index("section") // 2
    frames = halves(half, lax.axis_index("video"))

    def quarter(band, rows):
        start = pl.multiple_of(band * height, height)
        part = part_ref.at[pl.ds(start, height)][rows]
        return keep_ref[band, rows] + part.astype(jnp.float32)

    own_ref[...] = quarter(band, frames[0])
    across_ref[:half] = quarter(1 - band, frames[0]).astype(jnp.bfloat16)
    rest = across_ref.shape[0] - half
    across_ref[half:] = part_ref[2 * height + rest :]
    frame_ref[...] = quarter(band, frames[1]).astype(jnp.bfloat16)
    both_ref[...] = quarter(1 - band, frames[1]).astype(jnp.bfloat16)


def plane_kernel(own_ref, *refs):
    parts, out_ref = refs[:-1], refs[-1]
    total = own_ref[...]
    for part in parts:
        total = total + part[: out_ref.shape[0]].astype(jnp.float32)
    out_ref[...] = total.astype(jnp.bfloat16)


def add_kernel(one_ref, two_ref, out_ref):
    total = one_ref[...].astype(jnp.float32) + two_ref[...].astype(jnp.float32)
    out_ref[...] = total.astype(jnp.bfloat16)


def scaled_kernel(factor, *refs):
    out_ref = refs[-1]
    for block in range(2):
        one, two = (ref[...].astype(jnp.float32) for ref in refs[2 * block : 2 * block + 2])
        out_ref[block] = ((one + two) * factor).astype(jnp.bfloat16)


def place_kernel(*refs):
    shares, outs = refs[:-4], refs[-4:]
    band, frame = lax.axis_index("section"), lax.axis_index("video")
    halves = len(shares) // 4
    height = shares[0].shape[1]
    for n, share in enumerate(shares):
        place = jnp.bitwise_xor(band, n // halves)
        half = jnp.bitwise_xor(frame, n % halves) if halves == 2 else 0
        here = pl.ds(pl.multiple_of(half * height, height), height)

        @pl.when(place < 3)
        def _():
            for block in range(2):
                outs[2 * block][place, here] = share[block].astype(jnp.float32)

        @pl.when(place == 3)
        def _():
            for block in range(2):
                outs[2 * block + 1][here] = share[block].astype(jnp.float32)


def place(shares):
    across = [flipped(share, "section", 2) for share in shares]
    ch = shares[0].shape[2]
    outs = call(
        place_kernel,
        [f32(3, 3 * ch, ch), f32(3 * ch, ch)] * 2,
        [],
        12 * ch * ch,
        *shares,
        *[flipped(share, "section", 1) for share in shares],
        *across,
        *[flipped(share, "section", 1) for share in across],
    )
    return [x.reshape(3, 3, ch, ch) if x.ndim == 3 else x.reshape(3, ch, ch) for x in outs]


def on_device(
    grad_latent,
    input_one,
    preact_one,
    input_two,
    preact_two,
    spatial_one,
    temporal_one,
    spatial_two,
    temporal_two,
):
    shape = grad_latent.shape
    rows, cols, ch = shape[2:]
    bands, frames = lax.axis_size("section"), lax.axis_size("video")
    later = min(2, frames - 1)
    pixels = lax.axis_size("dp") * frames * bands * rows * cols
    factor = 1.0 / math.sqrt(pixels)
    grad, saved_one, pre_one, saved_two, pre_two = (
        x.reshape(rows, cols, ch)
        for x in (grad_latent, input_one, preact_one, input_two, preact_two)
    )
    conv = 2 * rows * cols * 9 * ch * ch
    views = pltpu.VMEM((rows, cols, 3 * ch), jnp.bfloat16)
    edge_views = pltpu.VMEM((6, cols, 3 * ch), jnp.bfloat16)
    act = pltpu.VMEM((rows, cols, ch), jnp.bfloat16)
    sums = pltpu.VMEM((4, 3 * ch, ch), jnp.float32)
    handed = [f32(2, 3 * ch, ch), bf16(6 * ch, ch)]
    inner_outs = [bf16(rows - 2, cols, ch), bf16(rows, cols, ch)]
    kernels = (temporal_two, spatial_two)

    def from_later(x):
        if frames == 2:
            return [flipped(x, "video", 1)]
        return [from_ahead(x, 0, n + 1) for n in range(later)]

    wholes = from_later(grad)
    packs = call(
        pack_kernel,
        [bf16(4, cols, ch)] * 2,
        [pltpu.SemaphoreType.DMA((8,))],
        1,
        grad,
        pre_two,
        saved_two,
        saved_one,
        spare_inputs=True,
        limit=58,
    )
    first, second = (flipped(pack, "section", 1) for pack in packs)
    pairs = [first, flipped(second, "section", 2)]

    known = ()
    if frames == 2:
        known = call(
            last_inner_kernel,
            inner_outs,
            [views],
            1.2 * conv,
            grad,
            pre_two,
            *kernels,
            after=(first, second),
        )
        sent = call(
            last_mid_kernel,
            [bf16(rows + 2, cols, ch)],
            [edge_views],
            conv // 8,
            grad,
            *pairs,
            *known,
            *kernels,
        )
        afters = from_later(sent)
    else:
        afters = from_later(jnp.concatenate(beside_band(pairs, 0)))
    inner, gpre_two = call(
        functools.partial(inner_kernel, later),
        inner_outs,
        [views],
        1.2 * conv,
        grad,
        pre_two,
        *wholes,
        *kernels,
        *known,
        after=(sent,) if frames == 2 else (),
    )
    parts_two = call(
        functools.partial(two_kernel, later),
        handed,
        [views, act, sums],
        1.2 * conv,
        saved_two,
        pre_two,
        gpre_two,
        *pairs,
        grad,
        *wholes,
    )
    height, half = 3 * ch, 3 * ch // 2
    keep_two, send_two = parts_two
    own_two, send_two = call(
        pair_kernel,
        [f32(height, ch), bf16(height, ch)],
        [],
        height * ch,
        keep_two,
        flipped(send_two, "section", 1),
    )
    across_two = flipped(send_two, "section", 2)
    mid_inputs = (grad, *pairs, inner, gpre_two)
    one_inputs = (saved_one, pre_one)
    mid_outs = [bf16(rows, cols, ch)]
    one_outs = [bf16(rows, cols, ch), f32(2, 3 * ch, ch), bf16(6 * ch + 2 * cols, ch)]
    if frames == 2:
        mid, gpre_one, *parts_one = call(
            mid_one_kernel,
            mid_outs + one_outs,
            [views, act, sums, act, pltpu.VMEM((2, cols, ch), jnp.bfloat16), edge_views],
            1.5 * conv,
            *mid_inputs,
            *afters,
            *kernels,
            *one_inputs,
            temporal_one,
            after=(own_two,),
        )
    else:
        mid = call(
            functools.partial(mid_kernel, later),
            mid_outs,
            [edge_views],
            conv // 8,
            *mid_inputs,
            *afters,
            *kernels,
        )
        gpre_one, *parts_one = call(
            functools.partial(one_kernel, later),
            one_outs,
            [views, act, sums],
            1.2 * conv,
            *one_inputs,
            *pairs,
            mid,
            *from_later(mid),
            temporal_one,
        )
    keep_one, send_one = parts_one
    split = frames == 2 and lax.axis_size("dp") == 4
    if split:
        send_one = later_than(send_one, across_two)
    pair_one = flipped(send_one, "section", 1)

    def input_gradient(edge, after):
        return call(
            input_kernel,
            [bf16(rows, cols, ch), f32(8, 128)],
            [pltpu.VMEM((rows + 2, cols, 3 * ch), jnp.bfloat16)],
            conv,
            mid,
            gpre_one,
            pair_one,
            edge,
            spatial_one,
            after=after,
        )

    if split:

        def added(one, two):
            return call(add_kernel, [bf16(half, ch)], [], half * ch, one, two)

        keep_two, send_two = call(
            band_kernel,
            [f32(half, ch), bf16(half, ch)],
            [],
            height * ch,
            own_two,
            across_two,
        )
        sum_two = added(keep_two, flipped(send_two, "video", 1))
        quarters = [f32(half, ch), bf16(half + cols, ch)] + [bf16(half, ch)] * 2
        own_one, *sends = call(
            pair_quarter_kernel, quarters, [], height * ch, keep_one, pair_one, after=(send_two,)
        )
        across = flipped(sends[0], "section", 2)
        parts = [across, flipped(sends[1], "video", 1), flipped_both(sends[2])]
        sum_one = call(plane_kernel, [bf16(half, ch)], [], 4 * half * ch, own_one, *parts)
        part_two = flipped(sum_two, "dp", 1)
        part_one = flipped(later_than(sum_one, sum_two), "dp", 1)
        sum_two = added(sum_two, part_two)
        sum_one = added(sum_one, part_one)
        last_two = flipped(sum_two, "dp", 2)
        last_one = flipped(later_than(sum_one, sum_two), "dp", 2)
        grad_in, token = input_gradient(across, (sum_one,))
        own = call(
            functools.partial(scaled_kernel, factor),
            [bf16(2, half, ch)],
            [],
            height * ch,
            sum_one,
            last_one,
            sum_two,
            last_two,
            after=(token,),
        )
        sums = place([own, flipped(own, "video", 1)])
    else:
        own_one, send_one = call(
            pair_kernel, [f32(height, ch), bf16(height, ch)], [], height * ch, keep_one, pair_one
        )
        edge = flipped(pair_one[pair_one.shape[0] - cols :], "section", 2)
        grad_in, _ = input_gradient(edge, ())
        own_one = own_one + flipped(send_one, "section", 2).astype(jnp.float32)
        own_two = own_two + across_two.astype(jnp.float32)
        share = lax.psum(jnp.stack((own_one, own_two)), ("video", "dp")) * factor
        sums = place([share.astype(jnp.bfloat16)])
    return (grad_in.reshape(shape), *sums)


def solution(mesh):
    whole = P("dp", "video", "section", None, None)
    return jax.shard_map(
        on_device,
        mesh=mesh,
        in_specs=(whole,) * 5 + (P(),) * 4,
        out_specs=(whole, P(), P(), P(), P()),
        check_vma=False,
    )
```

```python
import functools
import math

import jax
import jax.numpy as jnp
from jax import lax
from jax.experimental import pallas as pl
from jax.experimental.pallas import tpu as pltpu
from jax.sharding import PartitionSpec as P

MIB = 1024 * 1024


def sigmoid(value):
    return 1.0 / (1.0 + jnp.exp(-value))


def bf16(*shape):
    return jax.ShapeDtypeStruct(shape, jnp.bfloat16)


def f32(*shape):
    return jax.ShapeDtypeStruct(shape, jnp.float32)


def call(
    kernel, outs, scratch, flops, *operands, after=(), spare_inputs=False, outs_where=pltpu.VMEM, limit=24
):
    single = len(outs) == 1
    moved = sum(math.prod(x.shape) * x.dtype.itemsize for x in (*operands, *outs))
    vmem = pl.BlockSpec(memory_space=pltpu.VMEM)
    spare = pl.BlockSpec(memory_space=pl.ANY)
    spec = spare if spare_inputs else vmem
    out_spec = pl.BlockSpec(memory_space=outs_where)
    count = len(operands)
    operands = (*operands, *after)

    def body(*refs):
        kernel(*refs[:count], *refs[len(operands) :])

    return pl.pallas_call(
        body,
        out_shape=outs[0] if single else tuple(outs),
        in_specs=[spec] * count + [spare] * len(after),
        out_specs=out_spec if single else (out_spec,) * len(outs),
        scratch_shapes=scratch,
        compiler_params=pltpu.CompilerParams(vmem_limit_bytes=limit * MIB),
        cost_estimate=pl.CostEstimate(
            flops=int(flops), bytes_accessed=int(moved), transcendentals=0
        ),
    )(*operands)


def from_ahead(block, band_step, frame_step):
    bands, frames = lax.axis_size("section"), lax.axis_size("video")
    pairs = [
        ((band + band_step) * frames + frame + frame_step, band * frames + frame)
        for band in range(bands)
        for frame in range(frames)
        if 0 <= band + band_step < bands and frame + frame_step < frames
    ]
    return lax.ppermute(block, ("section", "video"), pairs)


def beside_band(pair_refs, row):
    band = lax.axis_index("section")
    odd = lax.rem(band, 2) == 1
    inside = (band > 0) & (band < lax.axis_size("section") - 1)
    first, second = (ref[row : row + 1] for ref in pair_refs)
    second = jnp.where(inside, second, jnp.zeros_like(second))
    return jnp.where(odd, first, second), jnp.where(odd, second, first)


def flipped(block, axis, flip):
    count = lax.axis_size(axis)
    return lax.ppermute(block, axis, [(place ^ flip, place) for place in range(count)])


def flipped_both(block):
    bands = lax.axis_size("section")
    pairs = [
        (2 * (band ^ 2) + 1 - frame, 2 * band + frame) for band in range(bands) for frame in range(2)
    ]
    return lax.ppermute(block, ("section", "video"), pairs)


def later_than(block, *others):
    return lax.optimization_barrier((block, *others))[0]


def beside(gpre, views_ref, start):
    count, cols, ch = gpre.shape
    at = lax.broadcasted_iota(jnp.int32, gpre.shape, 1)
    right = jnp.where(at == cols - 1, 0.0, pltpu.roll(gpre, cols - 1, 1))
    left = jnp.where(at == 0, 0.0, pltpu.roll(gpre, 1, 1))
    here = pl.ds(start, count)
    views_ref[here, :, 0:ch] = right.astype(jnp.bfloat16)
    views_ref[here, :, ch : 2 * ch] = gpre.astype(jnp.bfloat16)
    views_ref[here, :, 2 * ch : 3 * ch] = left.astype(jnp.bfloat16)


def pre_gradient(grads, preact, temporal_ref):
    count, cols, ch = preact.shape
    flat = jnp.concatenate([grad.reshape(count * cols, ch) for grad in grads], axis=1)
    kernel = jnp.concatenate([temporal_ref[2 - step] for step in range(len(grads))], axis=1)
    gact = lax.dot_general(
        flat, kernel, (((1,), (1,)), ((), ())), preferred_element_type=jnp.float32
    )
    gact = gact.astype(jnp.bfloat16).astype(jnp.float32).reshape(preact.shape)
    hval = preact.astype(jnp.float32)
    sig = sigmoid(hval)
    return gact * sig * (1.0 + hval * (1.0 - sig))


def convolved(views_ref, spatial_ref, start, first):
    count, cols, ch = first.shape
    total = first.astype(jnp.float32).reshape(count * cols, ch)
    for ky in range(3):
        view = views_ref[pl.ds(start + 2 - ky, count)].reshape(count * cols, 3 * ch)
        kernel = jnp.concatenate([spatial_ref[ky, kx] for kx in range(3)], axis=1)
        total = total + lax.dot_general(
            view, kernel, (((1,), (1,)), ((), ())), preferred_element_type=jnp.float32
        )
    return total.astype(jnp.bfloat16).reshape(first.shape)


def is_last():
    return lax.axis_index("video") == lax.axis_size("video") - 1


def kernel_sums(saved_ref, above, below, act, grads, views, sums_ref):
    rows, cols, ch = saved_ref.shape
    flat = (rows * cols, ch)
    saved = [
        jnp.concatenate([above, saved_ref[: rows - 1]], axis=0),
        saved_ref[...],
        jnp.concatenate([saved_ref[1:], below], axis=0),
    ]
    for ky in range(3):
        sums = jnp.dot(saved[ky].reshape(flat).T, views, preferred_element_type=jnp.float32)
        for kx in range(3):
            sums_ref[ky, kx * ch : (kx + 1) * ch] = sums[:, kx * ch : (kx + 1) * ch]
    sums = jnp.dot(
        act.reshape(flat).T,
        jnp.concatenate([grad.reshape(flat) for grad in grads], axis=1),
        preferred_element_type=jnp.float32,
    )
    zeros = jnp.zeros((ch, ch), jnp.float32)
    for k in range(3):
        step = 2 - k
        value = sums[:, step * ch : (step + 1) * ch] if step < len(grads) else zeros
        sums_ref[3, k * ch : (k + 1) * ch] = jnp.where(is_last(), zeros, value) if step else value


def hand_out(sums_ref, keep_ref, send_ref):
    odd = lax.rem(lax.axis_index("section"), 2)
    height = sums_ref.shape[1]
    for n in range(2):
        keep_ref[n] = sums_ref[2 * n + odd]
        send_ref[n * height : (n + 1) * height] = sums_ref[2 * n + 1 - odd].astype(jnp.bfloat16)


def pack_kernel(*refs):
    parts, outs, sems = refs[:4], refs[4:6], refs[6]
    last = parts[0].shape[0] - 1
    odd = lax.rem(lax.axis_index("section"), 2)
    copies = []
    for n, part in enumerate(parts):
        for out, row in zip(outs, ((1 - odd) * last, odd * last)):
            sem = sems.at[len(copies)]
            copies.append(
                pltpu.make_async_copy(part.at[pl.ds(row, 1)], out.at[pl.ds(n, 1)], sem)
            )
    for copy in copies:
        copy.start()
    for copy in copies:
        copy.wait()


def interior(grad_ref, preact_ref, wholes, temporal_ref, spatial_ref, inner_ref, gpre_ref, views_ref):
    rows, cols, ch = grad_ref.shape
    step = 4

    @pl.loop(0, rows // step)
    def _(n):
        here = pl.ds(n * step, step)
        grads = [ref[here] for ref in (grad_ref, *wholes)]
        gpre = pre_gradient(grads, preact_ref[here], temporal_ref)
        gpre_ref[here] = gpre.astype(jnp.bfloat16)
        beside(gpre, views_ref, n * step)

    half = rows // 2 - 1

    @pl.loop(0, 2)
    def _(n):
        first = grad_ref[pl.ds(n * half + 1, half)]
        inner_ref[pl.ds(n * half, half)] = convolved(views_ref, spatial_ref, n * half, first)


def edge_rows(grad_ref, pair_refs, afters, gpre_ref, temporal_ref, spatial_ref, views_ref):
    rows, cols, ch = grad_ref.shape
    (grad_above, grad_below), (above_pre, below_pre) = (beside_band(pair_refs, n) for n in (0, 1))
    above = [grad_above] + [ref[0:1] for ref in afters]
    below = [grad_below] + [ref[1:2] for ref in afters]
    beside(pre_gradient(above, above_pre, temporal_ref), views_ref, 0)
    beside(gpre_ref[0:2].astype(jnp.float32), views_ref, 1)
    beside(gpre_ref[rows - 2 : rows].astype(jnp.float32), views_ref, 3)
    beside(pre_gradient(below, below_pre, temporal_ref), views_ref, 5)
    return (
        convolved(views_ref, spatial_ref, 0, grad_ref[0:1]),
        convolved(views_ref, spatial_ref, 3, grad_ref[rows - 1 : rows]),
    )


def last_inner_kernel(grad_ref, preact_ref, temporal_ref, spatial_ref, inner_ref, gpre_ref, views_ref):
    @pl.when(is_last())
    def _():
        interior(
            grad_ref, preact_ref, [], temporal_ref, spatial_ref, inner_ref, gpre_ref, views_ref
        )


def last_mid_kernel(grad_ref, one_ref, two_ref, inner_ref, gpre_ref, temporal_ref, spatial_ref, sent_ref, views_ref):
    rows = grad_ref.shape[0]

    @pl.when(is_last())
    def _():
        sent_ref[0:1], sent_ref[rows - 1 : rows] = edge_rows(
            grad_ref, (one_ref, two_ref), [], gpre_ref, temporal_ref, spatial_ref, views_ref
        )
        sent_ref[1 : rows - 1] = inner_ref[...]
        sent_ref[rows : rows + 1], sent_ref[rows + 1 : rows + 2] = beside_band(
            (one_ref, two_ref), 0
        )


def inner_kernel(later, *refs):
    inputs, wholes, kernels = refs[:2], refs[2 : 2 + later], refs[2 + later : 4 + later]
    known, outs = refs[4 + later : -3], refs[-3:]
    if not known:
        interior(*inputs, wholes, *kernels, *outs)
        return

    @pl.when(is_last())
    def _():
        outs[0][...] = known[0][...]
        outs[1][...] = known[1][...]

    @pl.when(jnp.logical_not(is_last()))
    def _():
        interior(*inputs, wholes, *kernels, *outs)


def mid_kernel(later, *refs):
    grad_ref, inner_ref, gpre_ref = refs[0], refs[3], refs[4]
    afters, (temporal_ref, spatial_ref, mid_ref, views_ref) = refs[5 : 5 + later], refs[5 + later :]
    rows = grad_ref.shape[0]
    first, last = edge_rows(
        grad_ref, refs[1:3], afters, gpre_ref, temporal_ref, spatial_ref, views_ref
    )
    mid_ref[0:1], mid_ref[rows - 1 : rows] = first, last
    mid_ref[1 : rows - 1] = inner_ref[...]


def two_kernel(later, *refs):
    saved_ref, preact_ref, gpre_ref = refs[:3]
    pair_refs, grad_ref = refs[3:5], refs[5]
    wholes, outs = refs[6 : 6 + later], refs[6 + later : 8 + later]
    views_ref, act_ref, sums_ref = refs[8 + later :]
    rows, cols, ch = saved_ref.shape
    step = 4

    @pl.loop(0, rows // step)
    def _(n):
        here = pl.ds(n * step, step)
        beside(gpre_ref[here].astype(jnp.float32), views_ref, n * step)
        hval = preact_ref[here].astype(jnp.float32)
        act_ref[here] = (hval * sigmoid(hval)).astype(jnp.bfloat16)

    views = views_ref[...].reshape(rows * cols, 3 * ch)
    grads = [ref[...] for ref in (grad_ref, *wholes)]
    above, below = beside_band(pair_refs, 2)
    kernel_sums(saved_ref, above, below, act_ref[...], grads, views, sums_ref)
    hand_out(sums_ref, *outs)


def block_one(saved_ref, preact_ref, pair_refs, mids, temporal_ref, outs, scratch):
    gpre_ref, keep_ref, send_ref = outs
    views_ref, act_ref, sums_ref = scratch
    rows, cols, ch = saved_ref.shape
    step = 4

    @pl.loop(0, rows // step)
    def _(n):
        here = pl.ds(n * step, step)
        gpre = pre_gradient([ref[here] for ref in mids], preact_ref[here], temporal_ref)
        gpre_ref[here] = gpre.astype(jnp.bfloat16)
        beside(gpre, views_ref, n * step)
        hval = preact_ref[here].astype(jnp.float32)
        act_ref[here] = (hval * sigmoid(hval)).astype(jnp.bfloat16)

    odd = lax.rem(lax.axis_index("section"), 2)
    size = send_ref.shape[0] - 2 * cols
    send_ref[size : size + cols] = gpre_ref[(1 - odd) * (rows - 1)]
    send_ref[size + cols : size + 2 * cols] = gpre_ref[odd * (rows - 1)]
    views = views_ref[...].reshape(rows * cols, 3 * ch)
    grads = [ref[...] for ref in mids]
    above, below = beside_band(pair_refs, 3)
    kernel_sums(saved_ref, above, below, act_ref[...], grads, views, sums_ref)
    hand_out(sums_ref, keep_ref, send_ref)


def one_kernel(later, *refs):
    saved_ref, preact_ref, mid_ref = refs[0], refs[1], refs[4]
    nexts, temporal_ref = refs[5 : 5 + later], refs[5 + later]
    outs, scratch = refs[6 + later : 9 + later], refs[9 + later :]
    block_one(saved_ref, preact_ref, refs[2:4], [mid_ref, *nexts], temporal_ref, outs, scratch)


def mid_one_kernel(*refs):
    pair_refs, after_ref = refs[1:3], refs[5]
    temporal_two_ref, spatial_two_ref, saved_ref, preact_ref, temporal_ref = refs[6:11]
    mid_ref, outs, scratch = refs[11], refs[12:15], refs[15:18]
    next_ref, edge_ref, edge_views_ref = refs[18:]
    rows = next_ref.shape[0]

    @pl.when(is_last())
    def _():
        edge_ref[...] = jnp.zeros(edge_ref.shape, edge_ref.dtype)
        next_ref[...] = jnp.zeros(next_ref.shape, next_ref.dtype)

    @pl.when(jnp.logical_not(is_last()))
    def _():
        next_ref[...] = after_ref[:rows]
        edge_ref[...] = after_ref[rows:]

    mid_kernel(
        1, *refs[:5], edge_ref, temporal_two_ref, spatial_two_ref, mid_ref, edge_views_ref
    )
    block_one(saved_ref, preact_ref, pair_refs, [mid_ref, next_ref], temporal_ref, outs, scratch)


def input_kernel(mid_ref, gpre_ref, pair_ref, across_ref, spatial_ref, out_ref, token_ref, views_ref):
    rows, cols, ch = out_ref.shape
    pair = pair_ref[pair_ref.shape[0] - 2 * cols : pair_ref.shape[0] - cols]
    above, below = beside_band((pair[None], across_ref[across_ref.shape[0] - cols :][None]), 0)
    token_ref[...] = jnp.zeros(token_ref.shape, token_ref.dtype)
    step = 4
    beside(above.astype(jnp.float32), views_ref, 0)
    beside(below.astype(jnp.float32), views_ref, rows + 1)

    @pl.loop(0, rows // step)
    def _(n):
        gpre = gpre_ref[pl.ds(n * step, step)].astype(jnp.float32)
        beside(gpre, views_ref, n * step + 1)

    @pl.loop(0, rows // step)
    def _(n):
        here = pl.ds(n * step, step)
        out_ref[here] = convolved(views_ref, spatial_ref, n * step, mid_ref[here])


def halves(count, index):
    return [pl.ds(pl.multiple_of(n * count, count), count) for n in (index, 1 - index)]


def pair_kernel(keep_ref, part_ref, own_ref, send_ref):
    across = lax.axis_index("section") // 2
    mine, other = halves(own_ref.shape[0], across)
    own_ref[...] = keep_ref[across] + part_ref[mine].astype(jnp.float32)
    total = keep_ref[1 - across] + part_ref[other].astype(jnp.float32)
    send_ref[...] = total.astype(jnp.bfloat16)


def band_kernel(own_ref, part_ref, keep_ref, send_ref):
    mine, other = halves(keep_ref.shape[0], lax.axis_index("video"))
    keep_ref[...] = own_ref[mine] + part_ref[mine].astype(jnp.float32)
    send_ref[...] = (own_ref[other] + part_ref[other].astype(jnp.float32)).astype(jnp.bfloat16)


def pair_quarter_kernel(keep_ref, part_ref, own_ref, across_ref, frame_ref, both_ref):
    _, height, _ = keep_ref.shape
    half = own_ref.shape[0]
    band = lax.axis_index("section") // 2
    frames = halves(half, lax.axis_index("video"))

    def quarter(band, rows):
        start = pl.multiple_of(band * height, height)
        part = part_ref.at[pl.ds(start, height)][rows]
        return keep_ref[band, rows] + part.astype(jnp.float32)

    own_ref[...] = quarter(band, frames[0])
    across_ref[:half] = quarter(1 - band, frames[0]).astype(jnp.bfloat16)
    rest = across_ref.shape[0] - half
    across_ref[half:] = part_ref[2 * height + rest :]
    frame_ref[...] = quarter(band, frames[1]).astype(jnp.bfloat16)
    both_ref[...] = quarter(1 - band, frames[1]).astype(jnp.bfloat16)


def plane_kernel(own_ref, *refs):
    parts, out_ref = refs[:-1], refs[-1]
    total = own_ref[...]
    for part in parts:
        total = total + part[: out_ref.shape[0]].astype(jnp.float32)
    out_ref[...] = total.astype(jnp.bfloat16)


def add_kernel(one_ref, two_ref, out_ref):
    total = one_ref[...].astype(jnp.float32) + two_ref[...].astype(jnp.float32)
    out_ref[...] = total.astype(jnp.bfloat16)


def scaled_kernel(factor, one_ref, two_ref, out_ref):
    total = one_ref[...].astype(jnp.float32) + two_ref[...].astype(jnp.float32)
    out_ref[...] = (total * factor).astype(jnp.bfloat16)


def place_kernel(*refs):
    shares, (spatial_ref, temporal_ref, sums_ref, sems) = refs[:-4], refs[-4:]
    band, frame = lax.axis_index("section"), lax.axis_index("video")
    parts = len(shares) // 4
    height = shares[0].shape[0]
    for n, share in enumerate(shares):
        place = jnp.bitwise_xor(band, n // parts)
        half = jnp.bitwise_xor(frame, n % parts) if parts == 2 else 0
        here = pl.ds(pl.multiple_of(half * height, height), height)

        sums_ref[place, here] = share[...].astype(jnp.float32)

    copies = [
        pltpu.make_async_copy(sums_ref.at[pl.ds(0, 3)], spatial_ref, sems.at[0]),
        pltpu.make_async_copy(sums_ref.at[3], temporal_ref, sems.at[1]),
    ]
    for copy in copies:
        copy.start()
    for copy in copies:
        copy.wait()


def placed(shares, across, after=()):
    ch = shares[0].shape[1]
    spatial, temporal = call(
        place_kernel,
        [f32(3, 3 * ch, ch), f32(3 * ch, ch)],
        [pltpu.VMEM((4, 3 * ch, ch), jnp.float32), pltpu.SemaphoreType.DMA((2,))],
        12 * ch * ch,
        *shares,
        *[flipped(share, "section", 1) for share in shares],
        *across,
        *[flipped(share, "section", 1) for share in across],
        after=after,
        outs_where=pltpu.HBM,
    )
    return spatial.reshape(3, 3, ch, ch), temporal.reshape(3, ch, ch)


def on_device(
    grad_latent,
    input_one,
    preact_one,
    input_two,
    preact_two,
    spatial_one,
    temporal_one,
    spatial_two,
    temporal_two,
):
    shape = grad_latent.shape
    rows, cols, ch = shape[2:]
    bands, frames = lax.axis_size("section"), lax.axis_size("video")
    later = min(2, frames - 1)
    pixels = lax.axis_size("dp") * frames * bands * rows * cols
    factor = 1.0 / math.sqrt(pixels)
    grad, saved_one, pre_one, saved_two, pre_two = (
        x.reshape(rows, cols, ch)
        for x in (grad_latent, input_one, preact_one, input_two, preact_two)
    )
    conv = 2 * rows * cols * 9 * ch * ch
    views = pltpu.VMEM((rows, cols, 3 * ch), jnp.bfloat16)
    edge_views = pltpu.VMEM((6, cols, 3 * ch), jnp.bfloat16)
    act = pltpu.VMEM((rows, cols, ch), jnp.bfloat16)
    sums = pltpu.VMEM((4, 3 * ch, ch), jnp.float32)
    handed = [f32(2, 3 * ch, ch), bf16(6 * ch, ch)]
    inner_outs = [bf16(rows - 2, cols, ch), bf16(rows, cols, ch)]
    kernels = (temporal_two, spatial_two)

    def from_later(x):
        if frames == 2:
            return [flipped(x, "video", 1)]
        return [from_ahead(x, 0, n + 1) for n in range(later)]

    wholes = from_later(grad)
    packs = call(
        pack_kernel,
        [bf16(4, cols, ch)] * 2,
        [pltpu.SemaphoreType.DMA((8,))],
        1,
        grad,
        pre_two,
        saved_two,
        saved_one,
        spare_inputs=True,
        limit=58,
    )
    first, second = (flipped(pack, "section", 1) for pack in packs)
    pairs = [first, flipped(second, "section", 2)]

    known = ()
    if frames == 2:
        known = call(
            last_inner_kernel,
            inner_outs,
            [views],
            1.2 * conv,
            grad,
            pre_two,
            *kernels,
            after=(first, second),
        )
        sent = call(
            last_mid_kernel,
            [bf16(rows + 2, cols, ch)],
            [edge_views],
            conv // 8,
            grad,
            *pairs,
            *known,
            *kernels,
        )
        afters = from_later(sent)
    else:
        afters = from_later(jnp.concatenate(beside_band(pairs, 0)))
    inner, gpre_two = call(
        functools.partial(inner_kernel, later),
        inner_outs,
        [views],
        1.2 * conv,
        grad,
        pre_two,
        *wholes,
        *kernels,
        *known,
        after=(sent,) if frames == 2 else (),
    )
    parts_two = call(
        functools.partial(two_kernel, later),
        handed,
        [views, act, sums],
        1.2 * conv,
        saved_two,
        pre_two,
        gpre_two,
        *pairs,
        grad,
        *wholes,
    )
    height, half = 3 * ch, 3 * ch // 2
    keep_two, send_two = parts_two
    own_two, send_two = call(
        pair_kernel,
        [f32(height, ch), bf16(height, ch)],
        [],
        height * ch,
        keep_two,
        flipped(send_two, "section", 1),
    )
    across_two = flipped(send_two, "section", 2)
    mid_inputs = (grad, *pairs, inner, gpre_two)
    one_inputs = (saved_one, pre_one)
    mid_outs = [bf16(rows, cols, ch)]
    one_outs = [bf16(rows, cols, ch), f32(2, 3 * ch, ch), bf16(6 * ch + 2 * cols, ch)]
    if frames == 2:
        mid, gpre_one, *parts_one = call(
            mid_one_kernel,
            mid_outs + one_outs,
            [views, act, sums, act, pltpu.VMEM((2, cols, ch), jnp.bfloat16), edge_views],
            1.5 * conv,
            *mid_inputs,
            *afters,
            *kernels,
            *one_inputs,
            temporal_one,
            after=(own_two,),
        )
    else:
        mid = call(
            functools.partial(mid_kernel, later),
            mid_outs,
            [edge_views],
            conv // 8,
            *mid_inputs,
            *afters,
            *kernels,
        )
        gpre_one, *parts_one = call(
            functools.partial(one_kernel, later),
            one_outs,
            [views, act, sums],
            1.2 * conv,
            *one_inputs,
            *pairs,
            mid,
            *from_later(mid),
            temporal_one,
        )
    keep_one, send_one = parts_one
    split = frames == 2 and lax.axis_size("dp") == 4
    if split:
        send_one = later_than(send_one, across_two)
    pair_one = flipped(send_one, "section", 1)

    def input_gradient(edge, after):
        return call(
            input_kernel,
            [bf16(rows, cols, ch), f32(8, 128)],
            [pltpu.VMEM((rows + 2, cols, 3 * ch), jnp.bfloat16)],
            conv,
            mid,
            gpre_one,
            pair_one,
            edge,
            spatial_one,
            after=after,
        )

    if split:

        def added(one, two, after=()):
            return call(add_kernel, [bf16(half, ch)], [], half * ch, one, two, after=after)

        keep_two, send_two = call(
            band_kernel,
            [f32(half, ch), bf16(half, ch)],
            [],
            height * ch,
            own_two,
            across_two,
        )
        sum_two = added(keep_two, flipped(send_two, "video", 1))
        quarters = [f32(half, ch), bf16(half + cols, ch)] + [bf16(half, ch)] * 2
        own_one, *sends = call(
            pair_quarter_kernel, quarters, [], height * ch, keep_one, pair_one, after=(send_two,)
        )
        across = flipped(sends[0], "section", 2)
        parts = [across, flipped(sends[1], "video", 1), flipped_both(sends[2])]
        sum_one = call(plane_kernel, [bf16(half, ch)], [], 4 * half * ch, own_one, *parts)
        part_two = flipped(sum_two, "dp", 1)
        part_one = flipped(later_than(sum_one, sum_two), "dp", 1)
        sum_two = added(sum_two, part_two, after=(sum_one,))
        sum_one = added(sum_one, part_one)
        last_two = flipped(sum_two, "dp", 2)
        last_one = flipped(later_than(sum_one, sum_two), "dp", 2)

        def scaled(one, two, after=()):
            kernel = functools.partial(scaled_kernel, factor)
            return call(kernel, [bf16(half, ch)], [], half * ch, one, two, after=after)

        def gathered(own):
            shares = [own, flipped(own, "video", 1)]
            return shares, [flipped(own, "section", 2), flipped_both(own)]

        own_two = scaled(sum_two, last_two, after=(sum_one,))
        own_one = scaled(sum_one, last_one, after=(own_two,))
        parts_one, parts_two = gathered(own_one), gathered(own_two)
        sums_two = placed(*parts_two)
        grad_in, token = input_gradient(across, (own_one,))
        *parts_one, token = lax.optimization_barrier((*parts_one, token))
        sums_one = placed(*parts_one, after=(token,))
        sums = (*sums_one, *sums_two)
    else:
        own_one, send_one = call(
            pair_kernel, [f32(height, ch), bf16(height, ch)], [], height * ch, keep_one, pair_one
        )
        edge = flipped(pair_one[pair_one.shape[0] - cols :], "section", 2)
        grad_in, _ = input_gradient(edge, ())
        own_one = own_one + flipped(send_one, "section", 2).astype(jnp.float32)
        own_two = own_two + across_two.astype(jnp.float32)
        both = lax.psum((own_one, own_two), ("video", "dp"))
        sums = []
        for share in both:
            share = (share * factor).astype(jnp.bfloat16)
            sums += placed([share], [flipped(share, "section", 2)])
    return (grad_in.reshape(shape), *sums)


def solution(mesh):
    whole = P("dp", "video", "section", None, None)
    return jax.shard_map(
        on_device,
        mesh=mesh,
        in_specs=(whole,) * 5 + (P(),) * 4,
        out_specs=(whole, P(), P(), P(), P()),
        check_vma=False,
    )
```

```python
import functools
import math

import jax
import jax.numpy as jnp
from jax import lax
from jax.experimental import pallas as pl
from jax.experimental.pallas import tpu as pltpu
from jax.sharding import PartitionSpec as P

MIB = 1024 * 1024


def sigmoid(value):
    return 1.0 / (1.0 + jnp.exp(-value))


def bf16(*shape):
    return jax.ShapeDtypeStruct(shape, jnp.bfloat16)


def f32(*shape):
    return jax.ShapeDtypeStruct(shape, jnp.float32)


def call(kernel, outs, scratch, flops, *operands, after=(), spare_inputs=False, limit=24):
    single = len(outs) == 1
    moved = sum(math.prod(x.shape) * x.dtype.itemsize for x in (*operands, *outs))
    vmem = pl.BlockSpec(memory_space=pltpu.VMEM)
    spare = pl.BlockSpec(memory_space=pl.ANY)
    spec = spare if spare_inputs else vmem
    count = len(operands)
    operands = (*operands, *after)

    def body(*refs):
        kernel(*refs[:count], *refs[len(operands) :])

    return pl.pallas_call(
        body,
        out_shape=outs[0] if single else tuple(outs),
        in_specs=[spec] * count + [spare] * len(after),
        out_specs=vmem if single else (vmem,) * len(outs),
        scratch_shapes=scratch,
        compiler_params=pltpu.CompilerParams(vmem_limit_bytes=limit * MIB),
        cost_estimate=pl.CostEstimate(
            flops=int(flops), bytes_accessed=int(moved), transcendentals=0
        ),
    )(*operands)


def from_ahead(block, band_step, frame_step):
    bands, frames = lax.axis_size("section"), lax.axis_size("video")
    pairs = [
        ((band + band_step) * frames + frame + frame_step, band * frames + frame)
        for band in range(bands)
        for frame in range(frames)
        if 0 <= band + band_step < bands and frame + frame_step < frames
    ]
    return lax.ppermute(block, ("section", "video"), pairs)


def beside_band(pair_refs, row):
    band = lax.axis_index("section")
    odd = lax.rem(band, 2) == 1
    inside = (band > 0) & (band < lax.axis_size("section") - 1)
    first, second = (ref[row : row + 1] for ref in pair_refs)
    second = jnp.where(inside, second, jnp.zeros_like(second))
    return jnp.where(odd, first, second), jnp.where(odd, second, first)


def flipped(block, axis, flip):
    count = lax.axis_size(axis)
    return lax.ppermute(block, axis, [(place ^ flip, place) for place in range(count)])


def flipped_both(block):
    bands = lax.axis_size("section")
    pairs = [
        (2 * (band ^ 2) + 1 - frame, 2 * band + frame) for band in range(bands) for frame in range(2)
    ]
    return lax.ppermute(block, ("section", "video"), pairs)


def later_than(block, *others):
    return lax.optimization_barrier((block, *others))[0]


def beside(gpre, views_ref, start):
    count, cols, ch = gpre.shape
    at = lax.broadcasted_iota(jnp.int32, gpre.shape, 1)
    right = jnp.where(at == cols - 1, 0.0, pltpu.roll(gpre, cols - 1, 1))
    left = jnp.where(at == 0, 0.0, pltpu.roll(gpre, 1, 1))
    here = pl.ds(start, count)
    views_ref[here, :, 0:ch] = right.astype(jnp.bfloat16)
    views_ref[here, :, ch : 2 * ch] = gpre.astype(jnp.bfloat16)
    views_ref[here, :, 2 * ch : 3 * ch] = left.astype(jnp.bfloat16)


def pre_gradient(grads, preact, temporal_ref):
    count, cols, ch = preact.shape
    flat = jnp.concatenate([grad.reshape(count * cols, ch) for grad in grads], axis=1)
    kernel = jnp.concatenate([temporal_ref[2 - step] for step in range(len(grads))], axis=1)
    gact = lax.dot_general(
        flat, kernel, (((1,), (1,)), ((), ())), preferred_element_type=jnp.float32
    )
    gact = gact.astype(jnp.bfloat16).astype(jnp.float32).reshape(preact.shape)
    hval = preact.astype(jnp.float32)
    sig = sigmoid(hval)
    return gact * sig * (1.0 + hval * (1.0 - sig))


def convolved(views_ref, spatial_ref, start, first):
    count, cols, ch = first.shape
    total = first.astype(jnp.float32).reshape(count * cols, ch)
    for ky in range(3):
        view = views_ref[pl.ds(start + 2 - ky, count)].reshape(count * cols, 3 * ch)
        kernel = jnp.concatenate([spatial_ref[ky, kx] for kx in range(3)], axis=1)
        total = total + lax.dot_general(
            view, kernel, (((1,), (1,)), ((), ())), preferred_element_type=jnp.float32
        )
    return total.astype(jnp.bfloat16).reshape(first.shape)


def is_last():
    return lax.axis_index("video") == lax.axis_size("video") - 1


def left_sides(saved_ref, preact_ref, above, below, sides_ref):
    rows, cols, ch = saved_ref.shape
    flat = (rows * cols, ch)
    shifts = [
        jnp.concatenate([above, saved_ref[: rows - 1]], axis=0),
        saved_ref[...],
        jnp.concatenate([saved_ref[1:], below], axis=0),
    ]
    for n, shift in enumerate(shifts):
        sides_ref[n] = shift.reshape(flat).T
    hval = preact_ref[...].astype(jnp.float32)
    sides_ref[3] = (hval * sigmoid(hval)).astype(jnp.bfloat16).reshape(flat).T


def kernel_sums(sides_ref, grads, views, sums_ref):
    _, ch, pixels = sides_ref.shape
    shifts = sides_ref[0:3].reshape(3 * ch, pixels)
    sums = jnp.dot(shifts, views, preferred_element_type=jnp.float32)
    for ky in range(3):
        for kx in range(3):
            here = slice(kx * ch, (kx + 1) * ch)
            sums_ref[ky, here] = sums[ky * ch : (ky + 1) * ch, here]
    grads = jnp.concatenate([grad.reshape(pixels, ch) for grad in grads], axis=1)
    sums = jnp.dot(sides_ref[3], grads, preferred_element_type=jnp.float32)
    zeros = jnp.zeros((ch, ch), jnp.float32)
    for k in range(3):
        step = 2 - k
        value = sums[:, step * ch : (step + 1) * ch] if step * ch < grads.shape[1] else zeros
        sums_ref[3, k * ch : (k + 1) * ch] = jnp.where(is_last(), zeros, value) if step else value


def hand_out(sums_ref, keep_ref, send_ref):
    odd = lax.rem(lax.axis_index("section"), 2)
    height = sums_ref.shape[1]
    for n in range(2):
        keep_ref[n] = sums_ref[2 * n + odd]
        send_ref[n * height : (n + 1) * height] = sums_ref[2 * n + 1 - odd].astype(jnp.bfloat16)


def pack_kernel(*refs):
    parts, outs, sems = refs[:4], refs[4:6], refs[6]
    last = parts[0].shape[0] - 1
    odd = lax.rem(lax.axis_index("section"), 2)
    copies = []
    for n, part in enumerate(parts):
        for out, row in zip(outs, ((1 - odd) * last, odd * last)):
            sem = sems.at[len(copies)]
            copies.append(
                pltpu.make_async_copy(part.at[pl.ds(row, 1)], out.at[pl.ds(n, 1)], sem)
            )
    for copy in copies:
        copy.start()
    for copy in copies:
        copy.wait()


def interior(grad_ref, preact_ref, wholes, temporal_ref, spatial_ref, inner_ref, gpre_ref, views_ref):
    rows, cols, ch = grad_ref.shape
    step = 4

    @pl.loop(0, rows // step)
    def _(n):
        here = pl.ds(n * step, step)
        grads = [ref[here] for ref in (grad_ref, *wholes)]
        gpre = pre_gradient(grads, preact_ref[here], temporal_ref)
        gpre_ref[here] = gpre.astype(jnp.bfloat16)
        beside(gpre, views_ref, n * step)

    half = rows // 2 - 1

    @pl.loop(0, 2)
    def _(n):
        first = grad_ref[pl.ds(n * half + 1, half)]
        inner_ref[pl.ds(n * half, half)] = convolved(views_ref, spatial_ref, n * half, first)


def edge_rows(grad_ref, pair_refs, afters, gpre_ref, temporal_ref, spatial_ref, views_ref):
    rows, cols, ch = grad_ref.shape
    (grad_above, grad_below), (above_pre, below_pre) = (beside_band(pair_refs, n) for n in (0, 1))
    above = [grad_above] + [ref[0:1] for ref in afters]
    below = [grad_below] + [ref[1:2] for ref in afters]
    beside(pre_gradient(above, above_pre, temporal_ref), views_ref, 0)
    beside(gpre_ref[0:2].astype(jnp.float32), views_ref, 1)
    beside(gpre_ref[rows - 2 : rows].astype(jnp.float32), views_ref, 3)
    beside(pre_gradient(below, below_pre, temporal_ref), views_ref, 5)
    return (
        convolved(views_ref, spatial_ref, 0, grad_ref[0:1]),
        convolved(views_ref, spatial_ref, 3, grad_ref[rows - 1 : rows]),
    )


def last_inner_kernel(grad_ref, preact_ref, temporal_ref, spatial_ref, inner_ref, gpre_ref, views_ref):
    @pl.when(is_last())
    def _():
        interior(
            grad_ref, preact_ref, [], temporal_ref, spatial_ref, inner_ref, gpre_ref, views_ref
        )


def last_edge_kernel(grad_ref, one_ref, two_ref, gpre_ref, temporal_ref, spatial_ref, edge_ref, views_ref):
    @pl.when(is_last())
    def _():
        pair_refs = (one_ref, two_ref)
        edge_ref[0:1], edge_ref[1:2] = edge_rows(
            grad_ref, pair_refs, [], gpre_ref, temporal_ref, spatial_ref, views_ref
        )
        edge_ref[2:3], edge_ref[3:4] = beside_band(pair_refs, 0)


def inner_kernel(later, *refs):
    inputs, wholes, kernels = refs[:2], refs[2 : 2 + later], refs[2 + later : 4 + later]
    known, outs = refs[4 + later : -3], refs[-3:]
    if not known:
        interior(*inputs, wholes, *kernels, *outs)
        return

    @pl.when(is_last())
    def _():
        outs[0][...] = known[0][...]
        outs[1][...] = known[1][...]

    @pl.when(jnp.logical_not(is_last()))
    def _():
        interior(*inputs, wholes, *kernels, *outs)


def mid_kernel(later, *refs):
    grad_ref, inner_ref, gpre_ref = refs[0], refs[3], refs[4]
    afters, (temporal_ref, spatial_ref, mid_ref, views_ref) = refs[5 : 5 + later], refs[5 + later :]
    rows = grad_ref.shape[0]
    first, last = edge_rows(
        grad_ref, refs[1:3], afters, gpre_ref, temporal_ref, spatial_ref, views_ref
    )
    mid_ref[0:1], mid_ref[rows - 1 : rows] = first, last
    mid_ref[1 : rows - 1] = inner_ref[...]


def two_kernel(later, *refs):
    saved_ref, preact_ref, gpre_ref = refs[:3]
    pair_refs, grad_ref = refs[3:5], refs[5]
    wholes, outs = refs[6 : 6 + later], refs[6 + later : 8 + later]
    views_ref, sides_ref, sums_ref = refs[8 + later :]
    rows, cols, ch = saved_ref.shape
    step = 4

    @pl.loop(0, rows // step)
    def _(n):
        here = pl.ds(n * step, step)
        beside(gpre_ref[here].astype(jnp.float32), views_ref, n * step)

    views = views_ref[...].reshape(rows * cols, 3 * ch)
    grads = [ref[...] for ref in (grad_ref, *wholes)]
    left_sides(saved_ref, preact_ref, *beside_band(pair_refs, 2), sides_ref)
    kernel_sums(sides_ref, grads, views, sums_ref)
    hand_out(sums_ref, *outs)


def sides_kernel(saved_ref, preact_ref, one_ref, two_ref, sides_ref):
    left_sides(saved_ref, preact_ref, *beside_band((one_ref, two_ref), 3), sides_ref)


def block_one(sides_ref, preact_ref, mids, temporal_ref, outs, scratch):
    gpre_ref, keep_ref, send_ref = outs
    views_ref, sums_ref = scratch
    rows, cols, ch = preact_ref.shape
    step = 4

    @pl.loop(0, rows // step)
    def _(n):
        here = pl.ds(n * step, step)
        gpre = pre_gradient([ref[here] for ref in mids], preact_ref[here], temporal_ref)
        gpre_ref[here] = gpre.astype(jnp.bfloat16)
        beside(gpre, views_ref, n * step)

    odd = lax.rem(lax.axis_index("section"), 2)
    size = send_ref.shape[0] - 2 * cols
    send_ref[size : size + cols] = gpre_ref[(1 - odd) * (rows - 1)]
    send_ref[size + cols : size + 2 * cols] = gpre_ref[odd * (rows - 1)]
    views = views_ref[...].reshape(rows * cols, 3 * ch)
    kernel_sums(sides_ref, [ref[...] for ref in mids], views, sums_ref)
    hand_out(sums_ref, keep_ref, send_ref)


def one_kernel(later, *refs):
    sides_ref, preact_ref, mids = refs[0], refs[1], refs[2 : 3 + later]
    temporal_ref, outs, scratch = refs[3 + later], refs[4 + later : 7 + later], refs[7 + later :]
    block_one(sides_ref, preact_ref, mids, temporal_ref, outs, scratch)


def mid_one_kernel(*refs):
    after_inner_ref, after_edge_ref = refs[5:7]
    temporal_two_ref, spatial_two_ref, sides_ref, preact_ref, temporal_ref = refs[7:12]
    mid_ref, outs, scratch = refs[12], refs[13:16], refs[16:18]
    next_ref, edge_ref, edge_views_ref = refs[18:]
    rows = next_ref.shape[0]

    @pl.when(is_last())
    def _():
        edge_ref[...] = jnp.zeros(edge_ref.shape, edge_ref.dtype)
        next_ref[...] = jnp.zeros(next_ref.shape, next_ref.dtype)

    @pl.when(jnp.logical_not(is_last()))
    def _():
        edge_ref[...] = after_edge_ref[2:4]
        next_ref[0:1] = after_edge_ref[0:1]
        next_ref[1 : rows - 1] = after_inner_ref[...]
        next_ref[rows - 1 : rows] = after_edge_ref[1:2]

    mid_kernel(
        1, *refs[:5], edge_ref, temporal_two_ref, spatial_two_ref, mid_ref, edge_views_ref
    )
    block_one(sides_ref, preact_ref, [mid_ref, next_ref], temporal_ref, outs, scratch)


def input_kernel(mid_ref, gpre_ref, pair_ref, across_ref, spatial_ref, out_ref, token_ref, views_ref):
    rows, cols, ch = out_ref.shape
    pair = pair_ref[pair_ref.shape[0] - 2 * cols : pair_ref.shape[0] - cols]
    above, below = beside_band((pair[None], across_ref[across_ref.shape[0] - cols :][None]), 0)
    token_ref[...] = jnp.zeros(token_ref.shape, token_ref.dtype)
    step = 4
    beside(above.astype(jnp.float32), views_ref, 0)
    beside(below.astype(jnp.float32), views_ref, rows + 1)

    @pl.loop(0, rows // step)
    def _(n):
        gpre = gpre_ref[pl.ds(n * step, step)].astype(jnp.float32)
        beside(gpre, views_ref, n * step + 1)

    @pl.loop(0, rows // step)
    def _(n):
        here = pl.ds(n * step, step)
        out_ref[here] = convolved(views_ref, spatial_ref, n * step, mid_ref[here])


def halves(count, index):
    return [pl.ds(pl.multiple_of(n * count, count), count) for n in (index, 1 - index)]


def pair_kernel(keep_ref, part_ref, own_ref, send_ref):
    across = lax.axis_index("section") // 2
    mine, other = halves(own_ref.shape[0], across)
    own_ref[...] = keep_ref[across] + part_ref[mine].astype(jnp.float32)
    total = keep_ref[1 - across] + part_ref[other].astype(jnp.float32)
    send_ref[...] = total.astype(jnp.bfloat16)


def band_kernel(own_ref, part_ref, keep_ref, send_ref):
    mine, other = halves(keep_ref.shape[0], lax.axis_index("video"))
    keep_ref[...] = own_ref[mine] + part_ref[mine].astype(jnp.float32)
    send_ref[...] = (own_ref[other] + part_ref[other].astype(jnp.float32)).astype(jnp.bfloat16)


def pair_quarter_kernel(keep_ref, part_ref, own_ref, across_ref, frame_ref, both_ref):
    _, height, _ = keep_ref.shape
    half = own_ref.shape[0]
    band = lax.axis_index("section") // 2
    frames = halves(half, lax.axis_index("video"))

    def quarter(band, rows):
        start = pl.multiple_of(band * height, height)
        part = part_ref.at[pl.ds(start, height)][rows]
        return keep_ref[band, rows] + part.astype(jnp.float32)

    own_ref[...] = quarter(band, frames[0])
    across_ref[:half] = quarter(1 - band, frames[0]).astype(jnp.bfloat16)
    rest = across_ref.shape[0] - half
    across_ref[half:] = part_ref[2 * height + rest :]
    frame_ref[...] = quarter(band, frames[1]).astype(jnp.bfloat16)
    both_ref[...] = quarter(1 - band, frames[1]).astype(jnp.bfloat16)


def plane_kernel(own_ref, *refs):
    parts, out_ref = refs[:-1], refs[-1]
    total = own_ref[...]
    for part in parts:
        total = total + part[: out_ref.shape[0]].astype(jnp.float32)
    out_ref[...] = total.astype(jnp.bfloat16)


def add_kernel(one_ref, two_ref, out_ref):
    total = one_ref[...].astype(jnp.float32) + two_ref[...].astype(jnp.float32)
    out_ref[...] = total.astype(jnp.bfloat16)


def scaled_kernel(factor, *refs):
    out_ref = refs[-1]
    for block in range(2):
        one, two = (ref[...].astype(jnp.float32) for ref in refs[2 * block : 2 * block + 2])
        out_ref[block] = ((one + two) * factor).astype(jnp.bfloat16)


def place_kernel(*refs):
    shares, outs = refs[:-4], refs[-4:]
    band, frame = lax.axis_index("section"), lax.axis_index("video")
    halves = len(shares) // 4
    height = shares[0].shape[1]
    for n, share in enumerate(shares):
        place = jnp.bitwise_xor(band, n // halves)
        half = jnp.bitwise_xor(frame, n % halves) if halves == 2 else 0
        here = pl.ds(pl.multiple_of(half * height, height), height)

        @pl.when(place < 3)
        def _():
            for block in range(2):
                outs[2 * block][place, here] = share[block].astype(jnp.float32)

        @pl.when(place == 3)
        def _():
            for block in range(2):
                outs[2 * block + 1][here] = share[block].astype(jnp.float32)


def placed(shares, across):
    ch = shares[0].shape[2]
    outs = call(
        place_kernel,
        [f32(3, 3 * ch, ch), f32(3 * ch, ch)] * 2,
        [],
        12 * ch * ch,
        *shares,
        *[flipped(share, "section", 1) for share in shares],
        *across,
        *[flipped(share, "section", 1) for share in across],
    )
    return [x.reshape(3, 3, ch, ch) if x.ndim == 3 else x.reshape(3, ch, ch) for x in outs]


def on_device(
    grad_latent,
    input_one,
    preact_one,
    input_two,
    preact_two,
    spatial_one,
    temporal_one,
    spatial_two,
    temporal_two,
):
    shape = grad_latent.shape
    rows, cols, ch = shape[2:]
    bands, frames = lax.axis_size("section"), lax.axis_size("video")
    later = min(2, frames - 1)
    pixels = lax.axis_size("dp") * frames * bands * rows * cols
    factor = 1.0 / math.sqrt(pixels)
    grad, saved_one, pre_one, saved_two, pre_two = (
        x.reshape(rows, cols, ch)
        for x in (grad_latent, input_one, preact_one, input_two, preact_two)
    )
    conv = 2 * rows * cols * 9 * ch * ch
    views = pltpu.VMEM((rows, cols, 3 * ch), jnp.bfloat16)
    edge_views = pltpu.VMEM((6, cols, 3 * ch), jnp.bfloat16)
    act = pltpu.VMEM((rows, cols, ch), jnp.bfloat16)
    sides = bf16(4, ch, rows * cols)
    sums = pltpu.VMEM((4, 3 * ch, ch), jnp.float32)
    handed = [f32(2, 3 * ch, ch), bf16(6 * ch, ch)]
    inner_outs = [bf16(rows - 2, cols, ch), bf16(rows, cols, ch)]
    kernels = (temporal_two, spatial_two)

    def from_later(x):
        if frames == 2:
            return [flipped(x, "video", 1)]
        return [from_ahead(x, 0, n + 1) for n in range(later)]

    wholes = from_later(grad)
    packs = call(
        pack_kernel,
        [bf16(4, cols, ch)] * 2,
        [pltpu.SemaphoreType.DMA((8,))],
        1,
        grad,
        pre_two,
        saved_two,
        saved_one,
        spare_inputs=True,
        limit=58,
    )
    first, second = (flipped(pack, "section", 1) for pack in packs)
    pairs = [first, flipped(second, "section", 2)]

    known = ()
    if frames == 2:
        known = call(
            last_inner_kernel,
            inner_outs,
            [views],
            1.2 * conv,
            grad,
            pre_two,
            *kernels,
            after=(first, second),
        )
        afters = from_later(known[0])
    else:
        afters = from_later(jnp.concatenate(beside_band(pairs, 0)))
    inner, gpre_two = call(
        functools.partial(inner_kernel, later),
        inner_outs,
        [views],
        1.2 * conv,
        grad,
        pre_two,
        *wholes,
        *kernels,
        *known,
    )
    if frames == 2:
        edge = call(
            last_edge_kernel,
            [bf16(4, cols, ch)],
            [edge_views],
            conv // 8,
            grad,
            *pairs,
            known[1],
            *kernels,
            after=(gpre_two,),
        )
        afters += from_later(edge)
    parts_two = call(
        functools.partial(two_kernel, later),
        handed,
        [views, pltpu.VMEM(sides.shape, sides.dtype), sums],
        1.2 * conv,
        saved_two,
        pre_two,
        gpre_two,
        *pairs,
        grad,
        *wholes,
        after=(edge,) if frames == 2 else (),
    )
    sides_one = call(
        sides_kernel, [sides], [], conv // 8, saved_one, pre_one, *pairs, after=parts_two[:1]
    )
    height, half = 3 * ch, 3 * ch // 2
    keep_two, send_two = parts_two
    own_two, send_two = call(
        pair_kernel,
        [f32(height, ch), bf16(height, ch)],
        [],
        height * ch,
        keep_two,
        flipped(send_two, "section", 1),
        after=afters[:1] if frames == 2 else (),
    )
    across_two = flipped(send_two, "section", 2)
    mid_inputs = (grad, *pairs, inner, gpre_two)
    one_inputs = (sides_one, pre_one)
    mid_outs = [bf16(rows, cols, ch)]
    one_outs = [bf16(rows, cols, ch), f32(2, 3 * ch, ch), bf16(6 * ch + 2 * cols, ch)]
    if frames == 2:
        mid, gpre_one, *parts_one = call(
            mid_one_kernel,
            mid_outs + one_outs,
            [views, sums, act, pltpu.VMEM((2, cols, ch), jnp.bfloat16), edge_views],
            1.5 * conv,
            *mid_inputs,
            *afters,
            *kernels,
            *one_inputs,
            temporal_one,
            after=(own_two,),
        )
    else:
        mid = call(
            functools.partial(mid_kernel, later),
            mid_outs,
            [edge_views],
            conv // 8,
            *mid_inputs,
            *afters,
            *kernels,
        )
        gpre_one, *parts_one = call(
            functools.partial(one_kernel, later),
            one_outs,
            [views, sums],
            1.2 * conv,
            *one_inputs,
            mid,
            *from_later(mid),
            temporal_one,
        )
    keep_one, send_one = parts_one
    split = frames == 2 and lax.axis_size("dp") == 4
    if split:
        send_one = later_than(send_one, across_two)
    pair_one = flipped(send_one, "section", 1)

    def input_gradient(edge, after):
        return call(
            input_kernel,
            [bf16(rows, cols, ch), f32(8, 128)],
            [pltpu.VMEM((rows + 2, cols, 3 * ch), jnp.bfloat16)],
            conv,
            mid,
            gpre_one,
            pair_one,
            edge,
            spatial_one,
            after=after,
        )

    if split:

        def added(one, two):
            return call(add_kernel, [bf16(half, ch)], [], half * ch, one, two)

        keep_two, send_two = call(
            band_kernel,
            [f32(half, ch), bf16(half, ch)],
            [],
            height * ch,
            own_two,
            across_two,
        )
        sum_two = added(keep_two, flipped(send_two, "video", 1))
        quarters = [f32(half, ch), bf16(half + cols, ch)] + [bf16(half, ch)] * 2
        own_one, *sends = call(
            pair_quarter_kernel, quarters, [], height * ch, keep_one, pair_one, after=(send_two,)
        )
        across = flipped(sends[0], "section", 2)
        parts = [across, flipped(sends[1], "video", 1), flipped_both(sends[2])]
        sum_one = call(plane_kernel, [bf16(half, ch)], [], 4 * half * ch, own_one, *parts)
        part_two = flipped(sum_two, "dp", 1)
        part_one = flipped(later_than(sum_one, sum_two), "dp", 1)
        sum_two = added(sum_two, part_two)
        sum_one = added(sum_one, part_one)
        last_two = flipped(sum_two, "dp", 2)
        last_one = flipped(later_than(sum_one, sum_two), "dp", 2)
        grad_in, token = input_gradient(across, (sum_one,))
        own = call(
            functools.partial(scaled_kernel, factor),
            [bf16(2, half, ch)],
            [],
            height * ch,
            sum_one,
            last_one,
            sum_two,
            last_two,
            after=(token,),
        )
        shares = [own, flipped(own, "video", 1)]
        sums = placed(shares, [flipped(own, "section", 2), flipped_both(own)])
    else:
        own_one, send_one = call(
            pair_kernel, [f32(height, ch), bf16(height, ch)], [], height * ch, keep_one, pair_one
        )
        edge = flipped(pair_one[pair_one.shape[0] - cols :], "section", 2)
        grad_in, _ = input_gradient(edge, ())
        own_one = own_one + flipped(send_one, "section", 2).astype(jnp.float32)
        own_two = own_two + across_two.astype(jnp.float32)
        share = lax.psum(jnp.stack((own_one, own_two)), ("video", "dp")) * factor
        share = share.astype(jnp.bfloat16)
        sums = placed([share], [flipped(share, "section", 2)])
    return (grad_in.reshape(shape), *sums)


def solution(mesh):
    whole = P("dp", "video", "section", None, None)
    return jax.shard_map(
        on_device,
        mesh=mesh,
        in_specs=(whole,) * 5 + (P(),) * 4,
        out_specs=(whole, P(), P(), P(), P()),
        check_vma=False,
    )
```

```python
import functools
import math

import jax
import jax.numpy as jnp
from jax import lax
from jax.experimental import pallas as pl
from jax.experimental.pallas import tpu as pltpu
from jax.sharding import PartitionSpec as P

MIB = 1024 * 1024


def sigmoid(value):
    return 1.0 / (1.0 + jnp.exp(-value))


def bf16(*shape):
    return jax.ShapeDtypeStruct(shape, jnp.bfloat16)


def f32(*shape):
    return jax.ShapeDtypeStruct(shape, jnp.float32)


def call(kernel, outs, scratch, flops, *operands, after=(), early=(), spare_inputs=False, limit=24):
    single = len(outs) == 1
    moved = sum(math.prod(x.shape) * x.dtype.itemsize for x in (*operands, *outs))
    vmem = pl.BlockSpec(memory_space=pltpu.VMEM)
    spare = pl.BlockSpec(memory_space=pl.ANY)
    spec = spare if spare_inputs else vmem
    count = len(operands)
    operands = (*operands, *early, *after)

    def body(*refs):
        kernel(*refs[:count], *refs[len(operands) :])

    return pl.pallas_call(
        body,
        out_shape=outs[0] if single else tuple(outs),
        in_specs=[spec] * count + [vmem] * len(early) + [spare] * len(after),
        out_specs=vmem if single else (vmem,) * len(outs),
        scratch_shapes=scratch,
        compiler_params=pltpu.CompilerParams(vmem_limit_bytes=limit * MIB),
        cost_estimate=pl.CostEstimate(
            flops=int(flops), bytes_accessed=int(moved), transcendentals=0
        ),
    )(*operands)


def from_ahead(block, band_step, frame_step):
    bands, frames = lax.axis_size("section"), lax.axis_size("video")
    pairs = [
        ((band + band_step) * frames + frame + frame_step, band * frames + frame)
        for band in range(bands)
        for frame in range(frames)
        if 0 <= band + band_step < bands and frame + frame_step < frames
    ]
    return lax.ppermute(block, ("section", "video"), pairs)


def beside_band(pair_refs, row):
    band = lax.axis_index("section")
    odd = lax.rem(band, 2) == 1
    inside = (band > 0) & (band < lax.axis_size("section") - 1)
    first, second = (ref[row : row + 1] for ref in pair_refs)
    second = jnp.where(inside, second, jnp.zeros_like(second))
    return jnp.where(odd, first, second), jnp.where(odd, second, first)


def flipped(block, axis, flip):
    count = lax.axis_size(axis)
    return lax.ppermute(block, axis, [(place ^ flip, place) for place in range(count)])


def flipped_both(block):
    bands = lax.axis_size("section")
    pairs = [
        (2 * (band ^ 2) + 1 - frame, 2 * band + frame) for band in range(bands) for frame in range(2)
    ]
    return lax.ppermute(block, ("section", "video"), pairs)


def later_than(block, *others):
    return lax.optimization_barrier((block, *others))[0]


def beside(gpre, views_ref, start):
    count, cols, ch = gpre.shape
    at = lax.broadcasted_iota(jnp.int32, gpre.shape, 1)
    right = jnp.where(at == cols - 1, 0.0, pltpu.roll(gpre, cols - 1, 1))
    left = jnp.where(at == 0, 0.0, pltpu.roll(gpre, 1, 1))
    here = pl.ds(start, count)
    views_ref[here, :, 0:ch] = right.astype(jnp.bfloat16)
    views_ref[here, :, ch : 2 * ch] = gpre.astype(jnp.bfloat16)
    views_ref[here, :, 2 * ch : 3 * ch] = left.astype(jnp.bfloat16)


def pre_gradient(grads, preact, temporal_ref):
    count, cols, ch = preact.shape
    flat = jnp.concatenate([grad.reshape(count * cols, ch) for grad in grads], axis=1)
    kernel = jnp.concatenate([temporal_ref[2 - step] for step in range(len(grads))], axis=1)
    gact = lax.dot_general(
        flat, kernel, (((1,), (1,)), ((), ())), preferred_element_type=jnp.float32
    )
    gact = gact.astype(jnp.bfloat16).astype(jnp.float32).reshape(preact.shape)
    hval = preact.astype(jnp.float32)
    sig = sigmoid(hval)
    return gact * sig * (1.0 + hval * (1.0 - sig))


def convolved(views_ref, spatial_ref, start, first):
    count, cols, ch = first.shape
    total = first.astype(jnp.float32).reshape(count * cols, ch)
    for ky in range(3):
        view = views_ref[pl.ds(start + 2 - ky, count)].reshape(count * cols, 3 * ch)
        kernel = jnp.concatenate([spatial_ref[ky, kx] for kx in range(3)], axis=1)
        total = total + lax.dot_general(
            view, kernel, (((1,), (1,)), ((), ())), preferred_element_type=jnp.float32
        )
    return total.astype(jnp.bfloat16).reshape(first.shape)


def is_last():
    return lax.axis_index("video") == lax.axis_size("video") - 1


def left_sides(saved_ref, preact_ref, above, below, sides_ref):
    rows, cols, ch = saved_ref.shape
    flat = (rows * cols, ch)
    shifts = [
        jnp.concatenate([above, saved_ref[: rows - 1]], axis=0),
        saved_ref[...],
        jnp.concatenate([saved_ref[1:], below], axis=0),
    ]
    for n, shift in enumerate(shifts):
        sides_ref[n] = shift.reshape(flat).T
    hval = preact_ref[...].astype(jnp.float32)
    sides_ref[3] = (hval * sigmoid(hval)).astype(jnp.bfloat16).reshape(flat).T


def kernel_sums(sides_ref, grads, views, sums_ref):
    _, ch, pixels = sides_ref.shape
    shifts = sides_ref[0:3].reshape(3 * ch, pixels)
    sums = jnp.dot(shifts, views, preferred_element_type=jnp.float32)
    for ky in range(3):
        for kx in range(3):
            here = slice(kx * ch, (kx + 1) * ch)
            sums_ref[ky, here] = sums[ky * ch : (ky + 1) * ch, here]
    grads = jnp.concatenate([grad.reshape(pixels, ch) for grad in grads], axis=1)
    sums = jnp.dot(sides_ref[3], grads, preferred_element_type=jnp.float32)
    zeros = jnp.zeros((ch, ch), jnp.float32)
    for k in range(3):
        step = 2 - k
        value = sums[:, step * ch : (step + 1) * ch] if step * ch < grads.shape[1] else zeros
        sums_ref[3, k * ch : (k + 1) * ch] = jnp.where(is_last(), zeros, value) if step else value


def hand_out(sums_ref, keep_ref, send_ref):
    odd = lax.rem(lax.axis_index("section"), 2)
    height = sums_ref.shape[1]
    for n in range(2):
        keep_ref[n] = sums_ref[2 * n + odd]
        send_ref[n * height : (n + 1) * height] = sums_ref[2 * n + 1 - odd].astype(jnp.bfloat16)


def pack_kernel(*refs):
    parts, outs, sems = refs[:4], refs[4:6], refs[6]
    last = parts[0].shape[0] - 1
    odd = lax.rem(lax.axis_index("section"), 2)
    copies = []
    for n, part in enumerate(parts):
        for out, row in zip(outs, ((1 - odd) * last, odd * last)):
            sem = sems.at[len(copies)]
            copies.append(
                pltpu.make_async_copy(part.at[pl.ds(row, 1)], out.at[pl.ds(n, 1)], sem)
            )
    for copy in copies:
        copy.start()
    for copy in copies:
        copy.wait()


def interior(grad_ref, preact_ref, wholes, temporal_ref, spatial_ref, inner_ref, gpre_ref, views_ref):
    rows, cols, ch = grad_ref.shape
    step = 4

    for n in range(rows // step):
        here = pl.ds(n * step, step)
        grads = [ref[here] for ref in (grad_ref, *wholes)]
        gpre = pre_gradient(grads, preact_ref[here], temporal_ref)
        gpre_ref[here] = gpre.astype(jnp.bfloat16)
        beside(gpre, views_ref, n * step)

    half = rows // 2 - 1

    for n in range(2):
        first = grad_ref[pl.ds(n * half + 1, half)]
        inner_ref[pl.ds(n * half, half)] = convolved(views_ref, spatial_ref, n * half, first)


def edge_rows(grad_ref, pair_refs, afters, gpre_ref, temporal_ref, spatial_ref, views_ref):
    rows, cols, ch = grad_ref.shape
    (grad_above, grad_below), (above_pre, below_pre) = (beside_band(pair_refs, n) for n in (0, 1))
    above = [grad_above] + [ref[0:1] for ref in afters]
    below = [grad_below] + [ref[1:2] for ref in afters]
    beside(pre_gradient(above, above_pre, temporal_ref), views_ref, 0)
    beside(gpre_ref[0:2].astype(jnp.float32), views_ref, 1)
    beside(gpre_ref[rows - 2 : rows].astype(jnp.float32), views_ref, 3)
    beside(pre_gradient(below, below_pre, temporal_ref), views_ref, 5)
    return (
        convolved(views_ref, spatial_ref, 0, grad_ref[0:1]),
        convolved(views_ref, spatial_ref, 3, grad_ref[rows - 1 : rows]),
    )


def last_inner_kernel(grad_ref, preact_ref, temporal_ref, spatial_ref, inner_ref, gpre_ref, views_ref):
    @pl.when(is_last())
    def _():
        interior(
            grad_ref, preact_ref, [], temporal_ref, spatial_ref, inner_ref, gpre_ref, views_ref
        )


def last_edge_kernel(grad_ref, one_ref, two_ref, gpre_ref, temporal_ref, spatial_ref, edge_ref, views_ref):
    @pl.when(is_last())
    def _():
        pair_refs = (one_ref, two_ref)
        edge_ref[0:1], edge_ref[1:2] = edge_rows(
            grad_ref, pair_refs, [], gpre_ref, temporal_ref, spatial_ref, views_ref
        )
        edge_ref[2:3], edge_ref[3:4] = beside_band(pair_refs, 0)


def inner_kernel(later, *refs):
    inputs, wholes, kernels = refs[:2], refs[2 : 2 + later], refs[2 + later : 4 + later]
    known, outs = refs[4 + later : -3], refs[-3:]
    if not known:
        interior(*inputs, wholes, *kernels, *outs)
        return

    @pl.when(is_last())
    def _():
        outs[0][...] = known[0][...]
        outs[1][...] = known[1][...]

    @pl.when(jnp.logical_not(is_last()))
    def _():
        interior(*inputs, wholes, *kernels, *outs)


def mid_kernel(later, *refs):
    grad_ref, inner_ref, gpre_ref = refs[0], refs[3], refs[4]
    afters, (temporal_ref, spatial_ref, mid_ref, views_ref) = refs[5 : 5 + later], refs[5 + later :]
    rows = grad_ref.shape[0]
    first, last = edge_rows(
        grad_ref, refs[1:3], afters, gpre_ref, temporal_ref, spatial_ref, views_ref
    )
    mid_ref[0:1], mid_ref[rows - 1 : rows] = first, last
    mid_ref[1 : rows - 1] = inner_ref[...]


def two_kernel(later, *refs):
    saved_ref, preact_ref, gpre_ref = refs[:3]
    pair_refs, grad_ref = refs[3:5], refs[5]
    wholes, outs = refs[6 : 6 + later], refs[6 + later : 8 + later]
    views_ref, sides_ref, sums_ref = refs[8 + later :]
    rows, cols, ch = saved_ref.shape
    step = 4

    for n in range(rows // step):
        here = pl.ds(n * step, step)
        beside(gpre_ref[here].astype(jnp.float32), views_ref, n * step)

    views = views_ref[...].reshape(rows * cols, 3 * ch)
    grads = [ref[...] for ref in (grad_ref, *wholes)]
    left_sides(saved_ref, preact_ref, *beside_band(pair_refs, 2), sides_ref)
    kernel_sums(sides_ref, grads, views, sums_ref)
    hand_out(sums_ref, *outs)


def sides_kernel(saved_ref, preact_ref, one_ref, two_ref, sides_ref):
    left_sides(saved_ref, preact_ref, *beside_band((one_ref, two_ref), 3), sides_ref)


def block_one(sides_ref, preact_ref, mids, temporal_ref, outs, scratch):
    gpre_ref, keep_ref, send_ref = outs
    views_ref, sums_ref = scratch
    rows, cols, ch = preact_ref.shape
    step = 4

    for n in range(rows // step):
        here = pl.ds(n * step, step)
        gpre = pre_gradient([ref[here] for ref in mids], preact_ref[here], temporal_ref)
        gpre_ref[here] = gpre.astype(jnp.bfloat16)
        beside(gpre, views_ref, n * step)

    odd = lax.rem(lax.axis_index("section"), 2)
    size = send_ref.shape[0] - 2 * cols
    send_ref[size : size + cols] = gpre_ref[(1 - odd) * (rows - 1)]
    send_ref[size + cols : size + 2 * cols] = gpre_ref[odd * (rows - 1)]
    views = views_ref[...].reshape(rows * cols, 3 * ch)
    kernel_sums(sides_ref, [ref[...] for ref in mids], views, sums_ref)
    hand_out(sums_ref, keep_ref, send_ref)


def one_kernel(later, *refs):
    sides_ref, preact_ref, mids = refs[0], refs[1], refs[2 : 3 + later]
    temporal_ref, outs, scratch = refs[3 + later], refs[4 + later : 7 + later], refs[7 + later :]
    block_one(sides_ref, preact_ref, mids, temporal_ref, outs, scratch)


def mid_one_kernel(*refs):
    after_inner_ref, after_edge_ref = refs[5:7]
    temporal_two_ref, spatial_two_ref, sides_ref, preact_ref, temporal_ref = refs[7:12]
    mid_ref, outs, scratch = refs[12], refs[13:16], refs[16:18]
    next_ref, edge_ref, edge_views_ref = refs[18:]
    rows = next_ref.shape[0]

    @pl.when(is_last())
    def _():
        edge_ref[...] = jnp.zeros(edge_ref.shape, edge_ref.dtype)
        next_ref[...] = jnp.zeros(next_ref.shape, next_ref.dtype)

    @pl.when(jnp.logical_not(is_last()))
    def _():
        edge_ref[...] = after_edge_ref[2:4]
        next_ref[0:1] = after_edge_ref[0:1]
        next_ref[1 : rows - 1] = after_inner_ref[...]
        next_ref[rows - 1 : rows] = after_edge_ref[1:2]

    mid_kernel(
        1, *refs[:5], edge_ref, temporal_two_ref, spatial_two_ref, mid_ref, edge_views_ref
    )
    block_one(sides_ref, preact_ref, [mid_ref, next_ref], temporal_ref, outs, scratch)


def input_kernel(mid_ref, gpre_ref, pair_ref, across_ref, spatial_ref, out_ref, token_ref, views_ref):
    rows, cols, ch = out_ref.shape
    pair = pair_ref[pair_ref.shape[0] - 2 * cols : pair_ref.shape[0] - cols]
    above, below = beside_band((pair[None], across_ref[across_ref.shape[0] - cols :][None]), 0)
    token_ref[...] = jnp.zeros(token_ref.shape, token_ref.dtype)
    step = 4
    beside(above.astype(jnp.float32), views_ref, 0)
    beside(below.astype(jnp.float32), views_ref, rows + 1)

    for n in range(rows // step):
        gpre = gpre_ref[pl.ds(n * step, step)].astype(jnp.float32)
        beside(gpre, views_ref, n * step + 1)

    for n in range(rows // step):
        here = pl.ds(n * step, step)
        out_ref[here] = convolved(views_ref, spatial_ref, n * step, mid_ref[here])


def halves(count, index):
    return [pl.ds(pl.multiple_of(n * count, count), count) for n in (index, 1 - index)]


def pair_kernel(keep_ref, part_ref, own_ref, send_ref):
    across = lax.axis_index("section") // 2
    mine, other = halves(own_ref.shape[0], across)
    own_ref[...] = keep_ref[across] + part_ref[mine].astype(jnp.float32)
    total = keep_ref[1 - across] + part_ref[other].astype(jnp.float32)
    send_ref[...] = total.astype(jnp.bfloat16)


def band_kernel(own_ref, part_ref, keep_ref, send_ref):
    mine, other = halves(keep_ref.shape[0], lax.axis_index("video"))
    keep_ref[...] = own_ref[mine] + part_ref[mine].astype(jnp.float32)
    send_ref[...] = (own_ref[other] + part_ref[other].astype(jnp.float32)).astype(jnp.bfloat16)


def pair_quarter_kernel(keep_ref, part_ref, own_ref, across_ref, frame_ref, both_ref):
    _, height, _ = keep_ref.shape
    half = own_ref.shape[0]
    band = lax.axis_index("section") // 2
    frames = halves(half, lax.axis_index("video"))

    def quarter(band, rows):
        start = pl.multiple_of(band * height, height)
        part = part_ref.at[pl.ds(start, height)][rows]
        return keep_ref[band, rows] + part.astype(jnp.float32)

    own_ref[...] = quarter(band, frames[0])
    across_ref[:half] = quarter(1 - band, frames[0]).astype(jnp.bfloat16)
    rest = across_ref.shape[0] - half
    across_ref[half:] = part_ref[2 * height + rest :]
    frame_ref[...] = quarter(band, frames[1]).astype(jnp.bfloat16)
    both_ref[...] = quarter(1 - band, frames[1]).astype(jnp.bfloat16)


def plane_kernel(own_ref, *refs):
    parts, out_ref = refs[:-1], refs[-1]
    total = own_ref[...]
    for part in parts:
        total = total + part[: out_ref.shape[0]].astype(jnp.float32)
    out_ref[...] = total.astype(jnp.bfloat16)


def add_kernel(one_ref, two_ref, out_ref):
    total = one_ref[...].astype(jnp.float32) + two_ref[...].astype(jnp.float32)
    out_ref[...] = total.astype(jnp.bfloat16)


def scaled_kernel(factor, *refs):
    out_ref = refs[-1]
    for block in range(2):
        one, two = (ref[...].astype(jnp.float32) for ref in refs[2 * block : 2 * block + 2])
        out_ref[block] = ((one + two) * factor).astype(jnp.bfloat16)


def place_kernel(*refs):
    shares, outs = refs[:-4], refs[-4:]
    band, frame = lax.axis_index("section"), lax.axis_index("video")
    halves = len(shares) // 4
    height = shares[0].shape[1]
    for n, share in enumerate(shares):
        place = jnp.bitwise_xor(band, n // halves)
        half = jnp.bitwise_xor(frame, n % halves) if halves == 2 else 0
        here = pl.ds(pl.multiple_of(half * height, height), height)

        @pl.when(place < 3)
        def _():
            for block in range(2):
                outs[2 * block][place, here] = share[block].astype(jnp.float32)

        @pl.when(place == 3)
        def _():
            for block in range(2):
                outs[2 * block + 1][here] = share[block].astype(jnp.float32)


def placed(shares, across):
    ch = shares[0].shape[2]
    outs = call(
        place_kernel,
        [f32(3, 3 * ch, ch), f32(3 * ch, ch)] * 2,
        [],
        12 * ch * ch,
        *shares,
        *[flipped(share, "section", 1) for share in shares],
        *across,
        *[flipped(share, "section", 1) for share in across],
    )
    return [x.reshape(3, 3, ch, ch) if x.ndim == 3 else x.reshape(3, ch, ch) for x in outs]


def on_device(
    grad_latent,
    input_one,
    preact_one,
    input_two,
    preact_two,
    spatial_one,
    temporal_one,
    spatial_two,
    temporal_two,
):
    shape = grad_latent.shape
    rows, cols, ch = shape[2:]
    bands, frames = lax.axis_size("section"), lax.axis_size("video")
    later = min(2, frames - 1)
    pixels = lax.axis_size("dp") * frames * bands * rows * cols
    factor = 1.0 / math.sqrt(pixels)
    grad, saved_one, pre_one, saved_two, pre_two = (
        x.reshape(rows, cols, ch)
        for x in (grad_latent, input_one, preact_one, input_two, preact_two)
    )
    conv = 2 * rows * cols * 9 * ch * ch
    views = pltpu.VMEM((rows, cols, 3 * ch), jnp.bfloat16)
    edge_views = pltpu.VMEM((6, cols, 3 * ch), jnp.bfloat16)
    act = pltpu.VMEM((rows, cols, ch), jnp.bfloat16)
    sides = bf16(4, ch, rows * cols)
    sums = pltpu.VMEM((4, 3 * ch, ch), jnp.float32)
    handed = [f32(2, 3 * ch, ch), bf16(6 * ch, ch)]
    inner_outs = [bf16(rows - 2, cols, ch), bf16(rows, cols, ch)]
    kernels = (temporal_two, spatial_two)

    def from_later(x):
        if frames == 2:
            return [flipped(x, "video", 1)]
        return [from_ahead(x, 0, n + 1) for n in range(later)]

    wholes = from_later(grad)
    packs = call(
        pack_kernel,
        [bf16(4, cols, ch)] * 2,
        [pltpu.SemaphoreType.DMA((8,))],
        1,
        grad,
        pre_two,
        saved_two,
        saved_one,
        spare_inputs=True,
        limit=58,
    )
    first, second = (flipped(pack, "section", 1) for pack in packs)
    pairs = [first, flipped(second, "section", 2)]

    known = ()
    if frames == 2:
        known = call(
            last_inner_kernel,
            inner_outs,
            [views],
            1.2 * conv,
            grad,
            pre_two,
            *kernels,
            after=(first, second),
        )
        afters = from_later(known[0])
    else:
        afters = from_later(jnp.concatenate(beside_band(pairs, 0)))
    inner, gpre_two = call(
        functools.partial(inner_kernel, later),
        inner_outs,
        [views],
        1.2 * conv,
        grad,
        pre_two,
        *wholes,
        *kernels,
        *known,
        early=(saved_two,),
    )
    if frames == 2:
        edge = call(
            last_edge_kernel,
            [bf16(4, cols, ch)],
            [edge_views],
            conv // 8,
            grad,
            *pairs,
            known[1],
            *kernels,
            after=(gpre_two,),
        )
        afters += from_later(edge)
    parts_two = call(
        functools.partial(two_kernel, later),
        handed,
        [views, pltpu.VMEM(sides.shape, sides.dtype), sums],
        1.2 * conv,
        saved_two,
        pre_two,
        gpre_two,
        *pairs,
        grad,
        *wholes,
        after=(edge,) if frames == 2 else (),
        early=(saved_one, pre_one, temporal_one),
    )
    sides_one = call(
        sides_kernel, [sides], [], conv // 8, saved_one, pre_one, *pairs, after=parts_two[:1]
    )
    height, half = 3 * ch, 3 * ch // 2
    keep_two, send_two = parts_two
    own_two, send_two = call(
        pair_kernel,
        [f32(height, ch), bf16(height, ch)],
        [],
        height * ch,
        keep_two,
        flipped(send_two, "section", 1),
        after=afters[:1] if frames == 2 else (),
    )
    across_two = flipped(send_two, "section", 2)
    mid_inputs = (grad, *pairs, inner, gpre_two)
    one_inputs = (sides_one, pre_one)
    mid_outs = [bf16(rows, cols, ch)]
    one_outs = [bf16(rows, cols, ch), f32(2, 3 * ch, ch), bf16(6 * ch + 2 * cols, ch)]
    if frames == 2:
        mid, gpre_one, *parts_one = call(
            mid_one_kernel,
            mid_outs + one_outs,
            [views, sums, act, pltpu.VMEM((2, cols, ch), jnp.bfloat16), edge_views],
            1.5 * conv,
            *mid_inputs,
            *afters,
            *kernels,
            *one_inputs,
            temporal_one,
            after=(own_two,),
        )
    else:
        mid = call(
            functools.partial(mid_kernel, later),
            mid_outs,
            [edge_views],
            conv // 8,
            *mid_inputs,
            *afters,
            *kernels,
        )
        gpre_one, *parts_one = call(
            functools.partial(one_kernel, later),
            one_outs,
            [views, sums],
            1.2 * conv,
            *one_inputs,
            mid,
            *from_later(mid),
            temporal_one,
        )
    keep_one, send_one = parts_one
    split = frames == 2 and lax.axis_size("dp") == 4
    if split:
        send_one = later_than(send_one, across_two)
    pair_one = flipped(send_one, "section", 1)

    def input_gradient(edge, after):
        return call(
            input_kernel,
            [bf16(rows, cols, ch), f32(8, 128)],
            [pltpu.VMEM((rows + 2, cols, 3 * ch), jnp.bfloat16)],
            conv,
            mid,
            gpre_one,
            pair_one,
            edge,
            spatial_one,
            after=after,
        )

    if split:

        def added(one, two):
            return call(add_kernel, [bf16(half, ch)], [], half * ch, one, two)

        keep_two, send_two = call(
            band_kernel,
            [f32(half, ch), bf16(half, ch)],
            [],
            height * ch,
            own_two,
            across_two,
        )
        sum_two = added(keep_two, flipped(send_two, "video", 1))
        quarters = [f32(half, ch), bf16(half + cols, ch)] + [bf16(half, ch)] * 2
        own_one, *sends = call(
            pair_quarter_kernel, quarters, [], height * ch, keep_one, pair_one, after=(send_two,)
        )
        across = flipped(sends[0], "section", 2)
        parts = [across, flipped(sends[1], "video", 1), flipped_both(sends[2])]
        sum_one = call(plane_kernel, [bf16(half, ch)], [], 4 * half * ch, own_one, *parts)
        part_two = flipped(sum_two, "dp", 1)
        part_one = flipped(later_than(sum_one, sum_two), "dp", 1)
        sum_two = added(sum_two, part_two)
        sum_one = added(sum_one, part_one)
        last_two = flipped(sum_two, "dp", 2)
        last_one = flipped(later_than(sum_one, sum_two), "dp", 2)
        grad_in, token = input_gradient(across, (sum_one,))
        own = call(
            functools.partial(scaled_kernel, factor),
            [bf16(2, half, ch)],
            [],
            height * ch,
            sum_one,
            last_one,
            sum_two,
            last_two,
            after=(token,),
        )
        shares = [own, flipped(own, "video", 1)]
        sums = placed(shares, [flipped(own, "section", 2), flipped_both(own)])
    else:
        own_one, send_one = call(
            pair_kernel, [f32(height, ch), bf16(height, ch)], [], height * ch, keep_one, pair_one
        )
        edge = flipped(pair_one[pair_one.shape[0] - cols :], "section", 2)
        grad_in, _ = input_gradient(edge, ())
        own_one = own_one + flipped(send_one, "section", 2).astype(jnp.float32)
        own_two = own_two + across_two.astype(jnp.float32)
        share = lax.psum(jnp.stack((own_one, own_two)), ("video", "dp")) * factor
        share = share.astype(jnp.bfloat16)
        sums = placed([share], [flipped(share, "section", 2)])
    return (grad_in.reshape(shape), *sums)


def solution(mesh):
    whole = P("dp", "video", "section", None, None)
    return jax.shard_map(
        on_device,
        mesh=mesh,
        in_specs=(whole,) * 5 + (P(),) * 4,
        out_specs=(whole, P(), P(), P(), P()),
        check_vma=False,
    )
```

```python
import functools
import math

import jax
import jax.numpy as jnp
from jax import lax
from jax.experimental import pallas as pl
from jax.experimental.pallas import tpu as pltpu
from jax.sharding import PartitionSpec as P

MIB = 1024 * 1024


def sigmoid(value):
    return 1.0 / (1.0 + jnp.exp(-value))


def bf16(*shape):
    return jax.ShapeDtypeStruct(shape, jnp.bfloat16)


def f32(*shape):
    return jax.ShapeDtypeStruct(shape, jnp.float32)


def call(kernel, outs, scratch, flops, *operands, after=(), early=(), spare_inputs=False, limit=24):
    single = len(outs) == 1
    moved = sum(math.prod(x.shape) * x.dtype.itemsize for x in (*operands, *outs))
    vmem = pl.BlockSpec(memory_space=pltpu.VMEM)
    spare = pl.BlockSpec(memory_space=pl.ANY)
    spec = spare if spare_inputs else vmem
    count = len(operands)
    operands = (*operands, *early, *after)

    def body(*refs):
        kernel(*refs[:count], *refs[len(operands) :])

    return pl.pallas_call(
        body,
        out_shape=outs[0] if single else tuple(outs),
        in_specs=[spec] * count + [vmem] * len(early) + [spare] * len(after),
        out_specs=vmem if single else (vmem,) * len(outs),
        scratch_shapes=scratch,
        compiler_params=pltpu.CompilerParams(vmem_limit_bytes=limit * MIB),
        cost_estimate=pl.CostEstimate(
            flops=int(flops), bytes_accessed=int(moved), transcendentals=0
        ),
    )(*operands)


def from_ahead(block, band_step, frame_step):
    bands, frames = lax.axis_size("section"), lax.axis_size("video")
    pairs = [
        ((band + band_step) * frames + frame + frame_step, band * frames + frame)
        for band in range(bands)
        for frame in range(frames)
        if 0 <= band + band_step < bands and frame + frame_step < frames
    ]
    return lax.ppermute(block, ("section", "video"), pairs)


def beside_band(pair_refs, row):
    band = lax.axis_index("section")
    odd = lax.rem(band, 2) == 1
    inside = (band > 0) & (band < lax.axis_size("section") - 1)
    first, second = (ref[row : row + 1] for ref in pair_refs)
    second = jnp.where(inside, second, jnp.zeros_like(second))
    return jnp.where(odd, first, second), jnp.where(odd, second, first)


def flipped(block, axis, flip):
    count = lax.axis_size(axis)
    return lax.ppermute(block, axis, [(place ^ flip, place) for place in range(count)])


def flipped_odd(block, axis, flip):
    names = ("section", "video", "dp")
    counts = [lax.axis_size(name) for name in names]
    pairs = []
    for band in range(1, counts[0], 2):
        for frame in range(counts[1]):
            for clip in range(counts[2]):
                place = {"section": band, "video": frame, "dp": clip}
                source = dict(place)
                source[axis] ^= flip
                pairs.append(
                    tuple(
                        (at["section"] * counts[1] + at["video"]) * counts[2] + at["dp"]
                        for at in (source, place)
                    )
                )
    return lax.ppermute(block, names, pairs)


def flipped_both(block):
    bands = lax.axis_size("section")
    pairs = [
        (2 * (band ^ 2) + 1 - frame, 2 * band + frame) for band in range(bands) for frame in range(2)
    ]
    return lax.ppermute(block, ("section", "video"), pairs)


def later_than(block, *others):
    return lax.optimization_barrier((block, *others))[0]


def beside(gpre, views_ref, start):
    count, cols, ch = gpre.shape
    at = lax.broadcasted_iota(jnp.int32, gpre.shape, 1)
    right = jnp.where(at == cols - 1, 0.0, pltpu.roll(gpre, cols - 1, 1))
    left = jnp.where(at == 0, 0.0, pltpu.roll(gpre, 1, 1))
    here = pl.ds(start, count)
    views_ref[here, :, 0:ch] = right.astype(jnp.bfloat16)
    views_ref[here, :, ch : 2 * ch] = gpre.astype(jnp.bfloat16)
    views_ref[here, :, 2 * ch : 3 * ch] = left.astype(jnp.bfloat16)


def pre_gradient(grads, preact, temporal_ref):
    count, cols, ch = preact.shape
    flat = jnp.concatenate([grad.reshape(count * cols, ch) for grad in grads], axis=1)
    kernel = jnp.concatenate([temporal_ref[2 - step] for step in range(len(grads))], axis=1)
    gact = lax.dot_general(
        flat, kernel, (((1,), (1,)), ((), ())), preferred_element_type=jnp.float32
    )
    gact = gact.astype(jnp.bfloat16).astype(jnp.float32).reshape(preact.shape)
    hval = preact.astype(jnp.float32)
    sig = sigmoid(hval)
    return gact * sig * (1.0 + hval * (1.0 - sig))


def convolved(views_ref, spatial_ref, start, first):
    count, cols, ch = first.shape
    total = first.astype(jnp.float32).reshape(count * cols, ch)
    for ky in range(3):
        view = views_ref[pl.ds(start + 2 - ky, count)].reshape(count * cols, 3 * ch)
        kernel = jnp.concatenate([spatial_ref[ky, kx] for kx in range(3)], axis=1)
        total = total + lax.dot_general(
            view, kernel, (((1,), (1,)), ((), ())), preferred_element_type=jnp.float32
        )
    return total.astype(jnp.bfloat16).reshape(first.shape)


def is_last():
    return lax.axis_index("video") == lax.axis_size("video") - 1


def left_sides(saved_ref, preact_ref, above, below, sides_ref):
    rows, cols, ch = saved_ref.shape
    flat = (rows * cols, ch)
    shifts = [
        jnp.concatenate([above, saved_ref[: rows - 1]], axis=0),
        saved_ref[...],
        jnp.concatenate([saved_ref[1:], below], axis=0),
    ]
    for n, shift in enumerate(shifts):
        sides_ref[n] = shift.reshape(flat).T
    hval = preact_ref[...].astype(jnp.float32)
    sides_ref[3] = (hval * sigmoid(hval)).astype(jnp.bfloat16).reshape(flat).T


def kernel_sums(sides_ref, grads, views, sums_ref):
    _, ch, pixels = sides_ref.shape
    shifts = sides_ref[0:3].reshape(3 * ch, pixels)
    sums = jnp.dot(shifts, views, preferred_element_type=jnp.float32)
    for ky in range(3):
        for kx in range(3):
            here = slice(kx * ch, (kx + 1) * ch)
            sums_ref[ky, here] = sums[ky * ch : (ky + 1) * ch, here]
    grads = jnp.concatenate([grad.reshape(pixels, ch) for grad in grads], axis=1)
    sums = jnp.dot(sides_ref[3], grads, preferred_element_type=jnp.float32)
    zeros = jnp.zeros((ch, ch), jnp.float32)
    for k in range(3):
        step = 2 - k
        value = sums[:, step * ch : (step + 1) * ch] if step * ch < grads.shape[1] else zeros
        sums_ref[3, k * ch : (k + 1) * ch] = jnp.where(is_last(), zeros, value) if step else value


def hand_out(sums_ref, keep_ref, send_ref):
    odd = lax.rem(lax.axis_index("section"), 2)
    height = sums_ref.shape[1]
    for n in range(2):
        keep_ref[n] = sums_ref[2 * n + odd]
        send_ref[n * height : (n + 1) * height] = sums_ref[2 * n + 1 - odd].astype(jnp.bfloat16)


def pack_kernel(*refs):
    parts, outs, sems = refs[:4], refs[4:6], refs[6]
    last = parts[0].shape[0] - 1
    odd = lax.rem(lax.axis_index("section"), 2)
    copies = []
    for n, part in enumerate(parts):
        for out, row in zip(outs, ((1 - odd) * last, odd * last)):
            sem = sems.at[len(copies)]
            copies.append(
                pltpu.make_async_copy(part.at[pl.ds(row, 1)], out.at[pl.ds(n, 1)], sem)
            )
    for copy in copies:
        copy.start()
    for copy in copies:
        copy.wait()


def interior(grad_ref, preact_ref, wholes, temporal_ref, spatial_ref, inner_ref, gpre_ref, views_ref):
    rows, cols, ch = grad_ref.shape
    step = 4

    for n in range(rows // step):
        here = pl.ds(n * step, step)
        grads = [ref[here] for ref in (grad_ref, *wholes)]
        gpre = pre_gradient(grads, preact_ref[here], temporal_ref)
        gpre_ref[here] = gpre.astype(jnp.bfloat16)
        beside(gpre, views_ref, n * step)

    half = rows // 2 - 1

    for n in range(2):
        first = grad_ref[pl.ds(n * half + 1, half)]
        inner_ref[pl.ds(n * half, half)] = convolved(views_ref, spatial_ref, n * half, first)


def edge_rows(grad_ref, pair_refs, afters, gpre_ref, temporal_ref, spatial_ref, views_ref):
    rows, cols, ch = grad_ref.shape
    (grad_above, grad_below), (above_pre, below_pre) = (beside_band(pair_refs, n) for n in (0, 1))
    above = [grad_above] + [ref[0:1] for ref in afters]
    below = [grad_below] + [ref[1:2] for ref in afters]
    beside(pre_gradient(above, above_pre, temporal_ref), views_ref, 0)
    beside(gpre_ref[0:2].astype(jnp.float32), views_ref, 1)
    beside(gpre_ref[rows - 2 : rows].astype(jnp.float32), views_ref, 3)
    beside(pre_gradient(below, below_pre, temporal_ref), views_ref, 5)
    return (
        convolved(views_ref, spatial_ref, 0, grad_ref[0:1]),
        convolved(views_ref, spatial_ref, 3, grad_ref[rows - 1 : rows]),
    )


def last_inner_kernel(grad_ref, preact_ref, temporal_ref, spatial_ref, inner_ref, gpre_ref, views_ref):
    @pl.when(is_last())
    def _():
        interior(
            grad_ref, preact_ref, [], temporal_ref, spatial_ref, inner_ref, gpre_ref, views_ref
        )


def last_edge_kernel(grad_ref, one_ref, two_ref, gpre_ref, temporal_ref, spatial_ref, edge_ref, views_ref):
    @pl.when(is_last())
    def _():
        pair_refs = (one_ref, two_ref)
        edge_ref[0:1], edge_ref[1:2] = edge_rows(
            grad_ref, pair_refs, [], gpre_ref, temporal_ref, spatial_ref, views_ref
        )
        edge_ref[2:3], edge_ref[3:4] = beside_band(pair_refs, 0)


def inner_kernel(later, *refs):
    inputs, wholes, kernels = refs[:2], refs[2 : 2 + later], refs[2 + later : 4 + later]
    known, outs = refs[4 + later : -3], refs[-3:]
    if not known:
        interior(*inputs, wholes, *kernels, *outs)
        return

    @pl.when(is_last())
    def _():
        outs[0][...] = known[0][...]
        outs[1][...] = known[1][...]

    @pl.when(jnp.logical_not(is_last()))
    def _():
        interior(*inputs, wholes, *kernels, *outs)


def mid_kernel(later, *refs):
    grad_ref, inner_ref, gpre_ref = refs[0], refs[3], refs[4]
    afters, (temporal_ref, spatial_ref, mid_ref, views_ref) = refs[5 : 5 + later], refs[5 + later :]
    rows = grad_ref.shape[0]
    first, last = edge_rows(
        grad_ref, refs[1:3], afters, gpre_ref, temporal_ref, spatial_ref, views_ref
    )
    mid_ref[0:1], mid_ref[rows - 1 : rows] = first, last
    mid_ref[1 : rows - 1] = inner_ref[...]


def two_kernel(later, *refs):
    saved_ref, preact_ref, gpre_ref = refs[:3]
    pair_refs, grad_ref = refs[3:5], refs[5]
    wholes, outs = refs[6 : 6 + later], refs[6 + later : 9 + later]
    views_ref, sides_ref, sums_ref = refs[9 + later :]
    rows, cols, ch = saved_ref.shape
    step = 4

    for n in range(rows // step):
        here = pl.ds(n * step, step)
        beside(gpre_ref[here].astype(jnp.float32), views_ref, n * step)

    views = views_ref[...].reshape(rows * cols, 3 * ch)
    grads = [ref[...] for ref in (grad_ref, *wholes)]
    left_sides(saved_ref, preact_ref, *beside_band(pair_refs, 2), sides_ref)
    kernel_sums(sides_ref, grads, views, sums_ref)
    share_out(sums_ref, *outs)


def sides_kernel(saved_ref, preact_ref, one_ref, two_ref, sides_ref):
    left_sides(saved_ref, preact_ref, *beside_band((one_ref, two_ref), 3), sides_ref)


def block_one(sides_ref, preact_ref, mids, temporal_ref, outs, scratch):
    gpre_ref, keep_ref, send_ref = outs
    views_ref, sums_ref = scratch
    rows, cols, ch = preact_ref.shape
    step = 4

    for n in range(rows // step):
        here = pl.ds(n * step, step)
        gpre = pre_gradient([ref[here] for ref in mids], preact_ref[here], temporal_ref)
        gpre_ref[here] = gpre.astype(jnp.bfloat16)
        beside(gpre, views_ref, n * step)

    odd = lax.rem(lax.axis_index("section"), 2)
    size = send_ref.shape[0] - 2 * cols
    send_ref[size : size + cols] = gpre_ref[(1 - odd) * (rows - 1)]
    send_ref[size + cols : size + 2 * cols] = gpre_ref[odd * (rows - 1)]
    views = views_ref[...].reshape(rows * cols, 3 * ch)
    kernel_sums(sides_ref, [ref[...] for ref in mids], views, sums_ref)
    hand_out(sums_ref, keep_ref, send_ref)


def one_kernel(later, *refs):
    sides_ref, preact_ref, mids = refs[0], refs[1], refs[2 : 3 + later]
    temporal_ref, outs, scratch = refs[3 + later], refs[4 + later : 7 + later], refs[7 + later :]
    block_one(sides_ref, preact_ref, mids, temporal_ref, outs, scratch)


def mid_one_kernel(*refs):
    after_inner_ref, after_edge_ref = refs[5:7]
    temporal_two_ref, spatial_two_ref, sides_ref, preact_ref, temporal_ref = refs[7:12]
    mid_ref, outs, scratch = refs[12], refs[13:16], refs[16:18]
    next_ref, edge_ref, edge_views_ref = refs[18:]
    rows = next_ref.shape[0]

    @pl.when(is_last())
    def _():
        edge_ref[...] = jnp.zeros(edge_ref.shape, edge_ref.dtype)
        next_ref[...] = jnp.zeros(next_ref.shape, next_ref.dtype)

    @pl.when(jnp.logical_not(is_last()))
    def _():
        edge_ref[...] = after_edge_ref[2:4]
        next_ref[0:1] = after_edge_ref[0:1]
        next_ref[1 : rows - 1] = after_inner_ref[...]
        next_ref[rows - 1 : rows] = after_edge_ref[1:2]

    mid_kernel(
        1, *refs[:5], edge_ref, temporal_two_ref, spatial_two_ref, mid_ref, edge_views_ref
    )
    block_one(sides_ref, preact_ref, [mid_ref, next_ref], temporal_ref, outs, scratch)


def input_kernel(mid_ref, gpre_ref, pair_ref, across_ref, spatial_ref, out_ref, token_ref, views_ref):
    rows, cols, ch = out_ref.shape
    pair = pair_ref[pair_ref.shape[0] - 2 * cols : pair_ref.shape[0] - cols]
    above, below = beside_band((pair[None], across_ref[across_ref.shape[0] - cols :][None]), 0)
    token_ref[...] = jnp.zeros(token_ref.shape, token_ref.dtype)
    step = 4
    beside(above.astype(jnp.float32), views_ref, 0)
    beside(below.astype(jnp.float32), views_ref, rows + 1)

    for n in range(rows // step):
        gpre = gpre_ref[pl.ds(n * step, step)].astype(jnp.float32)
        beside(gpre, views_ref, n * step + 1)

    for n in range(rows // step):
        here = pl.ds(n * step, step)
        out_ref[here] = convolved(views_ref, spatial_ref, n * step, mid_ref[here])


def halves(count, index):
    return [pl.ds(pl.multiple_of(n * count, count), count) for n in (index, 1 - index)]


def is_odd():
    return lax.rem(lax.axis_index("section"), 2) == 1


def share_out(sums_ref, keep_ref, *send_refs):
    height = sums_ref.shape[1]
    for n in range(4):
        keep_ref[n] = sums_ref[n]
        start = n % 2 * height
        send_refs[n // 2][start : start + height] = sums_ref[n].astype(jnp.bfloat16)


def odd_pair_kernel(keep_ref, low_ref, high_ref, own_ref, send_ref):
    height = keep_ref.shape[1]

    @pl.when(is_odd())
    def _():
        across = lax.axis_index("section") // 2
        for n in range(2):
            here = slice(n * height, (n + 1) * height)
            low, high = (ref[here].astype(jnp.float32) for ref in (low_ref, high_ref))
            for where, ref in ((across, own_ref), (1 - across, send_ref)):
                total = keep_ref[2 * where + n] + jnp.where(where == 0, low, high)
                ref[here] = total.astype(ref.dtype)


def odd_band_kernel(own_ref, part_ref, keep_ref, send_ref):
    half = keep_ref.shape[1]

    @pl.when(is_odd())
    def _():
        frame = lax.axis_index("video")
        for n in range(2):
            for where, ref in ((frame, keep_ref), (1 - frame, send_ref)):
                rows = pl.ds(pl.multiple_of((2 * n + where) * half, half), half)
                total = own_ref[rows] + part_ref[rows].astype(jnp.float32)
                ref[n] = total.astype(ref.dtype)


def odd_add_kernel(one_ref, two_ref, out_ref):
    @pl.when(is_odd())
    def _():
        add_kernel(one_ref, two_ref, out_ref)


def odd_scaled_kernel(factor, one_ref, two_ref, own_ref, send_ref):
    @pl.when(is_odd())
    def _():
        total = one_ref[...].astype(jnp.float32) + two_ref[...].astype(jnp.float32)
        total = (total * factor).astype(jnp.bfloat16)
        send_ref[...], own_ref[...] = total[0], total[1]


def pair_kernel(keep_ref, part_ref, own_ref, send_ref):
    across = lax.axis_index("section") // 2
    mine, other = halves(own_ref.shape[0], across)
    own_ref[...] = keep_ref[across] + part_ref[mine].astype(jnp.float32)
    total = keep_ref[1 - across] + part_ref[other].astype(jnp.float32)
    send_ref[...] = total.astype(jnp.bfloat16)


def pair_quarter_kernel(keep_ref, part_ref, own_ref, across_ref, frame_ref, both_ref):
    _, height, _ = keep_ref.shape
    half = own_ref.shape[0]
    band = lax.axis_index("section") // 2
    frames = halves(half, lax.axis_index("video"))

    def quarter(band, rows):
        start = pl.multiple_of(band * height, height)
        part = part_ref.at[pl.ds(start, height)][rows]
        return keep_ref[band, rows] + part.astype(jnp.float32)

    own_ref[...] = quarter(band, frames[0])
    across_ref[:half] = quarter(1 - band, frames[0]).astype(jnp.bfloat16)
    rest = across_ref.shape[0] - half
    across_ref[half:] = part_ref[2 * height + rest :]
    frame_ref[...] = quarter(band, frames[1]).astype(jnp.bfloat16)
    both_ref[...] = quarter(1 - band, frames[1]).astype(jnp.bfloat16)


def plane_kernel(own_ref, *refs):
    parts, out_ref = refs[:-1], refs[-1]
    total = own_ref[...]
    for part in parts:
        total = total + part[: out_ref.shape[0]].astype(jnp.float32)
    out_ref[...] = total.astype(jnp.bfloat16)


def add_kernel(one_ref, two_ref, out_ref):
    total = one_ref[...].astype(jnp.float32) + two_ref[...].astype(jnp.float32)
    out_ref[...] = total.astype(jnp.bfloat16)


def scaled_kernel(factor, one_ref, two_ref, own_ref, given_ref, out_ref):
    total = one_ref[...].astype(jnp.float32) + two_ref[...].astype(jnp.float32)
    out_ref[0] = (total * factor).astype(jnp.bfloat16)
    out_ref[1] = jnp.where(is_odd(), own_ref[...], given_ref[...])


def place_kernel(*refs):
    shares, outs = refs[:-4], refs[-4:]
    band, frame = lax.axis_index("section"), lax.axis_index("video")
    halves = len(shares) // 4
    height = shares[0].shape[1]
    for n, share in enumerate(shares):
        place = jnp.bitwise_xor(band, n // halves)
        half = jnp.bitwise_xor(frame, n % halves) if halves == 2 else 0
        here = pl.ds(pl.multiple_of(half * height, height), height)

        @pl.when(place < 3)
        def _():
            for block in range(2):
                outs[2 * block][place, here] = share[block].astype(jnp.float32)

        @pl.when(place == 3)
        def _():
            for block in range(2):
                outs[2 * block + 1][here] = share[block].astype(jnp.float32)


def placed(shares, across):
    ch = shares[0].shape[2]
    outs = call(
        place_kernel,
        [f32(3, 3 * ch, ch), f32(3 * ch, ch)] * 2,
        [],
        12 * ch * ch,
        *shares,
        *[flipped(share, "section", 1) for share in shares],
        *across,
        *[flipped(share, "section", 1) for share in across],
    )
    return [x.reshape(3, 3, ch, ch) if x.ndim == 3 else x.reshape(3, ch, ch) for x in outs]


def on_device(
    grad_latent,
    input_one,
    preact_one,
    input_two,
    preact_two,
    spatial_one,
    temporal_one,
    spatial_two,
    temporal_two,
):
    shape = grad_latent.shape
    rows, cols, ch = shape[2:]
    bands, frames = lax.axis_size("section"), lax.axis_size("video")
    later = min(2, frames - 1)
    pixels = lax.axis_size("dp") * frames * bands * rows * cols
    factor = 1.0 / math.sqrt(pixels)
    grad, saved_one, pre_one, saved_two, pre_two = (
        x.reshape(rows, cols, ch)
        for x in (grad_latent, input_one, preact_one, input_two, preact_two)
    )
    conv = 2 * rows * cols * 9 * ch * ch
    views = pltpu.VMEM((rows, cols, 3 * ch), jnp.bfloat16)
    edge_views = pltpu.VMEM((6, cols, 3 * ch), jnp.bfloat16)
    act = pltpu.VMEM((rows, cols, ch), jnp.bfloat16)
    sides = bf16(4, ch, rows * cols)
    sums = pltpu.VMEM((4, 3 * ch, ch), jnp.float32)
    handed = [f32(4, 3 * ch, ch)] + [bf16(6 * ch, ch)] * 2
    inner_outs = [bf16(rows - 2, cols, ch), bf16(rows, cols, ch)]
    kernels = (temporal_two, spatial_two)

    def from_later(x):
        if frames == 2:
            return [flipped(x, "video", 1)]
        return [from_ahead(x, 0, n + 1) for n in range(later)]

    wholes = from_later(grad)
    packs = call(
        pack_kernel,
        [bf16(4, cols, ch)] * 2,
        [pltpu.SemaphoreType.DMA((8,))],
        1,
        grad,
        pre_two,
        saved_two,
        saved_one,
        spare_inputs=True,
        limit=58,
    )
    first, second = (flipped(pack, "section", 1) for pack in packs)
    pairs = [first, flipped(second, "section", 2)]

    known = ()
    if frames == 2:
        known = call(
            last_inner_kernel,
            inner_outs,
            [views],
            1.2 * conv,
            grad,
            pre_two,
            *kernels,
            after=(first, second),
        )
        afters = from_later(known[0])
    else:
        afters = from_later(jnp.concatenate(beside_band(pairs, 0)))
    inner, gpre_two = call(
        functools.partial(inner_kernel, later),
        inner_outs,
        [views],
        1.2 * conv,
        grad,
        pre_two,
        *wholes,
        *kernels,
        *known,
        early=(saved_two, saved_one, pre_one, temporal_one),
    )
    if frames == 2:
        edge = call(
            last_edge_kernel,
            [bf16(4, cols, ch)],
            [edge_views],
            conv // 8,
            grad,
            *pairs,
            known[1],
            *kernels,
            after=(gpre_two,),
        )
        afters += from_later(edge)
    parts_two = call(
        functools.partial(two_kernel, later),
        handed,
        [views, pltpu.VMEM(sides.shape, sides.dtype), sums],
        1.2 * conv,
        saved_two,
        pre_two,
        gpre_two,
        *pairs,
        grad,
        *wholes,
        after=(edge,) if frames == 2 else (),
    )
    sides_one = call(
        sides_kernel, [sides], [], conv // 8, saved_one, pre_one, *pairs, after=parts_two[:1]
    )
    height, half = 3 * ch, 3 * ch // 2
    keep_two, *sends_two = parts_two
    own_two, send_two = call(
        odd_pair_kernel,
        [f32(2 * height, ch), bf16(2 * height, ch)],
        [],
        2 * height * ch,
        keep_two,
        *[flipped(send, "section", 1) for send in sends_two],
        after=afters[:1] if frames == 2 else (),
    )
    across_two = flipped_odd(send_two, "section", 2)
    mid_inputs = (grad, *pairs, inner, gpre_two)
    one_inputs = (sides_one, pre_one)
    mid_outs = [bf16(rows, cols, ch)]
    one_outs = [bf16(rows, cols, ch), f32(2, 3 * ch, ch), bf16(6 * ch + 2 * cols, ch)]
    if frames == 2:
        mid, gpre_one, *parts_one = call(
            mid_one_kernel,
            mid_outs + one_outs,
            [views, sums, act, pltpu.VMEM((2, cols, ch), jnp.bfloat16), edge_views],
            8 * conv,
            *mid_inputs,
            *afters,
            *kernels,
            *one_inputs,
            temporal_one,
            after=(own_two,),
        )
    else:
        mid = call(
            functools.partial(mid_kernel, later),
            mid_outs,
            [edge_views],
            conv // 8,
            *mid_inputs,
            *afters,
            *kernels,
        )
        gpre_one, *parts_one = call(
            functools.partial(one_kernel, later),
            one_outs,
            [views, sums],
            1.2 * conv,
            *one_inputs,
            mid,
            *from_later(mid),
            temporal_one,
        )
    keep_one, send_one = parts_one
    split = frames == 2 and lax.axis_size("dp") == 4
    if split:
        send_one = later_than(send_one, across_two)
    pair_one = flipped(send_one, "section", 1)

    def input_gradient(edge, after):
        return call(
            input_kernel,
            [bf16(rows, cols, ch), f32(8, 128)],
            [pltpu.VMEM((rows + 2, cols, 3 * ch), jnp.bfloat16)],
            conv,
            mid,
            gpre_one,
            pair_one,
            edge,
            spatial_one,
            after=after,
        )

    if split:

        odd_cut = (2, half, ch)
        outs = [f32(*odd_cut), bf16(*odd_cut)]
        def odd_added(one, two, after):
            return call(odd_add_kernel, [bf16(*odd_cut)], [], height * ch, one, two, after=after)

        def added(one, two):
            return call(add_kernel, [bf16(half, ch)], [], half * ch, one, two)

        quarters = [f32(half, ch), bf16(half + cols, ch)] + [bf16(half, ch)] * 2
        own_one, *sends = call(
            pair_quarter_kernel, quarters, [], height * ch, keep_one, pair_one
        )
        keep_two, send_two = call(
            odd_band_kernel,
            outs,
            [],
            2 * height * ch,
            own_two,
            across_two,
            after=sends[2:],
        )
        across = flipped(sends[0], "section", 2)
        parts = [across, flipped(sends[1], "video", 1), flipped_both(sends[2])]
        sum_one = call(plane_kernel, [bf16(half, ch)], [], 4 * half * ch, own_one, *parts)
        sum_two = odd_added(keep_two, flipped_odd(send_two, "video", 1), (sum_one,))
        part_two = flipped_odd(sum_two, "dp", 1)
        part_one = flipped(sum_one, "dp", 1)
        sum_one = added(sum_one, part_one)
        sum_two = odd_added(sum_two, part_two, (sum_one,))
        last_two = flipped_odd(sum_two, "dp", 2)
        last_one = flipped(sum_one, "dp", 2)
        grad_in, token = input_gradient(across, (sum_one,))
        own_two, given_two = call(
            functools.partial(odd_scaled_kernel, factor),
            [bf16(half, ch)] * 2,
            [],
            height * ch,
            sum_two,
            last_two,
        )
        own = call(
            functools.partial(scaled_kernel, factor),
            [bf16(2, half, ch)],
            [],
            height * ch,
            sum_one,
            last_one,
            own_two,
            flipped(given_two, "section", 1),
            after=(token,),
        )
        shares = [own, flipped(own, "video", 1)]
        sums = placed(shares, [flipped(own, "section", 2), flipped_both(own)])
    else:
        own_one, send_one = call(
            pair_kernel, [f32(height, ch), bf16(height, ch)], [], height * ch, keep_one, pair_one
        )
        edge = flipped(pair_one[pair_one.shape[0] - cols :], "section", 2)
        grad_in, _ = input_gradient(edge, ())
        own_one = own_one + flipped(send_one, "section", 2).astype(jnp.float32)
        own_two = own_two + across_two.astype(jnp.float32)
        given_two = flipped(own_two[:height].astype(jnp.bfloat16), "section", 1)
        own_two = jnp.where(is_odd(), own_two[height:], given_two.astype(jnp.float32))
        share = lax.psum(jnp.stack((own_one, own_two)), ("video", "dp")) * factor
        share = share.astype(jnp.bfloat16)
        sums = placed([share], [flipped(share, "section", 2)])
    return (grad_in.reshape(shape), *sums)


def solution(mesh):
    whole = P("dp", "video", "section", None, None)
    return jax.shard_map(
        on_device,
        mesh=mesh,
        in_specs=(whole,) * 5 + (P(),) * 4,
        out_specs=(whole, P(), P(), P(), P()),
        check_vma=False,
    )
```

```python
import functools
import math

import jax
import jax.numpy as jnp
from jax import lax
from jax.experimental import pallas as pl
from jax.experimental.pallas import tpu as pltpu
from jax.sharding import PartitionSpec as P

MIB = 1024 * 1024


def sigmoid(value):
    return 1.0 / (1.0 + jnp.exp(-value))


def bf16(*shape):
    return jax.ShapeDtypeStruct(shape, jnp.bfloat16)


def f32(*shape):
    return jax.ShapeDtypeStruct(shape, jnp.float32)


def call(kernel, outs, scratch, flops, *operands, after=(), early=(), spare_inputs=False, limit=24):
    single = len(outs) == 1
    moved = sum(math.prod(x.shape) * x.dtype.itemsize for x in (*operands, *outs))
    vmem = pl.BlockSpec(memory_space=pltpu.VMEM)
    spare = pl.BlockSpec(memory_space=pl.ANY)
    spec = spare if spare_inputs else vmem
    count = len(operands)
    operands = (*operands, *early, *after)

    def body(*refs):
        kernel(*refs[:count], *refs[len(operands) :])

    return pl.pallas_call(
        body,
        out_shape=outs[0] if single else tuple(outs),
        in_specs=[spec] * count + [vmem] * len(early) + [spare] * len(after),
        out_specs=vmem if single else (vmem,) * len(outs),
        scratch_shapes=scratch,
        compiler_params=pltpu.CompilerParams(vmem_limit_bytes=limit * MIB),
        cost_estimate=pl.CostEstimate(
            flops=int(flops), bytes_accessed=int(moved), transcendentals=0
        ),
    )(*operands)


def from_ahead(block, band_step, frame_step):
    bands, frames = lax.axis_size("section"), lax.axis_size("video")
    pairs = [
        ((band + band_step) * frames + frame + frame_step, band * frames + frame)
        for band in range(bands)
        for frame in range(frames)
        if 0 <= band + band_step < bands and frame + frame_step < frames
    ]
    return lax.ppermute(block, ("section", "video"), pairs)


def beside_band(pair_refs, row):
    band = lax.axis_index("section")
    odd = lax.rem(band, 2) == 1
    inside = (band > 0) & (band < lax.axis_size("section") - 1)
    first, second = (ref[row : row + 1] for ref in pair_refs)
    second = jnp.where(inside, second, jnp.zeros_like(second))
    return jnp.where(odd, first, second), jnp.where(odd, second, first)


def flipped(block, axis, flip):
    count = lax.axis_size(axis)
    return lax.ppermute(block, axis, [(place ^ flip, place) for place in range(count)])


def flipped_both(block):
    bands = lax.axis_size("section")
    pairs = [
        (2 * (band ^ 2) + 1 - frame, 2 * band + frame) for band in range(bands) for frame in range(2)
    ]
    return lax.ppermute(block, ("section", "video"), pairs)


def later_than(block, *others):
    return lax.optimization_barrier((block, *others))[0]


def beside(gpre, views_ref, start):
    count, cols, ch = gpre.shape
    at = lax.broadcasted_iota(jnp.int32, gpre.shape, 1)
    right = jnp.where(at == cols - 1, 0.0, pltpu.roll(gpre, cols - 1, 1))
    left = jnp.where(at == 0, 0.0, pltpu.roll(gpre, 1, 1))
    here = pl.ds(start, count)
    views_ref[here, :, 0:ch] = right.astype(jnp.bfloat16)
    views_ref[here, :, ch : 2 * ch] = gpre.astype(jnp.bfloat16)
    views_ref[here, :, 2 * ch : 3 * ch] = left.astype(jnp.bfloat16)


def pre_gradient(grads, preact, temporal_ref):
    count, cols, ch = preact.shape
    flat = jnp.concatenate([grad.reshape(count * cols, ch) for grad in grads], axis=1)
    kernel = jnp.concatenate([temporal_ref[2 - step] for step in range(len(grads))], axis=1)
    gact = lax.dot_general(
        flat, kernel, (((1,), (1,)), ((), ())), preferred_element_type=jnp.float32
    )
    gact = gact.astype(jnp.bfloat16).astype(jnp.float32).reshape(preact.shape)
    hval = preact.astype(jnp.float32)
    sig = sigmoid(hval)
    return gact * sig * (1.0 + hval * (1.0 - sig))


def convolved(views_ref, spatial_ref, start, first):
    count, cols, ch = first.shape
    total = first.astype(jnp.float32).reshape(count * cols, ch)
    for ky in range(3):
        view = views_ref[pl.ds(start + 2 - ky, count)].reshape(count * cols, 3 * ch)
        kernel = jnp.concatenate([spatial_ref[ky, kx] for kx in range(3)], axis=1)
        total = total + lax.dot_general(
            view, kernel, (((1,), (1,)), ((), ())), preferred_element_type=jnp.float32
        )
    return total.astype(jnp.bfloat16).reshape(first.shape)


def is_last():
    return lax.axis_index("video") == lax.axis_size("video") - 1


def left_sides(saved_ref, preact_ref, above, below, sides_ref):
    rows, cols, ch = saved_ref.shape
    flat = (rows * cols, ch)
    shifts = [
        jnp.concatenate([above, saved_ref[: rows - 1]], axis=0),
        saved_ref[...],
        jnp.concatenate([saved_ref[1:], below], axis=0),
    ]
    for n, shift in enumerate(shifts):
        sides_ref[n] = shift.reshape(flat).T
    hval = preact_ref[...].astype(jnp.float32)
    sides_ref[3] = (hval * sigmoid(hval)).astype(jnp.bfloat16).reshape(flat).T


def kernel_sums(sides_ref, grads, views, sums_ref):
    _, ch, pixels = sides_ref.shape
    shifts = sides_ref[0:3].reshape(3 * ch, pixels)
    sums = jnp.dot(shifts, views, preferred_element_type=jnp.float32)
    for ky in range(3):
        for kx in range(3):
            here = slice(kx * ch, (kx + 1) * ch)
            sums_ref[ky, here] = sums[ky * ch : (ky + 1) * ch, here]
    grads = jnp.concatenate([grad.reshape(pixels, ch) for grad in grads], axis=1)
    sums = jnp.dot(sides_ref[3], grads, preferred_element_type=jnp.float32)
    zeros = jnp.zeros((ch, ch), jnp.float32)
    for k in range(3):
        step = 2 - k
        value = sums[:, step * ch : (step + 1) * ch] if step * ch < grads.shape[1] else zeros
        sums_ref[3, k * ch : (k + 1) * ch] = jnp.where(is_last(), zeros, value) if step else value


def hand_out(sums_ref, keep_ref, *send_refs):
    odd = lax.rem(lax.axis_index("section"), 2)
    for n, send_ref in enumerate(send_refs):
        keep_ref[n] = sums_ref[2 * n + odd]
        send_ref[...] = sums_ref[2 * n + 1 - odd].astype(jnp.bfloat16)


def pack_kernel(*refs):
    parts, outs, sems = refs[:4], refs[4:6], refs[6]
    last = parts[0].shape[0] - 1
    odd = lax.rem(lax.axis_index("section"), 2)
    copies = []
    for n, part in enumerate(parts):
        for out, row in zip(outs, ((1 - odd) * last, odd * last)):
            sem = sems.at[len(copies)]
            copies.append(
                pltpu.make_async_copy(part.at[pl.ds(row, 1)], out.at[pl.ds(n, 1)], sem)
            )
    for copy in copies:
        copy.start()
    for copy in copies:
        copy.wait()


def interior(grad_ref, preact_ref, wholes, temporal_ref, spatial_ref, inner_ref, gpre_ref, views_ref):
    rows, cols, ch = grad_ref.shape
    step = 4

    for n in range(rows // step):
        here = pl.ds(n * step, step)
        grads = [ref[here] for ref in (grad_ref, *wholes)]
        gpre = pre_gradient(grads, preact_ref[here], temporal_ref)
        gpre_ref[here] = gpre.astype(jnp.bfloat16)
        beside(gpre, views_ref, n * step)

    half = rows // 2 - 1

    for n in range(2):
        first = grad_ref[pl.ds(n * half + 1, half)]
        inner_ref[pl.ds(n * half, half)] = convolved(views_ref, spatial_ref, n * half, first)


def edge_rows(grad_ref, pair_refs, afters, gpre_ref, temporal_ref, spatial_ref, views_ref):
    rows, cols, ch = grad_ref.shape
    (grad_above, grad_below), (above_pre, below_pre) = (beside_band(pair_refs, n) for n in (0, 1))
    above = [grad_above] + [ref[0:1] for ref in afters]
    below = [grad_below] + [ref[1:2] for ref in afters]
    beside(pre_gradient(above, above_pre, temporal_ref), views_ref, 0)
    beside(gpre_ref[0:2].astype(jnp.float32), views_ref, 1)
    beside(gpre_ref[rows - 2 : rows].astype(jnp.float32), views_ref, 3)
    beside(pre_gradient(below, below_pre, temporal_ref), views_ref, 5)
    return (
        convolved(views_ref, spatial_ref, 0, grad_ref[0:1]),
        convolved(views_ref, spatial_ref, 3, grad_ref[rows - 1 : rows]),
    )


def last_inner_kernel(grad_ref, preact_ref, temporal_ref, spatial_ref, inner_ref, gpre_ref, views_ref):
    @pl.when(is_last())
    def _():
        interior(
            grad_ref, preact_ref, [], temporal_ref, spatial_ref, inner_ref, gpre_ref, views_ref
        )


def last_edge_kernel(grad_ref, one_ref, two_ref, gpre_ref, temporal_ref, spatial_ref, edge_ref, views_ref):
    @pl.when(is_last())
    def _():
        pair_refs = (one_ref, two_ref)
        edge_ref[0:1], edge_ref[1:2] = edge_rows(
            grad_ref, pair_refs, [], gpre_ref, temporal_ref, spatial_ref, views_ref
        )
        edge_ref[2:3], edge_ref[3:4] = beside_band(pair_refs, 0)


def inner_kernel(later, *refs):
    inputs, wholes, kernels = refs[:2], refs[2 : 2 + later], refs[2 + later : 4 + later]
    known, outs = refs[4 + later : -3], refs[-3:]
    if not known:
        interior(*inputs, wholes, *kernels, *outs)
        return

    @pl.when(is_last())
    def _():
        outs[0][...] = known[0][...]
        outs[1][...] = known[1][...]

    @pl.when(jnp.logical_not(is_last()))
    def _():
        interior(*inputs, wholes, *kernels, *outs)


def mid_kernel(later, *refs):
    grad_ref, inner_ref, gpre_ref = refs[0], refs[3], refs[4]
    afters, (temporal_ref, spatial_ref, mid_ref, views_ref) = refs[5 : 5 + later], refs[5 + later :]
    rows = grad_ref.shape[0]
    first, last = edge_rows(
        grad_ref, refs[1:3], afters, gpre_ref, temporal_ref, spatial_ref, views_ref
    )
    mid_ref[0:1], mid_ref[rows - 1 : rows] = first, last
    mid_ref[1 : rows - 1] = inner_ref[...]


def two_kernel(later, *refs):
    saved_ref, preact_ref, gpre_ref = refs[:3]
    pair_refs, grad_ref = refs[3:5], refs[5]
    wholes, outs = refs[6 : 6 + later], refs[6 + later : 9 + later]
    views_ref, sides_ref, sums_ref = refs[9 + later :]
    rows, cols, ch = saved_ref.shape
    step = 4

    for n in range(rows // step):
        here = pl.ds(n * step, step)
        beside(gpre_ref[here].astype(jnp.float32), views_ref, n * step)

    views = views_ref[...].reshape(rows * cols, 3 * ch)
    grads = [ref[...] for ref in (grad_ref, *wholes)]
    left_sides(saved_ref, preact_ref, *beside_band(pair_refs, 2), sides_ref)
    kernel_sums(sides_ref, grads, views, sums_ref)
    hand_out(sums_ref, *outs)


def sides_kernel(saved_ref, preact_ref, one_ref, two_ref, sides_ref):
    left_sides(saved_ref, preact_ref, *beside_band((one_ref, two_ref), 3), sides_ref)


def block_one(sides_ref, preact_ref, mids, temporal_ref, outs, scratch):
    gpre_ref, keep_ref, send_ref = outs
    views_ref, sums_ref = scratch
    rows, cols, ch = preact_ref.shape
    step = 4

    for n in range(rows // step):
        here = pl.ds(n * step, step)
        gpre = pre_gradient([ref[here] for ref in mids], preact_ref[here], temporal_ref)
        gpre_ref[here] = gpre.astype(jnp.bfloat16)
        beside(gpre, views_ref, n * step)

    odd = lax.rem(lax.axis_index("section"), 2)
    size = send_ref.shape[0] - 2 * cols
    send_ref[size : size + cols] = gpre_ref[(1 - odd) * (rows - 1)]
    send_ref[size + cols : size + 2 * cols] = gpre_ref[odd * (rows - 1)]
    views = views_ref[...].reshape(rows * cols, 3 * ch)
    kernel_sums(sides_ref, [ref[...] for ref in mids], views, sums_ref)
    height = sums_ref.shape[1]
    hand_out(sums_ref, keep_ref, send_ref.at[:height], send_ref.at[height : 2 * height])


def one_kernel(later, *refs):
    sides_ref, preact_ref, mids = refs[0], refs[1], refs[2 : 3 + later]
    temporal_ref, outs, scratch = refs[3 + later], refs[4 + later : 7 + later], refs[7 + later :]
    block_one(sides_ref, preact_ref, mids, temporal_ref, outs, scratch)


def mid_one_kernel(*refs):
    after_inner_ref, after_edge_ref = refs[5:7]
    temporal_two_ref, spatial_two_ref, sides_ref, preact_ref, temporal_ref = refs[7:12]
    mid_ref, outs, scratch = refs[12], refs[13:16], refs[16:18]
    next_ref, edge_ref, edge_views_ref = refs[18:]
    rows = next_ref.shape[0]

    @pl.when(is_last())
    def _():
        edge_ref[...] = jnp.zeros(edge_ref.shape, edge_ref.dtype)
        next_ref[...] = jnp.zeros(next_ref.shape, next_ref.dtype)

    @pl.when(jnp.logical_not(is_last()))
    def _():
        edge_ref[...] = after_edge_ref[2:4]
        next_ref[0:1] = after_edge_ref[0:1]
        next_ref[1 : rows - 1] = after_inner_ref[...]
        next_ref[rows - 1 : rows] = after_edge_ref[1:2]

    mid_kernel(
        1, *refs[:5], edge_ref, temporal_two_ref, spatial_two_ref, mid_ref, edge_views_ref
    )
    block_one(sides_ref, preact_ref, [mid_ref, next_ref], temporal_ref, outs, scratch)


def input_kernel(mid_ref, gpre_ref, pair_ref, across_ref, spatial_ref, out_ref, token_ref, views_ref):
    rows, cols, ch = out_ref.shape
    pair = pair_ref[pair_ref.shape[0] - 2 * cols : pair_ref.shape[0] - cols]
    above, below = beside_band((pair[None], across_ref[across_ref.shape[0] - cols :][None]), 0)
    token_ref[...] = jnp.zeros(token_ref.shape, token_ref.dtype)
    step = 4
    beside(above.astype(jnp.float32), views_ref, 0)
    beside(below.astype(jnp.float32), views_ref, rows + 1)

    for n in range(rows // step):
        gpre = gpre_ref[pl.ds(n * step, step)].astype(jnp.float32)
        beside(gpre, views_ref, n * step + 1)

    for n in range(rows // step):
        here = pl.ds(n * step, step)
        out_ref[here] = convolved(views_ref, spatial_ref, n * step, mid_ref[here])


def halves(count, index):
    return [pl.ds(pl.multiple_of(n * count, count), count) for n in (index, 1 - index)]


def pair_kernel(keep_ref, low_ref, high_ref, own_ref, send_ref):
    across = lax.axis_index("section") // 2
    parts = [ref[...].astype(jnp.float32) for ref in (low_ref, high_ref)]
    own_ref[...] = keep_ref[across] + jnp.where(across == 0, *parts)
    total = keep_ref[1 - across] + jnp.where(across == 0, *parts[::-1])
    send_ref[...] = total.astype(jnp.bfloat16)


def band_kernel(own_ref, part_ref, keep_ref, send_ref):
    mine, other = halves(keep_ref.shape[0], lax.axis_index("video"))
    keep_ref[...] = own_ref[mine] + part_ref[mine].astype(jnp.float32)
    send_ref[...] = (own_ref[other] + part_ref[other].astype(jnp.float32)).astype(jnp.bfloat16)


def pair_quarter_kernel(keep_ref, part_ref, own_ref, across_ref, frame_ref, both_ref):
    _, height, _ = keep_ref.shape
    half = own_ref.shape[0]
    band = lax.axis_index("section") // 2
    frames = halves(half, lax.axis_index("video"))

    def quarter(band, rows):
        start = pl.multiple_of(band * height, height)
        part = part_ref.at[pl.ds(start, height)][rows]
        return keep_ref[band, rows] + part.astype(jnp.float32)

    own_ref[...] = quarter(band, frames[0])
    across_ref[:half] = quarter(1 - band, frames[0]).astype(jnp.bfloat16)
    rest = across_ref.shape[0] - half
    across_ref[half:] = part_ref[2 * height + rest :]
    frame_ref[...] = quarter(band, frames[1]).astype(jnp.bfloat16)
    both_ref[...] = quarter(1 - band, frames[1]).astype(jnp.bfloat16)


def plane_kernel(own_ref, *refs):
    parts, out_ref = refs[:-1], refs[-1]
    total = own_ref[...]
    for part in parts:
        total = total + part[: out_ref.shape[0]].astype(jnp.float32)
    out_ref[...] = total.astype(jnp.bfloat16)


def add_kernel(one_ref, two_ref, out_ref):
    total = one_ref[...].astype(jnp.float32) + two_ref[...].astype(jnp.float32)
    out_ref[...] = total.astype(jnp.bfloat16)


def scaled_kernel(factor, *refs):
    out_ref = refs[-1]
    for block in range(2):
        one, two = (ref[...].astype(jnp.float32) for ref in refs[2 * block : 2 * block + 2])
        out_ref[block] = ((one + two) * factor).astype(jnp.bfloat16)


def place_kernel(*refs):
    shares, outs = refs[:-4], refs[-4:]
    band, frame = lax.axis_index("section"), lax.axis_index("video")
    halves = len(shares) // 4
    height = shares[0].shape[1]
    for n, share in enumerate(shares):
        place = jnp.bitwise_xor(band, n // halves)
        half = jnp.bitwise_xor(frame, n % halves) if halves == 2 else 0
        here = pl.ds(pl.multiple_of(half * height, height), height)

        @pl.when(place < 3)
        def _():
            for block in range(2):
                outs[2 * block][place, here] = share[block].astype(jnp.float32)

        @pl.when(place == 3)
        def _():
            for block in range(2):
                outs[2 * block + 1][here] = share[block].astype(jnp.float32)


def placed(shares, across):
    ch = shares[0].shape[2]
    outs = call(
        place_kernel,
        [f32(3, 3 * ch, ch), f32(3 * ch, ch)] * 2,
        [],
        12 * ch * ch,
        *shares,
        *[flipped(share, "section", 1) for share in shares],
        *across,
        *[flipped(share, "section", 1) for share in across],
    )
    return [x.reshape(3, 3, ch, ch) if x.ndim == 3 else x.reshape(3, ch, ch) for x in outs]


def on_device(
    grad_latent,
    input_one,
    preact_one,
    input_two,
    preact_two,
    spatial_one,
    temporal_one,
    spatial_two,
    temporal_two,
):
    shape = grad_latent.shape
    rows, cols, ch = shape[2:]
    bands, frames = lax.axis_size("section"), lax.axis_size("video")
    later = min(2, frames - 1)
    pixels = lax.axis_size("dp") * frames * bands * rows * cols
    factor = 1.0 / math.sqrt(pixels)
    grad, saved_one, pre_one, saved_two, pre_two = (
        x.reshape(rows, cols, ch)
        for x in (grad_latent, input_one, preact_one, input_two, preact_two)
    )
    conv = 2 * rows * cols * 9 * ch * ch
    views = pltpu.VMEM((rows, cols, 3 * ch), jnp.bfloat16)
    edge_views = pltpu.VMEM((6, cols, 3 * ch), jnp.bfloat16)
    act = pltpu.VMEM((rows, cols, ch), jnp.bfloat16)
    sides = bf16(4, ch, rows * cols)
    sums = pltpu.VMEM((4, 3 * ch, ch), jnp.float32)
    handed = [f32(2, 3 * ch, ch)] + [bf16(3 * ch, ch)] * 2
    inner_outs = [bf16(rows - 2, cols, ch), bf16(rows, cols, ch)]
    kernels = (temporal_two, spatial_two)

    def from_later(x):
        if frames == 2:
            return [flipped(x, "video", 1)]
        return [from_ahead(x, 0, n + 1) for n in range(later)]

    wholes = from_later(grad)
    packs = call(
        pack_kernel,
        [bf16(4, cols, ch)] * 2,
        [pltpu.SemaphoreType.DMA((8,))],
        1,
        grad,
        pre_two,
        saved_two,
        saved_one,
        spare_inputs=True,
        limit=58,
    )
    first, second = (flipped(pack, "section", 1) for pack in packs)
    pairs = [first, flipped(second, "section", 2)]

    known = ()
    if frames == 2:
        known = call(
            last_inner_kernel,
            inner_outs,
            [views],
            0.1 * conv,
            grad,
            pre_two,
            *kernels,
            after=(first, second),
        )
        afters = from_later(known[0])
    else:
        afters = from_later(jnp.concatenate(beside_band(pairs, 0)))
    inner, gpre_two = call(
        functools.partial(inner_kernel, later),
        inner_outs,
        [views],
        0.1 * conv,
        grad,
        pre_two,
        *wholes,
        *kernels,
        *known,
        early=(saved_two, saved_one, pre_one, temporal_one),
    )
    if frames == 2:
        edge = call(
            last_edge_kernel,
            [bf16(4, cols, ch)],
            [edge_views],
            conv // 8,
            grad,
            *pairs,
            known[1],
            *kernels,
            after=(gpre_two,),
        )
        afters += from_later(edge)
    parts_two = call(
        functools.partial(two_kernel, later),
        handed,
        [views, pltpu.VMEM(sides.shape, sides.dtype), sums],
        1.2 * conv,
        saved_two,
        pre_two,
        gpre_two,
        *pairs,
        grad,
        *wholes,
        after=(edge,) if frames == 2 else (),
    )
    sides_one = call(
        sides_kernel, [sides], [], conv // 8, saved_one, pre_one, *pairs, after=parts_two[:1]
    )
    height, half = 3 * ch, 3 * ch // 2
    keep_two, low_two, high_two = parts_two
    own_two, send_two = call(
        pair_kernel,
        [f32(height, ch), bf16(height, ch)],
        [],
        height * ch,
        keep_two,
        flipped(low_two, "section", 1),
        flipped(high_two, "section", 1),
    )
    across_two = flipped(send_two, "section", 2)
    mid_inputs = (grad, *pairs, inner, gpre_two)
    one_inputs = (sides_one, pre_one)
    mid_outs = [bf16(rows, cols, ch)]
    one_outs = [bf16(rows, cols, ch), f32(2, 3 * ch, ch), bf16(6 * ch + 2 * cols, ch)]
    if frames == 2:
        mid, gpre_one, *parts_one = call(
            mid_one_kernel,
            mid_outs + one_outs,
            [views, sums, act, pltpu.VMEM((2, cols, ch), jnp.bfloat16), edge_views],
            8 * conv,
            *mid_inputs,
            *afters,
            *kernels,
            *one_inputs,
            temporal_one,
            after=(own_two,),
        )
    else:
        mid = call(
            functools.partial(mid_kernel, later),
            mid_outs,
            [edge_views],
            conv // 8,
            *mid_inputs,
            *afters,
            *kernels,
        )
        gpre_one, *parts_one = call(
            functools.partial(one_kernel, later),
            one_outs,
            [views, sums],
            1.2 * conv,
            *one_inputs,
            mid,
            *from_later(mid),
            temporal_one,
        )
    keep_one, send_one = parts_one
    split = frames == 2 and lax.axis_size("dp") == 4
    if split:
        send_one = later_than(send_one, across_two)
    pair_one = flipped(send_one, "section", 1)

    def input_gradient(edge, after):
        return call(
            input_kernel,
            [bf16(rows, cols, ch), f32(8, 128)],
            [pltpu.VMEM((rows + 2, cols, 3 * ch), jnp.bfloat16)],
            conv,
            mid,
            gpre_one,
            pair_one,
            edge,
            spatial_one,
            after=after,
        )

    if split:

        def added(one, two):
            return call(add_kernel, [bf16(half, ch)], [], half * ch, one, two)

        keep_two, send_two = call(
            band_kernel,
            [f32(half, ch), bf16(half, ch)],
            [],
            height * ch,
            own_two,
            across_two,
        )
        sum_two = added(keep_two, flipped(send_two, "video", 1))
        quarters = [f32(half, ch), bf16(half + cols, ch)] + [bf16(half, ch)] * 2
        own_one, *sends = call(
            pair_quarter_kernel, quarters, [], height * ch, keep_one, pair_one, after=(send_two,)
        )
        across = flipped(sends[0], "section", 2)
        parts = [across, flipped(sends[1], "video", 1), flipped_both(sends[2])]
        sum_one = call(plane_kernel, [bf16(half, ch)], [], 4 * half * ch, own_one, *parts)
        part_two = flipped(sum_two, "dp", 1)
        part_one = flipped(later_than(sum_one, sum_two), "dp", 1)
        sum_two = added(sum_two, part_two)
        sum_one = added(sum_one, part_one)
        last_two = flipped(sum_two, "dp", 2)
        last_one = flipped(later_than(sum_one, sum_two), "dp", 2)
        grad_in, token = input_gradient(across, (sum_one,))
        own = call(
            functools.partial(scaled_kernel, factor),
            [bf16(2, half, ch)],
            [],
            height * ch,
            sum_one,
            last_one,
            sum_two,
            last_two,
            after=(token,),
        )
        shares = [own, flipped(own, "video", 1)]
        sums = placed(shares, [flipped(own, "section", 2), flipped_both(own)])
    else:
        own_one, send_one = call(
            pair_kernel,
            [f32(height, ch), bf16(height, ch)],
            [],
            height * ch,
            keep_one,
            pair_one[:height],
            pair_one[height : 2 * height],
        )
        edge = flipped(pair_one[pair_one.shape[0] - cols :], "section", 2)
        grad_in, _ = input_gradient(edge, ())
        own_one = own_one + flipped(send_one, "section", 2).astype(jnp.float32)
        own_two = own_two + across_two.astype(jnp.float32)
        share = lax.psum(jnp.stack((own_one, own_two)), ("video", "dp")) * factor
        share = share.astype(jnp.bfloat16)
        sums = placed([share], [flipped(share, "section", 2)])
    return (grad_in.reshape(shape), *sums)


def solution(mesh):
    whole = P("dp", "video", "section", None, None)
    return jax.shard_map(
        on_device,
        mesh=mesh,
        in_specs=(whole,) * 5 + (P(),) * 4,
        out_specs=(whole, P(), P(), P(), P()),
        check_vma=False,
    )
```

```python
import functools
import math

import jax
import jax.numpy as jnp
from jax import lax
from jax.experimental import pallas as pl
from jax.experimental.pallas import tpu as pltpu
from jax.sharding import PartitionSpec as P

MIB = 1024 * 1024


def sigmoid(value):
    return 1.0 / (1.0 + jnp.exp(-value))


def bf16(*shape):
    return jax.ShapeDtypeStruct(shape, jnp.bfloat16)


def f32(*shape):
    return jax.ShapeDtypeStruct(shape, jnp.float32)


def call(kernel, outs, scratch, flops, *operands, after=(), early=(), spare_inputs=False, limit=24):
    single = len(outs) == 1
    moved = sum(math.prod(x.shape) * x.dtype.itemsize for x in (*operands, *outs))
    vmem = pl.BlockSpec(memory_space=pltpu.VMEM)
    spare = pl.BlockSpec(memory_space=pl.ANY)
    spec = spare if spare_inputs else vmem
    count = len(operands)
    operands = (*operands, *early, *after)

    def body(*refs):
        kernel(*refs[:count], *refs[len(operands) :])

    return pl.pallas_call(
        body,
        out_shape=outs[0] if single else tuple(outs),
        in_specs=[spec] * count + [vmem] * len(early) + [spare] * len(after),
        out_specs=vmem if single else (vmem,) * len(outs),
        scratch_shapes=scratch,
        compiler_params=pltpu.CompilerParams(vmem_limit_bytes=limit * MIB),
        cost_estimate=pl.CostEstimate(
            flops=int(flops), bytes_accessed=int(moved) if flops else 0, transcendentals=0
        ),
    )(*operands)


def from_ahead(block, band_step, frame_step):
    bands, frames = lax.axis_size("section"), lax.axis_size("video")
    pairs = [
        ((band + band_step) * frames + frame + frame_step, band * frames + frame)
        for band in range(bands)
        for frame in range(frames)
        if 0 <= band + band_step < bands and frame + frame_step < frames
    ]
    return lax.ppermute(block, ("section", "video"), pairs)


def beside_band(pair_refs, row):
    band = lax.axis_index("section")
    odd = lax.rem(band, 2) == 1
    inside = (band > 0) & (band < lax.axis_size("section") - 1)
    first, second = (ref[row : row + 1] for ref in pair_refs)
    second = jnp.where(inside, second, jnp.zeros_like(second))
    return jnp.where(odd, first, second), jnp.where(odd, second, first)


def flipped(block, axis, flip):
    count = lax.axis_size(axis)
    return lax.ppermute(block, axis, [(place ^ flip, place) for place in range(count)])


def flipped_both(block):
    bands = lax.axis_size("section")
    pairs = [
        (2 * (band ^ 2) + 1 - frame, 2 * band + frame) for band in range(bands) for frame in range(2)
    ]
    return lax.ppermute(block, ("section", "video"), pairs)


def later_than(block, *others):
    return lax.optimization_barrier((block, *others))[0]


def beside(gpre, views_ref, start):
    count, cols, ch = gpre.shape
    at = lax.broadcasted_iota(jnp.int32, gpre.shape, 1)
    right = jnp.where(at == cols - 1, 0.0, pltpu.roll(gpre, cols - 1, 1))
    left = jnp.where(at == 0, 0.0, pltpu.roll(gpre, 1, 1))
    here = pl.ds(start, count)
    views_ref[here, :, 0:ch] = right.astype(jnp.bfloat16)
    views_ref[here, :, ch : 2 * ch] = gpre.astype(jnp.bfloat16)
    views_ref[here, :, 2 * ch : 3 * ch] = left.astype(jnp.bfloat16)


def pre_gradient(grads, preact, temporal_ref):
    count, cols, ch = preact.shape
    flat = jnp.concatenate([grad.reshape(count * cols, ch) for grad in grads], axis=1)
    kernel = jnp.concatenate([temporal_ref[2 - step] for step in range(len(grads))], axis=1)
    gact = lax.dot_general(
        flat, kernel, (((1,), (1,)), ((), ())), preferred_element_type=jnp.float32
    )
    gact = gact.astype(jnp.bfloat16).astype(jnp.float32).reshape(preact.shape)
    hval = preact.astype(jnp.float32)
    sig = sigmoid(hval)
    return gact * sig * (1.0 + hval * (1.0 - sig))


def convolved(views_ref, spatial_ref, start, first):
    count, cols, ch = first.shape
    total = first.astype(jnp.float32).reshape(count * cols, ch)
    for ky in range(3):
        view = views_ref[pl.ds(start + 2 - ky, count)].reshape(count * cols, 3 * ch)
        kernel = jnp.concatenate([spatial_ref[ky, kx] for kx in range(3)], axis=1)
        total = total + lax.dot_general(
            view, kernel, (((1,), (1,)), ((), ())), preferred_element_type=jnp.float32
        )
    return total.astype(jnp.bfloat16).reshape(first.shape)


def is_last():
    return lax.axis_index("video") == lax.axis_size("video") - 1


def left_sides(saved_ref, preact_ref, above, below, sides_ref):
    rows, cols, ch = saved_ref.shape
    flat = (rows * cols, ch)
    shifts = [
        jnp.concatenate([above, saved_ref[: rows - 1]], axis=0),
        saved_ref[...],
        jnp.concatenate([saved_ref[1:], below], axis=0),
    ]
    for n, shift in enumerate(shifts):
        sides_ref[n] = shift.reshape(flat).T
    hval = preact_ref[...].astype(jnp.float32)
    sides_ref[3] = (hval * sigmoid(hval)).astype(jnp.bfloat16).reshape(flat).T


def kernel_sums(sides_ref, grads, views, sums_ref):
    _, ch, pixels = sides_ref.shape
    shifts = sides_ref[0:3].reshape(3 * ch, pixels)
    sums = jnp.dot(shifts, views, preferred_element_type=jnp.float32)
    for ky in range(3):
        for kx in range(3):
            here = slice(kx * ch, (kx + 1) * ch)
            sums_ref[ky, here] = sums[ky * ch : (ky + 1) * ch, here]
    grads = jnp.concatenate([grad.reshape(pixels, ch) for grad in grads], axis=1)
    sums = jnp.dot(sides_ref[3], grads, preferred_element_type=jnp.float32)
    zeros = jnp.zeros((ch, ch), jnp.float32)
    for k in range(3):
        step = 2 - k
        value = sums[:, step * ch : (step + 1) * ch] if step * ch < grads.shape[1] else zeros
        sums_ref[3, k * ch : (k + 1) * ch] = jnp.where(is_last(), zeros, value) if step else value


def hand_out(sums_ref, keep_ref, *send_refs):
    odd = lax.rem(lax.axis_index("section"), 2)
    for n, send_ref in enumerate(send_refs):
        keep_ref[n] = sums_ref[2 * n + odd]
        send_ref[...] = sums_ref[2 * n + 1 - odd].astype(jnp.bfloat16)


def pack_kernel(*refs):
    parts, outs, sems = refs[:4], refs[4:6], refs[6]
    last = parts[0].shape[0] - 1
    odd = lax.rem(lax.axis_index("section"), 2)
    copies = []
    for n, part in enumerate(parts):
        for out, row in zip(outs, ((1 - odd) * last, odd * last)):
            sem = sems.at[len(copies)]
            copies.append(
                pltpu.make_async_copy(part.at[pl.ds(row, 1)], out.at[pl.ds(n, 1)], sem)
            )
    for copy in copies:
        copy.start()
    for copy in copies:
        copy.wait()


def interior(grad_ref, preact_ref, wholes, temporal_ref, spatial_ref, inner_ref, gpre_ref, views_ref):
    rows, cols, ch = grad_ref.shape
    step = 4

    for n in range(rows // step):
        here = pl.ds(n * step, step)
        grads = [ref[here] for ref in (grad_ref, *wholes)]
        gpre = pre_gradient(grads, preact_ref[here], temporal_ref)
        gpre_ref[here] = gpre.astype(jnp.bfloat16)
        beside(gpre, views_ref, n * step)

    half = rows // 2 - 1

    for n in range(2):
        first = grad_ref[pl.ds(n * half + 1, half)]
        inner_ref[pl.ds(n * half, half)] = convolved(views_ref, spatial_ref, n * half, first)


def edge_rows(grad_ref, pair_refs, afters, gpre_ref, temporal_ref, spatial_ref, views_ref):
    rows, cols, ch = grad_ref.shape
    (grad_above, grad_below), (above_pre, below_pre) = (beside_band(pair_refs, n) for n in (0, 1))
    above = [grad_above] + [ref[0:1] for ref in afters]
    below = [grad_below] + [ref[1:2] for ref in afters]
    beside(pre_gradient(above, above_pre, temporal_ref), views_ref, 0)
    beside(gpre_ref[0:2].astype(jnp.float32), views_ref, 1)
    beside(gpre_ref[rows - 2 : rows].astype(jnp.float32), views_ref, 3)
    beside(pre_gradient(below, below_pre, temporal_ref), views_ref, 5)
    return (
        convolved(views_ref, spatial_ref, 0, grad_ref[0:1]),
        convolved(views_ref, spatial_ref, 3, grad_ref[rows - 1 : rows]),
    )


def last_inner_kernel(grad_ref, preact_ref, temporal_ref, spatial_ref, inner_ref, gpre_ref, views_ref):
    @pl.when(is_last())
    def _():
        interior(
            grad_ref, preact_ref, [], temporal_ref, spatial_ref, inner_ref, gpre_ref, views_ref
        )


def last_edge_kernel(grad_ref, one_ref, two_ref, gpre_ref, temporal_ref, spatial_ref, edge_ref, views_ref):
    @pl.when(is_last())
    def _():
        pair_refs = (one_ref, two_ref)
        edge_ref[0:1], edge_ref[1:2] = edge_rows(
            grad_ref, pair_refs, [], gpre_ref, temporal_ref, spatial_ref, views_ref
        )
        edge_ref[2:3], edge_ref[3:4] = beside_band(pair_refs, 0)


def inner_kernel(later, *refs):
    inputs, wholes, kernels = refs[:2], refs[2 : 2 + later], refs[2 + later : 4 + later]
    known, outs = refs[4 + later : -3], refs[-3:]
    if not known:
        interior(*inputs, wholes, *kernels, *outs)
        return

    @pl.when(is_last())
    def _():
        outs[0][...] = known[0][...]
        outs[1][...] = known[1][...]

    @pl.when(jnp.logical_not(is_last()))
    def _():
        interior(*inputs, wholes, *kernels, *outs)


def mid_kernel(later, *refs):
    grad_ref, inner_ref, gpre_ref = refs[0], refs[3], refs[4]
    afters, (temporal_ref, spatial_ref, mid_ref, views_ref) = refs[5 : 5 + later], refs[5 + later :]
    rows = grad_ref.shape[0]
    first, last = edge_rows(
        grad_ref, refs[1:3], afters, gpre_ref, temporal_ref, spatial_ref, views_ref
    )
    mid_ref[0:1], mid_ref[rows - 1 : rows] = first, last
    mid_ref[1 : rows - 1] = inner_ref[...]


def two_kernel(later, *refs):
    saved_ref, preact_ref, gpre_ref = refs[:3]
    pair_refs, grad_ref = refs[3:5], refs[5]
    wholes, outs = refs[6 : 6 + later], refs[6 + later : 9 + later]
    views_ref, sides_ref, sums_ref = refs[9 + later :]
    rows, cols, ch = saved_ref.shape
    step = 4

    for n in range(rows // step):
        here = pl.ds(n * step, step)
        beside(gpre_ref[here].astype(jnp.float32), views_ref, n * step)

    views = views_ref[...].reshape(rows * cols, 3 * ch)
    grads = [ref[...] for ref in (grad_ref, *wholes)]
    left_sides(saved_ref, preact_ref, *beside_band(pair_refs, 2), sides_ref)
    kernel_sums(sides_ref, grads, views, sums_ref)
    hand_out(sums_ref, *outs)


def sides_kernel(saved_ref, preact_ref, one_ref, two_ref, sides_ref):
    left_sides(saved_ref, preact_ref, *beside_band((one_ref, two_ref), 3), sides_ref)


def block_one(sides_ref, preact_ref, mids, temporal_ref, outs, scratch):
    gpre_ref, keep_ref, send_ref = outs
    views_ref, sums_ref = scratch
    rows, cols, ch = preact_ref.shape
    step = 4

    for n in range(rows // step):
        here = pl.ds(n * step, step)
        gpre = pre_gradient([ref[here] for ref in mids], preact_ref[here], temporal_ref)
        gpre_ref[here] = gpre.astype(jnp.bfloat16)
        beside(gpre, views_ref, n * step)

    odd = lax.rem(lax.axis_index("section"), 2)
    size = send_ref.shape[0] - 2 * cols
    send_ref[size : size + cols] = gpre_ref[(1 - odd) * (rows - 1)]
    send_ref[size + cols : size + 2 * cols] = gpre_ref[odd * (rows - 1)]
    views = views_ref[...].reshape(rows * cols, 3 * ch)
    kernel_sums(sides_ref, [ref[...] for ref in mids], views, sums_ref)
    height = sums_ref.shape[1]
    hand_out(sums_ref, keep_ref, send_ref.at[:height], send_ref.at[height : 2 * height])


def one_kernel(later, *refs):
    sides_ref, preact_ref, mids = refs[0], refs[1], refs[2 : 3 + later]
    temporal_ref, outs, scratch = refs[3 + later], refs[4 + later : 7 + later], refs[7 + later :]
    block_one(sides_ref, preact_ref, mids, temporal_ref, outs, scratch)


def mid_one_kernel(*refs):
    after_inner_ref, after_edge_ref = refs[5:7]
    temporal_two_ref, spatial_two_ref, sides_ref, preact_ref, temporal_ref = refs[7:12]
    mid_ref, outs, scratch = refs[12], refs[13:16], refs[16:18]
    next_ref, edge_ref, edge_views_ref = refs[18:]
    rows = next_ref.shape[0]

    @pl.when(is_last())
    def _():
        edge_ref[...] = jnp.zeros(edge_ref.shape, edge_ref.dtype)
        next_ref[...] = jnp.zeros(next_ref.shape, next_ref.dtype)

    @pl.when(jnp.logical_not(is_last()))
    def _():
        edge_ref[...] = after_edge_ref[2:4]
        next_ref[0:1] = after_edge_ref[0:1]
        next_ref[1 : rows - 1] = after_inner_ref[...]
        next_ref[rows - 1 : rows] = after_edge_ref[1:2]

    mid_kernel(
        1, *refs[:5], edge_ref, temporal_two_ref, spatial_two_ref, mid_ref, edge_views_ref
    )
    block_one(sides_ref, preact_ref, [mid_ref, next_ref], temporal_ref, outs, scratch)


def input_kernel(mid_ref, gpre_ref, pair_ref, across_ref, spatial_ref, out_ref, token_ref, views_ref):
    rows, cols, ch = out_ref.shape
    pair = pair_ref[pair_ref.shape[0] - 2 * cols : pair_ref.shape[0] - cols]
    above, below = beside_band((pair[None], across_ref[across_ref.shape[0] - cols :][None]), 0)
    token_ref[...] = jnp.zeros(token_ref.shape, token_ref.dtype)
    step = 4
    beside(above.astype(jnp.float32), views_ref, 0)
    beside(below.astype(jnp.float32), views_ref, rows + 1)

    for n in range(rows // step):
        gpre = gpre_ref[pl.ds(n * step, step)].astype(jnp.float32)
        beside(gpre, views_ref, n * step + 1)

    for n in range(rows // step):
        here = pl.ds(n * step, step)
        out_ref[here] = convolved(views_ref, spatial_ref, n * step, mid_ref[here])


def halves(count, index):
    return [pl.ds(pl.multiple_of(n * count, count), count) for n in (index, 1 - index)]


def pair_kernel(keep_ref, low_ref, high_ref, own_ref, send_ref):
    across = lax.axis_index("section") // 2
    parts = [ref[...].astype(jnp.float32) for ref in (low_ref, high_ref)]
    own_ref[...] = keep_ref[across] + jnp.where(across == 0, *parts)
    total = keep_ref[1 - across] + jnp.where(across == 0, *parts[::-1])
    send_ref[...] = total.astype(jnp.bfloat16)


def band_kernel(own_ref, part_ref, keep_ref, send_ref):
    mine, other = halves(keep_ref.shape[0], lax.axis_index("video"))
    keep_ref[...] = own_ref[mine] + part_ref[mine].astype(jnp.float32)
    send_ref[...] = (own_ref[other] + part_ref[other].astype(jnp.float32)).astype(jnp.bfloat16)


def pair_quarter_kernel(keep_ref, part_ref, own_ref, across_ref, frame_ref, both_ref):
    _, height, _ = keep_ref.shape
    half = own_ref.shape[0]
    band = lax.axis_index("section") // 2
    frames = halves(half, lax.axis_index("video"))

    def quarter(band, rows):
        start = pl.multiple_of(band * height, height)
        part = part_ref.at[pl.ds(start, height)][rows]
        return keep_ref[band, rows] + part.astype(jnp.float32)

    own_ref[...] = quarter(band, frames[0])
    across_ref[:half] = quarter(1 - band, frames[0]).astype(jnp.bfloat16)
    rest = across_ref.shape[0] - half
    across_ref[half:] = part_ref[2 * height + rest :]
    frame_ref[...] = quarter(band, frames[1]).astype(jnp.bfloat16)
    both_ref[...] = quarter(1 - band, frames[1]).astype(jnp.bfloat16)


def plane_kernel(own_ref, *refs):
    parts, out_ref = refs[:-1], refs[-1]
    total = own_ref[...]
    for part in parts:
        total = total + part[: out_ref.shape[0]].astype(jnp.float32)
    out_ref[...] = total.astype(jnp.bfloat16)


def add_kernel(one_ref, two_ref, out_ref):
    total = one_ref[...].astype(jnp.float32) + two_ref[...].astype(jnp.float32)
    out_ref[...] = total.astype(jnp.bfloat16)


def scaled_kernel(factor, *refs):
    out_ref = refs[-1]
    for block in range(2):
        one, two = (ref[...].astype(jnp.float32) for ref in refs[2 * block : 2 * block + 2])
        out_ref[block] = ((one + two) * factor).astype(jnp.bfloat16)


def place_kernel(places, *refs):
    shares, outs = refs[: len(places)], refs[-6:-2]
    sums_ref, sems = refs[-2:]
    band, frame = lax.axis_index("section"), lax.axis_index("video")
    height = shares[0].shape[1]

    def copies(n, block):
        flip, other = places[n]
        place = jnp.bitwise_xor(band, flip)
        half = 0 if other is None else jnp.bitwise_xor(frame, int(other))
        here = pl.ds(pl.multiple_of(half * height, height), height)
        spatial, temporal = outs[2 * block : 2 * block + 2]
        source, sem = sums_ref.at[n, block], sems.at[n, block]
        return (
            (place < 3, lambda: pltpu.make_async_copy(source, spatial.at[place, here], sem)),
            (place == 3, lambda: pltpu.make_async_copy(source, temporal.at[here], sem)),
        )

    for n, share in enumerate(shares):
        for block in range(2):
            sums_ref[n, block] = share[block].astype(jnp.float32)
            for inside, copy in copies(n, block):
                pl.when(inside)(lambda: copy().start())
    for n in range(len(shares)):
        for block in range(2):
            for inside, copy in copies(n, block):
                pl.when(inside)(lambda: copy().wait())


def placed(shares, places, given=()):
    _, height, ch = shares[0].shape
    count = len(shares)
    outs = (f32(3, 3 * ch, ch), f32(3 * ch, ch)) * 2
    vmem, spare = (pl.BlockSpec(memory_space=space) for space in (pltpu.VMEM, pl.ANY))
    return pl.pallas_call(
        functools.partial(place_kernel, places),
        out_shape=outs,
        in_specs=[vmem] * count + [spare] * len(given),
        out_specs=(spare,) * 4,
        scratch_shapes=[
            pltpu.VMEM((count, 2, height, ch), jnp.float32),
            pltpu.SemaphoreType.DMA((count, 2)),
        ],
        input_output_aliases={count + n: n for n in range(len(given))},
        compiler_params=pltpu.CompilerParams(vmem_limit_bytes=24 * MIB),
        cost_estimate=pl.CostEstimate(
            flops=0, bytes_accessed=6 * count * height * ch * 2, transcendentals=0
        ),
    )(*shares, *given)


def unpacked(sums):
    ch = sums[0].shape[-1]
    return [x.reshape(3, 3, ch, ch) if x.ndim == 3 else x.reshape(3, ch, ch) for x in sums]


def on_device(
    grad_latent,
    input_one,
    preact_one,
    input_two,
    preact_two,
    spatial_one,
    temporal_one,
    spatial_two,
    temporal_two,
):
    shape = grad_latent.shape
    rows, cols, ch = shape[2:]
    bands, frames = lax.axis_size("section"), lax.axis_size("video")
    later = min(2, frames - 1)
    pixels = lax.axis_size("dp") * frames * bands * rows * cols
    factor = 1.0 / math.sqrt(pixels)
    grad, saved_one, pre_one, saved_two, pre_two = (
        x.reshape(rows, cols, ch)
        for x in (grad_latent, input_one, preact_one, input_two, preact_two)
    )
    conv = 2 * rows * cols * 9 * ch * ch
    views = pltpu.VMEM((rows, cols, 3 * ch), jnp.bfloat16)
    edge_views = pltpu.VMEM((6, cols, 3 * ch), jnp.bfloat16)
    act = pltpu.VMEM((rows, cols, ch), jnp.bfloat16)
    sides = bf16(4, ch, rows * cols)
    sums = pltpu.VMEM((4, 3 * ch, ch), jnp.float32)
    handed = [f32(2, 3 * ch, ch)] + [bf16(3 * ch, ch)] * 2
    inner_outs = [bf16(rows - 2, cols, ch), bf16(rows, cols, ch)]
    kernels = (temporal_two, spatial_two)

    def from_later(x):
        if frames == 2:
            return [flipped(x, "video", 1)]
        return [from_ahead(x, 0, n + 1) for n in range(later)]

    wholes = from_later(grad)
    packs = call(
        pack_kernel,
        [bf16(4, cols, ch)] * 2,
        [pltpu.SemaphoreType.DMA((8,))],
        1,
        grad,
        pre_two,
        saved_two,
        saved_one,
        spare_inputs=True,
        limit=58,
    )
    second = flipped(packs[1], "section", 1)
    first = flipped(later_than(packs[0], second), "section", 1)
    pairs = [first, flipped(second, "section", 2)]

    known = ()
    if frames == 2:
        known = call(
            last_inner_kernel,
            inner_outs,
            [views],
            0,
            grad,
            pre_two,
            *kernels,
            after=(first, second),
        )
        afters = from_later(known[0])
    else:
        afters = from_later(jnp.concatenate(beside_band(pairs, 0)))
    inner, gpre_two = call(
        functools.partial(inner_kernel, later),
        inner_outs,
        [views],
        0,
        grad,
        pre_two,
        *wholes,
        *kernels,
        *known,
        early=(saved_two, saved_one, pre_one, temporal_one),
    )
    if frames == 2:
        edge = call(
            last_edge_kernel,
            [bf16(4, cols, ch)],
            [edge_views],
            0,
            grad,
            *pairs,
            known[1],
            *kernels,
            after=(gpre_two,),
        )
        afters += from_later(edge)
    parts_two = call(
        functools.partial(two_kernel, later),
        handed,
        [views, pltpu.VMEM(sides.shape, sides.dtype), sums],
        8 * conv,
        saved_two,
        pre_two,
        gpre_two,
        *pairs,
        grad,
        *wholes,
        after=(edge,) if frames == 2 else (),
    )
    sides_one = call(
        sides_kernel, [sides], [], conv // 8, saved_one, pre_one, *pairs, after=parts_two[:1]
    )
    height, half = 3 * ch, 3 * ch // 2
    keep_two, low_two, high_two = parts_two
    own_two, send_two = call(
        pair_kernel,
        [f32(height, ch), bf16(height, ch)],
        [],
        height * ch,
        keep_two,
        flipped(low_two, "section", 1),
        flipped(high_two, "section", 1),
    )
    across_two = flipped(send_two, "section", 2)
    mid_inputs = (grad, *pairs, inner, gpre_two)
    one_inputs = (sides_one, pre_one)
    mid_outs = [bf16(rows, cols, ch)]
    one_outs = [bf16(rows, cols, ch), f32(2, 3 * ch, ch), bf16(6 * ch + 2 * cols, ch)]
    if frames == 2:
        mid, gpre_one, *parts_one = call(
            mid_one_kernel,
            mid_outs + one_outs,
            [views, sums, act, pltpu.VMEM((2, cols, ch), jnp.bfloat16), edge_views],
            8 * conv,
            *mid_inputs,
            *afters,
            *kernels,
            *one_inputs,
            temporal_one,
            after=(own_two,),
        )
    else:
        mid = call(
            functools.partial(mid_kernel, later),
            mid_outs,
            [edge_views],
            conv // 8,
            *mid_inputs,
            *afters,
            *kernels,
        )
        gpre_one, *parts_one = call(
            functools.partial(one_kernel, later),
            one_outs,
            [views, sums],
            1.2 * conv,
            *one_inputs,
            mid,
            *from_later(mid),
            temporal_one,
        )
    keep_one, send_one = parts_one
    split = frames == 2 and lax.axis_size("dp") == 4
    if split:
        send_one = later_than(send_one, across_two)
    pair_one = flipped(send_one, "section", 1)

    def input_gradient(edge, after):
        return call(
            input_kernel,
            [bf16(rows, cols, ch), f32(8, 128)],
            [pltpu.VMEM((rows + 2, cols, 3 * ch), jnp.bfloat16)],
            conv,
            mid,
            gpre_one,
            pair_one,
            edge,
            spatial_one,
            after=after,
        )

    if split:

        def added(one, two):
            return call(add_kernel, [bf16(half, ch)], [], half * ch, one, two)

        keep_two, send_two = call(
            band_kernel,
            [f32(half, ch), bf16(half, ch)],
            [],
            height * ch,
            own_two,
            across_two,
        )
        sum_two = added(keep_two, flipped(send_two, "video", 1))
        quarters = [f32(half, ch), bf16(half + cols, ch)] + [bf16(half, ch)] * 2
        own_one, *sends = call(
            pair_quarter_kernel, quarters, [], height * ch, keep_one, pair_one, after=(send_two,)
        )
        across = flipped(sends[0], "section", 2)
        parts = [across, flipped(sends[1], "video", 1), flipped_both(sends[2])]
        sum_one = call(plane_kernel, [bf16(half, ch)], [], 4 * half * ch, own_one, *parts)
        part_two = flipped(sum_two, "dp", 1)
        part_one = flipped(later_than(sum_one, sum_two), "dp", 1)
        sum_two = added(sum_two, part_two)
        sum_one = added(sum_one, part_one)
        last_two = flipped(sum_two, "dp", 2)
        last_one = flipped(later_than(sum_one, sum_two), "dp", 2)
        grad_in, token = input_gradient(across, (sum_one,))
        own = call(
            functools.partial(scaled_kernel, factor),
            [bf16(2, half, ch)],
            [],
            height * ch,
            sum_one,
            last_one,
            sum_two,
            last_two,
            after=(token,),
        )
        frame, across, both = flipped(own, "video", 1), flipped(own, "section", 2), flipped_both(own)
        shares = [own, frame, across]
        shares += [flipped(share, "section", 1) for share in shares]
        last = [both, flipped(both, "section", 1)]
        places = [(0, False), (0, True), (2, False), (1, False), (1, True), (3, False)]
        sums = placed(shares, places)
        sums = unpacked(placed(last, [(2, True), (3, True)], sums))
    else:
        own_one, send_one = call(
            pair_kernel,
            [f32(height, ch), bf16(height, ch)],
            [],
            height * ch,
            keep_one,
            pair_one[:height],
            pair_one[height : 2 * height],
        )
        edge = flipped(pair_one[pair_one.shape[0] - cols :], "section", 2)
        grad_in, _ = input_gradient(edge, ())
        own_one = own_one + flipped(send_one, "section", 2).astype(jnp.float32)
        own_two = own_two + across_two.astype(jnp.float32)
        share = lax.psum(jnp.stack((own_one, own_two)), ("video", "dp")) * factor
        share = share.astype(jnp.bfloat16)
        shares = [share, flipped(share, "section", 2)]
        shares += [flipped(share, "section", 1) for share in shares]
        sums = unpacked(placed(shares, [(0, None), (2, None), (1, None), (3, None)]))
    return (grad_in.reshape(shape), *sums)


def solution(mesh):
    whole = P("dp", "video", "section", None, None)
    return jax.shard_map(
        on_device,
        mesh=mesh,
        in_specs=(whole,) * 5 + (P(),) * 4,
        out_specs=(whole, P(), P(), P(), P()),
        check_vma=False,
    )
```

```python
import functools
import math

import jax
import jax.numpy as jnp
from jax import lax
from jax.experimental import pallas as pl
from jax.experimental.pallas import tpu as pltpu
from jax.sharding import PartitionSpec as P

MIB = 1024 * 1024


def sigmoid(value):
    return 1.0 / (1.0 + jnp.exp(-value))


def bf16(*shape):
    return jax.ShapeDtypeStruct(shape, jnp.bfloat16)


def f32(*shape):
    return jax.ShapeDtypeStruct(shape, jnp.float32)


def call(kernel, outs, scratch, flops, *operands, after=(), early=(), spare_inputs=False, limit=24):
    single = len(outs) == 1
    moved = sum(math.prod(x.shape) * x.dtype.itemsize for x in (*operands, *outs))
    vmem = pl.BlockSpec(memory_space=pltpu.VMEM)
    spare = pl.BlockSpec(memory_space=pl.ANY)
    spec = spare if spare_inputs else vmem
    count = len(operands)
    operands = (*operands, *early, *after)

    def body(*refs):
        kernel(*refs[:count], *refs[len(operands) :])

    return pl.pallas_call(
        body,
        out_shape=outs[0] if single else tuple(outs),
        in_specs=[spec] * count + [vmem] * len(early) + [spare] * len(after),
        out_specs=vmem if single else (vmem,) * len(outs),
        scratch_shapes=scratch,
        compiler_params=pltpu.CompilerParams(vmem_limit_bytes=limit * MIB),
        cost_estimate=pl.CostEstimate(
            flops=int(flops), bytes_accessed=int(moved) if flops else 0, transcendentals=0
        ),
    )(*operands)


def from_ahead(block, band_step, frame_step):
    bands, frames = lax.axis_size("section"), lax.axis_size("video")
    pairs = [
        ((band + band_step) * frames + frame + frame_step, band * frames + frame)
        for band in range(bands)
        for frame in range(frames)
        if 0 <= band + band_step < bands and frame + frame_step < frames
    ]
    return lax.ppermute(block, ("section", "video"), pairs)


def beside_band(pair_refs, row):
    band = lax.axis_index("section")
    odd = lax.rem(band, 2) == 1
    inside = (band > 0) & (band < lax.axis_size("section") - 1)
    first, second = (ref[row : row + 1] for ref in pair_refs)
    second = jnp.where(inside, second, jnp.zeros_like(second))
    return jnp.where(odd, first, second), jnp.where(odd, second, first)


def flipped(block, axis, flip):
    count = lax.axis_size(axis)
    return lax.ppermute(block, axis, [(place ^ flip, place) for place in range(count)])


def flipped_both(block):
    bands = lax.axis_size("section")
    pairs = [
        (2 * (band ^ 2) + 1 - frame, 2 * band + frame) for band in range(bands) for frame in range(2)
    ]
    return lax.ppermute(block, ("section", "video"), pairs)


def later_than(block, *others):
    return lax.optimization_barrier((block, *others))[0]


def beside(gpre, views_ref, start):
    count, cols, ch = gpre.shape
    at = lax.broadcasted_iota(jnp.int32, gpre.shape, 1)
    right = jnp.where(at == cols - 1, 0.0, pltpu.roll(gpre, cols - 1, 1))
    left = jnp.where(at == 0, 0.0, pltpu.roll(gpre, 1, 1))
    here = pl.ds(start, count)
    views_ref[here, :, 0:ch] = right.astype(jnp.bfloat16)
    views_ref[here, :, ch : 2 * ch] = gpre.astype(jnp.bfloat16)
    views_ref[here, :, 2 * ch : 3 * ch] = left.astype(jnp.bfloat16)


def pre_gradient(grads, preact, temporal_ref):
    count, cols, ch = preact.shape
    flat = jnp.concatenate([grad.reshape(count * cols, ch) for grad in grads], axis=1)
    kernel = jnp.concatenate([temporal_ref[2 - step] for step in range(len(grads))], axis=1)
    gact = lax.dot_general(
        flat, kernel, (((1,), (1,)), ((), ())), preferred_element_type=jnp.float32
    )
    gact = gact.astype(jnp.bfloat16).astype(jnp.float32).reshape(preact.shape)
    hval = preact.astype(jnp.float32)
    sig = sigmoid(hval)
    return gact * sig * (1.0 + hval * (1.0 - sig))


def convolved(views_ref, spatial_ref, start, first):
    count, cols, ch = first.shape
    total = first.astype(jnp.float32).reshape(count * cols, ch)
    for ky in range(3):
        view = views_ref[pl.ds(start + 2 - ky, count)].reshape(count * cols, 3 * ch)
        kernel = jnp.concatenate([spatial_ref[ky, kx] for kx in range(3)], axis=1)
        total = total + lax.dot_general(
            view, kernel, (((1,), (1,)), ((), ())), preferred_element_type=jnp.float32
        )
    return total.astype(jnp.bfloat16).reshape(first.shape)


def is_last():
    return lax.axis_index("video") == lax.axis_size("video") - 1


def left_sides(saved_ref, preact_ref, above, below, sides_ref):
    rows, cols, ch = saved_ref.shape
    flat = (rows * cols, ch)
    shifts = [
        jnp.concatenate([above, saved_ref[: rows - 1]], axis=0),
        saved_ref[...],
        jnp.concatenate([saved_ref[1:], below], axis=0),
    ]
    for n, shift in enumerate(shifts):
        sides_ref[n] = shift.reshape(flat).T
    hval = preact_ref[...].astype(jnp.float32)
    sides_ref[3] = (hval * sigmoid(hval)).astype(jnp.bfloat16).reshape(flat).T


def kernel_sums(sides_ref, grads, views, sums_ref):
    _, ch, pixels = sides_ref.shape
    shifts = sides_ref[0:3].reshape(3 * ch, pixels)
    sums = jnp.dot(shifts, views, preferred_element_type=jnp.float32)
    for ky in range(3):
        for kx in range(3):
            here = slice(kx * ch, (kx + 1) * ch)
            sums_ref[ky, here] = sums[ky * ch : (ky + 1) * ch, here]
    grads = jnp.concatenate([grad.reshape(pixels, ch) for grad in grads], axis=1)
    sums = jnp.dot(sides_ref[3], grads, preferred_element_type=jnp.float32)
    zeros = jnp.zeros((ch, ch), jnp.float32)
    for k in range(3):
        step = 2 - k
        value = sums[:, step * ch : (step + 1) * ch] if step * ch < grads.shape[1] else zeros
        sums_ref[3, k * ch : (k + 1) * ch] = jnp.where(is_last(), zeros, value) if step else value


def hand_out(sums_ref, keep_ref, *send_refs):
    odd = lax.rem(lax.axis_index("section"), 2)
    for n, send_ref in enumerate(send_refs):
        keep_ref[n] = sums_ref[2 * n + odd]
        send_ref[...] = sums_ref[2 * n + 1 - odd].astype(jnp.bfloat16)


def pack_kernel(*refs):
    parts, outs, sems = refs[:4], refs[4:6], refs[6]
    last = parts[0].shape[0] - 1
    odd = lax.rem(lax.axis_index("section"), 2)
    copies = []
    for n, part in enumerate(parts):
        for out, row in zip(outs, ((1 - odd) * last, odd * last)):
            sem = sems.at[len(copies)]
            copies.append(
                pltpu.make_async_copy(part.at[pl.ds(row, 1)], out.at[pl.ds(n, 1)], sem)
            )
    for copy in copies:
        copy.start()
    for copy in copies:
        copy.wait()


def interior(grad_ref, preact_ref, wholes, temporal_ref, spatial_ref, inner_ref, gpre_ref, views_ref):
    rows, cols, ch = grad_ref.shape
    step = 4

    for n in range(rows // step):
        here = pl.ds(n * step, step)
        grads = [ref[here] for ref in (grad_ref, *wholes)]
        gpre = pre_gradient(grads, preact_ref[here], temporal_ref)
        gpre_ref[here] = gpre.astype(jnp.bfloat16)
        beside(gpre, views_ref, n * step)

    half = rows // 2 - 1

    for n in range(2):
        first = grad_ref[pl.ds(n * half + 1, half)]
        inner_ref[pl.ds(n * half, half)] = convolved(views_ref, spatial_ref, n * half, first)


def edge_rows(grad_ref, pair_refs, afters, gpre_ref, temporal_ref, spatial_ref, views_ref):
    rows, cols, ch = grad_ref.shape
    (grad_above, grad_below), (above_pre, below_pre) = (beside_band(pair_refs, n) for n in (0, 1))
    above = [grad_above] + [ref[0:1] for ref in afters]
    below = [grad_below] + [ref[1:2] for ref in afters]
    beside(pre_gradient(above, above_pre, temporal_ref), views_ref, 0)
    beside(gpre_ref[0:2].astype(jnp.float32), views_ref, 1)
    beside(gpre_ref[rows - 2 : rows].astype(jnp.float32), views_ref, 3)
    beside(pre_gradient(below, below_pre, temporal_ref), views_ref, 5)
    return (
        convolved(views_ref, spatial_ref, 0, grad_ref[0:1]),
        convolved(views_ref, spatial_ref, 3, grad_ref[rows - 1 : rows]),
    )


def last_inner_kernel(grad_ref, preact_ref, temporal_ref, spatial_ref, inner_ref, gpre_ref, views_ref):
    @pl.when(is_last())
    def _():
        interior(
            grad_ref, preact_ref, [], temporal_ref, spatial_ref, inner_ref, gpre_ref, views_ref
        )


def last_edge_kernel(grad_ref, one_ref, two_ref, gpre_ref, temporal_ref, spatial_ref, edge_ref, views_ref):
    @pl.when(is_last())
    def _():
        pair_refs = (one_ref, two_ref)
        edge_ref[0:1], edge_ref[1:2] = edge_rows(
            grad_ref, pair_refs, [], gpre_ref, temporal_ref, spatial_ref, views_ref
        )
        edge_ref[2:3], edge_ref[3:4] = beside_band(pair_refs, 0)


def inner_kernel(later, *refs):
    inputs, wholes, kernels = refs[:2], refs[2 : 2 + later], refs[2 + later : 4 + later]
    known, outs = refs[4 + later : -3], refs[-3:]
    if not known:
        interior(*inputs, wholes, *kernels, *outs)
        return

    @pl.when(is_last())
    def _():
        outs[0][...] = known[0][...]
        outs[1][...] = known[1][...]

    @pl.when(jnp.logical_not(is_last()))
    def _():
        interior(*inputs, wholes, *kernels, *outs)


def mid_kernel(later, *refs):
    grad_ref, inner_ref, gpre_ref = refs[0], refs[3], refs[4]
    afters, (temporal_ref, spatial_ref, mid_ref, views_ref) = refs[5 : 5 + later], refs[5 + later :]
    rows = grad_ref.shape[0]
    first, last = edge_rows(
        grad_ref, refs[1:3], afters, gpre_ref, temporal_ref, spatial_ref, views_ref
    )
    mid_ref[0:1], mid_ref[rows - 1 : rows] = first, last
    mid_ref[1 : rows - 1] = inner_ref[...]


def two_kernel(later, *refs):
    saved_ref, preact_ref, gpre_ref = refs[:3]
    pair_refs, grad_ref = refs[3:5], refs[5]
    wholes, outs = refs[6 : 6 + later], refs[6 + later : 9 + later]
    views_ref, sides_ref, sums_ref = refs[9 + later :]
    rows, cols, ch = saved_ref.shape
    step = 4

    for n in range(rows // step):
        here = pl.ds(n * step, step)
        beside(gpre_ref[here].astype(jnp.float32), views_ref, n * step)

    views = views_ref[...].reshape(rows * cols, 3 * ch)
    grads = [ref[...] for ref in (grad_ref, *wholes)]
    left_sides(saved_ref, preact_ref, *beside_band(pair_refs, 2), sides_ref)
    kernel_sums(sides_ref, grads, views, sums_ref)
    hand_out(sums_ref, *outs)


def sides_kernel(saved_ref, preact_ref, one_ref, two_ref, sides_ref):
    left_sides(saved_ref, preact_ref, *beside_band((one_ref, two_ref), 3), sides_ref)


def pre_rows(preact, mids, temporal_ref, gpre_ref, views_ref, start):
    gpre = pre_gradient(mids, preact, temporal_ref)
    gpre_ref[start : start + preact.shape[0]] = gpre.astype(jnp.bfloat16)
    beside(gpre, views_ref, start)


def block_sums(gpre_ref, sides_ref, mids, views_ref, sums_ref, keep_ref, send_ref):
    rows, cols, ch = gpre_ref.shape
    odd = lax.rem(lax.axis_index("section"), 2)
    size = send_ref.shape[0] - 2 * cols
    send_ref[size : size + cols] = gpre_ref[(1 - odd) * (rows - 1)]
    send_ref[size + cols : size + 2 * cols] = gpre_ref[odd * (rows - 1)]
    views = views_ref[...].reshape(rows * cols, 3 * ch)
    kernel_sums(sides_ref, [ref[...] for ref in mids], views, sums_ref)
    height = sums_ref.shape[1]
    hand_out(sums_ref, keep_ref, send_ref.at[:height], send_ref.at[height : 2 * height])


def one_kernel(later, *refs):
    sides_ref, preact_ref, mids = refs[0], refs[1], refs[2 : 3 + later]
    temporal_ref, outs, scratch = refs[3 + later], refs[4 + later : 7 + later], refs[7 + later :]
    gpre_ref, keep_ref, send_ref = outs
    views_ref, sums_ref = scratch
    for n in range(preact_ref.shape[0] // 4):
        here = slice(4 * n, 4 * n + 4)
        grads = [ref[here] for ref in mids]
        pre_rows(preact_ref[here], grads, temporal_ref, gpre_ref, views_ref, 4 * n)
    block_sums(gpre_ref, sides_ref, mids, views_ref, sums_ref, keep_ref, send_ref)


def one_inner_kernel(preact_ref, inner_ref, after_ref, temporal_ref, gpre_ref, views_ref):
    rows = inner_ref.shape[0]
    for n in range(rows // 7):
        here = slice(7 * n, 7 * n + 7)
        after = after_ref[here]
        after = jnp.where(is_last(), jnp.zeros_like(after), after)
        preact = preact_ref[7 * n + 1 : 7 * n + 8]
        pre_rows(preact, [inner_ref[here], after], temporal_ref, gpre_ref, views_ref, 7 * n)


def mid_one_kernel(*refs):
    after_inner_ref, after_edge_ref = refs[5:7]
    temporal_two_ref, spatial_two_ref, sides_ref, preact_ref, temporal_ref = refs[7:12]
    inner_gpre_ref, inner_views_ref = refs[12:14]
    mid_ref, gpre_ref, keep_ref, send_ref = refs[14:18]
    views_ref, sums_ref, next_ref, edge_ref, edge_views_ref = refs[18:]
    rows = next_ref.shape[0]

    @pl.when(is_last())
    def _():
        edge_ref[...] = jnp.zeros(edge_ref.shape, edge_ref.dtype)
        next_ref[...] = jnp.zeros(next_ref.shape, next_ref.dtype)

    @pl.when(jnp.logical_not(is_last()))
    def _():
        edge_ref[...] = after_edge_ref[2:4]
        next_ref[0:1] = after_edge_ref[0:1]
        next_ref[1 : rows - 1] = after_inner_ref[...]
        next_ref[rows - 1 : rows] = after_edge_ref[1:2]

    mid_kernel(
        1, *refs[:5], edge_ref, temporal_two_ref, spatial_two_ref, mid_ref, edge_views_ref
    )
    gpre_ref[1 : rows - 1] = inner_gpre_ref[...]
    views_ref[1 : rows - 1] = inner_views_ref[...]
    for row in (0, rows - 1):
        here = slice(row, row + 1)
        grads = [mid_ref[here], next_ref[here]]
        pre_rows(preact_ref[here], grads, temporal_ref, gpre_ref, views_ref, row)
    block_sums(gpre_ref, sides_ref, [mid_ref, next_ref], views_ref, sums_ref, keep_ref, send_ref)


def input_kernel(mid_ref, gpre_ref, pair_ref, across_ref, spatial_ref, out_ref, token_ref, views_ref):
    rows, cols, ch = out_ref.shape
    pair = pair_ref[pair_ref.shape[0] - 2 * cols : pair_ref.shape[0] - cols]
    above, below = beside_band((pair[None], across_ref[across_ref.shape[0] - cols :][None]), 0)
    token_ref[...] = jnp.zeros(token_ref.shape, token_ref.dtype)
    step = 4
    beside(above.astype(jnp.float32), views_ref, 0)
    beside(below.astype(jnp.float32), views_ref, rows + 1)

    for n in range(rows // step):
        gpre = gpre_ref[pl.ds(n * step, step)].astype(jnp.float32)
        beside(gpre, views_ref, n * step + 1)

    for n in range(rows // step):
        here = pl.ds(n * step, step)
        out_ref[here] = convolved(views_ref, spatial_ref, n * step, mid_ref[here])


def halves(count, index):
    return [pl.ds(pl.multiple_of(n * count, count), count) for n in (index, 1 - index)]


def pair_kernel(keep_ref, low_ref, high_ref, own_ref, send_ref):
    across = lax.axis_index("section") // 2
    parts = [ref[...].astype(jnp.float32) for ref in (low_ref, high_ref)]
    own_ref[...] = keep_ref[across] + jnp.where(across == 0, *parts)
    total = keep_ref[1 - across] + jnp.where(across == 0, *parts[::-1])
    send_ref[...] = total.astype(jnp.bfloat16)


def band_kernel(own_ref, part_ref, keep_ref, send_ref):
    mine, other = halves(keep_ref.shape[0], lax.axis_index("video"))
    keep_ref[...] = own_ref[mine] + part_ref[mine].astype(jnp.float32)
    send_ref[...] = (own_ref[other] + part_ref[other].astype(jnp.float32)).astype(jnp.bfloat16)


def pair_quarter_kernel(keep_ref, part_ref, own_ref, across_ref, frame_ref, both_ref):
    _, height, _ = keep_ref.shape
    half = own_ref.shape[0]
    band = lax.axis_index("section") // 2
    frames = halves(half, lax.axis_index("video"))

    def quarter(band, rows):
        start = pl.multiple_of(band * height, height)
        part = part_ref.at[pl.ds(start, height)][rows]
        return keep_ref[band, rows] + part.astype(jnp.float32)

    own_ref[...] = quarter(band, frames[0])
    across_ref[:half] = quarter(1 - band, frames[0]).astype(jnp.bfloat16)
    rest = across_ref.shape[0] - half
    across_ref[half:] = part_ref[2 * height + rest :]
    frame_ref[...] = quarter(band, frames[1]).astype(jnp.bfloat16)
    both_ref[...] = quarter(1 - band, frames[1]).astype(jnp.bfloat16)


def plane_kernel(own_ref, *refs):
    parts, out_ref = refs[:-1], refs[-1]
    total = own_ref[...]
    for part in parts:
        total = total + part[: out_ref.shape[0]].astype(jnp.float32)
    out_ref[...] = total.astype(jnp.bfloat16)


def add_kernel(one_ref, two_ref, out_ref):
    total = one_ref[...].astype(jnp.float32) + two_ref[...].astype(jnp.float32)
    out_ref[...] = total.astype(jnp.bfloat16)


def scaled_kernel(factor, *refs):
    out_ref = refs[-1]
    for block in range(2):
        one, two = (ref[...].astype(jnp.float32) for ref in refs[2 * block : 2 * block + 2])
        out_ref[block] = ((one + two) * factor).astype(jnp.bfloat16)


def place_kernel(places, *refs):
    shares, outs = refs[: len(places)], refs[-6:-2]
    sums_ref, sems = refs[-2:]
    band, frame = lax.axis_index("section"), lax.axis_index("video")
    height = shares[0].shape[1]

    def copies(n, block):
        flip, other = places[n]
        place = jnp.bitwise_xor(band, flip)
        half = 0 if other is None else jnp.bitwise_xor(frame, int(other))
        here = pl.ds(pl.multiple_of(half * height, height), height)
        spatial, temporal = outs[2 * block : 2 * block + 2]
        source, sem = sums_ref.at[n, block], sems.at[n, block]
        return (
            (place < 3, lambda: pltpu.make_async_copy(source, spatial.at[place, here], sem)),
            (place == 3, lambda: pltpu.make_async_copy(source, temporal.at[here], sem)),
        )

    for n, share in enumerate(shares):
        for block in range(2):
            sums_ref[n, block] = share[block].astype(jnp.float32)
            for inside, copy in copies(n, block):
                pl.when(inside)(lambda: copy().start())
    for n in range(len(shares)):
        for block in range(2):
            for inside, copy in copies(n, block):
                pl.when(inside)(lambda: copy().wait())


def placed(shares, places, given=()):
    _, height, ch = shares[0].shape
    count = len(shares)
    outs = (f32(3, 3 * ch, ch), f32(3 * ch, ch)) * 2
    vmem, spare = (pl.BlockSpec(memory_space=space) for space in (pltpu.VMEM, pl.ANY))
    return pl.pallas_call(
        functools.partial(place_kernel, places),
        out_shape=outs,
        in_specs=[vmem] * count + [spare] * len(given),
        out_specs=(spare,) * 4,
        scratch_shapes=[
            pltpu.VMEM((count, 2, height, ch), jnp.float32),
            pltpu.SemaphoreType.DMA((count, 2)),
        ],
        input_output_aliases={count + n: n for n in range(len(given))},
        compiler_params=pltpu.CompilerParams(vmem_limit_bytes=24 * MIB),
        cost_estimate=pl.CostEstimate(
            flops=0, bytes_accessed=6 * count * height * ch * 2, transcendentals=0
        ),
    )(*shares, *given)


def unpacked(sums):
    ch = sums[0].shape[-1]
    return [x.reshape(3, 3, ch, ch) if x.ndim == 3 else x.reshape(3, ch, ch) for x in sums]


def on_device(
    grad_latent,
    input_one,
    preact_one,
    input_two,
    preact_two,
    spatial_one,
    temporal_one,
    spatial_two,
    temporal_two,
):
    shape = grad_latent.shape
    rows, cols, ch = shape[2:]
    bands, frames = lax.axis_size("section"), lax.axis_size("video")
    later = min(2, frames - 1)
    pixels = lax.axis_size("dp") * frames * bands * rows * cols
    factor = 1.0 / math.sqrt(pixels)
    grad, saved_one, pre_one, saved_two, pre_two = (
        x.reshape(rows, cols, ch)
        for x in (grad_latent, input_one, preact_one, input_two, preact_two)
    )
    conv = 2 * rows * cols * 9 * ch * ch
    views = pltpu.VMEM((rows, cols, 3 * ch), jnp.bfloat16)
    edge_views = pltpu.VMEM((6, cols, 3 * ch), jnp.bfloat16)
    act = pltpu.VMEM((rows, cols, ch), jnp.bfloat16)
    sides = bf16(4, ch, rows * cols)
    sums = pltpu.VMEM((4, 3 * ch, ch), jnp.float32)
    handed = [f32(2, 3 * ch, ch)] + [bf16(3 * ch, ch)] * 2
    inner_outs = [bf16(rows - 2, cols, ch), bf16(rows, cols, ch)]
    kernels = (temporal_two, spatial_two)

    def from_later(x):
        if frames == 2:
            return [flipped(x, "video", 1)]
        return [from_ahead(x, 0, n + 1) for n in range(later)]

    wholes = from_later(grad)
    packs = call(
        pack_kernel,
        [bf16(4, cols, ch)] * 2,
        [pltpu.SemaphoreType.DMA((8,))],
        1,
        grad,
        pre_two,
        saved_two,
        saved_one,
        spare_inputs=True,
        limit=58,
    )
    second = flipped(packs[1], "section", 1)
    first = flipped(later_than(packs[0], second), "section", 1)
    pairs = [first, flipped(second, "section", 2)]

    known = ()
    if frames == 2:
        known = call(
            last_inner_kernel,
            inner_outs,
            [views],
            0,
            grad,
            pre_two,
            *kernels,
            after=(first, second),
        )
        afters = from_later(known[0])
    else:
        afters = from_later(jnp.concatenate(beside_band(pairs, 0)))
    inner, gpre_two = call(
        functools.partial(inner_kernel, later),
        inner_outs,
        [views],
        0,
        grad,
        pre_two,
        *wholes,
        *kernels,
        *known,
        early=(saved_two, saved_one, pre_one, temporal_one),
    )
    if frames == 2:
        edge = call(
            last_edge_kernel,
            [bf16(4, cols, ch)],
            [edge_views],
            0,
            grad,
            *pairs,
            known[1],
            *kernels,
            after=(gpre_two,),
        )
        afters += from_later(edge)
    parts_two = call(
        functools.partial(two_kernel, later),
        handed,
        [views, pltpu.VMEM(sides.shape, sides.dtype), sums],
        8 * conv,
        saved_two,
        pre_two,
        gpre_two,
        *pairs,
        grad,
        *wholes,
        after=(edge,) if frames == 2 else (),
    )
    sides_one = call(
        sides_kernel, [sides], [], conv // 8, saved_one, pre_one, *pairs, after=parts_two[:1]
    )
    height, half = 3 * ch, 3 * ch // 2
    keep_two, low_two, high_two = parts_two
    own_two, send_two = call(
        pair_kernel,
        [f32(height, ch), bf16(height, ch)],
        [],
        height * ch,
        keep_two,
        flipped(low_two, "section", 1),
        flipped(high_two, "section", 1),
    )
    across_two = flipped(send_two, "section", 2)
    mid_inputs = (grad, *pairs, inner, gpre_two)
    one_inputs = (sides_one, pre_one)
    mid_outs = [bf16(rows, cols, ch)]
    one_outs = [bf16(rows, cols, ch), f32(2, 3 * ch, ch), bf16(6 * ch + 2 * cols, ch)]
    if frames == 2:
        inners_one = call(
            one_inner_kernel,
            [bf16(rows - 2, cols, ch), bf16(rows - 2, cols, 3 * ch)],
            [],
            conv // 8,
            pre_one,
            inner,
            afters[0],
            temporal_one,
        )
        mid, gpre_one, *parts_one = call(
            mid_one_kernel,
            mid_outs + one_outs,
            [views, sums, act, pltpu.VMEM((2, cols, ch), jnp.bfloat16), edge_views],
            8 * conv,
            *mid_inputs,
            *afters,
            *kernels,
            *one_inputs,
            temporal_one,
            *inners_one,
            after=(own_two,),
        )
    else:
        mid = call(
            functools.partial(mid_kernel, later),
            mid_outs,
            [edge_views],
            conv // 8,
            *mid_inputs,
            *afters,
            *kernels,
        )
        gpre_one, *parts_one = call(
            functools.partial(one_kernel, later),
            one_outs,
            [views, sums],
            1.2 * conv,
            *one_inputs,
            mid,
            *from_later(mid),
            temporal_one,
        )
    keep_one, send_one = parts_one
    split = frames == 2 and lax.axis_size("dp") == 4
    if split:
        send_one = later_than(send_one, across_two)
    pair_one = flipped(send_one, "section", 1)

    def input_gradient(edge, after):
        return call(
            input_kernel,
            [bf16(rows, cols, ch), f32(8, 128)],
            [pltpu.VMEM((rows + 2, cols, 3 * ch), jnp.bfloat16)],
            conv,
            mid,
            gpre_one,
            pair_one,
            edge,
            spatial_one,
            after=after,
        )

    if split:

        def added(one, two):
            return call(add_kernel, [bf16(half, ch)], [], half * ch, one, two)

        keep_two, send_two = call(
            band_kernel,
            [f32(half, ch), bf16(half, ch)],
            [],
            height * ch,
            own_two,
            across_two,
        )
        sum_two = added(keep_two, flipped(send_two, "video", 1))
        quarters = [f32(half, ch), bf16(half + cols, ch)] + [bf16(half, ch)] * 2
        own_one, *sends = call(
            pair_quarter_kernel, quarters, [], 8 * conv, keep_one, pair_one, after=(send_two,)
        )
        across = flipped(sends[0], "section", 2)
        parts = [across, flipped(sends[1], "video", 1), flipped_both(sends[2])]
        sum_one = call(plane_kernel, [bf16(half, ch)], [], 4 * half * ch, own_one, *parts)
        part_two = flipped(sum_two, "dp", 1)
        part_one = flipped(later_than(sum_one, sum_two), "dp", 1)
        sum_two = added(sum_two, part_two)
        sum_one = added(sum_one, part_one)
        last_two = flipped(sum_two, "dp", 2)
        last_one = flipped(later_than(sum_one, sum_two), "dp", 2)
        grad_in, token = input_gradient(across, (sum_one,))
        own = call(
            functools.partial(scaled_kernel, factor),
            [bf16(2, half, ch)],
            [],
            height * ch,
            sum_one,
            last_one,
            sum_two,
            last_two,
            after=(token,),
        )
        frame, across, both = flipped(own, "video", 1), flipped(own, "section", 2), flipped_both(own)
        shares = [own, frame, across]
        shares += [flipped(share, "section", 1) for share in shares]
        last = [both, flipped(both, "section", 1)]
        places = [(0, False), (0, True), (2, False), (1, False), (1, True), (3, False)]
        sums = placed(shares, places)
        sums = unpacked(placed(last, [(2, True), (3, True)], sums))
    else:
        own_one, send_one = call(
            pair_kernel,
            [f32(height, ch), bf16(height, ch)],
            [],
            height * ch,
            keep_one,
            pair_one[:height],
            pair_one[height : 2 * height],
        )
        edge = flipped(pair_one[pair_one.shape[0] - cols :], "section", 2)
        grad_in, _ = input_gradient(edge, ())
        own_one = own_one + flipped(send_one, "section", 2).astype(jnp.float32)
        own_two = own_two + across_two.astype(jnp.float32)
        share = lax.psum(jnp.stack((own_one, own_two)), ("video", "dp")) * factor
        share = share.astype(jnp.bfloat16)
        shares = [share, flipped(share, "section", 2)]
        shares += [flipped(share, "section", 1) for share in shares]
        sums = unpacked(placed(shares, [(0, None), (2, None), (1, None), (3, None)]))
    return (grad_in.reshape(shape), *sums)


def solution(mesh):
    whole = P("dp", "video", "section", None, None)
    return jax.shard_map(
        on_device,
        mesh=mesh,
        in_specs=(whole,) * 5 + (P(),) * 4,
        out_specs=(whole, P(), P(), P(), P()),
        check_vma=False,
    )
```

```python
import functools
import math

import jax
import jax.numpy as jnp
from jax import lax
from jax.experimental import pallas as pl
from jax.experimental.pallas import tpu as pltpu
from jax.sharding import PartitionSpec as P

MIB = 1024 * 1024


def sigmoid(value):
    return 1.0 / (1.0 + jnp.exp(-value))


def bf16(*shape):
    return jax.ShapeDtypeStruct(shape, jnp.bfloat16)


def f32(*shape):
    return jax.ShapeDtypeStruct(shape, jnp.float32)


def call(kernel, outs, scratch, flops, *operands, after=(), early=(), spare_inputs=False, limit=24):
    single = len(outs) == 1
    moved = sum(math.prod(x.shape) * x.dtype.itemsize for x in (*operands, *outs))
    vmem = pl.BlockSpec(memory_space=pltpu.VMEM)
    spare = pl.BlockSpec(memory_space=pl.ANY)
    spec = spare if spare_inputs else vmem
    count = len(operands)
    operands = (*operands, *early, *after)

    def body(*refs):
        kernel(*refs[:count], *refs[len(operands) :])

    return pl.pallas_call(
        body,
        out_shape=outs[0] if single else tuple(outs),
        in_specs=[spec] * count + [vmem] * len(early) + [spare] * len(after),
        out_specs=vmem if single else (vmem,) * len(outs),
        scratch_shapes=scratch,
        compiler_params=pltpu.CompilerParams(vmem_limit_bytes=limit * MIB),
        cost_estimate=pl.CostEstimate(
            flops=int(flops), bytes_accessed=int(moved) if flops else 0, transcendentals=0
        ),
    )(*operands)


def from_ahead(block, band_step, frame_step):
    bands, frames = lax.axis_size("section"), lax.axis_size("video")
    pairs = [
        ((band + band_step) * frames + frame + frame_step, band * frames + frame)
        for band in range(bands)
        for frame in range(frames)
        if 0 <= band + band_step < bands and frame + frame_step < frames
    ]
    return lax.ppermute(block, ("section", "video"), pairs)


def beside_band(pair_refs, row):
    band = lax.axis_index("section")
    odd = lax.rem(band, 2) == 1
    inside = (band > 0) & (band < lax.axis_size("section") - 1)
    first, second = (ref[row : row + 1] for ref in pair_refs)
    second = jnp.where(inside, second, jnp.zeros_like(second))
    return jnp.where(odd, first, second), jnp.where(odd, second, first)


def flipped(block, axis, flip):
    count = lax.axis_size(axis)
    return lax.ppermute(block, axis, [(place ^ flip, place) for place in range(count)])


def flipped_both(block):
    bands = lax.axis_size("section")
    pairs = [
        (2 * (band ^ 2) + 1 - frame, 2 * band + frame) for band in range(bands) for frame in range(2)
    ]
    return lax.ppermute(block, ("section", "video"), pairs)


def later_than(block, *others):
    return lax.optimization_barrier((block, *others))[0]


def beside(gpre, views_ref, start):
    count, cols, ch = gpre.shape
    at = lax.broadcasted_iota(jnp.int32, gpre.shape, 1)
    right = jnp.where(at == cols - 1, 0.0, pltpu.roll(gpre, cols - 1, 1))
    left = jnp.where(at == 0, 0.0, pltpu.roll(gpre, 1, 1))
    here = pl.ds(start, count)
    views_ref[here, :, 0:ch] = right.astype(jnp.bfloat16)
    views_ref[here, :, ch : 2 * ch] = gpre.astype(jnp.bfloat16)
    views_ref[here, :, 2 * ch : 3 * ch] = left.astype(jnp.bfloat16)


def pre_gradient(grads, preact, temporal_ref):
    count, cols, ch = preact.shape
    flat = jnp.concatenate([grad.reshape(count * cols, ch) for grad in grads], axis=1)
    kernel = jnp.concatenate([temporal_ref[2 - step] for step in range(len(grads))], axis=1)
    gact = lax.dot_general(
        flat, kernel, (((1,), (1,)), ((), ())), preferred_element_type=jnp.float32
    )
    gact = gact.astype(jnp.bfloat16).astype(jnp.float32).reshape(preact.shape)
    hval = preact.astype(jnp.float32)
    sig = sigmoid(hval)
    return gact * sig * (1.0 + hval * (1.0 - sig))


def convolved(views_ref, spatial_ref, start, first):
    count, cols, ch = first.shape
    total = first.astype(jnp.float32).reshape(count * cols, ch)
    for ky in range(3):
        view = views_ref[pl.ds(start + 2 - ky, count)].reshape(count * cols, 3 * ch)
        kernel = jnp.concatenate([spatial_ref[ky, kx] for kx in range(3)], axis=1)
        total = total + lax.dot_general(
            view, kernel, (((1,), (1,)), ((), ())), preferred_element_type=jnp.float32
        )
    return total.astype(jnp.bfloat16).reshape(first.shape)


def is_last():
    return lax.axis_index("video") == lax.axis_size("video") - 1


def left_sides(saved_ref, preact_ref, above, below, sides_ref):
    rows, cols, ch = saved_ref.shape
    flat = (rows * cols, ch)
    shifts = [
        jnp.concatenate([above, saved_ref[: rows - 1]], axis=0),
        saved_ref[...],
        jnp.concatenate([saved_ref[1:], below], axis=0),
    ]
    for n, shift in enumerate(shifts):
        sides_ref[n] = shift.reshape(flat).T
    hval = preact_ref[...].astype(jnp.float32)
    sides_ref[3] = (hval * sigmoid(hval)).astype(jnp.bfloat16).reshape(flat).T


def kernel_sums(sides_ref, grads, views, sums_ref):
    _, ch, pixels = sides_ref.shape
    shifts = sides_ref[0:3].reshape(3 * ch, pixels)
    sums = jnp.dot(shifts, views, preferred_element_type=jnp.float32)
    for ky in range(3):
        for kx in range(3):
            here = slice(kx * ch, (kx + 1) * ch)
            sums_ref[ky, here] = sums[ky * ch : (ky + 1) * ch, here]
    grads = jnp.concatenate([grad.reshape(pixels, ch) for grad in grads], axis=1)
    sums = jnp.dot(sides_ref[3], grads, preferred_element_type=jnp.float32)
    zeros = jnp.zeros((ch, ch), jnp.float32)
    for k in range(3):
        step = 2 - k
        value = sums[:, step * ch : (step + 1) * ch] if step * ch < grads.shape[1] else zeros
        sums_ref[3, k * ch : (k + 1) * ch] = jnp.where(is_last(), zeros, value) if step else value


def hand_out(sums_ref, keep_ref, *send_refs):
    odd = lax.rem(lax.axis_index("section"), 2)
    for n, send_ref in enumerate(send_refs):
        keep_ref[n] = sums_ref[2 * n + odd]
        send_ref[...] = sums_ref[2 * n + 1 - odd].astype(jnp.bfloat16)


def pack_kernel(*refs):
    parts, outs, sems = refs[:4], refs[4:6], refs[6]
    last = parts[0].shape[0] - 1
    odd = lax.rem(lax.axis_index("section"), 2)
    copies = []
    for n, part in enumerate(parts):
        for out, row in zip(outs, ((1 - odd) * last, odd * last)):
            sem = sems.at[len(copies)]
            copies.append(
                pltpu.make_async_copy(part.at[pl.ds(row, 1)], out.at[pl.ds(n, 1)], sem)
            )
    for copy in copies:
        copy.start()
    for copy in copies:
        copy.wait()


def interior(grad_ref, preact_ref, wholes, temporal_ref, spatial_ref, inner_ref, gpre_ref, views_ref):
    rows, cols, ch = grad_ref.shape
    step = 4

    for n in range(rows // step):
        here = pl.ds(n * step, step)
        grads = [ref[here] for ref in (grad_ref, *wholes)]
        gpre = pre_gradient(grads, preact_ref[here], temporal_ref)
        gpre_ref[here] = gpre.astype(jnp.bfloat16)
        beside(gpre, views_ref, n * step)

    half = rows // 2 - 1

    for n in range(2):
        first = grad_ref[pl.ds(n * half + 1, half)]
        inner_ref[pl.ds(n * half, half)] = convolved(views_ref, spatial_ref, n * half, first)


def edge_rows(grad_ref, pair_refs, afters, gpre_ref, temporal_ref, spatial_ref, views_ref):
    rows, cols, ch = grad_ref.shape
    (grad_above, grad_below), (above_pre, below_pre) = (beside_band(pair_refs, n) for n in (0, 1))
    above = [grad_above] + [ref[0:1] for ref in afters]
    below = [grad_below] + [ref[1:2] for ref in afters]
    beside(pre_gradient(above, above_pre, temporal_ref), views_ref, 0)
    beside(gpre_ref[0:2].astype(jnp.float32), views_ref, 1)
    beside(gpre_ref[rows - 2 : rows].astype(jnp.float32), views_ref, 3)
    beside(pre_gradient(below, below_pre, temporal_ref), views_ref, 5)
    return (
        convolved(views_ref, spatial_ref, 0, grad_ref[0:1]),
        convolved(views_ref, spatial_ref, 3, grad_ref[rows - 1 : rows]),
    )


def last_inner_kernel(grad_ref, preact_ref, temporal_ref, spatial_ref, inner_ref, gpre_ref, views_ref):
    @pl.when(is_last())
    def _():
        interior(
            grad_ref, preact_ref, [], temporal_ref, spatial_ref, inner_ref, gpre_ref, views_ref
        )


def last_edge_kernel(grad_ref, one_ref, two_ref, gpre_ref, temporal_ref, spatial_ref, edge_ref, views_ref):
    @pl.when(is_last())
    def _():
        pair_refs = (one_ref, two_ref)
        edge_ref[0:1], edge_ref[1:2] = edge_rows(
            grad_ref, pair_refs, [], gpre_ref, temporal_ref, spatial_ref, views_ref
        )
        edge_ref[2:3], edge_ref[3:4] = beside_band(pair_refs, 0)


def inner_kernel(later, *refs):
    inputs, wholes, kernels = refs[:2], refs[2 : 2 + later], refs[2 + later : 4 + later]
    known, outs = refs[4 + later : -3], refs[-3:]
    if not known:
        interior(*inputs, wholes, *kernels, *outs)
        return

    @pl.when(is_last())
    def _():
        outs[0][...] = known[0][...]
        outs[1][...] = known[1][...]

    @pl.when(jnp.logical_not(is_last()))
    def _():
        interior(*inputs, wholes, *kernels, *outs)


def mid_kernel(later, *refs):
    grad_ref, inner_ref, gpre_ref = refs[0], refs[3], refs[4]
    afters, (temporal_ref, spatial_ref, mid_ref, views_ref) = refs[5 : 5 + later], refs[5 + later :]
    rows = grad_ref.shape[0]
    first, last = edge_rows(
        grad_ref, refs[1:3], afters, gpre_ref, temporal_ref, spatial_ref, views_ref
    )
    mid_ref[0:1], mid_ref[rows - 1 : rows] = first, last
    mid_ref[1 : rows - 1] = inner_ref[...]


def two_kernel(later, *refs):
    saved_ref, preact_ref, gpre_ref = refs[:3]
    pair_refs, grad_ref = refs[3:5], refs[5]
    wholes, outs = refs[6 : 6 + later], refs[6 + later : 9 + later]
    views_ref, sides_ref, sums_ref = refs[9 + later :]
    rows, cols, ch = saved_ref.shape
    step = 4

    for n in range(rows // step):
        here = pl.ds(n * step, step)
        beside(gpre_ref[here].astype(jnp.float32), views_ref, n * step)

    views = views_ref[...].reshape(rows * cols, 3 * ch)
    grads = [ref[...] for ref in (grad_ref, *wholes)]
    left_sides(saved_ref, preact_ref, *beside_band(pair_refs, 2), sides_ref)
    kernel_sums(sides_ref, grads, views, sums_ref)
    hand_out(sums_ref, *outs)


def sides_kernel(saved_ref, preact_ref, one_ref, two_ref, sides_ref):
    left_sides(saved_ref, preact_ref, *beside_band((one_ref, two_ref), 3), sides_ref)


def pre_rows(preact, mids, temporal_ref, gpre_ref, views_ref, start):
    gpre = pre_gradient(mids, preact, temporal_ref)
    gpre_ref[start : start + preact.shape[0]] = gpre.astype(jnp.bfloat16)
    beside(gpre, views_ref, start)


def block_sums(gpre_ref, sides_ref, mids, views_ref, sums_ref, keep_ref, send_ref):
    rows, cols, ch = gpre_ref.shape
    odd = lax.rem(lax.axis_index("section"), 2)
    size = send_ref.shape[0] - 2 * cols
    send_ref[size : size + cols] = gpre_ref[(1 - odd) * (rows - 1)]
    send_ref[size + cols : size + 2 * cols] = gpre_ref[odd * (rows - 1)]
    views = views_ref[...].reshape(rows * cols, 3 * ch)
    kernel_sums(sides_ref, [ref[...] for ref in mids], views, sums_ref)
    height = sums_ref.shape[1]
    hand_out(sums_ref, keep_ref, send_ref.at[:height], send_ref.at[height : 2 * height])


def one_kernel(later, *refs):
    sides_ref, preact_ref, mids = refs[0], refs[1], refs[2 : 3 + later]
    temporal_ref, outs, scratch = refs[3 + later], refs[4 + later : 7 + later], refs[7 + later :]
    gpre_ref, keep_ref, send_ref = outs
    views_ref, sums_ref = scratch
    for n in range(preact_ref.shape[0] // 4):
        here = slice(4 * n, 4 * n + 4)
        grads = [ref[here] for ref in mids]
        pre_rows(preact_ref[here], grads, temporal_ref, gpre_ref, views_ref, 4 * n)
    block_sums(gpre_ref, sides_ref, mids, views_ref, sums_ref, keep_ref, send_ref)


def one_inner_kernel(preact_ref, inner_ref, after_ref, temporal_ref, gpre_ref, views_ref):
    rows = inner_ref.shape[0]
    for n in range(rows // 7):
        here = slice(7 * n, 7 * n + 7)
        after = after_ref[here]
        after = jnp.where(is_last(), jnp.zeros_like(after), after)
        preact = preact_ref[7 * n + 1 : 7 * n + 8]
        pre_rows(preact, [inner_ref[here], after], temporal_ref, gpre_ref, views_ref, 7 * n)


def mid_one_kernel(*refs):
    after_inner_ref, after_edge_ref = refs[5:7]
    temporal_two_ref, spatial_two_ref, sides_ref, preact_ref, temporal_ref = refs[7:12]
    inner_gpre_ref, inner_views_ref = refs[12:14]
    mid_ref, gpre_ref, keep_ref, send_ref = refs[14:18]
    views_ref, sums_ref, next_ref, edge_ref, edge_views_ref = refs[18:]
    rows = next_ref.shape[0]

    @pl.when(is_last())
    def _():
        edge_ref[...] = jnp.zeros(edge_ref.shape, edge_ref.dtype)
        next_ref[...] = jnp.zeros(next_ref.shape, next_ref.dtype)

    @pl.when(jnp.logical_not(is_last()))
    def _():
        edge_ref[...] = after_edge_ref[2:4]
        next_ref[0:1] = after_edge_ref[0:1]
        next_ref[1 : rows - 1] = after_inner_ref[...]
        next_ref[rows - 1 : rows] = after_edge_ref[1:2]

    mid_kernel(
        1, *refs[:5], edge_ref, temporal_two_ref, spatial_two_ref, mid_ref, edge_views_ref
    )
    gpre_ref[1 : rows - 1] = inner_gpre_ref[...]
    views_ref[1 : rows - 1] = inner_views_ref[...]
    for row in (0, rows - 1):
        here = slice(row, row + 1)
        grads = [mid_ref[here], next_ref[here]]
        pre_rows(preact_ref[here], grads, temporal_ref, gpre_ref, views_ref, row)
    block_sums(gpre_ref, sides_ref, [mid_ref, next_ref], views_ref, sums_ref, keep_ref, send_ref)


def input_kernel(mid_ref, gpre_ref, pair_ref, across_ref, spatial_ref, out_ref, token_ref, views_ref):
    rows, cols, ch = out_ref.shape
    pair = pair_ref[pair_ref.shape[0] - 2 * cols : pair_ref.shape[0] - cols]
    above, below = beside_band((pair[None], across_ref[across_ref.shape[0] - cols :][None]), 0)
    token_ref[...] = jnp.zeros(token_ref.shape, token_ref.dtype)
    step = 4
    beside(above.astype(jnp.float32), views_ref, 0)
    beside(below.astype(jnp.float32), views_ref, rows + 1)

    for n in range(rows // step):
        gpre = gpre_ref[pl.ds(n * step, step)].astype(jnp.float32)
        beside(gpre, views_ref, n * step + 1)

    for n in range(rows // step):
        here = pl.ds(n * step, step)
        out_ref[here] = convolved(views_ref, spatial_ref, n * step, mid_ref[here])


def halves(count, index):
    return [pl.ds(pl.multiple_of(n * count, count), count) for n in (index, 1 - index)]


def pair_kernel(keep_ref, low_ref, high_ref, own_ref, send_ref):
    across = lax.axis_index("section") // 2
    parts = [ref[...].astype(jnp.float32) for ref in (low_ref, high_ref)]
    own_ref[...] = keep_ref[across] + jnp.where(across == 0, *parts)
    total = keep_ref[1 - across] + jnp.where(across == 0, *parts[::-1])
    send_ref[...] = total.astype(jnp.bfloat16)


def band_kernel(own_ref, part_ref, keep_ref, send_ref):
    mine, other = halves(keep_ref.shape[0], lax.axis_index("video"))
    keep_ref[...] = own_ref[mine] + part_ref[mine].astype(jnp.float32)
    send_ref[...] = (own_ref[other] + part_ref[other].astype(jnp.float32)).astype(jnp.bfloat16)


def pair_quarter_kernel(keep_ref, part_ref, own_ref, across_ref, frame_ref, both_ref):
    _, height, _ = keep_ref.shape
    half = own_ref.shape[0]
    band = lax.axis_index("section") // 2
    frames = halves(half, lax.axis_index("video"))

    def quarter(band, rows):
        start = pl.multiple_of(band * height, height)
        part = part_ref.at[pl.ds(start, height)][rows]
        return keep_ref[band, rows] + part.astype(jnp.float32)

    own_ref[...] = quarter(band, frames[0])
    across_ref[:half] = quarter(1 - band, frames[0]).astype(jnp.bfloat16)
    rest = across_ref.shape[0] - half
    across_ref[half:] = part_ref[2 * height + rest :]
    frame_ref[...] = quarter(band, frames[1]).astype(jnp.bfloat16)
    both_ref[:half] = quarter(1 - band, frames[1]).astype(jnp.bfloat16)


def plane_kernel(own_ref, *refs):
    parts, out_ref = refs[:-1], refs[-1]
    total = own_ref[...]
    for part in parts:
        total = total + part[: out_ref.shape[0]].astype(jnp.float32)
    out_ref[...] = total.astype(jnp.bfloat16)


def add_kernel(one_ref, two_ref, out_ref):
    total = one_ref[...].astype(jnp.float32) + two_ref[...].astype(jnp.float32)
    out_ref[...] = total.astype(jnp.bfloat16)


def scaled_kernel(factor, *refs):
    out_ref = refs[-1]
    for block in range(2):
        one, two = (ref[...].astype(jnp.float32) for ref in refs[2 * block : 2 * block + 2])
        out_ref[block] = ((one + two) * factor).astype(jnp.bfloat16)


def place_kernel(places, *refs):
    shares, outs = refs[: len(places)], refs[-6:-2]
    sums_ref, sems = refs[-2:]
    band, frame = lax.axis_index("section"), lax.axis_index("video")
    height = shares[0].shape[1]

    def copies(n, block):
        flip, other = places[n]
        place = jnp.bitwise_xor(band, flip)
        half = 0 if other is None else jnp.bitwise_xor(frame, int(other))
        here = pl.ds(pl.multiple_of(half * height, height), height)
        spatial, temporal = outs[2 * block : 2 * block + 2]
        source, sem = sums_ref.at[n, block], sems.at[n, block]
        return (
            (place < 3, lambda: pltpu.make_async_copy(source, spatial.at[place, here], sem)),
            (place == 3, lambda: pltpu.make_async_copy(source, temporal.at[here], sem)),
        )

    for n, share in enumerate(shares):
        for block in range(2):
            sums_ref[n, block] = share[block].astype(jnp.float32)
            for inside, copy in copies(n, block):
                pl.when(inside)(lambda: copy().start())
    for n in range(len(shares)):
        for block in range(2):
            for inside, copy in copies(n, block):
                pl.when(inside)(lambda: copy().wait())


def placed(shares, places, given=()):
    _, height, ch = shares[0].shape
    count = len(shares)
    outs = (f32(3, 3 * ch, ch), f32(3 * ch, ch)) * 2
    vmem, spare = (pl.BlockSpec(memory_space=space) for space in (pltpu.VMEM, pl.ANY))
    return pl.pallas_call(
        functools.partial(place_kernel, places),
        out_shape=outs,
        in_specs=[vmem] * count + [spare] * len(given),
        out_specs=(spare,) * 4,
        scratch_shapes=[
            pltpu.VMEM((count, 2, height, ch), jnp.float32),
            pltpu.SemaphoreType.DMA((count, 2)),
        ],
        input_output_aliases={count + n: n for n in range(len(given))},
        compiler_params=pltpu.CompilerParams(vmem_limit_bytes=24 * MIB),
        cost_estimate=pl.CostEstimate(
            flops=0, bytes_accessed=6 * count * height * ch * 2, transcendentals=0
        ),
    )(*shares, *given)


def unpacked(sums):
    ch = sums[0].shape[-1]
    return [x.reshape(3, 3, ch, ch) if x.ndim == 3 else x.reshape(3, ch, ch) for x in sums]


def on_device(
    grad_latent,
    input_one,
    preact_one,
    input_two,
    preact_two,
    spatial_one,
    temporal_one,
    spatial_two,
    temporal_two,
):
    shape = grad_latent.shape
    rows, cols, ch = shape[2:]
    bands, frames = lax.axis_size("section"), lax.axis_size("video")
    later = min(2, frames - 1)
    pixels = lax.axis_size("dp") * frames * bands * rows * cols
    factor = 1.0 / math.sqrt(pixels)
    grad, saved_one, pre_one, saved_two, pre_two = (
        x.reshape(rows, cols, ch)
        for x in (grad_latent, input_one, preact_one, input_two, preact_two)
    )
    conv = 2 * rows * cols * 9 * ch * ch
    views = pltpu.VMEM((rows, cols, 3 * ch), jnp.bfloat16)
    edge_views = pltpu.VMEM((6, cols, 3 * ch), jnp.bfloat16)
    act = pltpu.VMEM((rows, cols, ch), jnp.bfloat16)
    sides = bf16(4, ch, rows * cols)
    sums = pltpu.VMEM((4, 3 * ch, ch), jnp.float32)
    handed = [f32(2, 3 * ch, ch)] + [bf16(3 * ch, ch)] * 2
    inner_outs = [bf16(rows - 2, cols, ch), bf16(rows, cols, ch)]
    kernels = (temporal_two, spatial_two)

    def from_later(x):
        if frames == 2:
            return [flipped(x, "video", 1)]
        return [from_ahead(x, 0, n + 1) for n in range(later)]

    wholes = from_later(grad)
    packs = call(
        pack_kernel,
        [bf16(4, cols, ch)] * 2,
        [pltpu.SemaphoreType.DMA((8,))],
        1,
        grad,
        pre_two,
        saved_two,
        saved_one,
        spare_inputs=True,
        limit=58,
    )
    second = flipped(packs[1], "section", 1)
    first = flipped(later_than(packs[0], second), "section", 1)
    pairs = [first, flipped(second, "section", 2)]

    known = ()
    if frames == 2:
        known = call(
            last_inner_kernel,
            inner_outs,
            [views],
            0,
            grad,
            pre_two,
            *kernels,
            after=(first, second),
        )
        afters = from_later(known[0])
    else:
        afters = from_later(jnp.concatenate(beside_band(pairs, 0)))
    inner, gpre_two = call(
        functools.partial(inner_kernel, later),
        inner_outs,
        [views],
        0,
        grad,
        pre_two,
        *wholes,
        *kernels,
        *known,
        early=(saved_two, saved_one, pre_one, temporal_one),
    )
    if frames == 2:
        edge = call(
            last_edge_kernel,
            [bf16(4, cols, ch)],
            [edge_views],
            0,
            grad,
            *pairs,
            known[1],
            *kernels,
            after=(gpre_two,),
        )
        afters += from_later(edge)
    parts_two = call(
        functools.partial(two_kernel, later),
        handed,
        [views, pltpu.VMEM(sides.shape, sides.dtype), sums],
        8 * conv,
        saved_two,
        pre_two,
        gpre_two,
        *pairs,
        grad,
        *wholes,
        after=(edge,) if frames == 2 else (),
    )
    sides_one = call(
        sides_kernel, [sides], [], conv // 8, saved_one, pre_one, *pairs, after=parts_two[:1]
    )
    height, half = 3 * ch, 3 * ch // 2
    keep_two, low_two, high_two = parts_two
    own_two, send_two = call(
        pair_kernel,
        [f32(height, ch), bf16(height, ch)],
        [],
        height * ch,
        keep_two,
        flipped(low_two, "section", 1),
        flipped(high_two, "section", 1),
    )
    across_two = flipped(send_two, "section", 2)
    mid_inputs = (grad, *pairs, inner, gpre_two)
    one_inputs = (sides_one, pre_one)
    mid_outs = [bf16(rows, cols, ch)]
    one_outs = [bf16(rows, cols, ch), f32(2, 3 * ch, ch), bf16(6 * ch + 2 * cols, ch)]
    if frames == 2:
        inners_one = call(
            one_inner_kernel,
            [bf16(rows - 2, cols, ch), bf16(rows - 2, cols, 3 * ch)],
            [],
            conv // 8,
            pre_one,
            inner,
            afters[0],
            temporal_one,
        )
        mid, gpre_one, *parts_one = call(
            mid_one_kernel,
            mid_outs + one_outs,
            [views, sums, act, pltpu.VMEM((2, cols, ch), jnp.bfloat16), edge_views],
            8 * conv,
            *mid_inputs,
            *afters,
            *kernels,
            *one_inputs,
            temporal_one,
            *inners_one,
            after=(own_two,),
        )
    else:
        mid = call(
            functools.partial(mid_kernel, later),
            mid_outs,
            [edge_views],
            conv // 8,
            *mid_inputs,
            *afters,
            *kernels,
        )
        gpre_one, *parts_one = call(
            functools.partial(one_kernel, later),
            one_outs,
            [views, sums],
            1.2 * conv,
            *one_inputs,
            mid,
            *from_later(mid),
            temporal_one,
        )
    keep_one, send_one = parts_one
    split = frames == 2 and lax.axis_size("dp") == 4
    if split:
        send_one = later_than(send_one, across_two)
    pair_one = flipped(send_one, "section", 1)

    def input_gradient(edge, after):
        return call(
            input_kernel,
            [bf16(rows, cols, ch), f32(8, 128)],
            [pltpu.VMEM((rows + 2, cols, 3 * ch), jnp.bfloat16)],
            conv,
            mid,
            gpre_one,
            pair_one,
            edge,
            spatial_one,
            after=after,
        )

    if split:

        def added(one, two):
            return call(add_kernel, [bf16(half, ch)], [], half * ch, one, two)

        keep_two, send_two = call(
            band_kernel,
            [f32(half, ch), bf16(half, ch)],
            [],
            height * ch,
            own_two,
            across_two,
        )
        sum_two = added(keep_two, flipped(send_two, "video", 1))
        quarters = [f32(half, ch)] + [bf16(half + more, ch) for more in (cols, 0, cols + 16)]
        own_one, *sends = call(
            pair_quarter_kernel, quarters, [], 8 * conv, keep_one, pair_one, after=(send_two,)
        )
        across = flipped(sends[0], "section", 2)
        parts = [across, flipped(sends[1], "video", 1), flipped_both(sends[2])]
        sum_one = call(plane_kernel, [bf16(half, ch)], [], 4 * half * ch, own_one, *parts)
        part_two = flipped(sum_two, "dp", 1)
        part_one = flipped(later_than(sum_one, sum_two), "dp", 1)
        sum_two = added(sum_two, part_two)
        sum_one = added(sum_one, part_one)
        last_two = flipped(sum_two, "dp", 2)
        last_one = flipped(later_than(sum_one, sum_two), "dp", 2)
        grad_in, token = input_gradient(across, (sum_one,))
        own = call(
            functools.partial(scaled_kernel, factor),
            [bf16(2, half, ch)],
            [],
            height * ch,
            sum_one,
            last_one,
            sum_two,
            last_two,
            after=(token,),
        )
        frame, across, both = flipped(own, "video", 1), flipped(own, "section", 2), flipped_both(own)
        shares = [own, frame, across]
        shares += [flipped(share, "section", 1) for share in shares]
        places = [(0, False), (0, True), (2, False), (1, False), (1, True), (3, False)]
        sums = placed([*shares, both], [*places, (2, True)])
        sums = unpacked(placed([flipped(both, "section", 1)], [(3, True)], sums))
    else:
        own_one, send_one = call(
            pair_kernel,
            [f32(height, ch), bf16(height, ch)],
            [],
            height * ch,
            keep_one,
            pair_one[:height],
            pair_one[height : 2 * height],
        )
        edge = flipped(pair_one[pair_one.shape[0] - cols :], "section", 2)
        grad_in, _ = input_gradient(edge, ())
        own_one = own_one + flipped(send_one, "section", 2).astype(jnp.float32)
        own_two = own_two + across_two.astype(jnp.float32)
        share = lax.psum(jnp.stack((own_one, own_two)), ("video", "dp")) * factor
        share = share.astype(jnp.bfloat16)
        shares = [share, flipped(share, "section", 2)]
        shares += [flipped(share, "section", 1) for share in shares]
        sums = unpacked(placed(shares, [(0, None), (2, None), (1, None), (3, None)]))
    return (grad_in.reshape(shape), *sums)


def solution(mesh):
    whole = P("dp", "video", "section", None, None)
    return jax.shard_map(
        on_device,
        mesh=mesh,
        in_specs=(whole,) * 5 + (P(),) * 4,
        out_specs=(whole, P(), P(), P(), P()),
        check_vma=False,
    )
```

```python
import functools
import math

import jax
import jax.numpy as jnp
from jax import lax
from jax.experimental import pallas as pl
from jax.experimental.pallas import tpu as pltpu
from jax.sharding import PartitionSpec as P

MIB = 1024 * 1024


def sigmoid(value):
    return 1.0 / (1.0 + jnp.exp(-value))


def bf16(*shape):
    return jax.ShapeDtypeStruct(shape, jnp.bfloat16)


def f32(*shape):
    return jax.ShapeDtypeStruct(shape, jnp.float32)


def call(kernel, outs, scratch, flops, *operands, after=(), early=(), spare_inputs=False, limit=24):
    single = len(outs) == 1
    moved = sum(math.prod(x.shape) * x.dtype.itemsize for x in (*operands, *outs))
    vmem = pl.BlockSpec(memory_space=pltpu.VMEM)
    spare = pl.BlockSpec(memory_space=pl.ANY)
    spec = spare if spare_inputs else vmem
    count = len(operands)
    operands = (*operands, *early, *after)

    def body(*refs):
        kernel(*refs[:count], *refs[len(operands) :])

    return pl.pallas_call(
        body,
        out_shape=outs[0] if single else tuple(outs),
        in_specs=[spec] * count + [vmem] * len(early) + [spare] * len(after),
        out_specs=vmem if single else (vmem,) * len(outs),
        scratch_shapes=scratch,
        compiler_params=pltpu.CompilerParams(vmem_limit_bytes=limit * MIB),
        cost_estimate=pl.CostEstimate(
            flops=int(flops), bytes_accessed=int(moved) if flops else 0, transcendentals=0
        ),
    )(*operands)


def from_ahead(block, band_step, frame_step):
    bands, frames = lax.axis_size("section"), lax.axis_size("video")
    pairs = [
        ((band + band_step) * frames + frame + frame_step, band * frames + frame)
        for band in range(bands)
        for frame in range(frames)
        if 0 <= band + band_step < bands and frame + frame_step < frames
    ]
    return lax.ppermute(block, ("section", "video"), pairs)


def beside_band(pair_refs, row):
    band = lax.axis_index("section")
    odd = lax.rem(band, 2) == 1
    inside = (band > 0) & (band < lax.axis_size("section") - 1)
    first, second = (ref[row : row + 1] for ref in pair_refs)
    second = jnp.where(inside, second, jnp.zeros_like(second))
    return jnp.where(odd, first, second), jnp.where(odd, second, first)


def flipped(block, axis, flip):
    count = lax.axis_size(axis)
    return lax.ppermute(block, axis, [(place ^ flip, place) for place in range(count)])


def flipped_both(block):
    bands = lax.axis_size("section")
    pairs = [
        (2 * (band ^ 2) + 1 - frame, 2 * band + frame) for band in range(bands) for frame in range(2)
    ]
    return lax.ppermute(block, ("section", "video"), pairs)


def later_than(block, *others):
    return lax.optimization_barrier((block, *others))[0]


def beside(gpre, views_ref, start):
    count, cols, ch = gpre.shape
    at = lax.broadcasted_iota(jnp.int32, gpre.shape, 1)
    right = jnp.where(at == cols - 1, 0.0, pltpu.roll(gpre, cols - 1, 1))
    left = jnp.where(at == 0, 0.0, pltpu.roll(gpre, 1, 1))
    here = pl.ds(start, count)
    views_ref[here, :, 0:ch] = right.astype(jnp.bfloat16)
    views_ref[here, :, ch : 2 * ch] = gpre.astype(jnp.bfloat16)
    views_ref[here, :, 2 * ch : 3 * ch] = left.astype(jnp.bfloat16)


def pre_gradient(grads, preact, temporal_ref):
    count, cols, ch = preact.shape
    flat = jnp.concatenate([grad.reshape(count * cols, ch) for grad in grads], axis=1)
    kernel = jnp.concatenate([temporal_ref[2 - step] for step in range(len(grads))], axis=1)
    gact = lax.dot_general(
        flat, kernel, (((1,), (1,)), ((), ())), preferred_element_type=jnp.float32
    )
    gact = gact.astype(jnp.bfloat16).astype(jnp.float32).reshape(preact.shape)
    hval = preact.astype(jnp.float32)
    sig = sigmoid(hval)
    return gact * sig * (1.0 + hval * (1.0 - sig))


def convolved(views_ref, spatial_ref, start, first):
    count, cols, ch = first.shape
    total = first.astype(jnp.float32).reshape(count * cols, ch)
    for ky in range(3):
        view = views_ref[pl.ds(start + 2 - ky, count)].reshape(count * cols, 3 * ch)
        kernel = jnp.concatenate([spatial_ref[ky, kx] for kx in range(3)], axis=1)
        total = total + lax.dot_general(
            view, kernel, (((1,), (1,)), ((), ())), preferred_element_type=jnp.float32
        )
    return total.astype(jnp.bfloat16).reshape(first.shape)


def is_last():
    return lax.axis_index("video") == lax.axis_size("video") - 1


def left_sides(saved_ref, preact_ref, above, below, sides_ref):
    rows, cols, ch = saved_ref.shape
    flat = (rows * cols, ch)
    shifts = [
        jnp.concatenate([above, saved_ref[: rows - 1]], axis=0),
        saved_ref[...],
        jnp.concatenate([saved_ref[1:], below], axis=0),
    ]
    for n, shift in enumerate(shifts):
        sides_ref[n] = shift.reshape(flat).T
    hval = preact_ref[...].astype(jnp.float32)
    sides_ref[3] = (hval * sigmoid(hval)).astype(jnp.bfloat16).reshape(flat).T


def kernel_sums(sides_ref, grads, views, sums_ref):
    _, ch, pixels = sides_ref.shape
    shifts = sides_ref[0:3].reshape(3 * ch, pixels)
    sums = jnp.dot(shifts, views, preferred_element_type=jnp.float32)
    for ky in range(3):
        for kx in range(3):
            here = slice(kx * ch, (kx + 1) * ch)
            sums_ref[ky, here] = sums[ky * ch : (ky + 1) * ch, here]
    grads = jnp.concatenate([grad.reshape(pixels, ch) for grad in grads], axis=1)
    sums = jnp.dot(sides_ref[3], grads, preferred_element_type=jnp.float32)
    zeros = jnp.zeros((ch, ch), jnp.float32)
    for k in range(3):
        step = 2 - k
        value = sums[:, step * ch : (step + 1) * ch] if step * ch < grads.shape[1] else zeros
        sums_ref[3, k * ch : (k + 1) * ch] = jnp.where(is_last(), zeros, value) if step else value


def hand_out(sums_ref, keep_ref, *send_refs):
    odd = lax.rem(lax.axis_index("section"), 2)
    for n, send_ref in enumerate(send_refs):
        keep_ref[n] = sums_ref[2 * n + odd]
        send_ref[...] = sums_ref[2 * n + 1 - odd].astype(jnp.bfloat16)


def pack_kernel(*refs):
    parts, outs, sems = refs[:4], refs[4:6], refs[6]
    last = parts[0].shape[0] - 1
    odd = lax.rem(lax.axis_index("section"), 2)
    copies = []
    for n, part in enumerate(parts):
        for out, row in zip(outs, ((1 - odd) * last, odd * last)):
            sem = sems.at[len(copies)]
            copies.append(
                pltpu.make_async_copy(part.at[pl.ds(row, 1)], out.at[pl.ds(n, 1)], sem)
            )
    for copy in copies:
        copy.start()
    for copy in copies:
        copy.wait()


def interior(grad_ref, preact_ref, wholes, temporal_ref, spatial_ref, inner_ref, gpre_ref, views_ref):
    rows, cols, ch = grad_ref.shape
    step = 4

    for n in range(rows // step):
        here = pl.ds(n * step, step)
        grads = [ref[here] for ref in (grad_ref, *wholes)]
        gpre = pre_gradient(grads, preact_ref[here], temporal_ref)
        gpre_ref[here] = gpre.astype(jnp.bfloat16)
        beside(gpre, views_ref, n * step)

    half = rows // 2 - 1

    for n in range(2):
        first = grad_ref[pl.ds(n * half + 1, half)]
        inner_ref[pl.ds(n * half, half)] = convolved(views_ref, spatial_ref, n * half, first)


def edge_rows(grad_ref, pair_refs, afters, gpre_ref, temporal_ref, spatial_ref, views_ref):
    rows, cols, ch = grad_ref.shape
    (grad_above, grad_below), (above_pre, below_pre) = (beside_band(pair_refs, n) for n in (0, 1))
    above = [grad_above] + [ref[0:1] for ref in afters]
    below = [grad_below] + [ref[1:2] for ref in afters]
    beside(pre_gradient(above, above_pre, temporal_ref), views_ref, 0)
    beside(gpre_ref[0:2].astype(jnp.float32), views_ref, 1)
    beside(gpre_ref[rows - 2 : rows].astype(jnp.float32), views_ref, 3)
    beside(pre_gradient(below, below_pre, temporal_ref), views_ref, 5)
    return (
        convolved(views_ref, spatial_ref, 0, grad_ref[0:1]),
        convolved(views_ref, spatial_ref, 3, grad_ref[rows - 1 : rows]),
    )


def last_inner_kernel(grad_ref, preact_ref, temporal_ref, spatial_ref, inner_ref, gpre_ref, views_ref):
    @pl.when(is_last())
    def _():
        interior(
            grad_ref, preact_ref, [], temporal_ref, spatial_ref, inner_ref, gpre_ref, views_ref
        )


def last_edge_kernel(grad_ref, one_ref, two_ref, gpre_ref, temporal_ref, spatial_ref, edge_ref, views_ref):
    @pl.when(is_last())
    def _():
        pair_refs = (one_ref, two_ref)
        edge_ref[0:1], edge_ref[1:2] = edge_rows(
            grad_ref, pair_refs, [], gpre_ref, temporal_ref, spatial_ref, views_ref
        )
        edge_ref[2:3], edge_ref[3:4] = beside_band(pair_refs, 0)


def inner_kernel(later, *refs):
    inputs, wholes, kernels = refs[:2], refs[2 : 2 + later], refs[2 + later : 4 + later]
    known, outs = refs[4 + later : -3], refs[-3:]
    if not known:
        interior(*inputs, wholes, *kernels, *outs)
        return

    @pl.when(is_last())
    def _():
        outs[0][...] = known[0][...]
        outs[1][...] = known[1][...]

    @pl.when(jnp.logical_not(is_last()))
    def _():
        interior(*inputs, wholes, *kernels, *outs)


def mid_kernel(later, *refs):
    grad_ref, inner_ref, gpre_ref = refs[0], refs[3], refs[4]
    afters, (temporal_ref, spatial_ref, mid_ref, views_ref) = refs[5 : 5 + later], refs[5 + later :]
    rows = grad_ref.shape[0]
    first, last = edge_rows(
        grad_ref, refs[1:3], afters, gpre_ref, temporal_ref, spatial_ref, views_ref
    )
    mid_ref[0:1], mid_ref[rows - 1 : rows] = first, last
    mid_ref[1 : rows - 1] = inner_ref[...]


def two_kernel(later, *refs):
    saved_ref, preact_ref, gpre_ref = refs[:3]
    pair_refs, grad_ref = refs[3:5], refs[5]
    wholes, outs = refs[6 : 6 + later], refs[6 + later : 9 + later]
    views_ref, sides_ref, sums_ref = refs[9 + later :]
    rows, cols, ch = saved_ref.shape
    step = 4

    for n in range(rows // step):
        here = pl.ds(n * step, step)
        beside(gpre_ref[here].astype(jnp.float32), views_ref, n * step)

    views = views_ref[...].reshape(rows * cols, 3 * ch)
    grads = [ref[...] for ref in (grad_ref, *wholes)]
    left_sides(saved_ref, preact_ref, *beside_band(pair_refs, 2), sides_ref)
    kernel_sums(sides_ref, grads, views, sums_ref)
    hand_out(sums_ref, *outs)


def sides_kernel(saved_ref, preact_ref, one_ref, two_ref, sides_ref):
    left_sides(saved_ref, preact_ref, *beside_band((one_ref, two_ref), 3), sides_ref)


def pre_rows(preact, mids, temporal_ref, gpre_ref, views_ref, start):
    gpre = pre_gradient(mids, preact, temporal_ref)
    gpre_ref[start : start + preact.shape[0]] = gpre.astype(jnp.bfloat16)
    beside(gpre, views_ref, start)


def block_sums(gpre_ref, sides_ref, mids, views_ref, sums_ref, keep_ref, send_ref):
    rows, cols, ch = gpre_ref.shape
    odd = lax.rem(lax.axis_index("section"), 2)
    size = send_ref.shape[0] - 2 * cols
    send_ref[size : size + cols] = gpre_ref[(1 - odd) * (rows - 1)]
    send_ref[size + cols : size + 2 * cols] = gpre_ref[odd * (rows - 1)]
    views = views_ref[...].reshape(rows * cols, 3 * ch)
    kernel_sums(sides_ref, [ref[...] for ref in mids], views, sums_ref)
    height = sums_ref.shape[1]
    hand_out(sums_ref, keep_ref, send_ref.at[:height], send_ref.at[height : 2 * height])


def one_kernel(later, *refs):
    sides_ref, preact_ref, mids = refs[0], refs[1], refs[2 : 3 + later]
    temporal_ref, outs, scratch = refs[3 + later], refs[4 + later : 7 + later], refs[7 + later :]
    gpre_ref, keep_ref, send_ref = outs
    views_ref, sums_ref = scratch
    for n in range(preact_ref.shape[0] // 4):
        here = slice(4 * n, 4 * n + 4)
        grads = [ref[here] for ref in mids]
        pre_rows(preact_ref[here], grads, temporal_ref, gpre_ref, views_ref, 4 * n)
    block_sums(gpre_ref, sides_ref, mids, views_ref, sums_ref, keep_ref, send_ref)


def one_inner_kernel(preact_ref, inner_ref, after_ref, temporal_ref, gpre_ref, views_ref):
    rows = inner_ref.shape[0]
    for n in range(rows // 7):
        here = slice(7 * n, 7 * n + 7)
        after = after_ref[here]
        after = jnp.where(is_last(), jnp.zeros_like(after), after)
        preact = preact_ref[7 * n + 1 : 7 * n + 8]
        pre_rows(preact, [inner_ref[here], after], temporal_ref, gpre_ref, views_ref, 7 * n)


def mid_one_kernel(*refs):
    after_inner_ref, after_edge_ref = refs[5:7]
    temporal_two_ref, spatial_two_ref, sides_ref, preact_ref, temporal_ref = refs[7:12]
    inner_gpre_ref, inner_views_ref = refs[12:14]
    mid_ref, gpre_ref, keep_ref, send_ref = refs[14:18]
    views_ref, sums_ref, next_ref, edge_ref, edge_views_ref = refs[18:]
    rows = next_ref.shape[0]

    @pl.when(is_last())
    def _():
        edge_ref[...] = jnp.zeros(edge_ref.shape, edge_ref.dtype)
        next_ref[...] = jnp.zeros(next_ref.shape, next_ref.dtype)

    @pl.when(jnp.logical_not(is_last()))
    def _():
        edge_ref[...] = after_edge_ref[2:4]
        next_ref[0:1] = after_edge_ref[0:1]
        next_ref[1 : rows - 1] = after_inner_ref[...]
        next_ref[rows - 1 : rows] = after_edge_ref[1:2]

    mid_kernel(
        1, *refs[:5], edge_ref, temporal_two_ref, spatial_two_ref, mid_ref, edge_views_ref
    )
    gpre_ref[1 : rows - 1] = inner_gpre_ref[...]
    views_ref[1 : rows - 1] = inner_views_ref[...]
    for row in (0, rows - 1):
        here = slice(row, row + 1)
        grads = [mid_ref[here], next_ref[here]]
        pre_rows(preact_ref[here], grads, temporal_ref, gpre_ref, views_ref, row)
    block_sums(gpre_ref, sides_ref, [mid_ref, next_ref], views_ref, sums_ref, keep_ref, send_ref)


def input_kernel(mid_ref, gpre_ref, pair_ref, across_ref, spatial_ref, out_ref, token_ref, views_ref):
    rows, cols, ch = out_ref.shape
    pair = pair_ref[pair_ref.shape[0] - 2 * cols : pair_ref.shape[0] - cols]
    above, below = beside_band((pair[None], across_ref[across_ref.shape[0] - cols :][None]), 0)
    token_ref[...] = jnp.zeros(token_ref.shape, token_ref.dtype)
    step = 4
    beside(above.astype(jnp.float32), views_ref, 0)
    beside(below.astype(jnp.float32), views_ref, rows + 1)

    for n in range(rows // step):
        gpre = gpre_ref[pl.ds(n * step, step)].astype(jnp.float32)
        beside(gpre, views_ref, n * step + 1)

    for n in range(rows // step):
        here = pl.ds(n * step, step)
        out_ref[here] = convolved(views_ref, spatial_ref, n * step, mid_ref[here])


def halves(count, index):
    return [pl.ds(pl.multiple_of(n * count, count), count) for n in (index, 1 - index)]


def pair_kernel(keep_ref, low_ref, high_ref, own_ref, send_ref):
    across = lax.axis_index("section") // 2
    parts = [ref[...].astype(jnp.float32) for ref in (low_ref, high_ref)]
    own_ref[...] = keep_ref[across] + jnp.where(across == 0, *parts)
    total = keep_ref[1 - across] + jnp.where(across == 0, *parts[::-1])
    send_ref[...] = total.astype(jnp.bfloat16)


def band_kernel(own_ref, part_ref, keep_ref, send_ref):
    mine, other = halves(keep_ref.shape[0], lax.axis_index("video"))
    half = keep_ref.shape[0]
    keep_ref[...] = own_ref[mine] + part_ref[mine].astype(jnp.float32)
    send_ref[:half] = (own_ref[other] + part_ref[other].astype(jnp.float32)).astype(jnp.bfloat16)


def pair_quarter_kernel(keep_ref, part_ref, own_ref, across_ref, frame_ref, both_ref):
    _, height, _ = keep_ref.shape
    half = own_ref.shape[0]
    band = lax.axis_index("section") // 2
    frames = halves(half, lax.axis_index("video"))

    def quarter(band, rows):
        start = pl.multiple_of(band * height, height)
        part = part_ref.at[pl.ds(start, height)][rows]
        return keep_ref[band, rows] + part.astype(jnp.float32)

    own_ref[...] = quarter(band, frames[0])
    across_ref[:half] = quarter(1 - band, frames[0]).astype(jnp.bfloat16)
    rest = across_ref.shape[0] - half
    across_ref[half:] = part_ref[2 * height + rest :]
    frame_ref[...] = quarter(band, frames[1]).astype(jnp.bfloat16)
    both_ref[...] = quarter(1 - band, frames[1]).astype(jnp.bfloat16)


def plane_kernel(own_ref, *refs):
    parts, out_ref = refs[:-1], refs[-1]
    total = own_ref[...]
    for part in parts:
        total = total + part[: out_ref.shape[0]].astype(jnp.float32)
    out_ref[...] = total.astype(jnp.bfloat16)


def add_kernel(one_ref, two_ref, out_ref):
    total = one_ref[...].astype(jnp.float32) + two_ref[: one_ref.shape[0]].astype(jnp.float32)
    out_ref[...] = total.astype(jnp.bfloat16)


def scaled_kernel(factor, *refs):
    out_ref = refs[-1]
    for block in range(2):
        one, two = (ref[...].astype(jnp.float32) for ref in refs[2 * block : 2 * block + 2])
        out_ref[block] = ((one + two) * factor).astype(jnp.bfloat16)


def place_kernel(places, *refs):
    shares, outs = refs[: len(places)], refs[-6:-2]
    sums_ref, sems = refs[-2:]
    band, frame = lax.axis_index("section"), lax.axis_index("video")
    height = shares[0].shape[1]

    def copies(n, block):
        flip, other = places[n]
        place = jnp.bitwise_xor(band, flip)
        half = 0 if other is None else jnp.bitwise_xor(frame, int(other))
        here = pl.ds(pl.multiple_of(half * height, height), height)
        spatial, temporal = outs[2 * block : 2 * block + 2]
        source, sem = sums_ref.at[n, block], sems.at[n, block]
        return (
            (place < 3, lambda: pltpu.make_async_copy(source, spatial.at[place, here], sem)),
            (place == 3, lambda: pltpu.make_async_copy(source, temporal.at[here], sem)),
        )

    for n, share in enumerate(shares):
        for block in range(2):
            sums_ref[n, block] = share[block].astype(jnp.float32)
            for inside, copy in copies(n, block):
                pl.when(inside)(lambda: copy().start())
    for n in range(len(shares)):
        for block in range(2):
            for inside, copy in copies(n, block):
                pl.when(inside)(lambda: copy().wait())


def placed(shares, places, given=()):
    _, height, ch = shares[0].shape
    count = len(shares)
    outs = (f32(3, 3 * ch, ch), f32(3 * ch, ch)) * 2
    vmem, spare = (pl.BlockSpec(memory_space=space) for space in (pltpu.VMEM, pl.ANY))
    return pl.pallas_call(
        functools.partial(place_kernel, places),
        out_shape=outs,
        in_specs=[vmem] * count + [spare] * len(given),
        out_specs=(spare,) * 4,
        scratch_shapes=[
            pltpu.VMEM((count, 2, height, ch), jnp.float32),
            pltpu.SemaphoreType.DMA((count, 2)),
        ],
        input_output_aliases={count + n: n for n in range(len(given))},
        compiler_params=pltpu.CompilerParams(vmem_limit_bytes=24 * MIB),
        cost_estimate=pl.CostEstimate(
            flops=0, bytes_accessed=6 * count * height * ch * 2, transcendentals=0
        ),
    )(*shares, *given)


def unpacked(sums):
    ch = sums[0].shape[-1]
    return [x.reshape(3, 3, ch, ch) if x.ndim == 3 else x.reshape(3, ch, ch) for x in sums]


def on_device(
    grad_latent,
    input_one,
    preact_one,
    input_two,
    preact_two,
    spatial_one,
    temporal_one,
    spatial_two,
    temporal_two,
):
    shape = grad_latent.shape
    rows, cols, ch = shape[2:]
    bands, frames = lax.axis_size("section"), lax.axis_size("video")
    later = min(2, frames - 1)
    pixels = lax.axis_size("dp") * frames * bands * rows * cols
    factor = 1.0 / math.sqrt(pixels)
    grad, saved_one, pre_one, saved_two, pre_two = (
        x.reshape(rows, cols, ch)
        for x in (grad_latent, input_one, preact_one, input_two, preact_two)
    )
    conv = 2 * rows * cols * 9 * ch * ch
    views = pltpu.VMEM((rows, cols, 3 * ch), jnp.bfloat16)
    edge_views = pltpu.VMEM((6, cols, 3 * ch), jnp.bfloat16)
    act = pltpu.VMEM((rows, cols, ch), jnp.bfloat16)
    sides = bf16(4, ch, rows * cols)
    sums = pltpu.VMEM((4, 3 * ch, ch), jnp.float32)
    handed = [f32(2, 3 * ch, ch)] + [bf16(3 * ch, ch)] * 2
    inner_outs = [bf16(rows - 2, cols, ch), bf16(rows, cols, ch)]
    kernels = (temporal_two, spatial_two)

    def from_later(x):
        if frames == 2:
            return [flipped(x, "video", 1)]
        return [from_ahead(x, 0, n + 1) for n in range(later)]

    wholes = from_later(grad)
    packs = call(
        pack_kernel,
        [bf16(4, cols, ch)] * 2,
        [pltpu.SemaphoreType.DMA((8,))],
        1,
        grad,
        pre_two,
        saved_two,
        saved_one,
        spare_inputs=True,
        limit=58,
    )
    second = flipped(packs[1], "section", 1)
    first = flipped(later_than(packs[0], second), "section", 1)
    pairs = [first, flipped(second, "section", 2)]

    known = ()
    if frames == 2:
        known = call(
            last_inner_kernel,
            inner_outs,
            [views],
            0,
            grad,
            pre_two,
            *kernels,
            after=(first, second),
        )
        afters = from_later(known[0])
    else:
        afters = from_later(jnp.concatenate(beside_band(pairs, 0)))
    inner, gpre_two = call(
        functools.partial(inner_kernel, later),
        inner_outs,
        [views],
        0,
        grad,
        pre_two,
        *wholes,
        *kernels,
        *known,
        early=(saved_two, saved_one, pre_one, temporal_one),
    )
    if frames == 2:
        edge = call(
            last_edge_kernel,
            [bf16(4, cols, ch)],
            [edge_views],
            0,
            grad,
            *pairs,
            known[1],
            *kernels,
            after=(gpre_two,),
        )
        afters += from_later(edge)
    parts_two = call(
        functools.partial(two_kernel, later),
        handed,
        [views, pltpu.VMEM(sides.shape, sides.dtype), sums],
        8 * conv,
        saved_two,
        pre_two,
        gpre_two,
        *pairs,
        grad,
        *wholes,
        after=(edge,) if frames == 2 else (),
    )
    sides_one = call(
        sides_kernel, [sides], [], conv // 8, saved_one, pre_one, *pairs, after=parts_two[:1]
    )
    height, half = 3 * ch, 3 * ch // 2
    keep_two, low_two, high_two = parts_two
    own_two, send_two = call(
        pair_kernel,
        [f32(height, ch), bf16(height, ch)],
        [],
        height * ch,
        keep_two,
        flipped(low_two, "section", 1),
        flipped(high_two, "section", 1),
    )
    across_two = flipped(send_two, "section", 2)
    mid_inputs = (grad, *pairs, inner, gpre_two)
    one_inputs = (sides_one, pre_one)
    mid_outs = [bf16(rows, cols, ch)]
    one_outs = [bf16(rows, cols, ch), f32(2, 3 * ch, ch), bf16(6 * ch + 2 * cols, ch)]
    if frames == 2:
        inners_one = call(
            one_inner_kernel,
            [bf16(rows - 2, cols, ch), bf16(rows - 2, cols, 3 * ch)],
            [],
            conv // 8,
            pre_one,
            inner,
            afters[0],
            temporal_one,
        )
        mid, gpre_one, *parts_one = call(
            mid_one_kernel,
            mid_outs + one_outs,
            [views, sums, act, pltpu.VMEM((2, cols, ch), jnp.bfloat16), edge_views],
            8 * conv,
            *mid_inputs,
            *afters,
            *kernels,
            *one_inputs,
            temporal_one,
            *inners_one,
            after=(own_two,),
        )
    else:
        mid = call(
            functools.partial(mid_kernel, later),
            mid_outs,
            [edge_views],
            conv // 8,
            *mid_inputs,
            *afters,
            *kernels,
        )
        gpre_one, *parts_one = call(
            functools.partial(one_kernel, later),
            one_outs,
            [views, sums],
            1.2 * conv,
            *one_inputs,
            mid,
            *from_later(mid),
            temporal_one,
        )
    keep_one, send_one = parts_one
    split = frames == 2 and lax.axis_size("dp") == 4
    if split:
        send_one = later_than(send_one, across_two)
    pair_one = flipped(send_one, "section", 1)

    def input_gradient(edge, after):
        return call(
            input_kernel,
            [bf16(rows, cols, ch), f32(8, 128)],
            [pltpu.VMEM((rows + 2, cols, 3 * ch), jnp.bfloat16)],
            conv,
            mid,
            gpre_one,
            pair_one,
            edge,
            spatial_one,
            after=after,
        )

    if split:

        def added(one, two):
            return call(add_kernel, [bf16(half, ch)], [], half * ch, one, two)

        keep_two, send_two = call(
            band_kernel,
            [f32(half, ch), bf16(half + cols + 16, ch)],
            [],
            0,
            own_two,
            across_two,
        )
        sum_two = added(keep_two, flipped(send_two, "video", 1))
        quarters = [f32(half, ch), bf16(half + cols, ch)] + [bf16(half, ch)] * 2
        own_one, *sends = call(
            pair_quarter_kernel, quarters, [], 0, keep_one, pair_one, after=(send_two,)
        )
        across = flipped(sends[0], "section", 2)
        parts = [across, flipped(sends[1], "video", 1), flipped_both(sends[2])]
        sum_one = call(plane_kernel, [bf16(half, ch)], [], 4 * half * ch, own_one, *parts)
        part_two = flipped(sum_two, "dp", 1)
        part_one = flipped(later_than(sum_one, sum_two), "dp", 1)
        sum_two = added(sum_two, part_two)
        sum_one = added(sum_one, part_one)
        last_two = flipped(sum_two, "dp", 2)
        last_one = flipped(later_than(sum_one, sum_two), "dp", 2)
        grad_in, token = input_gradient(across, (sum_one,))
        own = call(
            functools.partial(scaled_kernel, factor),
            [bf16(2, half, ch)],
            [],
            height * ch,
            sum_one,
            last_one,
            sum_two,
            last_two,
            after=(token,),
        )
        frame, across, both = flipped(own, "video", 1), flipped(own, "section", 2), flipped_both(own)
        shares = [own, frame, across]
        shares += [flipped(share, "section", 1) for share in shares]
        places = [(0, False), (0, True), (2, False), (1, False), (1, True), (3, False)]
        sums = placed([*shares, both], [*places, (2, True)])
        sums = unpacked(placed([flipped(both, "section", 1)], [(3, True)], sums))
    else:
        own_one, send_one = call(
            pair_kernel,
            [f32(height, ch), bf16(height, ch)],
            [],
            height * ch,
            keep_one,
            pair_one[:height],
            pair_one[height : 2 * height],
        )
        edge = flipped(pair_one[pair_one.shape[0] - cols :], "section", 2)
        grad_in, _ = input_gradient(edge, ())
        own_one = own_one + flipped(send_one, "section", 2).astype(jnp.float32)
        own_two = own_two + across_two.astype(jnp.float32)
        share = lax.psum(jnp.stack((own_one, own_two)), ("video", "dp")) * factor
        share = share.astype(jnp.bfloat16)
        shares = [share, flipped(share, "section", 2)]
        shares += [flipped(share, "section", 1) for share in shares]
        sums = unpacked(placed(shares, [(0, None), (2, None), (1, None), (3, None)]))
    return (grad_in.reshape(shape), *sums)


def solution(mesh):
    whole = P("dp", "video", "section", None, None)
    return jax.shard_map(
        on_device,
        mesh=mesh,
        in_specs=(whole,) * 5 + (P(),) * 4,
        out_specs=(whole, P(), P(), P(), P()),
        check_vma=False,
    )
```

```python
import functools
import math

import jax
import jax.numpy as jnp
from jax import lax
from jax.experimental import pallas as pl
from jax.experimental.pallas import tpu as pltpu
from jax.sharding import PartitionSpec as P

MIB = 1024 * 1024


def sigmoid(value):
    return 1.0 / (1.0 + jnp.exp(-value))


def bf16(*shape):
    return jax.ShapeDtypeStruct(shape, jnp.bfloat16)


def f32(*shape):
    return jax.ShapeDtypeStruct(shape, jnp.float32)


def call(kernel, outs, scratch, flops, *operands, after=(), early=(), spare_inputs=False, limit=24):
    single = len(outs) == 1
    moved = sum(math.prod(x.shape) * x.dtype.itemsize for x in (*operands, *outs))
    vmem = pl.BlockSpec(memory_space=pltpu.VMEM)
    spare = pl.BlockSpec(memory_space=pl.ANY)
    spec = spare if spare_inputs else vmem
    count = len(operands)
    operands = (*operands, *early, *after)

    def body(*refs):
        kernel(*refs[:count], *refs[len(operands) :])

    return pl.pallas_call(
        body,
        out_shape=outs[0] if single else tuple(outs),
        in_specs=[spec] * count + [vmem] * len(early) + [spare] * len(after),
        out_specs=vmem if single else (vmem,) * len(outs),
        scratch_shapes=scratch,
        compiler_params=pltpu.CompilerParams(vmem_limit_bytes=limit * MIB),
        cost_estimate=pl.CostEstimate(
            flops=int(flops), bytes_accessed=int(moved) if flops else 0, transcendentals=0
        ),
    )(*operands)


def from_ahead(block, band_step, frame_step):
    bands, frames = lax.axis_size("section"), lax.axis_size("video")
    pairs = [
        ((band + band_step) * frames + frame + frame_step, band * frames + frame)
        for band in range(bands)
        for frame in range(frames)
        if 0 <= band + band_step < bands and frame + frame_step < frames
    ]
    return lax.ppermute(block, ("section", "video"), pairs)


def beside_band(pair_refs, row):
    band = lax.axis_index("section")
    odd = lax.rem(band, 2) == 1
    inside = (band > 0) & (band < lax.axis_size("section") - 1)
    first, second = (ref[row : row + 1] for ref in pair_refs)
    second = jnp.where(inside, second, jnp.zeros_like(second))
    return jnp.where(odd, first, second), jnp.where(odd, second, first)


def flipped(block, axis, flip):
    count = lax.axis_size(axis)
    return lax.ppermute(block, axis, [(place ^ flip, place) for place in range(count)])


def flipped_both(block):
    bands = lax.axis_size("section")
    pairs = [
        (2 * (band ^ 2) + 1 - frame, 2 * band + frame) for band in range(bands) for frame in range(2)
    ]
    return lax.ppermute(block, ("section", "video"), pairs)


def later_than(block, *others):
    return lax.optimization_barrier((block, *others))[0]


def beside(gpre, views_ref, start):
    count, cols, ch = gpre.shape
    at = lax.broadcasted_iota(jnp.int32, gpre.shape, 1)
    right = jnp.where(at == cols - 1, 0.0, pltpu.roll(gpre, cols - 1, 1))
    left = jnp.where(at == 0, 0.0, pltpu.roll(gpre, 1, 1))
    here = pl.ds(start, count)
    views_ref[here, :, 0:ch] = right.astype(jnp.bfloat16)
    views_ref[here, :, ch : 2 * ch] = gpre.astype(jnp.bfloat16)
    views_ref[here, :, 2 * ch : 3 * ch] = left.astype(jnp.bfloat16)


def pre_gradient(grads, preact, temporal_ref):
    count, cols, ch = preact.shape
    flat = jnp.concatenate([grad.reshape(count * cols, ch) for grad in grads], axis=1)
    kernel = jnp.concatenate([temporal_ref[2 - step] for step in range(len(grads))], axis=1)
    gact = lax.dot_general(
        flat, kernel, (((1,), (1,)), ((), ())), preferred_element_type=jnp.float32
    )
    gact = gact.astype(jnp.bfloat16).astype(jnp.float32).reshape(preact.shape)
    hval = preact.astype(jnp.float32)
    sig = sigmoid(hval)
    return gact * sig * (1.0 + hval * (1.0 - sig))


def convolved(views_ref, spatial_ref, start, first):
    count, cols, ch = first.shape
    total = first.astype(jnp.float32).reshape(count * cols, ch)
    for ky in range(3):
        view = views_ref[pl.ds(start + 2 - ky, count)].reshape(count * cols, 3 * ch)
        kernel = jnp.concatenate([spatial_ref[ky, kx] for kx in range(3)], axis=1)
        total = total + lax.dot_general(
            view, kernel, (((1,), (1,)), ((), ())), preferred_element_type=jnp.float32
        )
    return total.astype(jnp.bfloat16).reshape(first.shape)


def is_last():
    return lax.axis_index("video") == lax.axis_size("video") - 1


def left_sides(saved_ref, preact_ref, above, below, sides_ref):
    rows, cols, ch = saved_ref.shape
    flat = (rows * cols, ch)
    shifts = [
        jnp.concatenate([above, saved_ref[: rows - 1]], axis=0),
        saved_ref[...],
        jnp.concatenate([saved_ref[1:], below], axis=0),
    ]
    for n, shift in enumerate(shifts):
        sides_ref[n] = shift.reshape(flat).T
    hval = preact_ref[...].astype(jnp.float32)
    sides_ref[3] = (hval * sigmoid(hval)).astype(jnp.bfloat16).reshape(flat).T


def kernel_sums(sides_ref, grads, views, sums_ref):
    _, ch, pixels = sides_ref.shape
    shifts = sides_ref[0:3].reshape(3 * ch, pixels)
    sums = jnp.dot(shifts, views, preferred_element_type=jnp.float32)
    for ky in range(3):
        for kx in range(3):
            here = slice(kx * ch, (kx + 1) * ch)
            sums_ref[ky, here] = sums[ky * ch : (ky + 1) * ch, here]
    grads = jnp.concatenate([grad.reshape(pixels, ch) for grad in grads], axis=1)
    sums = jnp.dot(sides_ref[3], grads, preferred_element_type=jnp.float32)
    zeros = jnp.zeros((ch, ch), jnp.float32)
    for k in range(3):
        step = 2 - k
        value = sums[:, step * ch : (step + 1) * ch] if step * ch < grads.shape[1] else zeros
        sums_ref[3, k * ch : (k + 1) * ch] = jnp.where(is_last(), zeros, value) if step else value


def hand_out(sums_ref, keep_ref, *send_refs):
    odd = lax.rem(lax.axis_index("section"), 2)
    for n, send_ref in enumerate(send_refs):
        keep_ref[n] = sums_ref[2 * n + odd]
        send_ref[...] = sums_ref[2 * n + 1 - odd].astype(jnp.bfloat16)


def pack_kernel(*refs):
    parts, outs, sems = refs[:4], refs[4:6], refs[6]
    last = parts[0].shape[0] - 1
    odd = lax.rem(lax.axis_index("section"), 2)
    copies = []
    for n, part in enumerate(parts):
        for out, row in zip(outs, ((1 - odd) * last, odd * last)):
            sem = sems.at[len(copies)]
            copies.append(
                pltpu.make_async_copy(part.at[pl.ds(row, 1)], out.at[pl.ds(n, 1)], sem)
            )
    for copy in copies:
        copy.start()
    for copy in copies:
        copy.wait()


def interior(grad_ref, preact_ref, wholes, temporal_ref, spatial_ref, inner_ref, gpre_ref, views_ref):
    rows, cols, ch = grad_ref.shape
    step = 4

    for n in range(rows // step):
        here = pl.ds(n * step, step)
        grads = [ref[here] for ref in (grad_ref, *wholes)]
        gpre = pre_gradient(grads, preact_ref[here], temporal_ref)
        gpre_ref[here] = gpre.astype(jnp.bfloat16)
        beside(gpre, views_ref, n * step)

    half = rows // 2 - 1

    for n in range(2):
        first = grad_ref[pl.ds(n * half + 1, half)]
        inner_ref[pl.ds(n * half, half)] = convolved(views_ref, spatial_ref, n * half, first)


def edge_rows(grad_ref, pair_refs, afters, gpre_ref, temporal_ref, spatial_ref, views_ref):
    rows, cols, ch = grad_ref.shape
    (grad_above, grad_below), (above_pre, below_pre) = (beside_band(pair_refs, n) for n in (0, 1))
    above = [grad_above] + [ref[0:1] for ref in afters]
    below = [grad_below] + [ref[1:2] for ref in afters]
    beside(pre_gradient(above, above_pre, temporal_ref), views_ref, 0)
    beside(gpre_ref[0:2].astype(jnp.float32), views_ref, 1)
    beside(gpre_ref[rows - 2 : rows].astype(jnp.float32), views_ref, 3)
    beside(pre_gradient(below, below_pre, temporal_ref), views_ref, 5)
    return (
        convolved(views_ref, spatial_ref, 0, grad_ref[0:1]),
        convolved(views_ref, spatial_ref, 3, grad_ref[rows - 1 : rows]),
    )


def last_inner_kernel(grad_ref, preact_ref, temporal_ref, spatial_ref, inner_ref, gpre_ref, views_ref):
    @pl.when(is_last())
    def _():
        interior(
            grad_ref, preact_ref, [], temporal_ref, spatial_ref, inner_ref, gpre_ref, views_ref
        )


def last_edge_kernel(grad_ref, one_ref, two_ref, gpre_ref, temporal_ref, spatial_ref, edge_ref, views_ref):
    @pl.when(is_last())
    def _():
        pair_refs = (one_ref, two_ref)
        edge_ref[0:1], edge_ref[1:2] = edge_rows(
            grad_ref, pair_refs, [], gpre_ref, temporal_ref, spatial_ref, views_ref
        )
        edge_ref[2:3], edge_ref[3:4] = beside_band(pair_refs, 0)


def inner_kernel(later, *refs):
    inputs, wholes, kernels = refs[:2], refs[2 : 2 + later], refs[2 + later : 4 + later]
    known, outs = refs[4 + later : -3], refs[-3:]
    if not known:
        interior(*inputs, wholes, *kernels, *outs)
        return

    @pl.when(is_last())
    def _():
        outs[0][...] = known[0][...]
        outs[1][...] = known[1][...]

    @pl.when(jnp.logical_not(is_last()))
    def _():
        interior(*inputs, wholes, *kernels, *outs)


def mid_kernel(later, *refs):
    grad_ref, inner_ref, gpre_ref = refs[0], refs[3], refs[4]
    afters, (temporal_ref, spatial_ref, mid_ref, views_ref) = refs[5 : 5 + later], refs[5 + later :]
    rows = grad_ref.shape[0]
    first, last = edge_rows(
        grad_ref, refs[1:3], afters, gpre_ref, temporal_ref, spatial_ref, views_ref
    )
    mid_ref[0:1], mid_ref[rows - 1 : rows] = first, last
    mid_ref[1 : rows - 1] = inner_ref[...]


def two_kernel(later, *refs):
    saved_ref, preact_ref, gpre_ref = refs[:3]
    pair_refs, grad_ref = refs[3:5], refs[5]
    wholes, outs = refs[6 : 6 + later], refs[6 + later : 9 + later]
    views_ref, sides_ref, sums_ref = refs[9 + later :]
    rows, cols, ch = saved_ref.shape
    step = 4

    for n in range(rows // step):
        here = pl.ds(n * step, step)
        beside(gpre_ref[here].astype(jnp.float32), views_ref, n * step)

    views = views_ref[...].reshape(rows * cols, 3 * ch)
    grads = [ref[...] for ref in (grad_ref, *wholes)]
    left_sides(saved_ref, preact_ref, *beside_band(pair_refs, 2), sides_ref)
    kernel_sums(sides_ref, grads, views, sums_ref)
    hand_out(sums_ref, *outs)


def sides_kernel(saved_ref, preact_ref, one_ref, two_ref, sides_ref):
    left_sides(saved_ref, preact_ref, *beside_band((one_ref, two_ref), 3), sides_ref)


def pre_rows(preact, mids, temporal_ref, gpre_ref, views_ref, start):
    gpre = pre_gradient(mids, preact, temporal_ref)
    gpre_ref[start : start + preact.shape[0]] = gpre.astype(jnp.bfloat16)
    beside(gpre, views_ref, start)


def block_sums(gpre_ref, sides_ref, mids, views_ref, sums_ref, keep_ref, send_ref):
    rows, cols, ch = gpre_ref.shape
    odd = lax.rem(lax.axis_index("section"), 2)
    size = send_ref.shape[0] - 2 * cols
    send_ref[size : size + cols] = gpre_ref[(1 - odd) * (rows - 1)]
    send_ref[size + cols : size + 2 * cols] = gpre_ref[odd * (rows - 1)]
    views = views_ref[...].reshape(rows * cols, 3 * ch)
    kernel_sums(sides_ref, [ref[...] for ref in mids], views, sums_ref)
    height = sums_ref.shape[1]
    hand_out(sums_ref, keep_ref, send_ref.at[:height], send_ref.at[height : 2 * height])


def one_kernel(later, *refs):
    sides_ref, preact_ref, mids = refs[0], refs[1], refs[2 : 3 + later]
    temporal_ref, outs, scratch = refs[3 + later], refs[4 + later : 7 + later], refs[7 + later :]
    gpre_ref, keep_ref, send_ref = outs
    views_ref, sums_ref = scratch
    for n in range(preact_ref.shape[0] // 4):
        here = slice(4 * n, 4 * n + 4)
        grads = [ref[here] for ref in mids]
        pre_rows(preact_ref[here], grads, temporal_ref, gpre_ref, views_ref, 4 * n)
    block_sums(gpre_ref, sides_ref, mids, views_ref, sums_ref, keep_ref, send_ref)


def one_inner_kernel(preact_ref, inner_ref, after_ref, temporal_ref, gpre_ref, views_ref):
    rows = inner_ref.shape[0]
    for n in range(rows // 7):
        here = slice(7 * n, 7 * n + 7)
        after = after_ref[here]
        after = jnp.where(is_last(), jnp.zeros_like(after), after)
        preact = preact_ref[7 * n + 1 : 7 * n + 8]
        pre_rows(preact, [inner_ref[here], after], temporal_ref, gpre_ref, views_ref, 7 * n)


def mid_one_kernel(*refs):
    after_inner_ref, after_edge_ref = refs[5:7]
    temporal_two_ref, spatial_two_ref, sides_ref, preact_ref, temporal_ref = refs[7:12]
    inner_gpre_ref, inner_views_ref = refs[12:14]
    mid_ref, gpre_ref, keep_ref, send_ref = refs[14:18]
    views_ref, sums_ref, next_ref, edge_ref, edge_views_ref = refs[18:]
    rows = next_ref.shape[0]

    @pl.when(is_last())
    def _():
        edge_ref[...] = jnp.zeros(edge_ref.shape, edge_ref.dtype)
        next_ref[...] = jnp.zeros(next_ref.shape, next_ref.dtype)

    @pl.when(jnp.logical_not(is_last()))
    def _():
        edge_ref[...] = after_edge_ref[2:4]
        next_ref[0:1] = after_edge_ref[0:1]
        next_ref[1 : rows - 1] = after_inner_ref[...]
        next_ref[rows - 1 : rows] = after_edge_ref[1:2]

    mid_kernel(
        1, *refs[:5], edge_ref, temporal_two_ref, spatial_two_ref, mid_ref, edge_views_ref
    )
    gpre_ref[1 : rows - 1] = inner_gpre_ref[...]
    views_ref[1 : rows - 1] = inner_views_ref[...]
    for row in (0, rows - 1):
        here = slice(row, row + 1)
        grads = [mid_ref[here], next_ref[here]]
        pre_rows(preact_ref[here], grads, temporal_ref, gpre_ref, views_ref, row)
    block_sums(gpre_ref, sides_ref, [mid_ref, next_ref], views_ref, sums_ref, keep_ref, send_ref)


def input_kernel(mid_ref, gpre_ref, pair_ref, across_ref, spatial_ref, out_ref, token_ref, views_ref):
    rows, cols, ch = out_ref.shape
    pair = pair_ref[pair_ref.shape[0] - 2 * cols : pair_ref.shape[0] - cols]
    above, below = beside_band((pair[None], across_ref[across_ref.shape[0] - cols :][None]), 0)
    token_ref[...] = jnp.zeros(token_ref.shape, token_ref.dtype)
    step = 4
    beside(above.astype(jnp.float32), views_ref, 0)
    beside(below.astype(jnp.float32), views_ref, rows + 1)

    for n in range(rows // step):
        gpre = gpre_ref[pl.ds(n * step, step)].astype(jnp.float32)
        beside(gpre, views_ref, n * step + 1)

    for n in range(rows // step):
        here = pl.ds(n * step, step)
        out_ref[here] = convolved(views_ref, spatial_ref, n * step, mid_ref[here])


def halves(count, index):
    return [pl.ds(pl.multiple_of(n * count, count), count) for n in (index, 1 - index)]


def pair_kernel(keep_ref, low_ref, high_ref, own_ref, send_ref):
    across = lax.axis_index("section") // 2
    parts = [ref[...].astype(jnp.float32) for ref in (low_ref, high_ref)]
    own_ref[...] = keep_ref[across] + jnp.where(across == 0, *parts)
    total = keep_ref[1 - across] + jnp.where(across == 0, *parts[::-1])
    send_ref[...] = total.astype(jnp.bfloat16)


def band_kernel(own_ref, part_ref, keep_ref, send_ref):
    mine, other = halves(keep_ref.shape[0], lax.axis_index("video"))
    half = keep_ref.shape[0]
    keep_ref[...] = own_ref[mine] + part_ref[mine].astype(jnp.float32)
    send_ref[:half] = (own_ref[other] + part_ref[other].astype(jnp.float32)).astype(jnp.bfloat16)


def pair_quarter_kernel(keep_ref, part_ref, own_ref, across_ref, frame_ref, both_ref):
    _, height, _ = keep_ref.shape
    half = own_ref.shape[0]
    band = lax.axis_index("section") // 2
    frames = halves(half, lax.axis_index("video"))

    def quarter(band, rows):
        start = pl.multiple_of(band * height, height)
        part = part_ref.at[pl.ds(start, height)][rows]
        return keep_ref[band, rows] + part.astype(jnp.float32)

    own_ref[...] = quarter(band, frames[0])
    across_ref[:half] = quarter(1 - band, frames[0]).astype(jnp.bfloat16)
    rest = across_ref.shape[0] - half
    across_ref[half:] = part_ref[2 * height + rest :]
    frame_ref[...] = quarter(band, frames[1]).astype(jnp.bfloat16)
    both_ref[:half] = quarter(1 - band, frames[1]).astype(jnp.bfloat16)


def plane_kernel(own_ref, *refs):
    parts, out_ref = refs[:-1], refs[-1]
    total = own_ref[...]
    for part in parts:
        total = total + part[: out_ref.shape[0]].astype(jnp.float32)
    out_ref[...] = total.astype(jnp.bfloat16)


def add_kernel(one_ref, two_ref, out_ref):
    total = one_ref[...].astype(jnp.float32) + two_ref[: one_ref.shape[0]].astype(jnp.float32)
    out_ref[...] = total.astype(jnp.bfloat16)


def scaled_kernel(factor, *refs):
    out_ref = refs[-1]
    for block in range(2):
        one, two = (ref[...].astype(jnp.float32) for ref in refs[2 * block : 2 * block + 2])
        out_ref[block] = ((one + two) * factor).astype(jnp.bfloat16)


def place_kernel(places, *refs):
    shares, outs = refs[: len(places)], refs[-6:-2]
    sums_ref, sems = refs[-2:]
    band, frame = lax.axis_index("section"), lax.axis_index("video")
    height = shares[0].shape[1]

    def copies(n, block):
        flip, other = places[n]
        place = jnp.bitwise_xor(band, flip)
        half = 0 if other is None else jnp.bitwise_xor(frame, int(other))
        here = pl.ds(pl.multiple_of(half * height, height), height)
        spatial, temporal = outs[2 * block : 2 * block + 2]
        source, sem = sums_ref.at[n, block], sems.at[n, block]
        return (
            (place < 3, lambda: pltpu.make_async_copy(source, spatial.at[place, here], sem)),
            (place == 3, lambda: pltpu.make_async_copy(source, temporal.at[here], sem)),
        )

    for n, share in enumerate(shares):
        for block in range(2):
            sums_ref[n, block] = share[block].astype(jnp.float32)
            for inside, copy in copies(n, block):
                pl.when(inside)(lambda: copy().start())
    for n in range(len(shares)):
        for block in range(2):
            for inside, copy in copies(n, block):
                pl.when(inside)(lambda: copy().wait())


def placed(shares, places, given=()):
    _, height, ch = shares[0].shape
    count = len(shares)
    outs = (f32(3, 3 * ch, ch), f32(3 * ch, ch)) * 2
    vmem, spare = (pl.BlockSpec(memory_space=space) for space in (pltpu.VMEM, pl.ANY))
    return pl.pallas_call(
        functools.partial(place_kernel, places),
        out_shape=outs,
        in_specs=[vmem] * count + [spare] * len(given),
        out_specs=(spare,) * 4,
        scratch_shapes=[
            pltpu.VMEM((count, 2, height, ch), jnp.float32),
            pltpu.SemaphoreType.DMA((count, 2)),
        ],
        input_output_aliases={count + n: n for n in range(len(given))},
        compiler_params=pltpu.CompilerParams(vmem_limit_bytes=24 * MIB),
        cost_estimate=pl.CostEstimate(
            flops=0, bytes_accessed=6 * count * height * ch * 2, transcendentals=0
        ),
    )(*shares, *given)


def unpacked(sums):
    ch = sums[0].shape[-1]
    return [x.reshape(3, 3, ch, ch) if x.ndim == 3 else x.reshape(3, ch, ch) for x in sums]


def on_device(
    grad_latent,
    input_one,
    preact_one,
    input_two,
    preact_two,
    spatial_one,
    temporal_one,
    spatial_two,
    temporal_two,
):
    shape = grad_latent.shape
    rows, cols, ch = shape[2:]
    bands, frames = lax.axis_size("section"), lax.axis_size("video")
    later = min(2, frames - 1)
    pixels = lax.axis_size("dp") * frames * bands * rows * cols
    factor = 1.0 / math.sqrt(pixels)
    grad, saved_one, pre_one, saved_two, pre_two = (
        x.reshape(rows, cols, ch)
        for x in (grad_latent, input_one, preact_one, input_two, preact_two)
    )
    conv = 2 * rows * cols * 9 * ch * ch
    views = pltpu.VMEM((rows, cols, 3 * ch), jnp.bfloat16)
    edge_views = pltpu.VMEM((6, cols, 3 * ch), jnp.bfloat16)
    act = pltpu.VMEM((rows, cols, ch), jnp.bfloat16)
    sides = bf16(4, ch, rows * cols)
    sums = pltpu.VMEM((4, 3 * ch, ch), jnp.float32)
    handed = [f32(2, 3 * ch, ch)] + [bf16(3 * ch, ch)] * 2
    inner_outs = [bf16(rows - 2, cols, ch), bf16(rows, cols, ch)]
    kernels = (temporal_two, spatial_two)

    def from_later(x):
        if frames == 2:
            return [flipped(x, "video", 1)]
        return [from_ahead(x, 0, n + 1) for n in range(later)]

    wholes = from_later(grad)
    packs = call(
        pack_kernel,
        [bf16(4, cols, ch)] * 2,
        [pltpu.SemaphoreType.DMA((8,))],
        1,
        grad,
        pre_two,
        saved_two,
        saved_one,
        spare_inputs=True,
        limit=58,
    )
    second = flipped(packs[1], "section", 1)
    first = flipped(later_than(packs[0], second), "section", 1)
    pairs = [first, flipped(second, "section", 2)]

    known = ()
    if frames == 2:
        known = call(
            last_inner_kernel,
            inner_outs,
            [views],
            0,
            grad,
            pre_two,
            *kernels,
            after=(first, second),
        )
        afters = from_later(known[0])
    else:
        afters = from_later(jnp.concatenate(beside_band(pairs, 0)))
    inner, gpre_two = call(
        functools.partial(inner_kernel, later),
        inner_outs,
        [views],
        0,
        grad,
        pre_two,
        *wholes,
        *kernels,
        *known,
        early=(saved_two, saved_one, pre_one, temporal_one),
    )
    if frames == 2:
        edge = call(
            last_edge_kernel,
            [bf16(4, cols, ch)],
            [edge_views],
            0,
            grad,
            *pairs,
            known[1],
            *kernels,
            after=(gpre_two,),
        )
        afters += from_later(edge)
    parts_two = call(
        functools.partial(two_kernel, later),
        handed,
        [views, pltpu.VMEM(sides.shape, sides.dtype), sums],
        8 * conv,
        saved_two,
        pre_two,
        gpre_two,
        *pairs,
        grad,
        *wholes,
        after=(edge,) if frames == 2 else (),
    )
    sides_one = call(
        sides_kernel, [sides], [], conv // 8, saved_one, pre_one, *pairs, after=parts_two[:1]
    )
    height, half = 3 * ch, 3 * ch // 2
    keep_two, low_two, high_two = parts_two
    own_two, send_two = call(
        pair_kernel,
        [f32(height, ch), bf16(height, ch)],
        [],
        height * ch,
        keep_two,
        flipped(low_two, "section", 1),
        flipped(high_two, "section", 1),
    )
    across_two = flipped(send_two, "section", 2)
    mid_inputs = (grad, *pairs, inner, gpre_two)
    one_inputs = (sides_one, pre_one)
    mid_outs = [bf16(rows, cols, ch)]
    one_outs = [bf16(rows, cols, ch), f32(2, 3 * ch, ch), bf16(6 * ch + 2 * cols, ch)]
    if frames == 2:
        inners_one = call(
            one_inner_kernel,
            [bf16(rows - 2, cols, ch), bf16(rows - 2, cols, 3 * ch)],
            [],
            conv // 8,
            pre_one,
            inner,
            afters[0],
            temporal_one,
        )
        mid, gpre_one, *parts_one = call(
            mid_one_kernel,
            mid_outs + one_outs,
            [views, sums, act, pltpu.VMEM((2, cols, ch), jnp.bfloat16), edge_views],
            8 * conv,
            *mid_inputs,
            *afters,
            *kernels,
            *one_inputs,
            temporal_one,
            *inners_one,
            after=(own_two,),
        )
    else:
        mid = call(
            functools.partial(mid_kernel, later),
            mid_outs,
            [edge_views],
            conv // 8,
            *mid_inputs,
            *afters,
            *kernels,
        )
        gpre_one, *parts_one = call(
            functools.partial(one_kernel, later),
            one_outs,
            [views, sums],
            1.2 * conv,
            *one_inputs,
            mid,
            *from_later(mid),
            temporal_one,
        )
    keep_one, send_one = parts_one
    split = frames == 2 and lax.axis_size("dp") == 4
    if split:
        send_one = later_than(send_one, across_two)
    pair_one = flipped(send_one, "section", 1)

    def input_gradient(edge, after):
        return call(
            input_kernel,
            [bf16(rows, cols, ch), f32(8, 128)],
            [pltpu.VMEM((rows + 2, cols, 3 * ch), jnp.bfloat16)],
            conv,
            mid,
            gpre_one,
            pair_one,
            edge,
            spatial_one,
            after=after,
        )

    if split:

        def added(one, two):
            return call(add_kernel, [bf16(half, ch)], [], half * ch, one, two)

        keep_two, send_two = call(
            band_kernel,
            [f32(half, ch), bf16(half + 2 * cols, ch)],
            [],
            0,
            own_two,
            across_two,
        )
        sum_two = added(keep_two, flipped(send_two, "video", 1))
        quarters = [f32(half, ch)] + [bf16(half + more, ch) for more in (cols, 0, cols + 16)]
        own_one, *sends = call(
            pair_quarter_kernel, quarters, [], 0, keep_one, pair_one, after=(send_two,)
        )
        across = flipped(sends[0], "section", 2)
        parts = [across, flipped(sends[1], "video", 1), flipped_both(sends[2])]
        sum_one = call(plane_kernel, [bf16(half, ch)], [], 4 * half * ch, own_one, *parts)
        part_two = flipped(sum_two, "dp", 1)
        part_one = flipped(later_than(sum_one, sum_two), "dp", 1)
        sum_two = added(sum_two, part_two)
        sum_one = added(sum_one, part_one)
        last_two = flipped(sum_two, "dp", 2)
        last_one = flipped(later_than(sum_one, sum_two), "dp", 2)
        grad_in, token = input_gradient(across, (sum_one,))
        own = call(
            functools.partial(scaled_kernel, factor),
            [bf16(2, half, ch)],
            [],
            height * ch,
            sum_one,
            last_one,
            sum_two,
            last_two,
            after=(token,),
        )
        frame, across, both = flipped(own, "video", 1), flipped(own, "section", 2), flipped_both(own)
        shares = [own, frame, across]
        shares += [flipped(share, "section", 1) for share in shares]
        places = [(0, False), (0, True), (2, False), (1, False), (1, True), (3, False)]
        sums = placed([*shares, both], [*places, (2, True)])
        sums = unpacked(placed([flipped(both, "section", 1)], [(3, True)], sums))
    else:
        own_one, send_one = call(
            pair_kernel,
            [f32(height, ch), bf16(height, ch)],
            [],
            height * ch,
            keep_one,
            pair_one[:height],
            pair_one[height : 2 * height],
        )
        edge = flipped(pair_one[pair_one.shape[0] - cols :], "section", 2)
        grad_in, _ = input_gradient(edge, ())
        own_one = own_one + flipped(send_one, "section", 2).astype(jnp.float32)
        own_two = own_two + across_two.astype(jnp.float32)
        share = lax.psum(jnp.stack((own_one, own_two)), ("video", "dp")) * factor
        share = share.astype(jnp.bfloat16)
        shares = [share, flipped(share, "section", 2)]
        shares += [flipped(share, "section", 1) for share in shares]
        sums = unpacked(placed(shares, [(0, None), (2, None), (1, None), (3, None)]))
    return (grad_in.reshape(shape), *sums)


def solution(mesh):
    whole = P("dp", "video", "section", None, None)
    return jax.shard_map(
        on_device,
        mesh=mesh,
        in_specs=(whole,) * 5 + (P(),) * 4,
        out_specs=(whole, P(), P(), P(), P()),
        check_vma=False,
    )
```

```python
import functools
import math

import jax
import jax.numpy as jnp
from jax import lax
from jax.experimental import pallas as pl
from jax.experimental.pallas import tpu as pltpu
from jax.sharding import PartitionSpec as P

MIB = 1024 * 1024


def sigmoid(value):
    return 1.0 / (1.0 + jnp.exp(-value))


def bf16(*shape):
    return jax.ShapeDtypeStruct(shape, jnp.bfloat16)


def f32(*shape):
    return jax.ShapeDtypeStruct(shape, jnp.float32)


def call(kernel, outs, scratch, flops, *operands, after=(), early=(), spare_inputs=False, limit=24):
    single = len(outs) == 1
    moved = sum(math.prod(x.shape) * x.dtype.itemsize for x in (*operands, *outs))
    vmem = pl.BlockSpec(memory_space=pltpu.VMEM)
    spare = pl.BlockSpec(memory_space=pl.ANY)
    spec = spare if spare_inputs else vmem
    count = len(operands)
    operands = (*operands, *early, *after)

    def body(*refs):
        kernel(*refs[:count], *refs[len(operands) :])

    return pl.pallas_call(
        body,
        out_shape=outs[0] if single else tuple(outs),
        in_specs=[spec] * count + [vmem] * len(early) + [spare] * len(after),
        out_specs=vmem if single else (vmem,) * len(outs),
        scratch_shapes=scratch,
        compiler_params=pltpu.CompilerParams(vmem_limit_bytes=limit * MIB),
        cost_estimate=pl.CostEstimate(
            flops=int(flops), bytes_accessed=int(moved) if flops else 0, transcendentals=0
        ),
    )(*operands)


def from_ahead(block, band_step, frame_step):
    bands, frames = lax.axis_size("section"), lax.axis_size("video")
    pairs = [
        ((band + band_step) * frames + frame + frame_step, band * frames + frame)
        for band in range(bands)
        for frame in range(frames)
        if 0 <= band + band_step < bands and frame + frame_step < frames
    ]
    return lax.ppermute(block, ("section", "video"), pairs)


def beside_band(pair_refs, row):
    band = lax.axis_index("section")
    odd = lax.rem(band, 2) == 1
    inside = (band > 0) & (band < lax.axis_size("section") - 1)
    first, second = (ref[row : row + 1] for ref in pair_refs)
    second = jnp.where(inside, second, jnp.zeros_like(second))
    return jnp.where(odd, first, second), jnp.where(odd, second, first)


def flipped(block, axis, flip):
    count = lax.axis_size(axis)
    return lax.ppermute(block, axis, [(place ^ flip, place) for place in range(count)])


def flipped_both(block):
    bands = lax.axis_size("section")
    pairs = [
        (2 * (band ^ 2) + 1 - frame, 2 * band + frame) for band in range(bands) for frame in range(2)
    ]
    return lax.ppermute(block, ("section", "video"), pairs)


def later_than(block, *others):
    return lax.optimization_barrier((block, *others))[0]


def beside(gpre, views_ref, start):
    count, cols, ch = gpre.shape
    at = lax.broadcasted_iota(jnp.int32, gpre.shape, 1)
    right = jnp.where(at == cols - 1, 0.0, pltpu.roll(gpre, cols - 1, 1))
    left = jnp.where(at == 0, 0.0, pltpu.roll(gpre, 1, 1))
    here = pl.ds(start, count)
    views_ref[here, :, 0:ch] = right.astype(jnp.bfloat16)
    views_ref[here, :, ch : 2 * ch] = gpre.astype(jnp.bfloat16)
    views_ref[here, :, 2 * ch : 3 * ch] = left.astype(jnp.bfloat16)


def pre_gradient(grads, preact, temporal_ref):
    count, cols, ch = preact.shape
    flat = jnp.concatenate([grad.reshape(count * cols, ch) for grad in grads], axis=1)
    kernel = jnp.concatenate([temporal_ref[2 - step] for step in range(len(grads))], axis=1)
    gact = lax.dot_general(
        flat, kernel, (((1,), (1,)), ((), ())), preferred_element_type=jnp.float32
    )
    gact = gact.astype(jnp.bfloat16).astype(jnp.float32).reshape(preact.shape)
    hval = preact.astype(jnp.float32)
    sig = sigmoid(hval)
    return gact * sig * (1.0 + hval * (1.0 - sig))


def convolved(views_ref, spatial_ref, start, first):
    count, cols, ch = first.shape
    total = first.astype(jnp.float32).reshape(count * cols, ch)
    for ky in range(3):
        view = views_ref[pl.ds(start + 2 - ky, count)].reshape(count * cols, 3 * ch)
        kernel = jnp.concatenate([spatial_ref[ky, kx] for kx in range(3)], axis=1)
        total = total + lax.dot_general(
            view, kernel, (((1,), (1,)), ((), ())), preferred_element_type=jnp.float32
        )
    return total.astype(jnp.bfloat16).reshape(first.shape)


def is_last():
    return lax.axis_index("video") == lax.axis_size("video") - 1


def moved_rows(rows):
    count = min(4, (rows - 4) // 3)
    return slice(rows - 1 - count, rows - 1)


def left_sides(saved_ref, preact_ref, above, below, sides_ref, moved=None):
    rows, cols, ch = saved_ref.shape
    flat = (rows * cols, ch)

    def flipped_over(x):
        if moved is not None:
            kept = jnp.where(is_last(), x[moved], jnp.zeros_like(x[moved]))
            x = jnp.concatenate([x[: moved.start], kept, x[moved.stop :]], axis=0)
        return x.reshape(flat).T

    shifts = [
        jnp.concatenate([above, saved_ref[: rows - 1]], axis=0),
        saved_ref[...],
        jnp.concatenate([saved_ref[1:], below], axis=0),
    ]
    for n, shift in enumerate(shifts):
        sides_ref[n] = flipped_over(shift)
    hval = preact_ref[...].astype(jnp.float32)
    sides_ref[3] = flipped_over((hval * sigmoid(hval)).astype(jnp.bfloat16))


def kernel_sums(sides_ref, grads, views, sums_ref):
    _, ch, pixels = sides_ref.shape
    shifts = sides_ref[0:3].reshape(3 * ch, pixels)
    sums = jnp.dot(shifts, views, preferred_element_type=jnp.float32)
    for ky in range(3):
        for kx in range(3):
            here = slice(kx * ch, (kx + 1) * ch)
            sums_ref[ky, here] = sums[ky * ch : (ky + 1) * ch, here]
    grads = jnp.concatenate([grad.reshape(pixels, ch) for grad in grads], axis=1)
    sums = jnp.dot(sides_ref[3], grads, preferred_element_type=jnp.float32)
    zeros = jnp.zeros((ch, ch), jnp.float32)
    for k in range(3):
        step = 2 - k
        value = sums[:, step * ch : (step + 1) * ch] if step * ch < grads.shape[1] else zeros
        sums_ref[3, k * ch : (k + 1) * ch] = jnp.where(is_last(), zeros, value) if step else value


def hand_out(sums_ref, keep_ref, *send_refs):
    odd = lax.rem(lax.axis_index("section"), 2)
    for n, send_ref in enumerate(send_refs):
        keep_ref[n] = sums_ref[2 * n + odd]
        send_ref[...] = sums_ref[2 * n + 1 - odd].astype(jnp.bfloat16)


def pack_kernel(moved, *refs):
    parts, refs = refs[:4], refs[4:]
    outs, sems = refs[-3:-1] if moved is None else refs[-4:-2], refs[-1]
    last = parts[0].shape[0] - 1
    odd = lax.rem(lax.axis_index("section"), 2)
    moves = [
        (part.at[pl.ds(row, 1)], out.at[pl.ds(n, 1)])
        for n, part in enumerate(parts)
        for out, row in zip(outs, ((1 - odd) * last, odd * last))
    ]
    if moved is not None:
        count = moved.stop - moved.start
        sent_ref = refs[-2]
        moves += [
            (refs[0].at[pl.ds(moved.start, count)], sent_ref.at[pl.ds(0, count)]),
            (
                parts[3].at[pl.ds(moved.start - 1, count + 2)],
                sent_ref.at[pl.ds(count, count + 2)],
            ),
        ]
    copies = [
        pltpu.make_async_copy(source, target, sems.at[n])
        for n, (source, target) in enumerate(moves)
    ]
    for copy in copies:
        copy.start()
    for copy in copies:
        copy.wait()


def interior(grad_ref, preact_ref, wholes, temporal_ref, spatial_ref, inner_ref, gpre_ref, views_ref):
    rows, cols, ch = grad_ref.shape
    step = 4

    for n in range(rows // step):
        here = pl.ds(n * step, step)
        grads = [ref[here] for ref in (grad_ref, *wholes)]
        gpre = pre_gradient(grads, preact_ref[here], temporal_ref)
        gpre_ref[here] = gpre.astype(jnp.bfloat16)
        beside(gpre, views_ref, n * step)

    half = rows // 2 - 1

    for n in range(2):
        first = grad_ref[pl.ds(n * half + 1, half)]
        inner_ref[pl.ds(n * half, half)] = convolved(views_ref, spatial_ref, n * half, first)


def edge_rows(grad_ref, pair_refs, afters, gpre_ref, temporal_ref, spatial_ref, views_ref):
    rows, cols, ch = grad_ref.shape
    (grad_above, grad_below), (above_pre, below_pre) = (beside_band(pair_refs, n) for n in (0, 1))
    above = [grad_above] + [ref[0:1] for ref in afters]
    below = [grad_below] + [ref[1:2] for ref in afters]
    beside(pre_gradient(above, above_pre, temporal_ref), views_ref, 0)
    beside(gpre_ref[0:2].astype(jnp.float32), views_ref, 1)
    beside(gpre_ref[rows - 2 : rows].astype(jnp.float32), views_ref, 3)
    beside(pre_gradient(below, below_pre, temporal_ref), views_ref, 5)
    return (
        convolved(views_ref, spatial_ref, 0, grad_ref[0:1]),
        convolved(views_ref, spatial_ref, 3, grad_ref[rows - 1 : rows]),
    )


def last_inner_kernel(*refs):
    grad_ref, preact_ref, kernels = refs[0], refs[1], refs[2:4]
    sent_ref, outs, sem = refs[7], refs[8:11], refs[11]

    @pl.when(is_last())
    def _():
        interior(grad_ref, preact_ref, [], *kernels, *outs)
        count = sent_ref.shape[0]
        copy = pltpu.make_async_copy(outs[0].at[pl.ds(0, count)], sent_ref, sem)
        copy.start()
        copy.wait()


def last_edge_kernel(*refs):
    grad_ref, pair_refs, gpre_ref, inner_ref = refs[0], refs[1:3], refs[3], refs[4]
    temporal_ref, spatial_ref, edge_ref, views_ref = refs[5:]

    @pl.when(is_last())
    def _():
        edge_ref[0:1], edge_ref[1:2] = edge_rows(
            grad_ref, pair_refs, [], gpre_ref, temporal_ref, spatial_ref, views_ref
        )
        edge_ref[2:3], edge_ref[3:4] = beside_band(pair_refs, 0)

    @pl.when(jnp.logical_not(is_last()))
    def _():
        moved = moved_rows(grad_ref.shape[0])
        edge_ref[: moved.stop - moved.start] = inner_ref[moved.start - 1 : moved.stop - 1]


def inner_kernel(later, *refs):
    inputs, wholes, kernels = refs[:2], refs[2 : 2 + later], refs[2 + later : 4 + later]
    known, outs = refs[4 + later : -3], refs[-3:]
    if not known:
        interior(*inputs, wholes, *kernels, *outs)
        return

    @pl.when(is_last())
    def _():
        outs[0][...] = known[0][...]
        outs[1][...] = known[1][...]

    @pl.when(jnp.logical_not(is_last()))
    def _():
        interior(*inputs, wholes, *kernels, *outs)


def mid_kernel(later, *refs):
    grad_ref, inner_ref, gpre_ref = refs[0], refs[3], refs[4]
    afters, (temporal_ref, spatial_ref, mid_ref, views_ref) = refs[5 : 5 + later], refs[5 + later :]
    rows = grad_ref.shape[0]
    first, last = edge_rows(
        grad_ref, refs[1:3], afters, gpre_ref, temporal_ref, spatial_ref, views_ref
    )
    mid_ref[0:1], mid_ref[rows - 1 : rows] = first, last
    mid_ref[1 : rows - 1] = inner_ref[...]


def two_kernel(later, *refs):
    saved_ref, preact_ref, gpre_ref = refs[:3]
    pair_refs, grad_ref = refs[3:5], refs[5]
    wholes, outs = refs[6 : 6 + later], refs[6 + later : 9 + later]
    views_ref, sides_ref, sums_ref = refs[9 + later :]
    rows, cols, ch = saved_ref.shape
    step = 4

    for n in range(rows // step):
        here = pl.ds(n * step, step)
        beside(gpre_ref[here].astype(jnp.float32), views_ref, n * step)

    views = views_ref[...].reshape(rows * cols, 3 * ch)
    grads = [ref[...] for ref in (grad_ref, *wholes)]
    left_sides(saved_ref, preact_ref, *beside_band(pair_refs, 2), sides_ref)
    kernel_sums(sides_ref, grads, views, sums_ref)
    hand_out(sums_ref, *outs)


def sides_kernel(moved, saved_ref, preact_ref, one_ref, two_ref, sides_ref):
    left_sides(saved_ref, preact_ref, *beside_band((one_ref, two_ref), 3), sides_ref, moved)


def pre_rows(preact, mids, temporal_ref, gpre_ref, views_ref, start):
    gpre = pre_gradient(mids, preact, temporal_ref)
    gpre_ref[start : start + preact.shape[0]] = gpre.astype(jnp.bfloat16)
    beside(gpre, views_ref, start)


def block_sums(gpre_ref, sides_ref, mids, views_ref, sums_ref, keep_ref, send_ref, more=None):
    rows, cols, ch = gpre_ref.shape
    odd = lax.rem(lax.axis_index("section"), 2)
    size = send_ref.shape[0] - 2 * cols
    send_ref[size : size + cols] = gpre_ref[(1 - odd) * (rows - 1)]
    send_ref[size + cols : size + 2 * cols] = gpre_ref[odd * (rows - 1)]
    views = views_ref[...].reshape(rows * cols, 3 * ch)
    kernel_sums(sides_ref, [ref[...] for ref in mids], views, sums_ref)
    if more is not None:
        more()
    height = sums_ref.shape[1]
    hand_out(sums_ref, keep_ref, send_ref.at[:height], send_ref.at[height : 2 * height])


def one_kernel(later, *refs):
    sides_ref, preact_ref, mids = refs[0], refs[1], refs[2 : 3 + later]
    temporal_ref, outs, scratch = refs[3 + later], refs[4 + later : 7 + later], refs[7 + later :]
    gpre_ref, keep_ref, send_ref = outs
    views_ref, sums_ref = scratch
    for n in range(preact_ref.shape[0] // 4):
        here = slice(4 * n, 4 * n + 4)
        grads = [ref[here] for ref in mids]
        pre_rows(preact_ref[here], grads, temporal_ref, gpre_ref, views_ref, 4 * n)
    block_sums(gpre_ref, sides_ref, mids, views_ref, sums_ref, keep_ref, send_ref)


def one_inner_kernel(preact_ref, inner_ref, after_ref, temporal_ref, gpre_ref, views_ref):
    known = after_ref.shape[0]
    for rows in (slice(0, known // 2), slice(known // 2, known), slice(known, inner_ref.shape[0])):
        grads = [inner_ref[rows]]
        if rows.start < known:
            after = after_ref[rows]
            grads.append(jnp.where(is_last(), jnp.zeros_like(after), after))
        preact = preact_ref[rows.start + 1 : rows.stop + 1]
        pre_rows(preact, grads, temporal_ref, gpre_ref, views_ref, rows.start)


def moved_sums(given_ref, moved_ref, mid, temporal_ref, extra_ref, views_ref, sums_ref):
    count, cols, ch = mid.shape
    flat = (count * cols, ch)
    preact = given_ref[:count]
    before = moved_ref[:count]
    gpre = pre_gradient([before, mid], preact, temporal_ref)
    extra_ref[...] = gpre.astype(jnp.bfloat16).reshape(flat)
    beside(gpre, views_ref, 0)
    sides = [given_ref[count + ky : 2 * count + ky].reshape(flat).T for ky in range(3)]
    views = views_ref[...].reshape(count * cols, 3 * ch)
    for ky in range(3):
        sums_ref[ky] += jnp.concatenate(
            [
                jnp.dot(sides[ky], views[:, kx * ch : (kx + 1) * ch], preferred_element_type=jnp.float32)
                for kx in range(3)
            ],
            axis=0,
        )
    hval = preact.astype(jnp.float32)
    act = (hval * sigmoid(hval)).astype(jnp.bfloat16).reshape(flat).T
    for k, grad in ((1, mid), (2, before)):
        sums_ref[3, k * ch : (k + 1) * ch] += jnp.dot(
            act, grad.reshape(flat), preferred_element_type=jnp.float32
        )


def mid_one_kernel(*refs):
    after_inner_ref, after_edge_ref = refs[5:7]
    temporal_two_ref, spatial_two_ref, sides_ref, preact_ref, temporal_ref = refs[7:12]
    inner_gpre_ref, inner_views_ref = refs[12:14]
    mid_ref, gpre_ref, keep_ref, send_ref, extra_ref = refs[14:19]
    views_ref, sums_ref, next_ref, edge_ref, edge_views_ref, extra_views_ref = refs[19:]
    rows, cols, ch = next_ref.shape
    moved = moved_rows(rows)
    next_ref[moved] = jnp.zeros((moved.stop - moved.start, cols, ch), next_ref.dtype)

    @pl.when(is_last())
    def _():
        edge_ref[...] = jnp.zeros(edge_ref.shape, edge_ref.dtype)
        next_ref[: moved.start] = jnp.zeros((moved.start, cols, ch), next_ref.dtype)
        next_ref[rows - 1 : rows] = jnp.zeros((1, cols, ch), next_ref.dtype)

    @pl.when(jnp.logical_not(is_last()))
    def _():
        edge_ref[...] = after_edge_ref[2:4]
        next_ref[0:1] = after_edge_ref[0:1]
        next_ref[1 : moved.start] = after_inner_ref[...]
        next_ref[rows - 1 : rows] = after_edge_ref[1:2]

    mid_kernel(
        1, *refs[:5], edge_ref, temporal_two_ref, spatial_two_ref, mid_ref, edge_views_ref
    )
    gpre_ref[1 : rows - 1] = inner_gpre_ref[...]
    views_ref[1 : rows - 1] = inner_views_ref[...]
    for row in (0, rows - 1):
        here = slice(row, row + 1)
        grads = [mid_ref[here], next_ref[here]]
        pre_rows(preact_ref[here], grads, temporal_ref, gpre_ref, views_ref, row)

    def more():
        @pl.when(is_last())
        def _():
            moved_sums(
                after_inner_ref,
                after_edge_ref,
                mid_ref[moved],
                temporal_ref,
                extra_ref,
                extra_views_ref,
                sums_ref,
            )

    mids = [mid_ref, next_ref]
    block_sums(gpre_ref, sides_ref, mids, views_ref, sums_ref, keep_ref, send_ref, more)


def input_kernel(*refs):
    mid_ref, gpre_ref, pair_ref, across_ref, spatial_ref = refs[:5]
    given, (out_ref, token_ref, views_ref) = refs[5:-3], refs[-3:]
    rows, cols, ch = out_ref.shape
    pair = pair_ref[pair_ref.shape[0] - 2 * cols : pair_ref.shape[0] - cols]
    above, below = beside_band((pair[None], across_ref[across_ref.shape[0] - cols :][None]), 0)
    token_ref[...] = jnp.zeros(token_ref.shape, token_ref.dtype)
    step = 4
    beside(above.astype(jnp.float32), views_ref, 0)
    beside(below.astype(jnp.float32), views_ref, rows + 1)

    for n in range(rows // step):
        gpre = gpre_ref[pl.ds(n * step, step)].astype(jnp.float32)
        beside(gpre, views_ref, n * step + 1)

    if given:

        @pl.when(jnp.logical_not(is_last()))
        def _():
            moved = moved_rows(rows)
            count = moved.stop - moved.start
            size = given[0].shape[0] - count * cols
            gpre = given[0][size:].reshape(count, cols, ch)
            beside(gpre.astype(jnp.float32), views_ref, moved.start + 1)

    for n in range(rows // step):
        here = pl.ds(n * step, step)
        out_ref[here] = convolved(views_ref, spatial_ref, n * step, mid_ref[here])


def halves(count, index):
    return [pl.ds(pl.multiple_of(n * count, count), count) for n in (index, 1 - index)]


def pair_kernel(keep_ref, low_ref, high_ref, own_ref, send_ref):
    across = lax.axis_index("section") // 2
    parts = [ref[...].astype(jnp.float32) for ref in (low_ref, high_ref)]
    own_ref[...] = keep_ref[across] + jnp.where(across == 0, *parts)
    total = keep_ref[1 - across] + jnp.where(across == 0, *parts[::-1])
    send_ref[...] = total.astype(jnp.bfloat16)


def band_kernel(own_ref, part_ref, extra_ref, keep_ref, send_ref):
    mine, other = halves(keep_ref.shape[0], lax.axis_index("video"))
    half = keep_ref.shape[0]
    keep_ref[...] = own_ref[mine] + part_ref[mine].astype(jnp.float32)
    send_ref[:half] = (own_ref[other] + part_ref[other].astype(jnp.float32)).astype(jnp.bfloat16)
    send_ref[half:] = extra_ref[...]


def pair_quarter_kernel(keep_ref, part_ref, own_ref, across_ref, frame_ref, both_ref):
    _, height, _ = keep_ref.shape
    half = own_ref.shape[0]
    band = lax.axis_index("section") // 2
    frames = halves(half, lax.axis_index("video"))

    def quarter(band, rows):
        start = pl.multiple_of(band * height, height)
        part = part_ref.at[pl.ds(start, height)][rows]
        return keep_ref[band, rows] + part.astype(jnp.float32)

    own_ref[...] = quarter(band, frames[0])
    across_ref[:half] = quarter(1 - band, frames[0]).astype(jnp.bfloat16)
    rest = across_ref.shape[0] - half
    across_ref[half:] = part_ref[2 * height + rest :]
    frame_ref[...] = quarter(band, frames[1]).astype(jnp.bfloat16)
    both_ref[:half] = quarter(1 - band, frames[1]).astype(jnp.bfloat16)


def plane_kernel(own_ref, *refs):
    parts, out_ref = refs[:-1], refs[-1]
    total = own_ref[...]
    for part in parts:
        total = total + part[: out_ref.shape[0]].astype(jnp.float32)
    out_ref[...] = total.astype(jnp.bfloat16)


def add_kernel(one_ref, two_ref, out_ref):
    total = one_ref[...].astype(jnp.float32) + two_ref[: one_ref.shape[0]].astype(jnp.float32)
    out_ref[...] = total.astype(jnp.bfloat16)


def scaled_kernel(factor, *refs):
    out_ref = refs[-1]
    for block in range(2):
        one, two = (ref[...].astype(jnp.float32) for ref in refs[2 * block : 2 * block + 2])
        out_ref[block] = ((one + two) * factor).astype(jnp.bfloat16)


def place_kernel(places, *refs):
    shares, outs = refs[: len(places)], refs[-6:-2]
    sums_ref, sems = refs[-2:]
    band, frame = lax.axis_index("section"), lax.axis_index("video")
    height = shares[0].shape[1]

    def copies(n, block):
        flip, other = places[n]
        place = jnp.bitwise_xor(band, flip)
        half = 0 if other is None else jnp.bitwise_xor(frame, int(other))
        here = pl.ds(pl.multiple_of(half * height, height), height)
        spatial, temporal = outs[2 * block : 2 * block + 2]
        source, sem = sums_ref.at[n, block], sems.at[n, block]
        return (
            (place < 3, lambda: pltpu.make_async_copy(source, spatial.at[place, here], sem)),
            (place == 3, lambda: pltpu.make_async_copy(source, temporal.at[here], sem)),
        )

    for n, share in enumerate(shares):
        for block in range(2):
            sums_ref[n, block] = share[block].astype(jnp.float32)
            for inside, copy in copies(n, block):
                pl.when(inside)(lambda: copy().start())
    for n in range(len(shares)):
        for block in range(2):
            for inside, copy in copies(n, block):
                pl.when(inside)(lambda: copy().wait())


def placed(shares, places, given=()):
    _, height, ch = shares[0].shape
    count = len(shares)
    outs = (f32(3, 3 * ch, ch), f32(3 * ch, ch)) * 2
    vmem, spare = (pl.BlockSpec(memory_space=space) for space in (pltpu.VMEM, pl.ANY))
    return pl.pallas_call(
        functools.partial(place_kernel, places),
        out_shape=outs,
        in_specs=[vmem] * count + [spare] * len(given),
        out_specs=(spare,) * 4,
        scratch_shapes=[
            pltpu.VMEM((count, 2, height, ch), jnp.float32),
            pltpu.SemaphoreType.DMA((count, 2)),
        ],
        input_output_aliases={count + n: n for n in range(len(given))},
        compiler_params=pltpu.CompilerParams(vmem_limit_bytes=24 * MIB),
        cost_estimate=pl.CostEstimate(
            flops=0, bytes_accessed=6 * count * height * ch * 2, transcendentals=0
        ),
    )(*shares, *given)


def unpacked(sums):
    ch = sums[0].shape[-1]
    return [x.reshape(3, 3, ch, ch) if x.ndim == 3 else x.reshape(3, ch, ch) for x in sums]


def on_device(
    grad_latent,
    input_one,
    preact_one,
    input_two,
    preact_two,
    spatial_one,
    temporal_one,
    spatial_two,
    temporal_two,
):
    shape = grad_latent.shape
    rows, cols, ch = shape[2:]
    bands, frames = lax.axis_size("section"), lax.axis_size("video")
    later = min(2, frames - 1)
    pixels = lax.axis_size("dp") * frames * bands * rows * cols
    factor = 1.0 / math.sqrt(pixels)
    grad, saved_one, pre_one, saved_two, pre_two = (
        x.reshape(rows, cols, ch)
        for x in (grad_latent, input_one, preact_one, input_two, preact_two)
    )
    conv = 2 * rows * cols * 9 * ch * ch
    views = pltpu.VMEM((rows, cols, 3 * ch), jnp.bfloat16)
    edge_views = pltpu.VMEM((6, cols, 3 * ch), jnp.bfloat16)
    act = pltpu.VMEM((rows, cols, ch), jnp.bfloat16)
    sides = bf16(4, ch, rows * cols)
    sums = pltpu.VMEM((4, 3 * ch, ch), jnp.float32)
    handed = [f32(2, 3 * ch, ch)] + [bf16(3 * ch, ch)] * 2
    inner_outs = [bf16(rows - 2, cols, ch), bf16(rows, cols, ch)]
    kernels = (temporal_two, spatial_two)

    def from_later(x):
        if frames == 2:
            return [flipped(x, "video", 1)]
        return [from_ahead(x, 0, n + 1) for n in range(later)]

    wholes = from_later(grad)
    moved = moved_rows(rows) if frames == 2 else None
    count = moved.stop - moved.start if moved else 0
    packs = call(
        functools.partial(pack_kernel, moved),
        [bf16(4, cols, ch)] * 2 + ([bf16(rows - 2 - count, cols, ch)] if moved else []),
        [pltpu.SemaphoreType.DMA((10,))],
        1,
        grad,
        pre_two,
        saved_two,
        saved_one,
        *([pre_one] if moved else []),
        spare_inputs=True,
        limit=58,
    )
    second = flipped(packs[1], "section", 1)
    first = flipped(later_than(packs[0], second), "section", 1)
    pairs = [first, flipped(second, "section", 2)]

    known = ()
    if frames == 2:
        vmem, spare = (pl.BlockSpec(memory_space=space) for space in (pltpu.VMEM, pl.ANY))
        sent, *known = pl.pallas_call(
            last_inner_kernel,
            out_shape=(bf16(*packs[2].shape), *inner_outs),
            in_specs=[vmem] * 4 + [spare] * 3,
            out_specs=(spare, vmem, vmem),
            scratch_shapes=[views, pltpu.SemaphoreType.DMA],
            input_output_aliases={4: 0},
            compiler_params=pltpu.CompilerParams(vmem_limit_bytes=24 * MIB),
            cost_estimate=pl.CostEstimate(flops=0, bytes_accessed=0, transcendentals=0),
        )(grad, pre_two, *kernels, packs[2], first, second)
        afters = from_later(sent)
    else:
        afters = from_later(jnp.concatenate(beside_band(pairs, 0)))
    inner, gpre_two = call(
        functools.partial(inner_kernel, later),
        inner_outs,
        [views],
        0,
        grad,
        pre_two,
        *wholes,
        *kernels,
        *known,
        early=(saved_two, temporal_one),
    )
    if frames == 2:
        edge = call(
            last_edge_kernel,
            [bf16(4, cols, ch)],
            [edge_views],
            0,
            grad,
            *pairs,
            known[1],
            inner,
            *kernels,
        )
        afters += from_later(edge)
    parts_two = call(
        functools.partial(two_kernel, later),
        handed,
        [views, pltpu.VMEM(sides.shape, sides.dtype), sums],
        8 * conv,
        saved_two,
        pre_two,
        gpre_two,
        *pairs,
        grad,
        *wholes,
        after=(edge,) if frames == 2 else (),
    )
    sides_one = call(
        functools.partial(sides_kernel, moved),
        [sides],
        [],
        conv // 8,
        saved_one,
        pre_one,
        *pairs,
        after=parts_two[:1],
    )
    height, half = 3 * ch, 3 * ch // 2
    keep_two, low_two, high_two = parts_two
    own_two, send_two = call(
        pair_kernel,
        [f32(height, ch), bf16(height, ch)],
        [],
        height * ch,
        keep_two,
        flipped(low_two, "section", 1),
        flipped(high_two, "section", 1),
    )
    across_two = flipped(send_two, "section", 2)
    mid_inputs = (grad, *pairs, inner, gpre_two)
    one_inputs = (sides_one, pre_one)
    mid_outs = [bf16(rows, cols, ch)]
    one_outs = [bf16(rows, cols, ch), f32(2, 3 * ch, ch), bf16(6 * ch + 2 * cols, ch)]
    if frames == 2:
        inners_one = call(
            one_inner_kernel,
            [bf16(rows - 2, cols, ch), bf16(rows - 2, cols, 3 * ch)],
            [],
            conv // 8,
            pre_one,
            inner,
            afters[0],
            temporal_one,
            after=(own_two,),
        )
        more_views = pltpu.VMEM((count, cols, 3 * ch), jnp.bfloat16)
        edge_pair = pltpu.VMEM((2, cols, ch), jnp.bfloat16)
        mid, gpre_one, *parts_one, extra = call(
            mid_one_kernel,
            mid_outs + one_outs + [bf16(count * cols, ch)],
            [views, sums, act, edge_pair, edge_views, more_views],
            8 * conv,
            *mid_inputs,
            *afters,
            *kernels,
            *one_inputs,
            temporal_one,
            *inners_one,
            after=(own_two,),
        )
    else:
        mid = call(
            functools.partial(mid_kernel, later),
            mid_outs,
            [edge_views],
            conv // 8,
            *mid_inputs,
            *afters,
            *kernels,
        )
        gpre_one, *parts_one = call(
            functools.partial(one_kernel, later),
            one_outs,
            [views, sums],
            1.2 * conv,
            *one_inputs,
            mid,
            *from_later(mid),
            temporal_one,
        )
    keep_one, send_one = parts_one
    split = frames == 2 and lax.axis_size("dp") == 4
    if split:
        send_one = later_than(send_one, across_two)
    pair_one = flipped(send_one, "section", 1)

    def input_gradient(edge, after, *given):
        return call(
            input_kernel,
            [bf16(rows, cols, ch), f32(8, 128)],
            [pltpu.VMEM((rows + 2, cols, 3 * ch), jnp.bfloat16)],
            conv,
            mid,
            gpre_one,
            pair_one,
            edge,
            spatial_one,
            *given,
            after=after,
        )

    if split:

        def added(one, two):
            return call(add_kernel, [bf16(half, ch)], [], half * ch, one, two)

        keep_two, send_two = call(
            band_kernel,
            [f32(half, ch), bf16(half + extra.shape[0], ch)],
            [],
            0,
            own_two,
            across_two,
            extra,
        )
        given_two = flipped(send_two, "video", 1)
        sum_two = added(keep_two, given_two)
        quarters = [f32(half, ch)] + [bf16(half + more, ch) for more in (cols, 0, cols + 16)]
        own_one, *sends = call(
            pair_quarter_kernel, quarters, [], 0, keep_one, pair_one, after=(send_two,)
        )
        across = flipped(sends[0], "section", 2)
        parts = [across, flipped(sends[1], "video", 1), flipped_both(sends[2])]
        sum_one = call(plane_kernel, [bf16(half, ch)], [], 4 * half * ch, own_one, *parts)
        part_two = flipped(sum_two, "dp", 1)
        part_one = flipped(later_than(sum_one, sum_two), "dp", 1)
        sum_two = added(sum_two, part_two)
        sum_one = added(sum_one, part_one)
        last_two = flipped(sum_two, "dp", 2)
        last_one = flipped(later_than(sum_one, sum_two), "dp", 2)
        grad_in, token = input_gradient(across, (sum_one,), given_two)
        own = call(
            functools.partial(scaled_kernel, factor),
            [bf16(2, half, ch)],
            [],
            height * ch,
            sum_one,
            last_one,
            sum_two,
            last_two,
            after=(token,),
        )
        frame, across, both = flipped(own, "video", 1), flipped(own, "section", 2), flipped_both(own)
        shares = [own, frame, across]
        shares += [flipped(share, "section", 1) for share in shares]
        places = [(0, False), (0, True), (2, False), (1, False), (1, True), (3, False)]
        sums = placed([*shares, both], [*places, (2, True)])
        sums = unpacked(placed([flipped(both, "section", 1)], [(3, True)], sums))
    else:
        own_one, send_one = call(
            pair_kernel,
            [f32(height, ch), bf16(height, ch)],
            [],
            height * ch,
            keep_one,
            pair_one[:height],
            pair_one[height : 2 * height],
        )
        edge = flipped(pair_one[pair_one.shape[0] - cols :], "section", 2)
        grad_in, _ = input_gradient(edge, (), *(from_later(extra) if frames == 2 else []))
        own_one = own_one + flipped(send_one, "section", 2).astype(jnp.float32)
        own_two = own_two + across_two.astype(jnp.float32)
        share = lax.psum(jnp.stack((own_one, own_two)), ("video", "dp")) * factor
        share = share.astype(jnp.bfloat16)
        shares = [share, flipped(share, "section", 2)]
        shares += [flipped(share, "section", 1) for share in shares]
        sums = unpacked(placed(shares, [(0, None), (2, None), (1, None), (3, None)]))
    return (grad_in.reshape(shape), *sums)


def solution(mesh):
    whole = P("dp", "video", "section", None, None)
    return jax.shard_map(
        on_device,
        mesh=mesh,
        in_specs=(whole,) * 5 + (P(),) * 4,
        out_specs=(whole, P(), P(), P(), P()),
        check_vma=False,
    )
```

```python
import functools
import math

import jax
import jax.numpy as jnp
from jax import lax
from jax.experimental import pallas as pl
from jax.experimental.pallas import tpu as pltpu
from jax.sharding import PartitionSpec as P

MIB = 1024 * 1024


def sigmoid(value):
    return 1.0 / (1.0 + jnp.exp(-value))


def bf16(*shape):
    return jax.ShapeDtypeStruct(shape, jnp.bfloat16)


def f32(*shape):
    return jax.ShapeDtypeStruct(shape, jnp.float32)


def call(kernel, outs, scratch, flops, *operands, after=(), early=(), spare_inputs=False, limit=24):
    single = len(outs) == 1
    moved = sum(math.prod(x.shape) * x.dtype.itemsize for x in (*operands, *outs))
    vmem = pl.BlockSpec(memory_space=pltpu.VMEM)
    spare = pl.BlockSpec(memory_space=pl.ANY)
    spec = spare if spare_inputs else vmem
    count = len(operands)
    operands = (*operands, *early, *after)

    def body(*refs):
        kernel(*refs[:count], *refs[len(operands) :])

    return pl.pallas_call(
        body,
        out_shape=outs[0] if single else tuple(outs),
        in_specs=[spec] * count + [vmem] * len(early) + [spare] * len(after),
        out_specs=vmem if single else (vmem,) * len(outs),
        scratch_shapes=scratch,
        compiler_params=pltpu.CompilerParams(vmem_limit_bytes=limit * MIB),
        cost_estimate=pl.CostEstimate(
            flops=int(flops), bytes_accessed=int(moved) if flops else 0, transcendentals=0
        ),
    )(*operands)


def from_ahead(block, band_step, frame_step):
    bands, frames = lax.axis_size("section"), lax.axis_size("video")
    pairs = [
        ((band + band_step) * frames + frame + frame_step, band * frames + frame)
        for band in range(bands)
        for frame in range(frames)
        if 0 <= band + band_step < bands and frame + frame_step < frames
    ]
    return lax.ppermute(block, ("section", "video"), pairs)


def beside_band(pair_refs, row):
    band = lax.axis_index("section")
    odd = lax.rem(band, 2) == 1
    inside = (band > 0) & (band < lax.axis_size("section") - 1)
    first, second = (ref[row : row + 1] for ref in pair_refs)
    second = jnp.where(inside, second, jnp.zeros_like(second))
    return jnp.where(odd, first, second), jnp.where(odd, second, first)


def flipped(block, axis, flip):
    count = lax.axis_size(axis)
    return lax.ppermute(block, axis, [(place ^ flip, place) for place in range(count)])


def flipped_both(block):
    bands = lax.axis_size("section")
    pairs = [
        (2 * (band ^ 2) + 1 - frame, 2 * band + frame) for band in range(bands) for frame in range(2)
    ]
    return lax.ppermute(block, ("section", "video"), pairs)


def later_than(block, *others):
    return lax.optimization_barrier((block, *others))[0]


def beside(gpre, views_ref, start):
    count, cols, ch = gpre.shape
    at = lax.broadcasted_iota(jnp.int32, gpre.shape, 1)
    right = jnp.where(at == cols - 1, 0.0, pltpu.roll(gpre, cols - 1, 1))
    left = jnp.where(at == 0, 0.0, pltpu.roll(gpre, 1, 1))
    here = pl.ds(start, count)
    views_ref[here, :, 0:ch] = right.astype(jnp.bfloat16)
    views_ref[here, :, ch : 2 * ch] = gpre.astype(jnp.bfloat16)
    views_ref[here, :, 2 * ch : 3 * ch] = left.astype(jnp.bfloat16)


def pre_gradient(grads, preact, temporal_ref):
    count, cols, ch = preact.shape
    flat = jnp.concatenate([grad.reshape(count * cols, ch) for grad in grads], axis=1)
    kernel = jnp.concatenate([temporal_ref[2 - step] for step in range(len(grads))], axis=1)
    gact = lax.dot_general(
        flat, kernel, (((1,), (1,)), ((), ())), preferred_element_type=jnp.float32
    )
    gact = gact.astype(jnp.bfloat16).astype(jnp.float32).reshape(preact.shape)
    hval = preact.astype(jnp.float32)
    sig = sigmoid(hval)
    return gact * sig * (1.0 + hval * (1.0 - sig))


def convolved(views_ref, spatial_ref, start, first):
    count, cols, ch = first.shape
    total = first.astype(jnp.float32).reshape(count * cols, ch)
    for ky in range(3):
        view = views_ref[pl.ds(start + 2 - ky, count)].reshape(count * cols, 3 * ch)
        kernel = jnp.concatenate([spatial_ref[ky, kx] for kx in range(3)], axis=1)
        total = total + lax.dot_general(
            view, kernel, (((1,), (1,)), ((), ())), preferred_element_type=jnp.float32
        )
    return total.astype(jnp.bfloat16).reshape(first.shape)


def is_last():
    return lax.axis_index("video") == lax.axis_size("video") - 1


def left_sides(saved_ref, preact_ref, above, below, sides_ref):
    rows, cols, ch = saved_ref.shape
    flat = (rows * cols, ch)
    shifts = [
        jnp.concatenate([above, saved_ref[: rows - 1]], axis=0),
        saved_ref[...],
        jnp.concatenate([saved_ref[1:], below], axis=0),
    ]
    for n, shift in enumerate(shifts):
        sides_ref[n] = shift.reshape(flat).T
    hval = preact_ref[...].astype(jnp.float32)
    sides_ref[3] = (hval * sigmoid(hval)).astype(jnp.bfloat16).reshape(flat).T


def kernel_sums(sides_ref, grads, views, sums_ref):
    _, ch, pixels = sides_ref.shape
    shifts = sides_ref[0:3].reshape(3 * ch, pixels)
    sums = jnp.dot(shifts, views, preferred_element_type=jnp.float32)
    for ky in range(3):
        for kx in range(3):
            value = sums[ky * ch : (ky + 1) * ch, kx * ch : (kx + 1) * ch]
            sums_ref[(3 * ky + kx) * ch : (3 * ky + kx + 1) * ch] = value
    steps = len(grads)
    grads = jnp.concatenate([grad.reshape(pixels, ch) for grad in grads], axis=1)
    sums = jnp.dot(sides_ref[3], grads, preferred_element_type=jnp.float32)
    for step in range(steps):
        value = sums[:, step * ch : (step + 1) * ch]
        start = (8 + steps - step) * ch
        sums_ref[start : start + ch] = (
            jnp.where(is_last(), jnp.zeros_like(value), value) if step else value
        )


def hand_out(sums_ref, keep_ref, *send_refs):
    odd = lax.rem(lax.axis_index("section"), 2)
    height = keep_ref.shape[1]

    def share(band):
        return sums_ref[pl.ds(pl.multiple_of(band * height, height), height)]

    for n, send_ref in enumerate(send_refs):
        keep_ref[n] = share(2 * n + odd)
        send_ref[...] = share(2 * n + 1 - odd).astype(jnp.bfloat16)


def pack_kernel(*refs):
    parts, outs, sems = refs[:4], refs[4:6], refs[6]
    last = parts[0].shape[0] - 1
    odd = lax.rem(lax.axis_index("section"), 2)
    copies = []
    for n, part in enumerate(parts):
        for out, row in zip(outs, ((1 - odd) * last, odd * last)):
            sem = sems.at[len(copies)]
            copies.append(
                pltpu.make_async_copy(part.at[pl.ds(row, 1)], out.at[pl.ds(n, 1)], sem)
            )
    for copy in copies:
        copy.start()
    for copy in copies:
        copy.wait()


def interior(grad_ref, preact_ref, wholes, temporal_ref, spatial_ref, inner_ref, gpre_ref, views_ref):
    rows, cols, ch = grad_ref.shape
    step = 4

    for n in range(rows // step):
        here = pl.ds(n * step, step)
        grads = [ref[here] for ref in (grad_ref, *wholes)]
        gpre = pre_gradient(grads, preact_ref[here], temporal_ref)
        gpre_ref[here] = gpre.astype(jnp.bfloat16)
        beside(gpre, views_ref, n * step)

    half = rows // 2 - 1

    for n in range(2):
        first = grad_ref[pl.ds(n * half + 1, half)]
        inner_ref[pl.ds(n * half, half)] = convolved(views_ref, spatial_ref, n * half, first)


def edge_rows(grad_ref, pair_refs, afters, gpre_ref, temporal_ref, spatial_ref, views_ref):
    rows, cols, ch = grad_ref.shape
    (grad_above, grad_below), (above_pre, below_pre) = (beside_band(pair_refs, n) for n in (0, 1))
    above = [grad_above] + [ref[0:1] for ref in afters]
    below = [grad_below] + [ref[1:2] for ref in afters]
    beside(pre_gradient(above, above_pre, temporal_ref), views_ref, 0)
    beside(gpre_ref[0:2].astype(jnp.float32), views_ref, 1)
    beside(gpre_ref[rows - 2 : rows].astype(jnp.float32), views_ref, 3)
    beside(pre_gradient(below, below_pre, temporal_ref), views_ref, 5)
    return (
        convolved(views_ref, spatial_ref, 0, grad_ref[0:1]),
        convolved(views_ref, spatial_ref, 3, grad_ref[rows - 1 : rows]),
    )


def last_inner_kernel(grad_ref, preact_ref, temporal_ref, spatial_ref, inner_ref, gpre_ref, views_ref):
    @pl.when(is_last())
    def _():
        interior(
            grad_ref, preact_ref, [], temporal_ref, spatial_ref, inner_ref, gpre_ref, views_ref
        )


def last_edge_kernel(grad_ref, one_ref, two_ref, gpre_ref, temporal_ref, spatial_ref, edge_ref, views_ref):
    @pl.when(is_last())
    def _():
        pair_refs = (one_ref, two_ref)
        edge_ref[0:1], edge_ref[1:2] = edge_rows(
            grad_ref, pair_refs, [], gpre_ref, temporal_ref, spatial_ref, views_ref
        )
        edge_ref[2:3], edge_ref[3:4] = beside_band(pair_refs, 0)


def inner_kernel(later, *refs):
    inputs, wholes, kernels = refs[:2], refs[2 : 2 + later], refs[2 + later : 4 + later]
    known, outs = refs[4 + later : -3], refs[-3:]
    if not known:
        interior(*inputs, wholes, *kernels, *outs)
        return

    @pl.when(is_last())
    def _():
        outs[0][...] = known[0][...]
        outs[1][...] = known[1][...]

    @pl.when(jnp.logical_not(is_last()))
    def _():
        interior(*inputs, wholes, *kernels, *outs)


def mid_kernel(later, *refs):
    grad_ref, inner_ref, gpre_ref = refs[0], refs[3], refs[4]
    afters, (temporal_ref, spatial_ref, mid_ref, views_ref) = refs[5 : 5 + later], refs[5 + later :]
    rows = grad_ref.shape[0]
    first, last = edge_rows(
        grad_ref, refs[1:3], afters, gpre_ref, temporal_ref, spatial_ref, views_ref
    )
    mid_ref[0:1], mid_ref[rows - 1 : rows] = first, last
    mid_ref[1 : rows - 1] = inner_ref[...]


def two_kernel(later, *refs):
    saved_ref, preact_ref, gpre_ref = refs[:3]
    pair_refs, grad_ref = refs[3:5], refs[5]
    wholes, outs = refs[6 : 6 + later], refs[6 + later : 9 + later]
    views_ref, sides_ref, sums_ref = refs[9 + later :]
    rows, cols, ch = saved_ref.shape
    step = 4

    for n in range(rows // step):
        here = pl.ds(n * step, step)
        beside(gpre_ref[here].astype(jnp.float32), views_ref, n * step)

    views = views_ref[...].reshape(rows * cols, 3 * ch)
    grads = [ref[...] for ref in (grad_ref, *wholes)]
    left_sides(saved_ref, preact_ref, *beside_band(pair_refs, 2), sides_ref)
    kernel_sums(sides_ref, grads, views, sums_ref)
    hand_out(sums_ref, *outs)


def sides_kernel(saved_ref, preact_ref, one_ref, two_ref, sides_ref):
    left_sides(saved_ref, preact_ref, *beside_band((one_ref, two_ref), 3), sides_ref)


def pre_rows(preact, mids, temporal_ref, gpre_ref, views_ref, start):
    gpre = pre_gradient(mids, preact, temporal_ref)
    gpre_ref[start : start + preact.shape[0]] = gpre.astype(jnp.bfloat16)
    beside(gpre, views_ref, start)


def block_sums(gpre_ref, sides_ref, mids, views_ref, sums_ref, keep_ref, send_ref):
    rows, cols, ch = gpre_ref.shape
    odd = lax.rem(lax.axis_index("section"), 2)
    size = send_ref.shape[0] - 2 * cols
    send_ref[size : size + cols] = gpre_ref[(1 - odd) * (rows - 1)]
    send_ref[size + cols : size + 2 * cols] = gpre_ref[odd * (rows - 1)]
    views = views_ref[...].reshape(rows * cols, 3 * ch)
    kernel_sums(sides_ref, [ref[...] for ref in mids], views, sums_ref)
    height = keep_ref.shape[1]
    hand_out(sums_ref, keep_ref, send_ref.at[:height], send_ref.at[height : 2 * height])


def one_kernel(later, *refs):
    sides_ref, preact_ref, mids = refs[0], refs[1], refs[2 : 3 + later]
    temporal_ref, outs, scratch = refs[3 + later], refs[4 + later : 7 + later], refs[7 + later :]
    gpre_ref, keep_ref, send_ref = outs
    views_ref, sums_ref = scratch
    for n in range(preact_ref.shape[0] // 4):
        here = slice(4 * n, 4 * n + 4)
        grads = [ref[here] for ref in mids]
        pre_rows(preact_ref[here], grads, temporal_ref, gpre_ref, views_ref, 4 * n)
    block_sums(gpre_ref, sides_ref, mids, views_ref, sums_ref, keep_ref, send_ref)


def one_inner_kernel(preact_ref, inner_ref, after_ref, temporal_ref, gpre_ref, views_ref):
    rows = inner_ref.shape[0]
    for n in range(rows // 7):
        here = slice(7 * n, 7 * n + 7)
        after = after_ref[here]
        after = jnp.where(is_last(), jnp.zeros_like(after), after)
        preact = preact_ref[7 * n + 1 : 7 * n + 8]
        pre_rows(preact, [inner_ref[here], after], temporal_ref, gpre_ref, views_ref, 7 * n)


def mid_one_kernel(*refs):
    after_inner_ref, after_edge_ref = refs[5:7]
    temporal_two_ref, spatial_two_ref, sides_ref, preact_ref, temporal_ref = refs[7:12]
    inner_gpre_ref, inner_views_ref = refs[12:14]
    mid_ref, gpre_ref, keep_ref, send_ref = refs[14:18]
    views_ref, sums_ref, next_ref, edge_ref, edge_views_ref = refs[18:]
    rows = next_ref.shape[0]

    @pl.when(is_last())
    def _():
        edge_ref[...] = jnp.zeros(edge_ref.shape, edge_ref.dtype)
        next_ref[...] = jnp.zeros(next_ref.shape, next_ref.dtype)

    @pl.when(jnp.logical_not(is_last()))
    def _():
        edge_ref[...] = after_edge_ref[2:4]
        next_ref[0:1] = after_edge_ref[0:1]
        next_ref[1 : rows - 1] = after_inner_ref[...]
        next_ref[rows - 1 : rows] = after_edge_ref[1:2]

    mid_kernel(
        1, *refs[:5], edge_ref, temporal_two_ref, spatial_two_ref, mid_ref, edge_views_ref
    )
    gpre_ref[1 : rows - 1] = inner_gpre_ref[...]
    views_ref[1 : rows - 1] = inner_views_ref[...]
    for row in (0, rows - 1):
        here = slice(row, row + 1)
        grads = [mid_ref[here], next_ref[here]]
        pre_rows(preact_ref[here], grads, temporal_ref, gpre_ref, views_ref, row)
    block_sums(gpre_ref, sides_ref, [mid_ref, next_ref], views_ref, sums_ref, keep_ref, send_ref)


def input_kernel(mid_ref, gpre_ref, pair_ref, across_ref, spatial_ref, out_ref, token_ref, views_ref):
    rows, cols, ch = out_ref.shape
    pair = pair_ref[pair_ref.shape[0] - 2 * cols : pair_ref.shape[0] - cols]
    above, below = beside_band((pair[None], across_ref[across_ref.shape[0] - cols :][None]), 0)
    token_ref[...] = jnp.zeros(token_ref.shape, token_ref.dtype)
    step = 4
    beside(above.astype(jnp.float32), views_ref, 0)
    beside(below.astype(jnp.float32), views_ref, rows + 1)

    for n in range(rows // step):
        gpre = gpre_ref[pl.ds(n * step, step)].astype(jnp.float32)
        beside(gpre, views_ref, n * step + 1)

    for n in range(rows // step):
        here = pl.ds(n * step, step)
        out_ref[here] = convolved(views_ref, spatial_ref, n * step, mid_ref[here])


def halves(count, index):
    return [pl.ds(pl.multiple_of(n * count, count), count) for n in (index, 1 - index)]


def pair_kernel(keep_ref, low_ref, high_ref, own_ref, send_ref):
    across = lax.axis_index("section") // 2
    parts = [ref[...].astype(jnp.float32) for ref in (low_ref, high_ref)]
    own_ref[...] = keep_ref[across] + jnp.where(across == 0, *parts)
    total = keep_ref[1 - across] + jnp.where(across == 0, *parts[::-1])
    send_ref[...] = total.astype(jnp.bfloat16)


def band_kernel(own_ref, part_ref, keep_ref, send_ref):
    mine, other = halves(keep_ref.shape[0], lax.axis_index("video"))
    half = keep_ref.shape[0]
    keep_ref[...] = own_ref[mine] + part_ref[mine].astype(jnp.float32)
    send_ref[:half] = (own_ref[other] + part_ref[other].astype(jnp.float32)).astype(jnp.bfloat16)


def pair_quarter_kernel(keep_ref, part_ref, own_ref, across_ref, frame_ref, both_ref):
    _, height, _ = keep_ref.shape
    half = own_ref.shape[0]
    band = lax.axis_index("section") // 2
    frames = halves(half, lax.axis_index("video"))

    def quarter(band, rows):
        start = pl.multiple_of(band * height, height)
        part = part_ref.at[pl.ds(start, height)][rows]
        return keep_ref[band, rows] + part.astype(jnp.float32)

    own_ref[...] = quarter(band, frames[0])
    across_ref[:half] = quarter(1 - band, frames[0]).astype(jnp.bfloat16)
    rest = across_ref.shape[0] - half
    across_ref[half:] = part_ref[2 * height + rest :]
    frame_ref[...] = quarter(band, frames[1]).astype(jnp.bfloat16)
    both_ref[:half] = quarter(1 - band, frames[1]).astype(jnp.bfloat16)


def plane_kernel(own_ref, *refs):
    parts, out_ref = refs[:-1], refs[-1]
    total = own_ref[...]
    for part in parts:
        total = total + part[: out_ref.shape[0]].astype(jnp.float32)
    out_ref[...] = total.astype(jnp.bfloat16)


def add_kernel(one_ref, two_ref, out_ref):
    total = one_ref[...].astype(jnp.float32) + two_ref[: one_ref.shape[0]].astype(jnp.float32)
    out_ref[...] = total.astype(jnp.bfloat16)


def scaled_kernel(factor, *refs):
    out_ref = refs[-1]
    for block in range(2):
        one, two = (ref[...].astype(jnp.float32) for ref in refs[2 * block : 2 * block + 2])
        out_ref[block] = ((one + two) * factor).astype(jnp.bfloat16)


def place_kernel(places, skipped, zeros, *refs):
    shares, outs = refs[: len(places)], refs[-8:-4]
    sums_ref, sems, zeros_ref, zeros_sems = refs[-4:]
    band, frame = lax.axis_index("section"), lax.axis_index("video")
    _, rows, _ = shares[0].shape
    size = outs[0].shape[0]
    whole, cut = size // rows, size % rows

    def copies(n, block):
        flip, other = places[n]
        at = jnp.bitwise_xor(band, flip)
        if other is not None:
            at = 2 * at + jnp.bitwise_xor(frame, int(other))
        spatial, temporal = outs[2 * block : 2 * block + 2]
        source = sums_ref.at[n, block]
        start = pl.multiple_of(at * rows, 16)
        inside = [(at < whole, [(source, spatial.at[pl.ds(start, rows)])])]
        first = whole
        if cut:
            upper = source.at[pl.ds(0, cut)], spatial.at[pl.ds(whole * rows, cut)]
            lower = source.at[pl.ds(cut, rows - cut)], temporal.at[pl.ds(skipped, rows - cut)]
            inside.append((at == whole, [upper, lower]))
            first += 1
        start = pl.multiple_of((at - first) * rows + first * rows - size + skipped, 16)
        inside.append((at >= first, [(source, temporal.at[pl.ds(start, rows)])]))
        return [
            (here, [(*pair, sems.at[n, block, part]) for part, pair in enumerate(pairs)])
            for here, pairs in inside
        ]

    def each(act):
        for n in range(len(shares)):
            for block in range(2):
                if act == "start":
                    sums_ref[n, block] = shares[n][block].astype(jnp.float32)
                for here, pairs in copies(n, block):

                    @pl.when(here)
                    def _():
                        for pair in pairs:
                            getattr(pltpu.make_async_copy(*pair), act)()

        if zeros and skipped:
            for block in range(2):
                target = outs[2 * block + 1].at[pl.ds(0, skipped)]
                copy = pltpu.make_async_copy(zeros_ref, target, zeros_sems.at[block])
                getattr(copy, act)()

    zeros_ref[...] = jnp.zeros(zeros_ref.shape, zeros_ref.dtype)
    each("start")
    each("wait")


def placed(shares, places, skipped, given=()):
    _, rows, ch = shares[0].shape
    count = len(shares)
    outs = (f32(9 * ch, ch), f32(3 * ch, ch)) * 2
    vmem, spare = (pl.BlockSpec(memory_space=space) for space in (pltpu.VMEM, pl.ANY))
    return pl.pallas_call(
        functools.partial(place_kernel, places, skipped, not given),
        out_shape=outs,
        in_specs=[vmem] * count + [spare] * len(given),
        out_specs=(spare,) * 4,
        scratch_shapes=[
            pltpu.VMEM((count, 2, rows, ch), jnp.float32),
            pltpu.SemaphoreType.DMA((count, 2, 2)),
            pltpu.VMEM((max(skipped, 8), ch), jnp.float32),
            pltpu.SemaphoreType.DMA((2,)),
        ],
        input_output_aliases={count + n: n for n in range(len(given))},
        compiler_params=pltpu.CompilerParams(vmem_limit_bytes=24 * MIB),
        cost_estimate=pl.CostEstimate(
            flops=0, bytes_accessed=6 * count * rows * ch * 2, transcendentals=0
        ),
    )(*shares, *given)


def unpacked(sums):
    ch = sums[0].shape[-1]
    return [x.reshape((3,) * (1 + (x.shape[0] > 3 * ch)) + (ch, ch)) for x in sums]


def on_device(
    grad_latent,
    input_one,
    preact_one,
    input_two,
    preact_two,
    spatial_one,
    temporal_one,
    spatial_two,
    temporal_two,
):
    shape = grad_latent.shape
    rows, cols, ch = shape[2:]
    bands, frames = lax.axis_size("section"), lax.axis_size("video")
    later = min(2, frames - 1)
    pixels = lax.axis_size("dp") * frames * bands * rows * cols
    factor = 1.0 / math.sqrt(pixels)
    grad, saved_one, pre_one, saved_two, pre_two = (
        x.reshape(rows, cols, ch)
        for x in (grad_latent, input_one, preact_one, input_two, preact_two)
    )
    conv = 2 * rows * cols * 9 * ch * ch
    views = pltpu.VMEM((rows, cols, 3 * ch), jnp.bfloat16)
    edge_views = pltpu.VMEM((6, cols, 3 * ch), jnp.bfloat16)
    act = pltpu.VMEM((rows, cols, ch), jnp.bfloat16)
    sides = bf16(4, ch, rows * cols)
    blocks = 10 + later
    height = blocks * ch // 4
    half = height // 2
    skipped = (2 - later) * ch
    sums = pltpu.VMEM((blocks * ch, ch), jnp.float32)
    handed = [f32(2, height, ch)] + [bf16(height, ch)] * 2
    inner_outs = [bf16(rows - 2, cols, ch), bf16(rows, cols, ch)]
    kernels = (temporal_two, spatial_two)

    def from_later(x):
        if frames == 2:
            return [flipped(x, "video", 1)]
        return [from_ahead(x, 0, n + 1) for n in range(later)]

    wholes = from_later(grad)
    packs = call(
        pack_kernel,
        [bf16(4, cols, ch)] * 2,
        [pltpu.SemaphoreType.DMA((8,))],
        1,
        grad,
        pre_two,
        saved_two,
        saved_one,
        spare_inputs=True,
        limit=58,
    )
    second = flipped(packs[1], "section", 1)
    first = flipped(later_than(packs[0], second), "section", 1)
    pairs = [first, flipped(second, "section", 2)]

    known = ()
    if frames == 2:
        known = call(
            last_inner_kernel,
            inner_outs,
            [views],
            0,
            grad,
            pre_two,
            *kernels,
            after=(first, second),
        )
        afters = from_later(known[0])
    else:
        afters = from_later(jnp.concatenate(beside_band(pairs, 0)))
    inner, gpre_two = call(
        functools.partial(inner_kernel, later),
        inner_outs,
        [views],
        0,
        grad,
        pre_two,
        *wholes,
        *kernels,
        *known,
        early=(saved_two, saved_one, pre_one, temporal_one),
    )
    if frames == 2:
        edge = call(
            last_edge_kernel,
            [bf16(4, cols, ch)],
            [edge_views],
            0,
            grad,
            *pairs,
            known[1],
            *kernels,
            after=(gpre_two,),
        )
        afters += from_later(edge)
    parts_two = call(
        functools.partial(two_kernel, later),
        handed,
        [views, pltpu.VMEM(sides.shape, sides.dtype), sums],
        8 * conv,
        saved_two,
        pre_two,
        gpre_two,
        *pairs,
        grad,
        *wholes,
        after=(edge,) if frames == 2 else (),
    )
    sides_one = call(
        sides_kernel, [sides], [], conv // 8, saved_one, pre_one, *pairs, after=parts_two[:1]
    )
    keep_two, low_two, high_two = parts_two
    own_two, send_two = call(
        pair_kernel,
        [f32(height, ch), bf16(height, ch)],
        [],
        height * ch,
        keep_two,
        flipped(low_two, "section", 1),
        flipped(high_two, "section", 1),
    )
    across_two = flipped(send_two, "section", 2)
    mid_inputs = (grad, *pairs, inner, gpre_two)
    one_inputs = (sides_one, pre_one)
    mid_outs = [bf16(rows, cols, ch)]
    one_outs = [bf16(rows, cols, ch), f32(2, height, ch), bf16(2 * height + 2 * cols, ch)]
    if frames == 2:
        inners_one = call(
            one_inner_kernel,
            [bf16(rows - 2, cols, ch), bf16(rows - 2, cols, 3 * ch)],
            [],
            conv // 8,
            pre_one,
            inner,
            afters[0],
            temporal_one,
        )
        mid, gpre_one, *parts_one = call(
            mid_one_kernel,
            mid_outs + one_outs,
            [views, sums, act, pltpu.VMEM((2, cols, ch), jnp.bfloat16), edge_views],
            8 * conv,
            *mid_inputs,
            *afters,
            *kernels,
            *one_inputs,
            temporal_one,
            *inners_one,
            after=(own_two,),
        )
    else:
        mid = call(
            functools.partial(mid_kernel, later),
            mid_outs,
            [edge_views],
            conv // 8,
            *mid_inputs,
            *afters,
            *kernels,
        )
        gpre_one, *parts_one = call(
            functools.partial(one_kernel, later),
            one_outs,
            [views, sums],
            1.2 * conv,
            *one_inputs,
            mid,
            *from_later(mid),
            temporal_one,
        )
    keep_one, send_one = parts_one
    split = frames == 2 and lax.axis_size("dp") == 4
    if split:
        send_one = later_than(send_one, across_two)
    pair_one = flipped(send_one, "section", 1)

    def input_gradient(edge, after):
        return call(
            input_kernel,
            [bf16(rows, cols, ch), f32(8, 128)],
            [pltpu.VMEM((rows + 2, cols, 3 * ch), jnp.bfloat16)],
            conv,
            mid,
            gpre_one,
            pair_one,
            edge,
            spatial_one,
            after=after,
        )

    if split:

        def added(one, two):
            return call(add_kernel, [bf16(half, ch)], [], half * ch, one, two)

        keep_two, send_two = call(
            band_kernel,
            [f32(half, ch), bf16(half + 2 * cols, ch)],
            [],
            0,
            own_two,
            across_two,
        )
        sum_two = added(keep_two, flipped(send_two, "video", 1))
        quarters = [f32(half, ch)] + [bf16(half + more, ch) for more in (cols, 0, cols + 16)]
        own_one, *sends = call(
            pair_quarter_kernel, quarters, [], 0, keep_one, pair_one, after=(send_two,)
        )
        across = flipped(sends[0], "section", 2)
        parts = [across, flipped(sends[1], "video", 1), flipped_both(sends[2])]
        sum_one = call(plane_kernel, [bf16(half, ch)], [], 4 * half * ch, own_one, *parts)
        part_two = flipped(sum_two, "dp", 1)
        part_one = flipped(later_than(sum_one, sum_two), "dp", 1)
        sum_two = added(sum_two, part_two)
        sum_one = added(sum_one, part_one)
        last_two = flipped(sum_two, "dp", 2)
        last_one = flipped(later_than(sum_one, sum_two), "dp", 2)
        grad_in, token = input_gradient(across, (sum_one,))
        own = call(
            functools.partial(scaled_kernel, factor),
            [bf16(2, half, ch)],
            [],
            height * ch,
            sum_one,
            last_one,
            sum_two,
            last_two,
            after=(token,),
        )
        frame, across, both = flipped(own, "video", 1), flipped(own, "section", 2), flipped_both(own)
        shares = [own, frame, across]
        shares += [flipped(share, "section", 1) for share in shares]
        places = [(0, False), (0, True), (2, False), (1, False), (1, True), (3, False)]
        sums = placed([*shares, both], [*places, (2, True)], skipped)
        sums = unpacked(placed([flipped(both, "section", 1)], [(3, True)], skipped, sums))
    else:
        own_one, send_one = call(
            pair_kernel,
            [f32(height, ch), bf16(height, ch)],
            [],
            height * ch,
            keep_one,
            pair_one[:height],
            pair_one[height : 2 * height],
        )
        edge = flipped(pair_one[pair_one.shape[0] - cols :], "section", 2)
        grad_in, _ = input_gradient(edge, ())
        own_one = own_one + flipped(send_one, "section", 2).astype(jnp.float32)
        own_two = own_two + across_two.astype(jnp.float32)
        share = lax.psum(jnp.stack((own_one, own_two)), ("video", "dp")) * factor
        share = share.astype(jnp.bfloat16)
        shares = [share, flipped(share, "section", 2)]
        shares += [flipped(share, "section", 1) for share in shares]
        places = [(0, None), (2, None), (1, None), (3, None)]
        sums = unpacked(placed(shares, places, skipped))
    return (grad_in.reshape(shape), *sums)


def solution(mesh):
    whole = P("dp", "video", "section", None, None)
    return jax.shard_map(
        on_device,
        mesh=mesh,
        in_specs=(whole,) * 5 + (P(),) * 4,
        out_specs=(whole, P(), P(), P(), P()),
        check_vma=False,
    )
```

```python
import functools
import math

import jax
import jax.numpy as jnp
from jax import lax
from jax.experimental import pallas as pl
from jax.experimental.pallas import tpu as pltpu
from jax.sharding import PartitionSpec as P

MIB = 1024 * 1024


def sigmoid(value):
    return 1.0 / (1.0 + jnp.exp(-value))


def bf16(*shape):
    return jax.ShapeDtypeStruct(shape, jnp.bfloat16)


def f32(*shape):
    return jax.ShapeDtypeStruct(shape, jnp.float32)


def call(kernel, outs, scratch, flops, *operands, after=(), early=(), spare_inputs=False, limit=24):
    single = len(outs) == 1
    moved = sum(math.prod(x.shape) * x.dtype.itemsize for x in (*operands, *outs))
    vmem = pl.BlockSpec(memory_space=pltpu.VMEM)
    spare = pl.BlockSpec(memory_space=pl.ANY)
    spec = spare if spare_inputs else vmem
    count = len(operands)
    operands = (*operands, *early, *after)

    def body(*refs):
        kernel(*refs[:count], *refs[len(operands) :])

    return pl.pallas_call(
        body,
        out_shape=outs[0] if single else tuple(outs),
        in_specs=[spec] * count + [vmem] * len(early) + [spare] * len(after),
        out_specs=vmem if single else (vmem,) * len(outs),
        scratch_shapes=scratch,
        compiler_params=pltpu.CompilerParams(vmem_limit_bytes=limit * MIB),
        cost_estimate=pl.CostEstimate(
            flops=int(flops), bytes_accessed=int(moved) if flops else 0, transcendentals=0
        ),
    )(*operands)


def from_ahead(block, band_step, frame_step):
    bands, frames = lax.axis_size("section"), lax.axis_size("video")
    pairs = [
        ((band + band_step) * frames + frame + frame_step, band * frames + frame)
        for band in range(bands)
        for frame in range(frames)
        if 0 <= band + band_step < bands and frame + frame_step < frames
    ]
    return lax.ppermute(block, ("section", "video"), pairs)


def beside_band(pair_refs, row):
    band = lax.axis_index("section")
    odd = lax.rem(band, 2) == 1
    inside = (band > 0) & (band < lax.axis_size("section") - 1)
    first, second = (ref[row : row + 1] for ref in pair_refs)
    second = jnp.where(inside, second, jnp.zeros_like(second))
    return jnp.where(odd, first, second), jnp.where(odd, second, first)


def flipped(block, axis, flip):
    count = lax.axis_size(axis)
    return lax.ppermute(block, axis, [(place ^ flip, place) for place in range(count)])


def flipped_both(block):
    bands = lax.axis_size("section")
    pairs = [
        (2 * (band ^ 2) + 1 - frame, 2 * band + frame) for band in range(bands) for frame in range(2)
    ]
    return lax.ppermute(block, ("section", "video"), pairs)


def later_than(block, *others):
    return lax.optimization_barrier((block, *others))[0]


def beside(gpre, views_ref, start):
    count, cols, ch = gpre.shape
    at = lax.broadcasted_iota(jnp.int32, gpre.shape, 1)
    right = jnp.where(at == cols - 1, 0.0, pltpu.roll(gpre, cols - 1, 1))
    left = jnp.where(at == 0, 0.0, pltpu.roll(gpre, 1, 1))
    here = pl.ds(start, count)
    views_ref[here, :, 0:ch] = right.astype(jnp.bfloat16)
    views_ref[here, :, ch : 2 * ch] = gpre.astype(jnp.bfloat16)
    views_ref[here, :, 2 * ch : 3 * ch] = left.astype(jnp.bfloat16)


def pre_gradient(grads, preact, temporal_ref):
    count, cols, ch = preact.shape
    flat = jnp.concatenate([grad.reshape(count * cols, ch) for grad in grads], axis=1)
    kernel = jnp.concatenate([temporal_ref[2 - step] for step in range(len(grads))], axis=1)
    gact = lax.dot_general(
        flat, kernel, (((1,), (1,)), ((), ())), preferred_element_type=jnp.float32
    )
    gact = gact.astype(jnp.bfloat16).astype(jnp.float32).reshape(preact.shape)
    hval = preact.astype(jnp.float32)
    sig = sigmoid(hval)
    return gact * sig * (1.0 + hval * (1.0 - sig))


def convolved(views_ref, spatial_ref, start, first):
    count, cols, ch = first.shape
    total = first.astype(jnp.float32).reshape(count * cols, ch)
    for ky in range(3):
        view = views_ref[pl.ds(start + 2 - ky, count)].reshape(count * cols, 3 * ch)
        kernel = jnp.concatenate([spatial_ref[ky, kx] for kx in range(3)], axis=1)
        total = total + lax.dot_general(
            view, kernel, (((1,), (1,)), ((), ())), preferred_element_type=jnp.float32
        )
    return total.astype(jnp.bfloat16).reshape(first.shape)


def is_last():
    return lax.axis_index("video") == lax.axis_size("video") - 1


def left_sides(saved_ref, preact_ref, above, below, sides_ref):
    rows, cols, ch = saved_ref.shape
    flat = (rows * cols, ch)
    shifts = [
        jnp.concatenate([above, saved_ref[: rows - 1]], axis=0),
        saved_ref[...],
        jnp.concatenate([saved_ref[1:], below], axis=0),
    ]
    for n, shift in enumerate(shifts):
        sides_ref[n] = shift.reshape(flat).T
    hval = preact_ref[...].astype(jnp.float32)
    sides_ref[3] = (hval * sigmoid(hval)).astype(jnp.bfloat16).reshape(flat).T


def kernel_sums(sides_ref, grads, views, sums_ref):
    _, ch, pixels = sides_ref.shape
    shifts = sides_ref[0:3].reshape(3 * ch, pixels)
    sums = jnp.dot(shifts, views, preferred_element_type=jnp.float32)
    for ky in range(3):
        for kx in range(3):
            here = slice(kx * ch, (kx + 1) * ch)
            sums_ref[ky, here] = sums[ky * ch : (ky + 1) * ch, here]
    grads = jnp.concatenate([grad.reshape(pixels, ch) for grad in grads], axis=1)
    sums = jnp.dot(sides_ref[3], grads, preferred_element_type=jnp.float32)
    zeros = jnp.zeros((ch, ch), jnp.float32)
    for k in range(3):
        step = 2 - k
        value = sums[:, step * ch : (step + 1) * ch] if step * ch < grads.shape[1] else zeros
        sums_ref[3, k * ch : (k + 1) * ch] = jnp.where(is_last(), zeros, value) if step else value


def hand_out(sums_ref, keep_ref, *send_refs):
    odd = lax.rem(lax.axis_index("section"), 2)
    for n, send_ref in enumerate(send_refs):
        keep_ref[n] = sums_ref[2 * n + odd]
        send_ref[...] = sums_ref[2 * n + 1 - odd].astype(jnp.bfloat16)


def pack_kernel(*refs):
    parts, outs, sems = refs[:4], refs[4:6], refs[6]
    last = parts[0].shape[0] - 1
    odd = lax.rem(lax.axis_index("section"), 2)
    copies = []
    for n, part in enumerate(parts):
        for out, row in zip(outs, ((1 - odd) * last, odd * last)):
            sem = sems.at[len(copies)]
            copies.append(
                pltpu.make_async_copy(part.at[pl.ds(row, 1)], out.at[pl.ds(n, 1)], sem)
            )
    for copy in copies:
        copy.start()
    for copy in copies:
        copy.wait()


def interior(grad_ref, preact_ref, wholes, temporal_ref, spatial_ref, inner_ref, gpre_ref, views_ref):
    rows, cols, ch = grad_ref.shape
    step = 4

    for n in range(rows // step):
        here = pl.ds(n * step, step)
        grads = [ref[here] for ref in (grad_ref, *wholes)]
        gpre = pre_gradient(grads, preact_ref[here], temporal_ref)
        gpre_ref[here] = gpre.astype(jnp.bfloat16)
        beside(gpre, views_ref, n * step)

    half = rows // 2 - 1

    for n in range(2):
        first = grad_ref[pl.ds(n * half + 1, half)]
        inner_ref[pl.ds(n * half, half)] = convolved(views_ref, spatial_ref, n * half, first)


def edge_rows(grad_ref, pair_refs, afters, gpre_ref, temporal_ref, spatial_ref, views_ref):
    rows, cols, ch = grad_ref.shape
    (grad_above, grad_below), (above_pre, below_pre) = (beside_band(pair_refs, n) for n in (0, 1))
    above = [grad_above] + [ref[0:1] for ref in afters]
    below = [grad_below] + [ref[1:2] for ref in afters]
    beside(pre_gradient(above, above_pre, temporal_ref), views_ref, 0)
    beside(gpre_ref[0:2].astype(jnp.float32), views_ref, 1)
    beside(gpre_ref[rows - 2 : rows].astype(jnp.float32), views_ref, 3)
    beside(pre_gradient(below, below_pre, temporal_ref), views_ref, 5)
    return (
        convolved(views_ref, spatial_ref, 0, grad_ref[0:1]),
        convolved(views_ref, spatial_ref, 3, grad_ref[rows - 1 : rows]),
    )


def last_inner_kernel(grad_ref, preact_ref, temporal_ref, spatial_ref, inner_ref, gpre_ref, views_ref):
    @pl.when(is_last())
    def _():
        interior(
            grad_ref, preact_ref, [], temporal_ref, spatial_ref, inner_ref, gpre_ref, views_ref
        )


def last_edge_kernel(grad_ref, one_ref, two_ref, gpre_ref, temporal_ref, spatial_ref, edge_ref, views_ref):
    @pl.when(is_last())
    def _():
        pair_refs = (one_ref, two_ref)
        edge_ref[0:1], edge_ref[1:2] = edge_rows(
            grad_ref, pair_refs, [], gpre_ref, temporal_ref, spatial_ref, views_ref
        )
        edge_ref[2:3], edge_ref[3:4] = beside_band(pair_refs, 0)


def inner_kernel(later, *refs):
    inputs, wholes, kernels = refs[:2], refs[2 : 2 + later], refs[2 + later : 4 + later]
    known, outs = refs[4 + later : -3], refs[-3:]
    if not known:
        interior(*inputs, wholes, *kernels, *outs)
        return

    @pl.when(is_last())
    def _():
        outs[0][...] = known[0][...]
        outs[1][...] = known[1][...]

    @pl.when(jnp.logical_not(is_last()))
    def _():
        interior(*inputs, wholes, *kernels, *outs)


def mid_kernel(later, *refs):
    grad_ref, inner_ref, gpre_ref = refs[0], refs[3], refs[4]
    afters, (temporal_ref, spatial_ref, mid_ref, views_ref) = refs[5 : 5 + later], refs[5 + later :]
    rows = grad_ref.shape[0]
    first, last = edge_rows(
        grad_ref, refs[1:3], afters, gpre_ref, temporal_ref, spatial_ref, views_ref
    )
    mid_ref[0:1], mid_ref[rows - 1 : rows] = first, last
    mid_ref[1 : rows - 1] = inner_ref[...]


def two_kernel(later, *refs):
    saved_ref, preact_ref, gpre_ref = refs[:3]
    pair_refs, grad_ref = refs[3:5], refs[5]
    wholes, outs = refs[6 : 6 + later], refs[6 + later : 9 + later]
    views_ref, sides_ref, sums_ref = refs[9 + later :]
    rows, cols, ch = saved_ref.shape
    step = 4

    for n in range(rows // step):
        here = pl.ds(n * step, step)
        beside(gpre_ref[here].astype(jnp.float32), views_ref, n * step)

    views = views_ref[...].reshape(rows * cols, 3 * ch)
    grads = [ref[...] for ref in (grad_ref, *wholes)]
    left_sides(saved_ref, preact_ref, *beside_band(pair_refs, 2), sides_ref)
    kernel_sums(sides_ref, grads, views, sums_ref)
    hand_out(sums_ref, *outs)


def sides_kernel(saved_ref, preact_ref, one_ref, two_ref, sides_ref):
    left_sides(saved_ref, preact_ref, *beside_band((one_ref, two_ref), 3), sides_ref)


def pre_rows(preact, mids, temporal_ref, gpre_ref, views_ref, start):
    gpre = pre_gradient(mids, preact, temporal_ref)
    gpre_ref[start : start + preact.shape[0]] = gpre.astype(jnp.bfloat16)
    beside(gpre, views_ref, start)


def block_sums(gpre_ref, sides_ref, mids, views_ref, sums_ref, keep_ref, send_ref):
    rows, cols, ch = gpre_ref.shape
    odd = lax.rem(lax.axis_index("section"), 2)
    size = send_ref.shape[0] - 2 * cols
    send_ref[size : size + cols] = gpre_ref[(1 - odd) * (rows - 1)]
    send_ref[size + cols : size + 2 * cols] = gpre_ref[odd * (rows - 1)]
    views = views_ref[...].reshape(rows * cols, 3 * ch)
    kernel_sums(sides_ref, [ref[...] for ref in mids], views, sums_ref)
    height = sums_ref.shape[1]
    hand_out(sums_ref, keep_ref, send_ref.at[:height], send_ref.at[height : 2 * height])


def one_kernel(later, *refs):
    sides_ref, preact_ref, mids = refs[0], refs[1], refs[2 : 3 + later]
    temporal_ref, outs, scratch = refs[3 + later], refs[4 + later : 7 + later], refs[7 + later :]
    gpre_ref, keep_ref, send_ref = outs
    views_ref, sums_ref = scratch
    for n in range(preact_ref.shape[0] // 4):
        here = slice(4 * n, 4 * n + 4)
        grads = [ref[here] for ref in mids]
        pre_rows(preact_ref[here], grads, temporal_ref, gpre_ref, views_ref, 4 * n)
    block_sums(gpre_ref, sides_ref, mids, views_ref, sums_ref, keep_ref, send_ref)


def one_inner_kernel(preact_ref, inner_ref, after_ref, temporal_ref, gpre_ref, views_ref):
    rows = inner_ref.shape[0]
    for n in range(rows // 7):
        here = slice(7 * n, 7 * n + 7)
        after = after_ref[here]
        after = jnp.where(is_last(), jnp.zeros_like(after), after)
        preact = preact_ref[7 * n + 1 : 7 * n + 8]
        pre_rows(preact, [inner_ref[here], after], temporal_ref, gpre_ref, views_ref, 7 * n)


def mid_one_kernel(*refs):
    after_inner_ref, after_edge_ref = refs[5:7]
    temporal_two_ref, spatial_two_ref, sides_ref, preact_ref, temporal_ref = refs[7:12]
    inner_gpre_ref, inner_views_ref = refs[12:14]
    mid_ref, gpre_ref, keep_ref, send_ref = refs[14:18]
    views_ref, sums_ref, next_ref, edge_ref, edge_views_ref = refs[18:]
    rows = next_ref.shape[0]

    @pl.when(is_last())
    def _():
        edge_ref[...] = jnp.zeros(edge_ref.shape, edge_ref.dtype)
        next_ref[...] = jnp.zeros(next_ref.shape, next_ref.dtype)

    @pl.when(jnp.logical_not(is_last()))
    def _():
        edge_ref[...] = after_edge_ref[2:4]
        next_ref[0:1] = after_edge_ref[0:1]
        next_ref[1 : rows - 1] = after_inner_ref[...]
        next_ref[rows - 1 : rows] = after_edge_ref[1:2]

    mid_kernel(
        1, *refs[:5], edge_ref, temporal_two_ref, spatial_two_ref, mid_ref, edge_views_ref
    )
    gpre_ref[1 : rows - 1] = inner_gpre_ref[...]
    views_ref[1 : rows - 1] = inner_views_ref[...]
    for row in (0, rows - 1):
        here = slice(row, row + 1)
        grads = [mid_ref[here], next_ref[here]]
        pre_rows(preact_ref[here], grads, temporal_ref, gpre_ref, views_ref, row)
    block_sums(gpre_ref, sides_ref, [mid_ref, next_ref], views_ref, sums_ref, keep_ref, send_ref)


def input_kernel(mid_ref, gpre_ref, pair_ref, across_ref, spatial_ref, out_ref, token_ref, views_ref):
    rows, cols, ch = out_ref.shape
    pair = pair_ref[pair_ref.shape[0] - 2 * cols : pair_ref.shape[0] - cols]
    above, below = beside_band((pair[None], across_ref[across_ref.shape[0] - cols :][None]), 0)
    token_ref[...] = jnp.zeros(token_ref.shape, token_ref.dtype)
    step = 4
    beside(above.astype(jnp.float32), views_ref, 0)
    beside(below.astype(jnp.float32), views_ref, rows + 1)

    for n in range(rows // step):
        gpre = gpre_ref[pl.ds(n * step, step)].astype(jnp.float32)
        beside(gpre, views_ref, n * step + 1)

    for n in range(rows // step):
        here = pl.ds(n * step, step)
        out_ref[here] = convolved(views_ref, spatial_ref, n * step, mid_ref[here])


def halves(count, index):
    return [pl.ds(pl.multiple_of(n * count, count), count) for n in (index, 1 - index)]


def pair_kernel(keep_ref, low_ref, high_ref, own_ref, send_ref):
    across = lax.axis_index("section") // 2
    parts = [ref[...].astype(jnp.float32) for ref in (low_ref, high_ref)]
    own_ref[...] = keep_ref[across] + jnp.where(across == 0, *parts)
    total = keep_ref[1 - across] + jnp.where(across == 0, *parts[::-1])
    send_ref[...] = total.astype(jnp.bfloat16)


def band_kernel(own_ref, part_ref, keep_ref, send_ref):
    mine, other = halves(keep_ref.shape[0], lax.axis_index("video"))
    half = keep_ref.shape[0]
    keep_ref[...] = own_ref[mine] + part_ref[mine].astype(jnp.float32)
    send_ref[:half] = (own_ref[other] + part_ref[other].astype(jnp.float32)).astype(jnp.bfloat16)


def pair_quarter_kernel(keep_ref, part_ref, own_ref, across_ref, frame_ref, both_ref):
    _, height, _ = keep_ref.shape
    half = own_ref.shape[0]
    band = lax.axis_index("section") // 2
    frames = halves(half, lax.axis_index("video"))

    def quarter(band, rows):
        start = pl.multiple_of(band * height, height)
        part = part_ref.at[pl.ds(start, height)][rows]
        return keep_ref[band, rows] + part.astype(jnp.float32)

    own_ref[...] = quarter(band, frames[0])
    across_ref[:half] = quarter(1 - band, frames[0]).astype(jnp.bfloat16)
    rest = across_ref.shape[0] - half
    across_ref[half:] = part_ref[2 * height + rest :]
    frame_ref[...] = quarter(band, frames[1]).astype(jnp.bfloat16)
    both_ref[:half] = quarter(1 - band, frames[1]).astype(jnp.bfloat16)


def plane_kernel(own_ref, *refs):
    parts, out_ref = refs[:-1], refs[-1]
    total = own_ref[...]
    for part in parts:
        total = total + part[: out_ref.shape[0]].astype(jnp.float32)
    out_ref[...] = total.astype(jnp.bfloat16)


def add_kernel(one_ref, two_ref, out_ref):
    total = one_ref[...].astype(jnp.float32) + two_ref[: one_ref.shape[0]].astype(jnp.float32)
    out_ref[...] = total.astype(jnp.bfloat16)


def scaled_kernel(factor, *refs):
    out_ref, long_ref = refs[-2:]
    height = out_ref.shape[1]
    for block in range(2):
        one, two = (ref[...].astype(jnp.float32) for ref in refs[2 * block : 2 * block + 2])
        total = ((one + two) * factor).astype(jnp.bfloat16)
        out_ref[block] = total
        long_ref[block, :height] = total


def place_kernel(places, *refs):
    shares, outs = refs[: len(places)], refs[-6:-2]
    sums_ref, sems = refs[-2:]
    band, frame = lax.axis_index("section"), lax.axis_index("video")
    height = sums_ref.shape[2]

    def copies(n, block):
        flip, other = places[n]
        place = jnp.bitwise_xor(band, flip)
        half = 0 if other is None else jnp.bitwise_xor(frame, int(other))
        here = pl.ds(pl.multiple_of(half * height, height), height)
        spatial, temporal = outs[2 * block : 2 * block + 2]
        source, sem = sums_ref.at[n, block], sems.at[n, block]
        return (
            (place < 3, lambda: pltpu.make_async_copy(source, spatial.at[place, here], sem)),
            (place == 3, lambda: pltpu.make_async_copy(source, temporal.at[here], sem)),
        )

    for n, share in enumerate(shares):
        for block in range(2):
            sums_ref[n, block] = share[block, :height].astype(jnp.float32)
            for inside, copy in copies(n, block):
                pl.when(inside)(lambda: copy().start())
    for n in range(len(shares)):
        for block in range(2):
            for inside, copy in copies(n, block):
                pl.when(inside)(lambda: copy().wait())


def placed(shares, places, given=()):
    ch = shares[0].shape[2]
    height = 3 * ch if places[0][1] is None else 3 * ch // 2
    count = len(shares)
    outs = (f32(3, 3 * ch, ch), f32(3 * ch, ch)) * 2
    vmem, spare = (pl.BlockSpec(memory_space=space) for space in (pltpu.VMEM, pl.ANY))
    return pl.pallas_call(
        functools.partial(place_kernel, places),
        out_shape=outs,
        in_specs=[vmem] * count + [spare] * len(given),
        out_specs=(spare,) * 4,
        scratch_shapes=[
            pltpu.VMEM((count, 2, height, ch), jnp.float32),
            pltpu.SemaphoreType.DMA((count, 2)),
        ],
        input_output_aliases={count + n: n for n in range(len(given))},
        compiler_params=pltpu.CompilerParams(vmem_limit_bytes=24 * MIB),
        cost_estimate=pl.CostEstimate(
            flops=0, bytes_accessed=6 * count * height * ch * 2, transcendentals=0
        ),
    )(*shares, *given)


def unpacked(sums):
    ch = sums[0].shape[-1]
    return [x.reshape(3, 3, ch, ch) if x.ndim == 3 else x.reshape(3, ch, ch) for x in sums]


def on_device(
    grad_latent,
    input_one,
    preact_one,
    input_two,
    preact_two,
    spatial_one,
    temporal_one,
    spatial_two,
    temporal_two,
):
    shape = grad_latent.shape
    rows, cols, ch = shape[2:]
    bands, frames = lax.axis_size("section"), lax.axis_size("video")
    later = min(2, frames - 1)
    pixels = lax.axis_size("dp") * frames * bands * rows * cols
    factor = 1.0 / math.sqrt(pixels)
    grad, saved_one, pre_one, saved_two, pre_two = (
        x.reshape(rows, cols, ch)
        for x in (grad_latent, input_one, preact_one, input_two, preact_two)
    )
    conv = 2 * rows * cols * 9 * ch * ch
    views = pltpu.VMEM((rows, cols, 3 * ch), jnp.bfloat16)
    edge_views = pltpu.VMEM((6, cols, 3 * ch), jnp.bfloat16)
    act = pltpu.VMEM((rows, cols, ch), jnp.bfloat16)
    sides = bf16(4, ch, rows * cols)
    sums = pltpu.VMEM((4, 3 * ch, ch), jnp.float32)
    handed = [f32(2, 3 * ch, ch)] + [bf16(3 * ch, ch)] * 2
    inner_outs = [bf16(rows - 2, cols, ch), bf16(rows, cols, ch)]
    kernels = (temporal_two, spatial_two)

    def from_later(x):
        if frames == 2:
            return [flipped(x, "video", 1)]
        return [from_ahead(x, 0, n + 1) for n in range(later)]

    wholes = from_later(grad)
    packs = call(
        pack_kernel,
        [bf16(4, cols, ch)] * 2,
        [pltpu.SemaphoreType.DMA((8,))],
        1,
        grad,
        pre_two,
        saved_two,
        saved_one,
        spare_inputs=True,
        limit=58,
    )
    second = flipped(packs[1], "section", 1)
    first = flipped(later_than(packs[0], second), "section", 1)
    pairs = [first, flipped(second, "section", 2)]

    known = ()
    if frames == 2:
        known = call(
            last_inner_kernel,
            inner_outs,
            [views],
            0,
            grad,
            pre_two,
            *kernels,
            after=(first, second),
        )
        afters = from_later(known[0])
    else:
        afters = from_later(jnp.concatenate(beside_band(pairs, 0)))
    inner, gpre_two = call(
        functools.partial(inner_kernel, later),
        inner_outs,
        [views],
        0,
        grad,
        pre_two,
        *wholes,
        *kernels,
        *known,
        early=(saved_two, saved_one, pre_one, temporal_one),
    )
    if frames == 2:
        edge = call(
            last_edge_kernel,
            [bf16(4, cols, ch)],
            [edge_views],
            0,
            grad,
            *pairs,
            known[1],
            *kernels,
            after=(gpre_two,),
        )
        afters += from_later(edge)
    parts_two = call(
        functools.partial(two_kernel, later),
        handed,
        [views, pltpu.VMEM(sides.shape, sides.dtype), sums],
        8 * conv,
        saved_two,
        pre_two,
        gpre_two,
        *pairs,
        grad,
        *wholes,
        after=(edge,) if frames == 2 else (),
    )
    sides_one = call(
        sides_kernel, [sides], [], conv // 8, saved_one, pre_one, *pairs, after=parts_two[:1]
    )
    height, half = 3 * ch, 3 * ch // 2
    keep_two, low_two, high_two = parts_two
    own_two, send_two = call(
        pair_kernel,
        [f32(height, ch), bf16(height, ch)],
        [],
        height * ch,
        keep_two,
        flipped(low_two, "section", 1),
        flipped(high_two, "section", 1),
    )
    across_two = flipped(send_two, "section", 2)
    mid_inputs = (grad, *pairs, inner, gpre_two)
    one_inputs = (sides_one, pre_one)
    mid_outs = [bf16(rows, cols, ch)]
    one_outs = [bf16(rows, cols, ch), f32(2, 3 * ch, ch), bf16(6 * ch + 2 * cols, ch)]
    if frames == 2:
        inners_one = call(
            one_inner_kernel,
            [bf16(rows - 2, cols, ch), bf16(rows - 2, cols, 3 * ch)],
            [],
            conv // 8,
            pre_one,
            inner,
            afters[0],
            temporal_one,
        )
        mid, gpre_one, *parts_one = call(
            mid_one_kernel,
            mid_outs + one_outs,
            [views, sums, act, pltpu.VMEM((2, cols, ch), jnp.bfloat16), edge_views],
            8 * conv,
            *mid_inputs,
            *afters,
            *kernels,
            *one_inputs,
            temporal_one,
            *inners_one,
            after=(own_two,),
        )
    else:
        mid = call(
            functools.partial(mid_kernel, later),
            mid_outs,
            [edge_views],
            conv // 8,
            *mid_inputs,
            *afters,
            *kernels,
        )
        gpre_one, *parts_one = call(
            functools.partial(one_kernel, later),
            one_outs,
            [views, sums],
            1.2 * conv,
            *one_inputs,
            mid,
            *from_later(mid),
            temporal_one,
        )
    keep_one, send_one = parts_one
    split = frames == 2 and lax.axis_size("dp") == 4
    if split:
        send_one = later_than(send_one, across_two)
    pair_one = flipped(send_one, "section", 1)

    def input_gradient(edge, after):
        return call(
            input_kernel,
            [bf16(rows, cols, ch), f32(8, 128)],
            [pltpu.VMEM((rows + 2, cols, 3 * ch), jnp.bfloat16)],
            conv,
            mid,
            gpre_one,
            pair_one,
            edge,
            spatial_one,
            after=after,
        )

    if split:

        def added(one, two):
            return call(add_kernel, [bf16(half, ch)], [], half * ch, one, two)

        keep_two, send_two = call(
            band_kernel,
            [f32(half, ch), bf16(half + 2 * cols, ch)],
            [],
            0,
            own_two,
            across_two,
        )
        sum_two = added(keep_two, flipped(send_two, "video", 1))
        quarters = [f32(half, ch)] + [bf16(half + more, ch) for more in (cols, 0, cols + 16)]
        own_one, *sends = call(
            pair_quarter_kernel, quarters, [], 0, keep_one, pair_one, after=(send_two,)
        )
        across = flipped(sends[0], "section", 2)
        parts = [across, flipped(sends[1], "video", 1), flipped_both(sends[2])]
        sum_one = call(plane_kernel, [bf16(half, ch)], [], 4 * half * ch, own_one, *parts)
        part_two = flipped(sum_two, "dp", 1)
        part_one = flipped(later_than(sum_one, sum_two), "dp", 1)
        sum_two = added(sum_two, part_two)
        sum_one = added(sum_one, part_one)
        last_two = flipped(sum_two, "dp", 2)
        last_one = flipped(later_than(sum_one, sum_two), "dp", 2)
        grad_in, token = input_gradient(across, (sum_one,))
        own, longer = call(
            functools.partial(scaled_kernel, factor),
            [bf16(2, half, ch), bf16(2, half + 16, ch)],
            [],
            height * ch,
            sum_one,
            last_one,
            sum_two,
            last_two,
            after=(token,),
        )
        shares = [own, flipped_both(longer), flipped(own, "video", 1)]
        shares += [flipped(share, "section", 1) for share in shares]
        across = flipped(own, "section", 2)
        places = [(0, False), (2, True), (0, True), (1, False), (3, True), (1, True)]
        sums = placed([*shares, across], [*places, (2, False)])
        sums = unpacked(placed([flipped(across, "section", 1)], [(3, False)], sums))
    else:
        own_one, send_one = call(
            pair_kernel,
            [f32(height, ch), bf16(height, ch)],
            [],
            height * ch,
            keep_one,
            pair_one[:height],
            pair_one[height : 2 * height],
        )
        edge = flipped(pair_one[pair_one.shape[0] - cols :], "section", 2)
        grad_in, _ = input_gradient(edge, ())
        own_one = own_one + flipped(send_one, "section", 2).astype(jnp.float32)
        own_two = own_two + across_two.astype(jnp.float32)
        share = lax.psum(jnp.stack((own_one, own_two)), ("video", "dp")) * factor
        share = share.astype(jnp.bfloat16)
        shares = [share, flipped(share, "section", 2)]
        shares += [flipped(share, "section", 1) for share in shares]
        sums = unpacked(placed(shares, [(0, None), (2, None), (1, None), (3, None)]))
    return (grad_in.reshape(shape), *sums)


def solution(mesh):
    whole = P("dp", "video", "section", None, None)
    return jax.shard_map(
        on_device,
        mesh=mesh,
        in_specs=(whole,) * 5 + (P(),) * 4,
        out_specs=(whole, P(), P(), P(), P()),
        check_vma=False,
    )
```

```python
import functools
import math

import jax
import jax.numpy as jnp
from jax import lax
from jax.experimental import pallas as pl
from jax.experimental.pallas import tpu as pltpu
from jax.sharding import PartitionSpec as P

MIB = 1024 * 1024


def sigmoid(value):
    return 1.0 / (1.0 + jnp.exp(-value))


def bf16(*shape):
    return jax.ShapeDtypeStruct(shape, jnp.bfloat16)


def f32(*shape):
    return jax.ShapeDtypeStruct(shape, jnp.float32)


def call(kernel, outs, scratch, flops, *operands, after=(), early=(), spare_inputs=False, limit=24):
    single = len(outs) == 1
    moved = sum(math.prod(x.shape) * x.dtype.itemsize for x in (*operands, *outs))
    vmem = pl.BlockSpec(memory_space=pltpu.VMEM)
    spare = pl.BlockSpec(memory_space=pl.ANY)
    spec = spare if spare_inputs else vmem
    count = len(operands)
    operands = (*operands, *early, *after)

    def body(*refs):
        kernel(*refs[:count], *refs[len(operands) :])

    return pl.pallas_call(
        body,
        out_shape=outs[0] if single else tuple(outs),
        in_specs=[spec] * count + [vmem] * len(early) + [spare] * len(after),
        out_specs=vmem if single else (vmem,) * len(outs),
        scratch_shapes=scratch,
        compiler_params=pltpu.CompilerParams(vmem_limit_bytes=limit * MIB),
        cost_estimate=pl.CostEstimate(
            flops=int(flops), bytes_accessed=int(moved) if flops else 0, transcendentals=0
        ),
    )(*operands)


def from_ahead(block, band_step, frame_step):
    bands, frames = lax.axis_size("section"), lax.axis_size("video")
    pairs = [
        ((band + band_step) * frames + frame + frame_step, band * frames + frame)
        for band in range(bands)
        for frame in range(frames)
        if 0 <= band + band_step < bands and frame + frame_step < frames
    ]
    return lax.ppermute(block, ("section", "video"), pairs)


def beside_band(pair_refs, row):
    band = lax.axis_index("section")
    odd = lax.rem(band, 2) == 1
    inside = (band > 0) & (band < lax.axis_size("section") - 1)
    first, second = (ref[row : row + 1] for ref in pair_refs)
    second = jnp.where(inside, second, jnp.zeros_like(second))
    return jnp.where(odd, first, second), jnp.where(odd, second, first)


def flipped(block, axis, flip):
    count = lax.axis_size(axis)
    return lax.ppermute(block, axis, [(place ^ flip, place) for place in range(count)])


def flipped_both(block):
    bands = lax.axis_size("section")
    pairs = [
        (2 * (band ^ 2) + 1 - frame, 2 * band + frame) for band in range(bands) for frame in range(2)
    ]
    return lax.ppermute(block, ("section", "video"), pairs)


def later_than(block, *others):
    return lax.optimization_barrier((block, *others))[0]


def beside(gpre, views_ref, start):
    count, cols, ch = gpre.shape
    at = lax.broadcasted_iota(jnp.int32, gpre.shape, 1)
    right = jnp.where(at == cols - 1, 0.0, pltpu.roll(gpre, cols - 1, 1))
    left = jnp.where(at == 0, 0.0, pltpu.roll(gpre, 1, 1))
    here = pl.ds(start, count)
    views_ref[here, :, 0:ch] = right.astype(jnp.bfloat16)
    views_ref[here, :, ch : 2 * ch] = gpre.astype(jnp.bfloat16)
    views_ref[here, :, 2 * ch : 3 * ch] = left.astype(jnp.bfloat16)


def pre_gradient(grads, preact, temporal_ref):
    count, cols, ch = preact.shape
    flat = jnp.concatenate([grad.reshape(count * cols, ch) for grad in grads], axis=1)
    kernel = jnp.concatenate([temporal_ref[2 - step] for step in range(len(grads))], axis=1)
    gact = lax.dot_general(
        flat, kernel, (((1,), (1,)), ((), ())), preferred_element_type=jnp.float32
    )
    gact = gact.astype(jnp.bfloat16).astype(jnp.float32).reshape(preact.shape)
    hval = preact.astype(jnp.float32)
    sig = sigmoid(hval)
    return gact * sig * (1.0 + hval * (1.0 - sig))


def convolved(views_ref, spatial_ref, start, first):
    count, cols, ch = first.shape
    total = first.astype(jnp.float32).reshape(count * cols, ch)
    for ky in range(3):
        view = views_ref[pl.ds(start + 2 - ky, count)].reshape(count * cols, 3 * ch)
        kernel = jnp.concatenate([spatial_ref[ky, kx] for kx in range(3)], axis=1)
        total = total + lax.dot_general(
            view, kernel, (((1,), (1,)), ((), ())), preferred_element_type=jnp.float32
        )
    return total.astype(jnp.bfloat16).reshape(first.shape)


def is_last():
    return lax.axis_index("video") == lax.axis_size("video") - 1


def left_sides(saved_ref, preact_ref, above, below, sides_ref):
    rows, cols, ch = saved_ref.shape
    flat = (rows * cols, ch)
    shifts = [
        jnp.concatenate([above, saved_ref[: rows - 1]], axis=0),
        saved_ref[...],
        jnp.concatenate([saved_ref[1:], below], axis=0),
    ]
    for n, shift in enumerate(shifts):
        sides_ref[n] = shift.reshape(flat).T
    hval = preact_ref[...].astype(jnp.float32)
    sides_ref[3] = (hval * sigmoid(hval)).astype(jnp.bfloat16).reshape(flat).T


def kernel_sums(sides_ref, grads, views, sums_ref):
    _, ch, pixels = sides_ref.shape
    shifts = sides_ref[0:3].reshape(3 * ch, pixels)
    sums = jnp.dot(shifts, views, preferred_element_type=jnp.float32)
    for ky in range(3):
        for kx in range(3):
            here = slice(kx * ch, (kx + 1) * ch)
            sums_ref[ky, here] = sums[ky * ch : (ky + 1) * ch, here]
    grads = jnp.concatenate([grad.reshape(pixels, ch) for grad in grads], axis=1)
    sums = jnp.dot(sides_ref[3], grads, preferred_element_type=jnp.float32)
    zeros = jnp.zeros((ch, ch), jnp.float32)
    for k in range(3):
        step = 2 - k
        value = sums[:, step * ch : (step + 1) * ch] if step * ch < grads.shape[1] else zeros
        sums_ref[3, k * ch : (k + 1) * ch] = jnp.where(is_last(), zeros, value) if step else value


def hand_out(sums_ref, keep_ref, *send_refs):
    odd = lax.rem(lax.axis_index("section"), 2)
    for n, send_ref in enumerate(send_refs):
        keep_ref[n] = sums_ref[2 * n + odd]
        send_ref[...] = sums_ref[2 * n + 1 - odd].astype(jnp.bfloat16)


def pack_kernel(*refs):
    parts, outs, sems = refs[:4], refs[4:6], refs[6]
    last = parts[0].shape[0] - 1
    odd = lax.rem(lax.axis_index("section"), 2)
    copies = []
    for n, part in enumerate(parts):
        for out, row in zip(outs, ((1 - odd) * last, odd * last)):
            sem = sems.at[len(copies)]
            copies.append(
                pltpu.make_async_copy(part.at[pl.ds(row, 1)], out.at[pl.ds(n, 1)], sem)
            )
    for copy in copies:
        copy.start()
    for copy in copies:
        copy.wait()


def interior(grad_ref, preact_ref, wholes, temporal_ref, spatial_ref, inner_ref, gpre_ref, views_ref):
    rows, cols, ch = grad_ref.shape
    step = 4

    for n in range(rows // step):
        here = pl.ds(n * step, step)
        grads = [ref[here] for ref in (grad_ref, *wholes)]
        gpre = pre_gradient(grads, preact_ref[here], temporal_ref)
        gpre_ref[here] = gpre.astype(jnp.bfloat16)
        beside(gpre, views_ref, n * step)

    half = rows // 2 - 1

    for n in range(2):
        first = grad_ref[pl.ds(n * half + 1, half)]
        inner_ref[pl.ds(n * half, half)] = convolved(views_ref, spatial_ref, n * half, first)


def edge_rows(grad_ref, pair_refs, afters, gpre_ref, temporal_ref, spatial_ref, views_ref):
    rows, cols, ch = grad_ref.shape
    (grad_above, grad_below), (above_pre, below_pre) = (beside_band(pair_refs, n) for n in (0, 1))
    above = [grad_above] + [ref[0:1] for ref in afters]
    below = [grad_below] + [ref[1:2] for ref in afters]
    beside(pre_gradient(above, above_pre, temporal_ref), views_ref, 0)
    beside(gpre_ref[0:2].astype(jnp.float32), views_ref, 1)
    beside(gpre_ref[rows - 2 : rows].astype(jnp.float32), views_ref, 3)
    beside(pre_gradient(below, below_pre, temporal_ref), views_ref, 5)
    return (
        convolved(views_ref, spatial_ref, 0, grad_ref[0:1]),
        convolved(views_ref, spatial_ref, 3, grad_ref[rows - 1 : rows]),
    )


def last_inner_kernel(grad_ref, preact_ref, temporal_ref, spatial_ref, inner_ref, gpre_ref, views_ref):
    @pl.when(is_last())
    def _():
        interior(
            grad_ref, preact_ref, [], temporal_ref, spatial_ref, inner_ref, gpre_ref, views_ref
        )


def last_edge_kernel(grad_ref, one_ref, two_ref, gpre_ref, temporal_ref, spatial_ref, edge_ref, views_ref):
    @pl.when(is_last())
    def _():
        pair_refs = (one_ref, two_ref)
        edge_ref[0:1], edge_ref[1:2] = edge_rows(
            grad_ref, pair_refs, [], gpre_ref, temporal_ref, spatial_ref, views_ref
        )
        edge_ref[2:3], edge_ref[3:4] = beside_band(pair_refs, 0)


def inner_kernel(later, *refs):
    inputs, wholes, kernels = refs[:2], refs[2 : 2 + later], refs[2 + later : 4 + later]
    known, outs = refs[4 + later : -3], refs[-3:]
    if not known:
        interior(*inputs, wholes, *kernels, *outs)
        return

    @pl.when(is_last())
    def _():
        outs[0][...] = known[0][...]
        outs[1][...] = known[1][...]

    @pl.when(jnp.logical_not(is_last()))
    def _():
        interior(*inputs, wholes, *kernels, *outs)


def mid_kernel(later, *refs):
    grad_ref, inner_ref, gpre_ref = refs[0], refs[3], refs[4]
    afters, (temporal_ref, spatial_ref, mid_ref, views_ref) = refs[5 : 5 + later], refs[5 + later :]
    rows = grad_ref.shape[0]
    first, last = edge_rows(
        grad_ref, refs[1:3], afters, gpre_ref, temporal_ref, spatial_ref, views_ref
    )
    mid_ref[0:1], mid_ref[rows - 1 : rows] = first, last
    mid_ref[1 : rows - 1] = inner_ref[...]


def two_kernel(later, *refs):
    saved_ref, preact_ref, gpre_ref = refs[:3]
    pair_refs, grad_ref = refs[3:5], refs[5]
    wholes, outs = refs[6 : 6 + later], refs[6 + later : 9 + later]
    views_ref, sides_ref, sums_ref = refs[9 + later :]
    rows, cols, ch = saved_ref.shape
    step = 4

    for n in range(rows // step):
        here = pl.ds(n * step, step)
        beside(gpre_ref[here].astype(jnp.float32), views_ref, n * step)

    views = views_ref[...].reshape(rows * cols, 3 * ch)
    grads = [ref[...] for ref in (grad_ref, *wholes)]
    left_sides(saved_ref, preact_ref, *beside_band(pair_refs, 2), sides_ref)
    kernel_sums(sides_ref, grads, views, sums_ref)
    hand_out(sums_ref, *outs)


def sides_kernel(saved_ref, preact_ref, one_ref, two_ref, sides_ref):
    left_sides(saved_ref, preact_ref, *beside_band((one_ref, two_ref), 3), sides_ref)


def pre_rows(preact, mids, temporal_ref, gpre_ref, views_ref, start):
    gpre = pre_gradient(mids, preact, temporal_ref)
    gpre_ref[start : start + preact.shape[0]] = gpre.astype(jnp.bfloat16)
    beside(gpre, views_ref, start)


def block_sums(gpre_ref, sides_ref, mids, views_ref, sums_ref, keep_ref, send_ref):
    rows, cols, ch = gpre_ref.shape
    odd = lax.rem(lax.axis_index("section"), 2)
    size = send_ref.shape[0] - 2 * cols
    send_ref[size : size + cols] = gpre_ref[(1 - odd) * (rows - 1)]
    send_ref[size + cols : size + 2 * cols] = gpre_ref[odd * (rows - 1)]
    views = views_ref[...].reshape(rows * cols, 3 * ch)
    kernel_sums(sides_ref, [ref[...] for ref in mids], views, sums_ref)
    height = sums_ref.shape[1]
    hand_out(sums_ref, keep_ref, send_ref.at[:height], send_ref.at[height : 2 * height])


def one_kernel(later, *refs):
    sides_ref, preact_ref, mids = refs[0], refs[1], refs[2 : 3 + later]
    temporal_ref, outs, scratch = refs[3 + later], refs[4 + later : 7 + later], refs[7 + later :]
    gpre_ref, keep_ref, send_ref = outs
    views_ref, sums_ref = scratch
    for n in range(preact_ref.shape[0] // 4):
        here = slice(4 * n, 4 * n + 4)
        grads = [ref[here] for ref in mids]
        pre_rows(preact_ref[here], grads, temporal_ref, gpre_ref, views_ref, 4 * n)
    block_sums(gpre_ref, sides_ref, mids, views_ref, sums_ref, keep_ref, send_ref)


def one_inner_kernel(preact_ref, inner_ref, after_ref, temporal_ref, gpre_ref, views_ref):
    rows = inner_ref.shape[0]
    for n in range(rows // 7):
        here = slice(7 * n, 7 * n + 7)
        after = after_ref[here]
        after = jnp.where(is_last(), jnp.zeros_like(after), after)
        preact = preact_ref[7 * n + 1 : 7 * n + 8]
        pre_rows(preact, [inner_ref[here], after], temporal_ref, gpre_ref, views_ref, 7 * n)


def mid_one_kernel(*refs):
    after_inner_ref, after_edge_ref = refs[5:7]
    temporal_two_ref, spatial_two_ref, sides_ref, preact_ref, temporal_ref = refs[7:12]
    inner_gpre_ref, inner_views_ref = refs[12:14]
    mid_ref, gpre_ref, keep_ref, send_ref = refs[14:18]
    views_ref, sums_ref, next_ref, edge_ref, edge_views_ref = refs[18:]
    rows = next_ref.shape[0]

    @pl.when(is_last())
    def _():
        edge_ref[...] = jnp.zeros(edge_ref.shape, edge_ref.dtype)
        next_ref[...] = jnp.zeros(next_ref.shape, next_ref.dtype)

    @pl.when(jnp.logical_not(is_last()))
    def _():
        edge_ref[...] = after_edge_ref[2:4]
        next_ref[0:1] = after_edge_ref[0:1]
        next_ref[1 : rows - 1] = after_inner_ref[...]
        next_ref[rows - 1 : rows] = after_edge_ref[1:2]

    mid_kernel(
        1, *refs[:5], edge_ref, temporal_two_ref, spatial_two_ref, mid_ref, edge_views_ref
    )
    gpre_ref[1 : rows - 1] = inner_gpre_ref[...]
    views_ref[1 : rows - 1] = inner_views_ref[...]
    for row in (0, rows - 1):
        here = slice(row, row + 1)
        grads = [mid_ref[here], next_ref[here]]
        pre_rows(preact_ref[here], grads, temporal_ref, gpre_ref, views_ref, row)
    block_sums(gpre_ref, sides_ref, [mid_ref, next_ref], views_ref, sums_ref, keep_ref, send_ref)


def input_kernel(mid_ref, gpre_ref, pair_ref, across_ref, spatial_ref, out_ref, token_ref, views_ref):
    rows, cols, ch = out_ref.shape
    pair = pair_ref[pair_ref.shape[0] - 2 * cols : pair_ref.shape[0] - cols]
    above, below = beside_band((pair[None], across_ref[across_ref.shape[0] - cols :][None]), 0)
    token_ref[...] = jnp.zeros(token_ref.shape, token_ref.dtype)
    step = 4
    beside(above.astype(jnp.float32), views_ref, 0)
    beside(below.astype(jnp.float32), views_ref, rows + 1)

    for n in range(rows // step):
        gpre = gpre_ref[pl.ds(n * step, step)].astype(jnp.float32)
        beside(gpre, views_ref, n * step + 1)

    for n in range(rows // step):
        here = pl.ds(n * step, step)
        out_ref[here] = convolved(views_ref, spatial_ref, n * step, mid_ref[here])


def halves(count, index):
    return [pl.ds(pl.multiple_of(n * count, count), count) for n in (index, 1 - index)]


def pair_kernel(keep_ref, low_ref, high_ref, own_ref, send_ref):
    across = lax.axis_index("section") // 2
    parts = [ref[...].astype(jnp.float32) for ref in (low_ref, high_ref)]
    own_ref[...] = keep_ref[across] + jnp.where(across == 0, *parts)
    total = keep_ref[1 - across] + jnp.where(across == 0, *parts[::-1])
    send_ref[...] = total.astype(jnp.bfloat16)


def band_kernel(own_ref, part_ref, keep_ref, send_ref):
    mine, other = halves(keep_ref.shape[0], lax.axis_index("video"))
    half = keep_ref.shape[0]
    keep_ref[...] = own_ref[mine] + part_ref[mine].astype(jnp.float32)
    send_ref[:half] = (own_ref[other] + part_ref[other].astype(jnp.float32)).astype(jnp.bfloat16)


def pair_quarter_kernel(keep_ref, part_ref, own_ref, across_ref, frame_ref, both_ref):
    _, height, _ = keep_ref.shape
    half = own_ref.shape[0]
    band = lax.axis_index("section") // 2
    frames = halves(half, lax.axis_index("video"))

    def quarter(band, rows):
        start = pl.multiple_of(band * height, height)
        part = part_ref.at[pl.ds(start, height)][rows]
        return keep_ref[band, rows] + part.astype(jnp.float32)

    own_ref[...] = quarter(band, frames[0])
    across_ref[:half] = quarter(1 - band, frames[0]).astype(jnp.bfloat16)
    rest = across_ref.shape[0] - half
    across_ref[half:] = part_ref[2 * height + rest :]
    frame_ref[...] = quarter(band, frames[1]).astype(jnp.bfloat16)
    both_ref[:half] = quarter(1 - band, frames[1]).astype(jnp.bfloat16)


def plane_kernel(own_ref, *refs):
    parts, out_ref = refs[:-1], refs[-1]
    total = own_ref[...]
    for part in parts:
        total = total + part[: out_ref.shape[0]].astype(jnp.float32)
    out_ref[...] = total.astype(jnp.bfloat16)


def add_kernel(one_ref, two_ref, out_ref):
    total = one_ref[...].astype(jnp.float32) + two_ref[: one_ref.shape[0]].astype(jnp.float32)
    out_ref[...] = total.astype(jnp.bfloat16)


def scaled_kernel(factor, *refs):
    outs = refs[4:]
    height = outs[0].shape[1]
    for block in range(2):
        one, two = (ref[...].astype(jnp.float32) for ref in refs[2 * block : 2 * block + 2])
        total = ((one + two) * factor).astype(jnp.bfloat16)
        for out_ref in outs:
            out_ref[block, :height] = total


def place_kernel(places, *refs):
    shares, outs = refs[: len(places)], refs[-6:-2]
    sums_ref, sems = refs[-2:]
    band, frame = lax.axis_index("section"), lax.axis_index("video")
    height = sums_ref.shape[2]

    def copies(n, block):
        flip, other = places[n]
        place = jnp.bitwise_xor(band, flip)
        half = 0 if other is None else jnp.bitwise_xor(frame, int(other))
        here = pl.ds(pl.multiple_of(half * height, height), height)
        spatial, temporal = outs[2 * block : 2 * block + 2]
        source, sem = sums_ref.at[n, block], sems.at[n, block]
        return (
            (place < 3, lambda: pltpu.make_async_copy(source, spatial.at[place, here], sem)),
            (place == 3, lambda: pltpu.make_async_copy(source, temporal.at[here], sem)),
        )

    for n, share in enumerate(shares):
        for block in range(2):
            sums_ref[n, block] = share[block, :height].astype(jnp.float32)
            for inside, copy in copies(n, block):
                pl.when(inside)(lambda: copy().start())
    for n in range(len(shares)):
        for block in range(2):
            for inside, copy in copies(n, block):
                pl.when(inside)(lambda: copy().wait())


def placed(shares, places, given=()):
    ch = shares[0].shape[2]
    height = 3 * ch if places[0][1] is None else 3 * ch // 2
    count = len(shares)
    outs = (f32(3, 3 * ch, ch), f32(3 * ch, ch)) * 2
    vmem, spare = (pl.BlockSpec(memory_space=space) for space in (pltpu.VMEM, pl.ANY))
    return pl.pallas_call(
        functools.partial(place_kernel, places),
        out_shape=outs,
        in_specs=[vmem] * count + [spare] * len(given),
        out_specs=(spare,) * 4,
        scratch_shapes=[
            pltpu.VMEM((count, 2, height, ch), jnp.float32),
            pltpu.SemaphoreType.DMA((count, 2)),
        ],
        input_output_aliases={count + n: n for n in range(len(given))},
        compiler_params=pltpu.CompilerParams(vmem_limit_bytes=24 * MIB),
        cost_estimate=pl.CostEstimate(
            flops=0, bytes_accessed=6 * count * height * ch * 2, transcendentals=0
        ),
    )(*shares, *given)


def unpacked(sums):
    ch = sums[0].shape[-1]
    return [x.reshape(3, 3, ch, ch) if x.ndim == 3 else x.reshape(3, ch, ch) for x in sums]


def on_device(
    grad_latent,
    input_one,
    preact_one,
    input_two,
    preact_two,
    spatial_one,
    temporal_one,
    spatial_two,
    temporal_two,
):
    shape = grad_latent.shape
    rows, cols, ch = shape[2:]
    bands, frames = lax.axis_size("section"), lax.axis_size("video")
    later = min(2, frames - 1)
    pixels = lax.axis_size("dp") * frames * bands * rows * cols
    factor = 1.0 / math.sqrt(pixels)
    grad, saved_one, pre_one, saved_two, pre_two = (
        x.reshape(rows, cols, ch)
        for x in (grad_latent, input_one, preact_one, input_two, preact_two)
    )
    conv = 2 * rows * cols * 9 * ch * ch
    views = pltpu.VMEM((rows, cols, 3 * ch), jnp.bfloat16)
    edge_views = pltpu.VMEM((6, cols, 3 * ch), jnp.bfloat16)
    act = pltpu.VMEM((rows, cols, ch), jnp.bfloat16)
    sides = bf16(4, ch, rows * cols)
    sums = pltpu.VMEM((4, 3 * ch, ch), jnp.float32)
    handed = [f32(2, 3 * ch, ch)] + [bf16(3 * ch, ch)] * 2
    inner_outs = [bf16(rows - 2, cols, ch), bf16(rows, cols, ch)]
    kernels = (temporal_two, spatial_two)

    def from_later(x):
        if frames == 2:
            return [flipped(x, "video", 1)]
        return [from_ahead(x, 0, n + 1) for n in range(later)]

    wholes = from_later(grad)
    packs = call(
        pack_kernel,
        [bf16(4, cols, ch)] * 2,
        [pltpu.SemaphoreType.DMA((8,))],
        1,
        grad,
        pre_two,
        saved_two,
        saved_one,
        spare_inputs=True,
        limit=58,
    )
    second = flipped(packs[1], "section", 1)
    first = flipped(later_than(packs[0], second), "section", 1)
    pairs = [first, flipped(second, "section", 2)]

    known = ()
    if frames == 2:
        known = call(
            last_inner_kernel,
            inner_outs,
            [views],
            0,
            grad,
            pre_two,
            *kernels,
            after=(first, second),
        )
        afters = from_later(known[0])
    else:
        afters = from_later(jnp.concatenate(beside_band(pairs, 0)))
    inner, gpre_two = call(
        functools.partial(inner_kernel, later),
        inner_outs,
        [views],
        0,
        grad,
        pre_two,
        *wholes,
        *kernels,
        *known,
        early=(saved_two, saved_one, pre_one, temporal_one),
    )
    if frames == 2:
        edge = call(
            last_edge_kernel,
            [bf16(4, cols, ch)],
            [edge_views],
            0,
            grad,
            *pairs,
            known[1],
            *kernels,
            after=(gpre_two,),
        )
        afters += from_later(edge)
    parts_two = call(
        functools.partial(two_kernel, later),
        handed,
        [views, pltpu.VMEM(sides.shape, sides.dtype), sums],
        8 * conv,
        saved_two,
        pre_two,
        gpre_two,
        *pairs,
        grad,
        *wholes,
        after=(edge,) if frames == 2 else (),
    )
    sides_one = call(
        sides_kernel, [sides], [], conv // 8, saved_one, pre_one, *pairs, after=parts_two[:1]
    )
    height, half = 3 * ch, 3 * ch // 2
    keep_two, low_two, high_two = parts_two
    own_two, send_two = call(
        pair_kernel,
        [f32(height, ch), bf16(height, ch)],
        [],
        height * ch,
        keep_two,
        flipped(low_two, "section", 1),
        flipped(high_two, "section", 1),
    )
    across_two = flipped(send_two, "section", 2)
    mid_inputs = (grad, *pairs, inner, gpre_two)
    one_inputs = (sides_one, pre_one)
    mid_outs = [bf16(rows, cols, ch)]
    one_outs = [bf16(rows, cols, ch), f32(2, 3 * ch, ch), bf16(6 * ch + 2 * cols, ch)]
    if frames == 2:
        inners_one = call(
            one_inner_kernel,
            [bf16(rows - 2, cols, ch), bf16(rows - 2, cols, 3 * ch)],
            [],
            conv // 8,
            pre_one,
            inner,
            afters[0],
            temporal_one,
        )
        mid, gpre_one, *parts_one = call(
            mid_one_kernel,
            mid_outs + one_outs,
            [views, sums, act, pltpu.VMEM((2, cols, ch), jnp.bfloat16), edge_views],
            8 * conv,
            *mid_inputs,
            *afters,
            *kernels,
            *one_inputs,
            temporal_one,
            *inners_one,
            after=(own_two,),
        )
    else:
        mid = call(
            functools.partial(mid_kernel, later),
            mid_outs,
            [edge_views],
            conv // 8,
            *mid_inputs,
            *afters,
            *kernels,
        )
        gpre_one, *parts_one = call(
            functools.partial(one_kernel, later),
            one_outs,
            [views, sums],
            1.2 * conv,
            *one_inputs,
            mid,
            *from_later(mid),
            temporal_one,
        )
    keep_one, send_one = parts_one
    split = frames == 2 and lax.axis_size("dp") == 4
    if split:
        send_one = later_than(send_one, across_two)
    pair_one = flipped(send_one, "section", 1)

    def input_gradient(edge, after):
        return call(
            input_kernel,
            [bf16(rows, cols, ch), f32(8, 128)],
            [pltpu.VMEM((rows + 2, cols, 3 * ch), jnp.bfloat16)],
            conv,
            mid,
            gpre_one,
            pair_one,
            edge,
            spatial_one,
            after=after,
        )

    if split:

        def added(one, two):
            return call(add_kernel, [bf16(half, ch)], [], half * ch, one, two)

        keep_two, send_two = call(
            band_kernel,
            [f32(half, ch), bf16(half + 2 * cols, ch)],
            [],
            0,
            own_two,
            across_two,
        )
        sum_two = added(keep_two, flipped(send_two, "video", 1))
        quarters = [f32(half, ch)] + [bf16(half + more, ch) for more in (cols, 0, cols + 16)]
        own_one, *sends = call(
            pair_quarter_kernel, quarters, [], 0, keep_one, pair_one, after=(send_two,)
        )
        across = flipped(sends[0], "section", 2)
        parts = [across, flipped(sends[1], "video", 1), flipped_both(sends[2])]
        sum_one = call(plane_kernel, [bf16(half, ch)], [], 4 * half * ch, own_one, *parts)
        part_two = flipped(sum_two, "dp", 1)
        part_one = flipped(later_than(sum_one, sum_two), "dp", 1)
        sum_two = added(sum_two, part_two)
        sum_one = added(sum_one, part_one)
        last_two = flipped(sum_two, "dp", 2)
        last_one = flipped(later_than(sum_one, sum_two), "dp", 2)
        grad_in, token = input_gradient(across, (sum_one,))
        own, longer, longest = call(
            functools.partial(scaled_kernel, factor),
            [bf16(2, half + more, ch) for more in (0, 16, 32)],
            [],
            height * ch,
            sum_one,
            last_one,
            sum_two,
            last_two,
            after=(token,),
        )
        frame, both = flipped(longest, "video", 1), flipped_both(longer)
        shares = [own, frame, flipped(own, "section", 2)]
        shares += [flipped(share, "section", 1) for share in shares]
        places = [(0, False), (0, True), (2, False), (1, False), (1, True), (3, False)]
        sums = placed([*shares, both], [*places, (2, True)])
        sums = unpacked(placed([flipped(both, "section", 1)], [(3, True)], sums))
    else:
        own_one, send_one = call(
            pair_kernel,
            [f32(height, ch), bf16(height, ch)],
            [],
            height * ch,
            keep_one,
            pair_one[:height],
            pair_one[height : 2 * height],
        )
        edge = flipped(pair_one[pair_one.shape[0] - cols :], "section", 2)
        grad_in, _ = input_gradient(edge, ())
        own_one = own_one + flipped(send_one, "section", 2).astype(jnp.float32)
        own_two = own_two + across_two.astype(jnp.float32)
        share = lax.psum(jnp.stack((own_one, own_two)), ("video", "dp")) * factor
        share = share.astype(jnp.bfloat16)
        shares = [share, flipped(share, "section", 2)]
        shares += [flipped(share, "section", 1) for share in shares]
        sums = unpacked(placed(shares, [(0, None), (2, None), (1, None), (3, None)]))
    return (grad_in.reshape(shape), *sums)


def solution(mesh):
    whole = P("dp", "video", "section", None, None)
    return jax.shard_map(
        on_device,
        mesh=mesh,
        in_specs=(whole,) * 5 + (P(),) * 4,
        out_specs=(whole, P(), P(), P(), P()),
        check_vma=False,
    )
```

```python
import functools
import math

import jax
import jax.numpy as jnp
from jax import lax
from jax.experimental import pallas as pl
from jax.experimental.pallas import tpu as pltpu
from jax.sharding import PartitionSpec as P

MIB = 1024 * 1024


def sigmoid(value):
    return 1.0 / (1.0 + jnp.exp(-value))


def bf16(*shape):
    return jax.ShapeDtypeStruct(shape, jnp.bfloat16)


def f32(*shape):
    return jax.ShapeDtypeStruct(shape, jnp.float32)


def call(kernel, outs, scratch, flops, *operands, after=(), early=(), spare_inputs=False, limit=24):
    single = len(outs) == 1
    moved = sum(math.prod(x.shape) * x.dtype.itemsize for x in (*operands, *outs))
    vmem = pl.BlockSpec(memory_space=pltpu.VMEM)
    spare = pl.BlockSpec(memory_space=pl.ANY)
    spec = spare if spare_inputs else vmem
    count = len(operands)
    operands = (*operands, *early, *after)

    def body(*refs):
        kernel(*refs[:count], *refs[len(operands) :])

    return pl.pallas_call(
        body,
        out_shape=outs[0] if single else tuple(outs),
        in_specs=[spec] * count + [vmem] * len(early) + [spare] * len(after),
        out_specs=vmem if single else (vmem,) * len(outs),
        scratch_shapes=scratch,
        compiler_params=pltpu.CompilerParams(vmem_limit_bytes=limit * MIB),
        cost_estimate=pl.CostEstimate(
            flops=int(flops), bytes_accessed=int(moved) if flops else 0, transcendentals=0
        ),
    )(*operands)


def from_ahead(block, band_step, frame_step):
    bands, frames = lax.axis_size("section"), lax.axis_size("video")
    pairs = [
        ((band + band_step) * frames + frame + frame_step, band * frames + frame)
        for band in range(bands)
        for frame in range(frames)
        if 0 <= band + band_step < bands and frame + frame_step < frames
    ]
    return lax.ppermute(block, ("section", "video"), pairs)


def beside_band(pair_refs, row):
    band = lax.axis_index("section")
    odd = lax.rem(band, 2) == 1
    inside = (band > 0) & (band < lax.axis_size("section") - 1)
    first, second = (ref[row : row + 1] for ref in pair_refs)
    second = jnp.where(inside, second, jnp.zeros_like(second))
    return jnp.where(odd, first, second), jnp.where(odd, second, first)


def flipped(block, axis, flip):
    count = lax.axis_size(axis)
    return lax.ppermute(block, axis, [(place ^ flip, place) for place in range(count)])


def flipped_both(block):
    bands = lax.axis_size("section")
    pairs = [
        (2 * (band ^ 2) + 1 - frame, 2 * band + frame) for band in range(bands) for frame in range(2)
    ]
    return lax.ppermute(block, ("section", "video"), pairs)


def later_than(block, *others):
    return lax.optimization_barrier((block, *others))[0]


def beside(gpre, views_ref, start):
    count, cols, ch = gpre.shape
    at = lax.broadcasted_iota(jnp.int32, gpre.shape, 1)
    right = jnp.where(at == cols - 1, 0.0, pltpu.roll(gpre, cols - 1, 1))
    left = jnp.where(at == 0, 0.0, pltpu.roll(gpre, 1, 1))
    here = pl.ds(start, count)
    views_ref[here, :, 0:ch] = right.astype(jnp.bfloat16)
    views_ref[here, :, ch : 2 * ch] = gpre.astype(jnp.bfloat16)
    views_ref[here, :, 2 * ch : 3 * ch] = left.astype(jnp.bfloat16)


def pre_gradient(grads, preact, temporal_ref):
    count, cols, ch = preact.shape
    flat = jnp.concatenate([grad.reshape(count * cols, ch) for grad in grads], axis=1)
    kernel = jnp.concatenate([temporal_ref[2 - step] for step in range(len(grads))], axis=1)
    gact = lax.dot_general(
        flat, kernel, (((1,), (1,)), ((), ())), preferred_element_type=jnp.float32
    )
    gact = gact.astype(jnp.bfloat16).astype(jnp.float32).reshape(preact.shape)
    hval = preact.astype(jnp.float32)
    sig = sigmoid(hval)
    return gact * sig * (1.0 + hval * (1.0 - sig))


def convolved(views_ref, spatial_ref, start, first):
    count, cols, ch = first.shape
    total = first.astype(jnp.float32).reshape(count * cols, ch)
    for ky in range(3):
        view = views_ref[pl.ds(start + 2 - ky, count)].reshape(count * cols, 3 * ch)
        kernel = jnp.concatenate([spatial_ref[ky, kx] for kx in range(3)], axis=1)
        total = total + lax.dot_general(
            view, kernel, (((1,), (1,)), ((), ())), preferred_element_type=jnp.float32
        )
    return total.astype(jnp.bfloat16).reshape(first.shape)


def is_last():
    return lax.axis_index("video") == lax.axis_size("video") - 1


def left_sides(saved_ref, preact_ref, above, below, sides_ref):
    rows, cols, ch = saved_ref.shape
    flat = (rows * cols, ch)
    shifts = [
        jnp.concatenate([above, saved_ref[: rows - 1]], axis=0),
        saved_ref[...],
        jnp.concatenate([saved_ref[1:], below], axis=0),
    ]
    for n, shift in enumerate(shifts):
        sides_ref[n] = shift.reshape(flat).T
    hval = preact_ref[...].astype(jnp.float32)
    sides_ref[3] = (hval * sigmoid(hval)).astype(jnp.bfloat16).reshape(flat).T


def kernel_sums(sides_ref, grads, views, sums_ref):
    _, ch, pixels = sides_ref.shape
    shifts = sides_ref[0:3].reshape(3 * ch, pixels)
    sums = jnp.dot(shifts, views, preferred_element_type=jnp.float32)
    for ky in range(3):
        for kx in range(3):
            here = slice(kx * ch, (kx + 1) * ch)
            sums_ref[ky, here] = sums[ky * ch : (ky + 1) * ch, here]
    grads = jnp.concatenate([grad.reshape(pixels, ch) for grad in grads], axis=1)
    sums = jnp.dot(sides_ref[3], grads, preferred_element_type=jnp.float32)
    zeros = jnp.zeros((ch, ch), jnp.float32)
    for k in range(3):
        step = 2 - k
        value = sums[:, step * ch : (step + 1) * ch] if step * ch < grads.shape[1] else zeros
        sums_ref[3, k * ch : (k + 1) * ch] = jnp.where(is_last(), zeros, value) if step else value


def hand_out(sums_ref, keep_ref, *send_refs):
    odd = lax.rem(lax.axis_index("section"), 2)
    for n, send_ref in enumerate(send_refs):
        keep_ref[n] = sums_ref[2 * n + odd]
        send_ref[...] = sums_ref[2 * n + 1 - odd].astype(jnp.bfloat16)


def pack_kernel(*refs):
    parts, outs, sems = refs[:4], refs[4:6], refs[6]
    last = parts[0].shape[0] - 1
    odd = lax.rem(lax.axis_index("section"), 2)
    copies = []
    for n, part in enumerate(parts):
        for out, row in zip(outs, ((1 - odd) * last, odd * last)):
            sem = sems.at[len(copies)]
            copies.append(
                pltpu.make_async_copy(part.at[pl.ds(row, 1)], out.at[pl.ds(n, 1)], sem)
            )
    for copy in copies:
        copy.start()
    for copy in copies:
        copy.wait()


def interior(grad_ref, preact_ref, wholes, temporal_ref, spatial_ref, inner_ref, gpre_ref, views_ref):
    rows, cols, ch = grad_ref.shape
    step = 4

    for n in range(rows // step):
        here = pl.ds(n * step, step)
        grads = [ref[here] for ref in (grad_ref, *wholes)]
        gpre = pre_gradient(grads, preact_ref[here], temporal_ref)
        gpre_ref[here] = gpre.astype(jnp.bfloat16)
        beside(gpre, views_ref, n * step)

    half = rows // 2 - 1

    for n in range(2):
        first = grad_ref[pl.ds(n * half + 1, half)]
        inner_ref[pl.ds(n * half, half)] = convolved(views_ref, spatial_ref, n * half, first)


def edge_rows(grad_ref, pair_refs, afters, gpre_ref, temporal_ref, spatial_ref, views_ref):
    rows, cols, ch = grad_ref.shape
    (grad_above, grad_below), (above_pre, below_pre) = (beside_band(pair_refs, n) for n in (0, 1))
    above = [grad_above] + [ref[0:1] for ref in afters]
    below = [grad_below] + [ref[1:2] for ref in afters]
    beside(pre_gradient(above, above_pre, temporal_ref), views_ref, 0)
    beside(gpre_ref[0:2].astype(jnp.float32), views_ref, 1)
    beside(gpre_ref[rows - 2 : rows].astype(jnp.float32), views_ref, 3)
    beside(pre_gradient(below, below_pre, temporal_ref), views_ref, 5)
    return (
        convolved(views_ref, spatial_ref, 0, grad_ref[0:1]),
        convolved(views_ref, spatial_ref, 3, grad_ref[rows - 1 : rows]),
    )


def last_inner_kernel(grad_ref, preact_ref, temporal_ref, spatial_ref, inner_ref, gpre_ref, views_ref):
    @pl.when(is_last())
    def _():
        interior(
            grad_ref, preact_ref, [], temporal_ref, spatial_ref, inner_ref, gpre_ref, views_ref
        )


def last_edge_kernel(grad_ref, one_ref, two_ref, gpre_ref, temporal_ref, spatial_ref, edge_ref, views_ref):
    @pl.when(is_last())
    def _():
        pair_refs = (one_ref, two_ref)
        edge_ref[0:1], edge_ref[1:2] = edge_rows(
            grad_ref, pair_refs, [], gpre_ref, temporal_ref, spatial_ref, views_ref
        )
        edge_ref[2:3], edge_ref[3:4] = beside_band(pair_refs, 0)


def inner_kernel(later, *refs):
    inputs, wholes, kernels = refs[:2], refs[2 : 2 + later], refs[2 + later : 4 + later]
    known, outs = refs[4 + later : -3], refs[-3:]
    if not known:
        interior(*inputs, wholes, *kernels, *outs)
        return

    @pl.when(is_last())
    def _():
        outs[0][...] = known[0][...]
        outs[1][...] = known[1][...]

    @pl.when(jnp.logical_not(is_last()))
    def _():
        interior(*inputs, wholes, *kernels, *outs)


def mid_kernel(later, *refs):
    grad_ref, inner_ref, gpre_ref = refs[0], refs[3], refs[4]
    afters, (temporal_ref, spatial_ref, mid_ref, views_ref) = refs[5 : 5 + later], refs[5 + later :]
    rows = grad_ref.shape[0]
    first, last = edge_rows(
        grad_ref, refs[1:3], afters, gpre_ref, temporal_ref, spatial_ref, views_ref
    )
    mid_ref[0:1], mid_ref[rows - 1 : rows] = first, last
    mid_ref[1 : rows - 1] = inner_ref[...]


def two_kernel(later, *refs):
    saved_ref, preact_ref, gpre_ref = refs[:3]
    pair_refs, grad_ref = refs[3:5], refs[5]
    wholes, outs = refs[6 : 6 + later], refs[6 + later : 9 + later]
    views_ref, sides_ref, sums_ref = refs[9 + later :]
    rows, cols, ch = saved_ref.shape
    step = 4

    for n in range(rows // step):
        here = pl.ds(n * step, step)
        beside(gpre_ref[here].astype(jnp.float32), views_ref, n * step)

    views = views_ref[...].reshape(rows * cols, 3 * ch)
    grads = [ref[...] for ref in (grad_ref, *wholes)]
    left_sides(saved_ref, preact_ref, *beside_band(pair_refs, 2), sides_ref)
    kernel_sums(sides_ref, grads, views, sums_ref)
    hand_out(sums_ref, *outs)


def sides_kernel(saved_ref, preact_ref, one_ref, two_ref, sides_ref):
    left_sides(saved_ref, preact_ref, *beside_band((one_ref, two_ref), 3), sides_ref)


def pre_rows(preact, mids, temporal_ref, gpre_ref, views_ref, start):
    gpre = pre_gradient(mids, preact, temporal_ref)
    gpre_ref[start : start + preact.shape[0]] = gpre.astype(jnp.bfloat16)
    beside(gpre, views_ref, start)


def block_sums(gpre_ref, sides_ref, mids, views_ref, sums_ref, keep_ref, send_ref):
    rows, cols, ch = gpre_ref.shape
    odd = lax.rem(lax.axis_index("section"), 2)
    size = send_ref.shape[0] - 2 * cols
    send_ref[size : size + cols] = gpre_ref[(1 - odd) * (rows - 1)]
    send_ref[size + cols : size + 2 * cols] = gpre_ref[odd * (rows - 1)]
    views = views_ref[...].reshape(rows * cols, 3 * ch)
    kernel_sums(sides_ref, [ref[...] for ref in mids], views, sums_ref)
    height = sums_ref.shape[1]
    hand_out(sums_ref, keep_ref, send_ref.at[:height], send_ref.at[height : 2 * height])


def one_kernel(later, *refs):
    sides_ref, preact_ref, mids = refs[0], refs[1], refs[2 : 3 + later]
    temporal_ref, outs, scratch = refs[3 + later], refs[4 + later : 7 + later], refs[7 + later :]
    gpre_ref, keep_ref, send_ref = outs
    views_ref, sums_ref = scratch
    for n in range(preact_ref.shape[0] // 4):
        here = slice(4 * n, 4 * n + 4)
        grads = [ref[here] for ref in mids]
        pre_rows(preact_ref[here], grads, temporal_ref, gpre_ref, views_ref, 4 * n)
    block_sums(gpre_ref, sides_ref, mids, views_ref, sums_ref, keep_ref, send_ref)


def one_inner_kernel(preact_ref, inner_ref, after_ref, temporal_ref, gpre_ref, views_ref):
    rows = inner_ref.shape[0]
    for n in range(rows // 7):
        here = slice(7 * n, 7 * n + 7)
        after = after_ref[here]
        after = jnp.where(is_last(), jnp.zeros_like(after), after)
        preact = preact_ref[7 * n + 1 : 7 * n + 8]
        pre_rows(preact, [inner_ref[here], after], temporal_ref, gpre_ref, views_ref, 7 * n)


def mid_one_kernel(*refs):
    after_inner_ref, after_edge_ref = refs[5:7]
    temporal_two_ref, spatial_two_ref, sides_ref, preact_ref, temporal_ref = refs[7:12]
    inner_gpre_ref, inner_views_ref = refs[12:14]
    mid_ref, gpre_ref, keep_ref, send_ref = refs[14:18]
    views_ref, sums_ref, next_ref, edge_ref, edge_views_ref = refs[18:]
    rows = next_ref.shape[0]

    @pl.when(is_last())
    def _():
        edge_ref[...] = jnp.zeros(edge_ref.shape, edge_ref.dtype)
        next_ref[...] = jnp.zeros(next_ref.shape, next_ref.dtype)

    @pl.when(jnp.logical_not(is_last()))
    def _():
        edge_ref[...] = after_edge_ref[2:4]
        next_ref[0:1] = after_edge_ref[0:1]
        next_ref[1 : rows - 1] = after_inner_ref[...]
        next_ref[rows - 1 : rows] = after_edge_ref[1:2]

    mid_kernel(
        1, *refs[:5], edge_ref, temporal_two_ref, spatial_two_ref, mid_ref, edge_views_ref
    )
    gpre_ref[1 : rows - 1] = inner_gpre_ref[...]
    views_ref[1 : rows - 1] = inner_views_ref[...]
    for row in (0, rows - 1):
        here = slice(row, row + 1)
        grads = [mid_ref[here], next_ref[here]]
        pre_rows(preact_ref[here], grads, temporal_ref, gpre_ref, views_ref, row)
    block_sums(gpre_ref, sides_ref, [mid_ref, next_ref], views_ref, sums_ref, keep_ref, send_ref)


def input_kernel(mid_ref, gpre_ref, pair_ref, across_ref, spatial_ref, out_ref, token_ref, views_ref):
    rows, cols, ch = out_ref.shape
    pair = pair_ref[pair_ref.shape[0] - 2 * cols : pair_ref.shape[0] - cols]
    above, below = beside_band((pair[None], across_ref[across_ref.shape[0] - cols :][None]), 0)
    token_ref[...] = jnp.zeros(token_ref.shape, token_ref.dtype)
    step = 4
    beside(above.astype(jnp.float32), views_ref, 0)
    beside(below.astype(jnp.float32), views_ref, rows + 1)

    for n in range(rows // step):
        gpre = gpre_ref[pl.ds(n * step, step)].astype(jnp.float32)
        beside(gpre, views_ref, n * step + 1)

    for n in range(rows // step):
        here = pl.ds(n * step, step)
        out_ref[here] = convolved(views_ref, spatial_ref, n * step, mid_ref[here])


def halves(count, index):
    return [pl.ds(pl.multiple_of(n * count, count), count) for n in (index, 1 - index)]


def pair_kernel(keep_ref, low_ref, high_ref, own_ref, send_ref):
    across = lax.axis_index("section") // 2
    parts = [ref[...].astype(jnp.float32) for ref in (low_ref, high_ref)]
    own_ref[...] = keep_ref[across] + jnp.where(across == 0, *parts)
    total = keep_ref[1 - across] + jnp.where(across == 0, *parts[::-1])
    send_ref[...] = total.astype(jnp.bfloat16)


def band_kernel(own_ref, part_ref, keep_ref, send_ref):
    mine, other = halves(keep_ref.shape[0], lax.axis_index("video"))
    half = keep_ref.shape[0]
    keep_ref[...] = own_ref[mine] + part_ref[mine].astype(jnp.float32)
    send_ref[:half] = (own_ref[other] + part_ref[other].astype(jnp.float32)).astype(jnp.bfloat16)


def pair_quarter_kernel(keep_ref, part_ref, own_ref, across_ref, frame_ref, both_ref):
    _, height, _ = keep_ref.shape
    half = own_ref.shape[0]
    band = lax.axis_index("section") // 2
    frames = halves(half, lax.axis_index("video"))

    def quarter(band, rows):
        start = pl.multiple_of(band * height, height)
        part = part_ref.at[pl.ds(start, height)][rows]
        return keep_ref[band, rows] + part.astype(jnp.float32)

    own_ref[...] = quarter(band, frames[0])
    across_ref[:half] = quarter(1 - band, frames[0]).astype(jnp.bfloat16)
    rest = across_ref.shape[0] - half
    across_ref[half:] = part_ref[2 * height + rest :]
    frame_ref[...] = quarter(band, frames[1]).astype(jnp.bfloat16)
    both_ref[:half] = quarter(1 - band, frames[1]).astype(jnp.bfloat16)


def plane_kernel(own_ref, *refs):
    parts, out_ref = refs[:-1], refs[-1]
    total = own_ref[...]
    for part in parts:
        total = total + part[: out_ref.shape[0]].astype(jnp.float32)
    out_ref[...] = total.astype(jnp.bfloat16)


def add_kernel(one_ref, two_ref, out_ref):
    total = one_ref[...].astype(jnp.float32) + two_ref[: one_ref.shape[0]].astype(jnp.float32)
    out_ref[...] = total.astype(jnp.bfloat16)


def scaled_kernel(factor, *refs):
    out_ref = refs[-1]
    for block in range(2):
        one, two = (ref[...].astype(jnp.float32) for ref in refs[2 * block : 2 * block + 2])
        out_ref[block] = ((one + two) * factor).astype(jnp.bfloat16)


def place_kernel(places, *refs):
    shares, outs = refs[: len(places)], refs[-6:-2]
    sums_ref, sems = refs[-2:]
    band, frame = lax.axis_index("section"), lax.axis_index("video")
    height = shares[0].shape[1]

    def copies(n, block):
        flip, other = places[n]
        place = jnp.bitwise_xor(band, flip)
        half = 0 if other is None else jnp.bitwise_xor(frame, int(other))
        here = pl.ds(pl.multiple_of(half * height, height), height)
        spatial, temporal = outs[2 * block : 2 * block + 2]
        source, sem = sums_ref.at[n, block], sems.at[n, block]
        return (
            (place < 3, lambda: pltpu.make_async_copy(source, spatial.at[place, here], sem)),
            (place == 3, lambda: pltpu.make_async_copy(source, temporal.at[here], sem)),
        )

    for n, share in enumerate(shares):
        for block in range(2):
            sums_ref[n, block] = share[block].astype(jnp.float32)
            for inside, copy in copies(n, block):
                pl.when(inside)(lambda: copy().start())
    for n in range(len(shares)):
        for block in range(2):
            for inside, copy in copies(n, block):
                pl.when(inside)(lambda: copy().wait())


def placed(shares, places, given=()):
    _, height, ch = shares[0].shape
    count = len(shares)
    outs = (f32(3, 3 * ch, ch), f32(3 * ch, ch)) * 2
    vmem, spare = (pl.BlockSpec(memory_space=space) for space in (pltpu.VMEM, pl.ANY))
    return pl.pallas_call(
        functools.partial(place_kernel, places),
        out_shape=outs,
        in_specs=[vmem] * count + [spare] * len(given),
        out_specs=(spare,) * 4,
        scratch_shapes=[
            pltpu.VMEM((count, 2, height, ch), jnp.float32),
            pltpu.SemaphoreType.DMA((count, 2)),
        ],
        input_output_aliases={count + n: n for n in range(len(given))},
        compiler_params=pltpu.CompilerParams(vmem_limit_bytes=24 * MIB),
        cost_estimate=pl.CostEstimate(
            flops=0, bytes_accessed=6 * count * height * ch * 2, transcendentals=0
        ),
    )(*shares, *given)


def unpacked(sums):
    ch = sums[0].shape[-1]
    return [x.reshape(3, 3, ch, ch) if x.ndim == 3 else x.reshape(3, ch, ch) for x in sums]


def on_device(
    grad_latent,
    input_one,
    preact_one,
    input_two,
    preact_two,
    spatial_one,
    temporal_one,
    spatial_two,
    temporal_two,
):
    shape = grad_latent.shape
    rows, cols, ch = shape[2:]
    bands, frames = lax.axis_size("section"), lax.axis_size("video")
    later = min(2, frames - 1)
    pixels = lax.axis_size("dp") * frames * bands * rows * cols
    factor = 1.0 / math.sqrt(pixels)
    grad, saved_one, pre_one, saved_two, pre_two = (
        x.reshape(rows, cols, ch)
        for x in (grad_latent, input_one, preact_one, input_two, preact_two)
    )
    conv = 2 * rows * cols * 9 * ch * ch
    views = pltpu.VMEM((rows, cols, 3 * ch), jnp.bfloat16)
    edge_views = pltpu.VMEM((6, cols, 3 * ch), jnp.bfloat16)
    act = pltpu.VMEM((rows, cols, ch), jnp.bfloat16)
    sides = bf16(4, ch, rows * cols)
    sums = pltpu.VMEM((4, 3 * ch, ch), jnp.float32)
    handed = [f32(2, 3 * ch, ch)] + [bf16(3 * ch, ch)] * 2
    inner_outs = [bf16(rows - 2, cols, ch), bf16(rows, cols, ch)]
    kernels = (temporal_two, spatial_two)

    def from_later(x):
        if frames == 2:
            return [flipped(x, "video", 1)]
        return [from_ahead(x, 0, n + 1) for n in range(later)]

    wholes = [from_ahead(grad, 0, n + 1) for n in range(later)]
    packs = call(
        pack_kernel,
        [bf16(4, cols, ch)] * 2,
        [pltpu.SemaphoreType.DMA((8,))],
        1,
        grad,
        pre_two,
        saved_two,
        saved_one,
        spare_inputs=True,
        limit=58,
    )
    second = flipped(packs[1], "section", 1)
    first = flipped(later_than(packs[0], second), "section", 1)
    pairs = [first, flipped(second, "section", 2)]

    known = ()
    if frames == 2:
        known = call(
            last_inner_kernel,
            inner_outs,
            [views],
            0,
            grad,
            pre_two,
            *kernels,
            after=(first, second),
        )
        afters = from_later(known[0])
    else:
        afters = from_later(jnp.concatenate(beside_band(pairs, 0)))
    inner, gpre_two = call(
        functools.partial(inner_kernel, later),
        inner_outs,
        [views],
        0,
        grad,
        pre_two,
        *wholes,
        *kernels,
        *known,
        early=(saved_two, saved_one, pre_one, temporal_one),
    )
    if frames == 2:
        edge = call(
            last_edge_kernel,
            [bf16(4, cols, ch)],
            [edge_views],
            0,
            grad,
            *pairs,
            known[1],
            *kernels,
            after=(gpre_two,),
        )
        afters += from_later(edge)
    parts_two = call(
        functools.partial(two_kernel, later),
        handed,
        [views, pltpu.VMEM(sides.shape, sides.dtype), sums],
        8 * conv,
        saved_two,
        pre_two,
        gpre_two,
        *pairs,
        grad,
        *wholes,
        after=(edge,) if frames == 2 else (),
    )
    sides_one = call(
        sides_kernel, [sides], [], conv // 8, saved_one, pre_one, *pairs, after=parts_two[:1]
    )
    height, half = 3 * ch, 3 * ch // 2
    keep_two, low_two, high_two = parts_two
    own_two, send_two = call(
        pair_kernel,
        [f32(height, ch), bf16(height, ch)],
        [],
        height * ch,
        keep_two,
        flipped(low_two, "section", 1),
        flipped(high_two, "section", 1),
    )
    across_two = flipped(send_two, "section", 2)
    mid_inputs = (grad, *pairs, inner, gpre_two)
    one_inputs = (sides_one, pre_one)
    mid_outs = [bf16(rows, cols, ch)]
    one_outs = [bf16(rows, cols, ch), f32(2, 3 * ch, ch), bf16(6 * ch + 2 * cols, ch)]
    if frames == 2:
        inners_one = call(
            one_inner_kernel,
            [bf16(rows - 2, cols, ch), bf16(rows - 2, cols, 3 * ch)],
            [],
            conv // 8,
            pre_one,
            inner,
            afters[0],
            temporal_one,
        )
        mid, gpre_one, *parts_one = call(
            mid_one_kernel,
            mid_outs + one_outs,
            [views, sums, act, pltpu.VMEM((2, cols, ch), jnp.bfloat16), edge_views],
            8 * conv,
            *mid_inputs,
            *afters,
            *kernels,
            *one_inputs,
            temporal_one,
            *inners_one,
            after=(own_two,),
        )
    else:
        mid = call(
            functools.partial(mid_kernel, later),
            mid_outs,
            [edge_views],
            conv // 8,
            *mid_inputs,
            *afters,
            *kernels,
        )
        gpre_one, *parts_one = call(
            functools.partial(one_kernel, later),
            one_outs,
            [views, sums],
            1.2 * conv,
            *one_inputs,
            mid,
            *from_later(mid),
            temporal_one,
        )
    keep_one, send_one = parts_one
    split = frames == 2 and lax.axis_size("dp") == 4
    if split:
        send_one = later_than(send_one, across_two)
    pair_one = flipped(send_one, "section", 1)

    def input_gradient(edge, after):
        return call(
            input_kernel,
            [bf16(rows, cols, ch), f32(8, 128)],
            [pltpu.VMEM((rows + 2, cols, 3 * ch), jnp.bfloat16)],
            conv,
            mid,
            gpre_one,
            pair_one,
            edge,
            spatial_one,
            after=after,
        )

    if split:

        def added(one, two):
            return call(add_kernel, [bf16(half, ch)], [], half * ch, one, two)

        keep_two, send_two = call(
            band_kernel,
            [f32(half, ch), bf16(half + 2 * cols, ch)],
            [],
            0,
            own_two,
            across_two,
        )
        sum_two = added(keep_two, flipped(send_two, "video", 1))
        quarters = [f32(half, ch)] + [bf16(half + more, ch) for more in (cols, 0, cols + 16)]
        own_one, *sends = call(
            pair_quarter_kernel, quarters, [], 0, keep_one, pair_one, after=(send_two,)
        )
        across = flipped(sends[0], "section", 2)
        parts = [across, flipped(sends[1], "video", 1), flipped_both(sends[2])]
        sum_one = call(plane_kernel, [bf16(half, ch)], [], 4 * half * ch, own_one, *parts)
        part_two = flipped(sum_two, "dp", 1)
        part_one = flipped(later_than(sum_one, sum_two), "dp", 1)
        sum_two = added(sum_two, part_two)
        sum_one = added(sum_one, part_one)
        last_two = flipped(sum_two, "dp", 2)
        last_one = flipped(later_than(sum_one, sum_two), "dp", 2)
        grad_in, token = input_gradient(across, (sum_one,))
        own = call(
            functools.partial(scaled_kernel, factor),
            [bf16(2, half, ch)],
            [],
            height * ch,
            sum_one,
            last_one,
            sum_two,
            last_two,
            after=(token,),
        )
        frame, across, both = flipped(own, "video", 1), flipped(own, "section", 2), flipped_both(own)
        shares = [own, frame, across]
        shares += [flipped(share, "section", 1) for share in shares]
        places = [(0, False), (0, True), (2, False), (1, False), (1, True), (3, False)]
        sums = placed([*shares, both], [*places, (2, True)])
        sums = unpacked(placed([flipped(both, "section", 1)], [(3, True)], sums))
    else:
        own_one, send_one = call(
            pair_kernel,
            [f32(height, ch), bf16(height, ch)],
            [],
            height * ch,
            keep_one,
            pair_one[:height],
            pair_one[height : 2 * height],
        )
        edge = flipped(pair_one[pair_one.shape[0] - cols :], "section", 2)
        grad_in, _ = input_gradient(edge, ())
        own_one = own_one + flipped(send_one, "section", 2).astype(jnp.float32)
        own_two = own_two + across_two.astype(jnp.float32)
        share = lax.psum(jnp.stack((own_one, own_two)), ("video", "dp")) * factor
        share = share.astype(jnp.bfloat16)
        shares = [share, flipped(share, "section", 2)]
        shares += [flipped(share, "section", 1) for share in shares]
        sums = unpacked(placed(shares, [(0, None), (2, None), (1, None), (3, None)]))
    return (grad_in.reshape(shape), *sums)


def solution(mesh):
    whole = P("dp", "video", "section", None, None)
    return jax.shard_map(
        on_device,
        mesh=mesh,
        in_specs=(whole,) * 5 + (P(),) * 4,
        out_specs=(whole, P(), P(), P(), P()),
        check_vma=False,
    )
```

```python
import functools
import math

import jax
import jax.numpy as jnp
from jax import lax
from jax.experimental import pallas as pl
from jax.experimental.pallas import tpu as pltpu
from jax.sharding import PartitionSpec as P

MIB = 1024 * 1024


def sigmoid(value):
    return 1.0 / (1.0 + jnp.exp(-value))


def bf16(*shape):
    return jax.ShapeDtypeStruct(shape, jnp.bfloat16)


def f32(*shape):
    return jax.ShapeDtypeStruct(shape, jnp.float32)


def call(kernel, outs, scratch, flops, *operands, after=(), early=(), spare_inputs=False, limit=24):
    single = len(outs) == 1
    moved = sum(math.prod(x.shape) * x.dtype.itemsize for x in (*operands, *outs))
    vmem = pl.BlockSpec(memory_space=pltpu.VMEM)
    spare = pl.BlockSpec(memory_space=pl.ANY)
    spec = spare if spare_inputs else vmem
    count = len(operands)
    operands = (*operands, *early, *after)

    def body(*refs):
        kernel(*refs[:count], *refs[len(operands) :])

    return pl.pallas_call(
        body,
        out_shape=outs[0] if single else tuple(outs),
        in_specs=[spec] * count + [vmem] * len(early) + [spare] * len(after),
        out_specs=vmem if single else (vmem,) * len(outs),
        scratch_shapes=scratch,
        compiler_params=pltpu.CompilerParams(vmem_limit_bytes=limit * MIB),
        cost_estimate=pl.CostEstimate(
            flops=int(flops), bytes_accessed=int(moved) if flops else 0, transcendentals=0
        ),
    )(*operands)


def from_ahead(block, band_step, frame_step):
    bands, frames = lax.axis_size("section"), lax.axis_size("video")
    pairs = [
        ((band + band_step) * frames + frame + frame_step, band * frames + frame)
        for band in range(bands)
        for frame in range(frames)
        if 0 <= band + band_step < bands and frame + frame_step < frames
    ]
    return lax.ppermute(block, ("section", "video"), pairs)


def beside_band(pair_refs, row):
    band = lax.axis_index("section")
    odd = lax.rem(band, 2) == 1
    inside = (band > 0) & (band < lax.axis_size("section") - 1)
    first, second = (ref[row : row + 1] for ref in pair_refs)
    second = jnp.where(inside, second, jnp.zeros_like(second))
    return jnp.where(odd, first, second), jnp.where(odd, second, first)


def flipped(block, axis, flip):
    count = lax.axis_size(axis)
    return lax.ppermute(block, axis, [(place ^ flip, place) for place in range(count)])


def flipped_both(block):
    bands = lax.axis_size("section")
    pairs = [
        (2 * (band ^ 2) + 1 - frame, 2 * band + frame) for band in range(bands) for frame in range(2)
    ]
    return lax.ppermute(block, ("section", "video"), pairs)


def later_than(block, *others):
    return lax.optimization_barrier((block, *others))[0]


def beside(gpre, views_ref, start):
    count, cols, ch = gpre.shape
    at = lax.broadcasted_iota(jnp.int32, gpre.shape, 1)
    right = jnp.where(at == cols - 1, 0.0, pltpu.roll(gpre, cols - 1, 1))
    left = jnp.where(at == 0, 0.0, pltpu.roll(gpre, 1, 1))
    here = pl.ds(start, count)
    views_ref[here, :, 0:ch] = right.astype(jnp.bfloat16)
    views_ref[here, :, ch : 2 * ch] = gpre.astype(jnp.bfloat16)
    views_ref[here, :, 2 * ch : 3 * ch] = left.astype(jnp.bfloat16)


def pre_gradient(grads, preact, temporal_ref):
    count, cols, ch = preact.shape
    flat = jnp.concatenate([grad.reshape(count * cols, ch) for grad in grads], axis=1)
    kernel = jnp.concatenate([temporal_ref[2 - step] for step in range(len(grads))], axis=1)
    gact = lax.dot_general(
        flat, kernel, (((1,), (1,)), ((), ())), preferred_element_type=jnp.float32
    )
    gact = gact.astype(jnp.bfloat16).astype(jnp.float32).reshape(preact.shape)
    hval = preact.astype(jnp.float32)
    sig = sigmoid(hval)
    return gact * sig * (1.0 + hval * (1.0 - sig))


def convolved(views_ref, spatial_ref, start, first):
    count, cols, ch = first.shape
    total = first.astype(jnp.float32).reshape(count * cols, ch)
    for ky in range(3):
        view = views_ref[pl.ds(start + 2 - ky, count)].reshape(count * cols, 3 * ch)
        kernel = jnp.concatenate([spatial_ref[ky, kx] for kx in range(3)], axis=1)
        total = total + lax.dot_general(
            view, kernel, (((1,), (1,)), ((), ())), preferred_element_type=jnp.float32
        )
    return total.astype(jnp.bfloat16).reshape(first.shape)


def is_last():
    return lax.axis_index("video") == lax.axis_size("video") - 1


def left_sides(saved_ref, preact_ref, above, below, sides_ref):
    rows, cols, ch = saved_ref.shape
    flat = (rows * cols, ch)
    shifts = [
        jnp.concatenate([above, saved_ref[: rows - 1]], axis=0),
        saved_ref[...],
        jnp.concatenate([saved_ref[1:], below], axis=0),
    ]
    for n, shift in enumerate(shifts):
        sides_ref[n] = shift.reshape(flat).T
    hval = preact_ref[...].astype(jnp.float32)
    sides_ref[3] = (hval * sigmoid(hval)).astype(jnp.bfloat16).reshape(flat).T


def kernel_sums(sides_ref, grads, views, sums_ref):
    _, ch, pixels = sides_ref.shape
    shifts = sides_ref[0:3].reshape(3 * ch, pixels)
    sums = jnp.dot(shifts, views, preferred_element_type=jnp.float32)
    for ky in range(3):
        for kx in range(3):
            here = slice(kx * ch, (kx + 1) * ch)
            sums_ref[ky, here] = sums[ky * ch : (ky + 1) * ch, here]
    grads = jnp.concatenate([grad.reshape(pixels, ch) for grad in grads], axis=1)
    sums = jnp.dot(sides_ref[3], grads, preferred_element_type=jnp.float32)
    zeros = jnp.zeros((ch, ch), jnp.float32)
    for k in range(3):
        step = 2 - k
        value = sums[:, step * ch : (step + 1) * ch] if step * ch < grads.shape[1] else zeros
        sums_ref[3, k * ch : (k + 1) * ch] = jnp.where(is_last(), zeros, value) if step else value


def hand_out(sums_ref, keep_ref, *send_refs):
    odd = lax.rem(lax.axis_index("section"), 2)
    for n, send_ref in enumerate(send_refs):
        keep_ref[n] = sums_ref[2 * n + odd]
        send_ref[...] = sums_ref[2 * n + 1 - odd].astype(jnp.bfloat16)


def pack_kernel(*refs):
    parts, outs, sems = refs[:4], refs[4:6], refs[6]
    last = parts[0].shape[0] - 1
    odd = lax.rem(lax.axis_index("section"), 2)
    copies = []
    for n, part in enumerate(parts):
        for out, row in zip(outs, ((1 - odd) * last, odd * last)):
            sem = sems.at[len(copies)]
            copies.append(
                pltpu.make_async_copy(part.at[pl.ds(row, 1)], out.at[pl.ds(n, 1)], sem)
            )
    for copy in copies:
        copy.start()
    for copy in copies:
        copy.wait()


def interior(grad_ref, preact_ref, wholes, temporal_ref, spatial_ref, inner_ref, gpre_ref, views_ref):
    rows, cols, ch = grad_ref.shape
    step = 4

    for n in range(rows // step):
        here = pl.ds(n * step, step)
        grads = [ref[here] for ref in (grad_ref, *wholes)]
        gpre = pre_gradient(grads, preact_ref[here], temporal_ref)
        gpre_ref[here] = gpre.astype(jnp.bfloat16)
        beside(gpre, views_ref, n * step)

    half = rows // 2 - 1

    for n in range(2):
        first = grad_ref[pl.ds(n * half + 1, half)]
        inner_ref[pl.ds(n * half, half)] = convolved(views_ref, spatial_ref, n * half, first)


def edge_rows(grad_ref, pair_refs, afters, gpre_ref, temporal_ref, spatial_ref, views_ref):
    rows, cols, ch = grad_ref.shape
    (grad_above, grad_below), (above_pre, below_pre) = (beside_band(pair_refs, n) for n in (0, 1))
    above = [grad_above] + [ref[0:1] for ref in afters]
    below = [grad_below] + [ref[1:2] for ref in afters]
    beside(pre_gradient(above, above_pre, temporal_ref), views_ref, 0)
    beside(gpre_ref[0:2].astype(jnp.float32), views_ref, 1)
    beside(gpre_ref[rows - 2 : rows].astype(jnp.float32), views_ref, 3)
    beside(pre_gradient(below, below_pre, temporal_ref), views_ref, 5)
    return (
        convolved(views_ref, spatial_ref, 0, grad_ref[0:1]),
        convolved(views_ref, spatial_ref, 3, grad_ref[rows - 1 : rows]),
    )


def last_inner_kernel(grad_ref, preact_ref, temporal_ref, spatial_ref, inner_ref, gpre_ref, views_ref):
    @pl.when(is_last())
    def _():
        interior(
            grad_ref, preact_ref, [], temporal_ref, spatial_ref, inner_ref, gpre_ref, views_ref
        )


def last_edge_kernel(grad_ref, one_ref, two_ref, gpre_ref, temporal_ref, spatial_ref, edge_ref, views_ref):
    @pl.when(is_last())
    def _():
        pair_refs = (one_ref, two_ref)
        edge_ref[0:1], edge_ref[1:2] = edge_rows(
            grad_ref, pair_refs, [], gpre_ref, temporal_ref, spatial_ref, views_ref
        )
        edge_ref[2:3], edge_ref[3:4] = beside_band(pair_refs, 0)


def inner_kernel(later, *refs):
    inputs, wholes, kernels = refs[:2], refs[2 : 2 + later], refs[2 + later : 4 + later]
    known, outs = refs[4 + later : -3], refs[-3:]
    if not known:
        interior(*inputs, wholes, *kernels, *outs)
        return

    @pl.when(is_last())
    def _():
        outs[0][...] = known[0][...]
        outs[1][...] = known[1][...]

    @pl.when(jnp.logical_not(is_last()))
    def _():
        interior(*inputs, wholes, *kernels, *outs)


def mid_kernel(later, *refs):
    grad_ref, inner_ref, gpre_ref = refs[0], refs[3], refs[4]
    afters, (temporal_ref, spatial_ref, mid_ref, views_ref) = refs[5 : 5 + later], refs[5 + later :]
    rows = grad_ref.shape[0]
    first, last = edge_rows(
        grad_ref, refs[1:3], afters, gpre_ref, temporal_ref, spatial_ref, views_ref
    )
    mid_ref[0:1], mid_ref[rows - 1 : rows] = first, last
    mid_ref[1 : rows - 1] = inner_ref[...]


def two_kernel(later, *refs):
    saved_ref, preact_ref, gpre_ref = refs[:3]
    pair_refs, grad_ref = refs[3:5], refs[5]
    wholes, outs = refs[6 : 6 + later], refs[6 + later : 9 + later]
    views_ref, sides_ref, sums_ref = refs[9 + later :]
    rows, cols, ch = saved_ref.shape
    step = 4

    for n in range(rows // step):
        here = pl.ds(n * step, step)
        beside(gpre_ref[here].astype(jnp.float32), views_ref, n * step)

    views = views_ref[...].reshape(rows * cols, 3 * ch)
    grads = [ref[...] for ref in (grad_ref, *wholes)]
    left_sides(saved_ref, preact_ref, *beside_band(pair_refs, 2), sides_ref)
    kernel_sums(sides_ref, grads, views, sums_ref)
    hand_out(sums_ref, *outs)


def sides_kernel(saved_ref, preact_ref, one_ref, two_ref, sides_ref):
    left_sides(saved_ref, preact_ref, *beside_band((one_ref, two_ref), 3), sides_ref)


def pre_rows(preact, mids, temporal_ref, gpre_ref, views_ref, start):
    gpre = pre_gradient(mids, preact, temporal_ref)
    gpre_ref[start : start + preact.shape[0]] = gpre.astype(jnp.bfloat16)
    beside(gpre, views_ref, start)


def block_sums(gpre_ref, sides_ref, mids, views_ref, sums_ref, keep_ref, send_ref):
    rows, cols, ch = gpre_ref.shape
    odd = lax.rem(lax.axis_index("section"), 2)
    size = send_ref.shape[0] - 2 * cols
    send_ref[size : size + cols] = gpre_ref[(1 - odd) * (rows - 1)]
    send_ref[size + cols : size + 2 * cols] = gpre_ref[odd * (rows - 1)]
    views = views_ref[...].reshape(rows * cols, 3 * ch)
    kernel_sums(sides_ref, [ref[...] for ref in mids], views, sums_ref)
    height = sums_ref.shape[1]
    hand_out(sums_ref, keep_ref, send_ref.at[:height], send_ref.at[height : 2 * height])


def one_kernel(later, *refs):
    sides_ref, preact_ref, mids = refs[0], refs[1], refs[2 : 3 + later]
    temporal_ref, outs, scratch = refs[3 + later], refs[4 + later : 7 + later], refs[7 + later :]
    gpre_ref, keep_ref, send_ref = outs
    views_ref, sums_ref = scratch
    for n in range(preact_ref.shape[0] // 4):
        here = slice(4 * n, 4 * n + 4)
        grads = [ref[here] for ref in mids]
        pre_rows(preact_ref[here], grads, temporal_ref, gpre_ref, views_ref, 4 * n)
    block_sums(gpre_ref, sides_ref, mids, views_ref, sums_ref, keep_ref, send_ref)


def one_inner_kernel(preact_ref, inner_ref, after_ref, temporal_ref, gpre_ref, views_ref):
    rows = inner_ref.shape[0]
    for n in range(rows // 7):
        here = slice(7 * n, 7 * n + 7)
        after = after_ref[here]
        after = jnp.where(is_last(), jnp.zeros_like(after), after)
        preact = preact_ref[7 * n + 1 : 7 * n + 8]
        pre_rows(preact, [inner_ref[here], after], temporal_ref, gpre_ref, views_ref, 7 * n)


def mid_one_kernel(*refs):
    after_inner_ref, after_edge_ref = refs[5:7]
    temporal_two_ref, spatial_two_ref, sides_ref, preact_ref, temporal_ref = refs[7:12]
    inner_gpre_ref, inner_views_ref = refs[12:14]
    mid_ref, gpre_ref, keep_ref, send_ref = refs[14:18]
    views_ref, sums_ref, next_ref, edge_ref, edge_views_ref = refs[18:]
    rows = next_ref.shape[0]

    @pl.when(is_last())
    def _():
        edge_ref[...] = jnp.zeros(edge_ref.shape, edge_ref.dtype)
        next_ref[...] = jnp.zeros(next_ref.shape, next_ref.dtype)

    @pl.when(jnp.logical_not(is_last()))
    def _():
        edge_ref[...] = after_edge_ref[2:4]
        next_ref[0:1] = after_edge_ref[0:1]
        next_ref[1 : rows - 1] = after_inner_ref[...]
        next_ref[rows - 1 : rows] = after_edge_ref[1:2]

    mid_kernel(
        1, *refs[:5], edge_ref, temporal_two_ref, spatial_two_ref, mid_ref, edge_views_ref
    )
    gpre_ref[1 : rows - 1] = inner_gpre_ref[...]
    views_ref[1 : rows - 1] = inner_views_ref[...]
    for row in (0, rows - 1):
        here = slice(row, row + 1)
        grads = [mid_ref[here], next_ref[here]]
        pre_rows(preact_ref[here], grads, temporal_ref, gpre_ref, views_ref, row)
    block_sums(gpre_ref, sides_ref, [mid_ref, next_ref], views_ref, sums_ref, keep_ref, send_ref)


def input_kernel(mid_ref, gpre_ref, pair_ref, across_ref, spatial_ref, out_ref, token_ref, views_ref):
    rows, cols, ch = out_ref.shape
    pair = pair_ref[pair_ref.shape[0] - 2 * cols : pair_ref.shape[0] - cols]
    above, below = beside_band((pair[None], across_ref[across_ref.shape[0] - cols :][None]), 0)
    token_ref[...] = jnp.zeros(token_ref.shape, token_ref.dtype)
    step = 4
    beside(above.astype(jnp.float32), views_ref, 0)
    beside(below.astype(jnp.float32), views_ref, rows + 1)

    for n in range(rows // step):
        gpre = gpre_ref[pl.ds(n * step, step)].astype(jnp.float32)
        beside(gpre, views_ref, n * step + 1)

    for n in range(rows // step):
        here = pl.ds(n * step, step)
        out_ref[here] = convolved(views_ref, spatial_ref, n * step, mid_ref[here])


def halves(count, index):
    return [pl.ds(pl.multiple_of(n * count, count), count) for n in (index, 1 - index)]


def pair_kernel(keep_ref, low_ref, high_ref, own_ref, send_ref):
    across = lax.axis_index("section") // 2
    parts = [ref[...].astype(jnp.float32) for ref in (low_ref, high_ref)]
    own_ref[...] = keep_ref[across] + jnp.where(across == 0, *parts)
    total = keep_ref[1 - across] + jnp.where(across == 0, *parts[::-1])
    send_ref[...] = total.astype(jnp.bfloat16)


def band_kernel(own_ref, part_ref, keep_ref, send_ref):
    mine, other = halves(keep_ref.shape[0], lax.axis_index("video"))
    half = keep_ref.shape[0]
    keep_ref[...] = own_ref[mine] + part_ref[mine].astype(jnp.float32)
    send_ref[:half] = (own_ref[other] + part_ref[other].astype(jnp.float32)).astype(jnp.bfloat16)


def pair_quarter_kernel(keep_ref, part_ref, own_ref, across_ref, frame_ref, both_ref):
    _, height, _ = keep_ref.shape
    half = own_ref.shape[0]
    band = lax.axis_index("section") // 2
    frames = halves(half, lax.axis_index("video"))

    def quarter(band, rows):
        start = pl.multiple_of(band * height, height)
        part = part_ref.at[pl.ds(start, height)][rows]
        return keep_ref[band, rows] + part.astype(jnp.float32)

    own_ref[...] = quarter(band, frames[0])
    across_ref[:half] = quarter(1 - band, frames[0]).astype(jnp.bfloat16)
    rest = across_ref.shape[0] - half
    across_ref[half:] = part_ref[2 * height + rest :]
    frame_ref[...] = quarter(band, frames[1]).astype(jnp.bfloat16)
    both_ref[:half] = quarter(1 - band, frames[1]).astype(jnp.bfloat16)


def plane_kernel(own_ref, *refs):
    parts, out_ref = refs[:-1], refs[-1]
    total = own_ref[...]
    for part in parts:
        total = total + part[: out_ref.shape[0]].astype(jnp.float32)
    out_ref[...] = total.astype(jnp.bfloat16)


def add_kernel(one_ref, two_ref, out_ref):
    total = one_ref[...].astype(jnp.float32) + two_ref[: one_ref.shape[0]].astype(jnp.float32)
    out_ref[...] = total.astype(jnp.bfloat16)


def scaled_kernel(factor, *refs):
    out_ref = refs[-1]
    for block in range(2):
        one, two = (ref[...].astype(jnp.float32) for ref in refs[2 * block : 2 * block + 2])
        out_ref[block] = ((one + two) * factor).astype(jnp.bfloat16)


def place_kernel(places, *refs):
    shares, outs = refs[: len(places)], refs[-6:-2]
    sums_ref, sems = refs[-2:]
    band, frame = lax.axis_index("section"), lax.axis_index("video")
    height = shares[0].shape[1]

    def copies(n, block):
        flip, other = places[n]
        place = jnp.bitwise_xor(band, flip)
        half = 0 if other is None else jnp.bitwise_xor(frame, int(other))
        here = pl.ds(pl.multiple_of(half * height, height), height)
        spatial, temporal = outs[2 * block : 2 * block + 2]
        source, sem = sums_ref.at[n, block], sems.at[n, block]
        return (
            (place < 3, lambda: pltpu.make_async_copy(source, spatial.at[place, here], sem)),
            (place == 3, lambda: pltpu.make_async_copy(source, temporal.at[here], sem)),
        )

    for n, share in enumerate(shares):
        for block in range(2):
            sums_ref[n, block] = share[block].astype(jnp.float32)
            for inside, copy in copies(n, block):
                pl.when(inside)(lambda: copy().start())
    for n in range(len(shares)):
        for block in range(2):
            for inside, copy in copies(n, block):
                pl.when(inside)(lambda: copy().wait())


def placed(shares, places, given=()):
    _, height, ch = shares[0].shape
    count = len(shares)
    outs = (f32(3, 3 * ch, ch), f32(3 * ch, ch)) * 2
    vmem, spare = (pl.BlockSpec(memory_space=space) for space in (pltpu.VMEM, pl.ANY))
    return pl.pallas_call(
        functools.partial(place_kernel, places),
        out_shape=outs,
        in_specs=[vmem] * count + [spare] * len(given),
        out_specs=(spare,) * 4,
        scratch_shapes=[
            pltpu.VMEM((count, 2, height, ch), jnp.float32),
            pltpu.SemaphoreType.DMA((count, 2)),
        ],
        input_output_aliases={count + n: n for n in range(len(given))},
        compiler_params=pltpu.CompilerParams(vmem_limit_bytes=24 * MIB),
        cost_estimate=pl.CostEstimate(
            flops=0, bytes_accessed=6 * count * height * ch * 2, transcendentals=0
        ),
    )(*shares, *given)


def unpacked(sums):
    ch = sums[0].shape[-1]
    return [x.reshape(3, 3, ch, ch) if x.ndim == 3 else x.reshape(3, ch, ch) for x in sums]


def on_device(
    grad_latent,
    input_one,
    preact_one,
    input_two,
    preact_two,
    spatial_one,
    temporal_one,
    spatial_two,
    temporal_two,
):
    shape = grad_latent.shape
    rows, cols, ch = shape[2:]
    bands, frames = lax.axis_size("section"), lax.axis_size("video")
    later = min(2, frames - 1)
    pixels = lax.axis_size("dp") * frames * bands * rows * cols
    factor = 1.0 / math.sqrt(pixels)
    grad, saved_one, pre_one, saved_two, pre_two = (
        x.reshape(rows, cols, ch)
        for x in (grad_latent, input_one, preact_one, input_two, preact_two)
    )
    conv = 2 * rows * cols * 9 * ch * ch
    views = pltpu.VMEM((rows, cols, 3 * ch), jnp.bfloat16)
    edge_views = pltpu.VMEM((6, cols, 3 * ch), jnp.bfloat16)
    act = pltpu.VMEM((rows, cols, ch), jnp.bfloat16)
    sides = bf16(4, ch, rows * cols)
    sums = pltpu.VMEM((4, 3 * ch, ch), jnp.float32)
    handed = [f32(2, 3 * ch, ch)] + [bf16(3 * ch, ch)] * 2
    inner_outs = [bf16(rows - 2, cols, ch), bf16(rows, cols, ch)]
    kernels = (temporal_two, spatial_two)

    def from_later(x):
        if frames == 2:
            return [flipped(x, "video", 1)]
        return [from_ahead(x, 0, n + 1) for n in range(later)]

    wholes = from_later(grad)
    packs = call(
        pack_kernel,
        [bf16(4, cols, ch)] * 2,
        [pltpu.SemaphoreType.DMA((8,))],
        1,
        grad,
        pre_two,
        saved_two,
        saved_one,
        spare_inputs=True,
        limit=58,
    )
    second = flipped(packs[1], "section", 1)
    first = flipped(later_than(packs[0], second), "section", 1)
    pairs = [first, flipped(second, "section", 2)]

    known = ()
    if frames == 2:
        known = call(
            last_inner_kernel,
            inner_outs,
            [views],
            0,
            grad,
            pre_two,
            *kernels,
            after=(first, second),
        )
        afters = from_later(known[0])
    else:
        afters = from_later(jnp.concatenate(beside_band(pairs, 0)))
    inner, gpre_two = call(
        functools.partial(inner_kernel, later),
        inner_outs,
        [views],
        0,
        grad,
        pre_two,
        *wholes,
        *kernels,
        *known,
        early=(saved_two, saved_one, pre_one, temporal_one),
    )
    if frames == 2:
        edge = call(
            last_edge_kernel,
            [bf16(4, cols, ch)],
            [edge_views],
            0,
            grad,
            *pairs,
            known[1],
            *kernels,
            after=(gpre_two,),
        )
        afters += from_later(edge)
    parts_two = call(
        functools.partial(two_kernel, later),
        handed,
        [views, pltpu.VMEM(sides.shape, sides.dtype), sums],
        8 * conv,
        saved_two,
        pre_two,
        gpre_two,
        *pairs,
        grad,
        *wholes,
        after=(edge,) if frames == 2 else (),
    )
    sides_one = call(
        sides_kernel, [sides], [], conv // 8, saved_one, pre_one, *pairs, after=parts_two[:1]
    )
    height, half = 3 * ch, 3 * ch // 2
    keep_two, low_two, high_two = parts_two
    own_two, send_two = call(
        pair_kernel,
        [f32(height, ch), bf16(height, ch)],
        [],
        height * ch,
        keep_two,
        flipped(low_two, "section", 1),
        flipped(high_two, "section", 1),
    )
    across_two = flipped(send_two, "section", 2)
    mid_inputs = (grad, *pairs, inner, gpre_two)
    one_inputs = (sides_one, pre_one)
    mid_outs = [bf16(rows, cols, ch)]
    one_outs = [bf16(rows, cols, ch), f32(2, 3 * ch, ch), bf16(6 * ch + 2 * cols, ch)]
    if frames == 2:
        inners_one = call(
            one_inner_kernel,
            [bf16(rows - 2, cols, ch), bf16(rows - 2, cols, 3 * ch)],
            [],
            conv // 8,
            pre_one,
            inner,
            afters[0],
            temporal_one,
        )
        mid, gpre_one, *parts_one = call(
            mid_one_kernel,
            mid_outs + one_outs,
            [views, sums, act, pltpu.VMEM((2, cols, ch), jnp.bfloat16), edge_views],
            8 * conv,
            *mid_inputs,
            *afters,
            *kernels,
            *one_inputs,
            temporal_one,
            *inners_one,
            after=(own_two,),
        )
    else:
        mid = call(
            functools.partial(mid_kernel, later),
            mid_outs,
            [edge_views],
            conv // 8,
            *mid_inputs,
            *afters,
            *kernels,
        )
        gpre_one, *parts_one = call(
            functools.partial(one_kernel, later),
            one_outs,
            [views, sums],
            1.2 * conv,
            *one_inputs,
            mid,
            *from_later(mid),
            temporal_one,
        )
    keep_one, send_one = parts_one
    split = frames == 2 and lax.axis_size("dp") == 4
    if split:
        send_one = later_than(send_one, across_two)
    pair_one = flipped(send_one, "section", 1)

    def input_gradient(edge, after):
        return call(
            input_kernel,
            [bf16(rows, cols, ch), f32(8, 128)],
            [pltpu.VMEM((rows + 2, cols, 3 * ch), jnp.bfloat16)],
            conv,
            mid,
            gpre_one,
            pair_one,
            edge,
            spatial_one,
            after=after,
        )

    if split:

        def added(one, two):
            return call(add_kernel, [bf16(half, ch)], [], half * ch, one, two)

        keep_two, send_two = call(
            band_kernel,
            [f32(half, ch), bf16(half + cols + 16, ch)],
            [],
            0,
            own_two,
            across_two,
        )
        sum_two = added(keep_two, flipped(send_two, "video", 1))
        quarters = [f32(half, ch)] + [bf16(half + more, ch) for more in (cols, 0, 16)]
        own_one, *sends = call(
            pair_quarter_kernel, quarters, [], 0, keep_one, pair_one, after=(send_two,)
        )
        across = flipped(sends[0], "section", 2)
        parts = [across, flipped(sends[1], "video", 1), flipped_both(sends[2])]
        sum_one = call(plane_kernel, [bf16(half, ch)], [], 4 * half * ch, own_one, *parts)
        part_two = flipped(sum_two, "dp", 1)
        part_one = flipped(later_than(sum_one, sum_two), "dp", 1)
        sum_two = added(sum_two, part_two)
        sum_one = added(sum_one, part_one)
        last_two = flipped(sum_two, "dp", 2)
        last_one = flipped(later_than(sum_one, sum_two), "dp", 2)
        grad_in, token = input_gradient(across, (sum_one,))
        own = call(
            functools.partial(scaled_kernel, factor),
            [bf16(2, half, ch)],
            [],
            height * ch,
            sum_one,
            last_one,
            sum_two,
            last_two,
            after=(token,),
        )
        frame, across, both = flipped(own, "video", 1), flipped(own, "section", 2), flipped_both(own)
        shares = [own, frame, across]
        shares += [flipped(share, "section", 1) for share in shares]
        places = [(0, False), (0, True), (2, False), (1, False), (1, True), (3, False)]
        sums = placed([*shares, both], [*places, (2, True)])
        sums = unpacked(placed([flipped(both, "section", 1)], [(3, True)], sums))
    else:
        own_one, send_one = call(
            pair_kernel,
            [f32(height, ch), bf16(height, ch)],
            [],
            height * ch,
            keep_one,
            pair_one[:height],
            pair_one[height : 2 * height],
        )
        edge = flipped(pair_one[pair_one.shape[0] - cols :], "section", 2)
        grad_in, _ = input_gradient(edge, ())
        own_one = own_one + flipped(send_one, "section", 2).astype(jnp.float32)
        own_two = own_two + across_two.astype(jnp.float32)
        share = lax.psum(jnp.stack((own_one, own_two)), ("video", "dp")) * factor
        share = share.astype(jnp.bfloat16)
        shares = [share, flipped(share, "section", 2)]
        shares += [flipped(share, "section", 1) for share in shares]
        sums = unpacked(placed(shares, [(0, None), (2, None), (1, None), (3, None)]))
    return (grad_in.reshape(shape), *sums)


def solution(mesh):
    whole = P("dp", "video", "section", None, None)
    return jax.shard_map(
        on_device,
        mesh=mesh,
        in_specs=(whole,) * 5 + (P(),) * 4,
        out_specs=(whole, P(), P(), P(), P()),
        check_vma=False,
    )
```

```python
import functools
import math

import jax
import jax.numpy as jnp
from jax import lax
from jax.experimental import pallas as pl
from jax.experimental.pallas import tpu as pltpu
from jax.sharding import PartitionSpec as P

MIB = 1024 * 1024


def sigmoid(value):
    return 1.0 / (1.0 + jnp.exp(-value))


def bf16(*shape):
    return jax.ShapeDtypeStruct(shape, jnp.bfloat16)


def f32(*shape):
    return jax.ShapeDtypeStruct(shape, jnp.float32)


def call(kernel, outs, scratch, flops, *operands, after=(), early=(), spare_inputs=False, limit=24):
    single = len(outs) == 1
    moved = sum(math.prod(x.shape) * x.dtype.itemsize for x in (*operands, *outs))
    vmem = pl.BlockSpec(memory_space=pltpu.VMEM)
    spare = pl.BlockSpec(memory_space=pl.ANY)
    spec = spare if spare_inputs else vmem
    count = len(operands)
    operands = (*operands, *early, *after)

    def body(*refs):
        kernel(*refs[:count], *refs[len(operands) :])

    return pl.pallas_call(
        body,
        out_shape=outs[0] if single else tuple(outs),
        in_specs=[spec] * count + [vmem] * len(early) + [spare] * len(after),
        out_specs=vmem if single else (vmem,) * len(outs),
        scratch_shapes=scratch,
        compiler_params=pltpu.CompilerParams(vmem_limit_bytes=limit * MIB),
        cost_estimate=pl.CostEstimate(
            flops=int(flops), bytes_accessed=int(moved) if flops else 0, transcendentals=0
        ),
    )(*operands)


def from_ahead(block, band_step, frame_step):
    bands, frames = lax.axis_size("section"), lax.axis_size("video")
    pairs = [
        ((band + band_step) * frames + frame + frame_step, band * frames + frame)
        for band in range(bands)
        for frame in range(frames)
        if 0 <= band + band_step < bands and frame + frame_step < frames
    ]
    return lax.ppermute(block, ("section", "video"), pairs)


def beside_band(pair_refs, row):
    band = lax.axis_index("section")
    odd = lax.rem(band, 2) == 1
    inside = (band > 0) & (band < lax.axis_size("section") - 1)
    first, second = (ref[row : row + 1] for ref in pair_refs)
    second = jnp.where(inside, second, jnp.zeros_like(second))
    return jnp.where(odd, first, second), jnp.where(odd, second, first)


def flipped(block, axis, flip):
    count = lax.axis_size(axis)
    return lax.ppermute(block, axis, [(place ^ flip, place) for place in range(count)])


def flipped_both(block):
    bands = lax.axis_size("section")
    pairs = [
        (2 * (band ^ 2) + 1 - frame, 2 * band + frame) for band in range(bands) for frame in range(2)
    ]
    return lax.ppermute(block, ("section", "video"), pairs)


def later_than(block, *others):
    return lax.optimization_barrier((block, *others))[0]


def beside(gpre, views_ref, start):
    count, cols, ch = gpre.shape
    at = lax.broadcasted_iota(jnp.int32, gpre.shape, 1)
    right = jnp.where(at == cols - 1, 0.0, pltpu.roll(gpre, cols - 1, 1))
    left = jnp.where(at == 0, 0.0, pltpu.roll(gpre, 1, 1))
    here = pl.ds(start, count)
    views_ref[here, :, 0:ch] = right.astype(jnp.bfloat16)
    views_ref[here, :, ch : 2 * ch] = gpre.astype(jnp.bfloat16)
    views_ref[here, :, 2 * ch : 3 * ch] = left.astype(jnp.bfloat16)


def pre_gradient(grads, preact, temporal_ref):
    count, cols, ch = preact.shape
    flat = jnp.concatenate([grad.reshape(count * cols, ch) for grad in grads], axis=1)
    kernel = jnp.concatenate([temporal_ref[2 - step] for step in range(len(grads))], axis=1)
    gact = lax.dot_general(
        flat, kernel, (((1,), (1,)), ((), ())), preferred_element_type=jnp.float32
    )
    gact = gact.astype(jnp.bfloat16).astype(jnp.float32).reshape(preact.shape)
    hval = preact.astype(jnp.float32)
    sig = sigmoid(hval)
    return gact * sig * (1.0 + hval * (1.0 - sig))


def convolved(views_ref, spatial_ref, start, first):
    count, cols, ch = first.shape
    total = first.astype(jnp.float32).reshape(count * cols, ch)
    for ky in range(3):
        view = views_ref[pl.ds(start + 2 - ky, count)].reshape(count * cols, 3 * ch)
        kernel = jnp.concatenate([spatial_ref[ky, kx] for kx in range(3)], axis=1)
        total = total + lax.dot_general(
            view, kernel, (((1,), (1,)), ((), ())), preferred_element_type=jnp.float32
        )
    return total.astype(jnp.bfloat16).reshape(first.shape)


def is_last():
    return lax.axis_index("video") == lax.axis_size("video") - 1


def left_sides(saved_ref, preact_ref, above, below, sides_ref):
    rows, cols, ch = saved_ref.shape
    flat = (rows * cols, ch)
    shifts = [
        jnp.concatenate([above, saved_ref[: rows - 1]], axis=0),
        saved_ref[...],
        jnp.concatenate([saved_ref[1:], below], axis=0),
    ]
    for n, shift in enumerate(shifts):
        sides_ref[n] = shift.reshape(flat).T
    hval = preact_ref[...].astype(jnp.float32)
    sides_ref[3] = (hval * sigmoid(hval)).astype(jnp.bfloat16).reshape(flat).T


def kernel_sums(sides_ref, grads, views, sums_ref):
    _, ch, pixels = sides_ref.shape
    shifts = sides_ref[0:3].reshape(3 * ch, pixels)
    sums = jnp.dot(shifts, views, preferred_element_type=jnp.float32)
    for ky in range(3):
        for kx in range(3):
            here = slice(kx * ch, (kx + 1) * ch)
            sums_ref[ky, here] = sums[ky * ch : (ky + 1) * ch, here]
    grads = jnp.concatenate([grad.reshape(pixels, ch) for grad in grads], axis=1)
    sums = jnp.dot(sides_ref[3], grads, preferred_element_type=jnp.float32)
    zeros = jnp.zeros((ch, ch), jnp.float32)
    for k in range(3):
        step = 2 - k
        value = sums[:, step * ch : (step + 1) * ch] if step * ch < grads.shape[1] else zeros
        sums_ref[3, k * ch : (k + 1) * ch] = jnp.where(is_last(), zeros, value) if step else value


def hand_out(sums_ref, keep_ref, *send_refs):
    odd = lax.rem(lax.axis_index("section"), 2)
    for n, send_ref in enumerate(send_refs):
        keep_ref[n] = sums_ref[2 * n + odd]
        send_ref[...] = sums_ref[2 * n + 1 - odd].astype(jnp.bfloat16)


def pack_kernel(*refs):
    parts, outs, sems = refs[:4], refs[4:6], refs[6]
    last = parts[0].shape[0] - 1
    odd = lax.rem(lax.axis_index("section"), 2)
    copies = []
    for n, part in enumerate(parts):
        for out, row in zip(outs, ((1 - odd) * last, odd * last)):
            sem = sems.at[len(copies)]
            copies.append(
                pltpu.make_async_copy(part.at[pl.ds(row, 1)], out.at[pl.ds(n, 1)], sem)
            )
    for copy in copies:
        copy.start()
    for copy in copies:
        copy.wait()


def interior(grad_ref, preact_ref, wholes, temporal_ref, spatial_ref, inner_ref, gpre_ref, views_ref):
    rows, cols, ch = grad_ref.shape
    step = 4

    for n in range(rows // step):
        here = pl.ds(n * step, step)
        grads = [ref[here] for ref in (grad_ref, *wholes)]
        gpre = pre_gradient(grads, preact_ref[here], temporal_ref)
        gpre_ref[here] = gpre.astype(jnp.bfloat16)
        beside(gpre, views_ref, n * step)

    half = rows // 2 - 1

    for n in range(2):
        first = grad_ref[pl.ds(n * half + 1, half)]
        inner_ref[pl.ds(n * half, half)] = convolved(views_ref, spatial_ref, n * half, first)


def edge_rows(grad_ref, pair_refs, afters, gpre_ref, temporal_ref, spatial_ref, views_ref):
    rows, cols, ch = grad_ref.shape
    (grad_above, grad_below), (above_pre, below_pre) = (beside_band(pair_refs, n) for n in (0, 1))
    above = [grad_above] + [ref[0:1] for ref in afters]
    below = [grad_below] + [ref[1:2] for ref in afters]
    beside(pre_gradient(above, above_pre, temporal_ref), views_ref, 0)
    beside(gpre_ref[0:2].astype(jnp.float32), views_ref, 1)
    beside(gpre_ref[rows - 2 : rows].astype(jnp.float32), views_ref, 3)
    beside(pre_gradient(below, below_pre, temporal_ref), views_ref, 5)
    return (
        convolved(views_ref, spatial_ref, 0, grad_ref[0:1]),
        convolved(views_ref, spatial_ref, 3, grad_ref[rows - 1 : rows]),
    )


def last_inner_kernel(grad_ref, preact_ref, temporal_ref, spatial_ref, inner_ref, gpre_ref, views_ref):
    @pl.when(is_last())
    def _():
        interior(
            grad_ref, preact_ref, [], temporal_ref, spatial_ref, inner_ref, gpre_ref, views_ref
        )


def last_edge_kernel(grad_ref, one_ref, two_ref, gpre_ref, temporal_ref, spatial_ref, edge_ref, views_ref):
    @pl.when(is_last())
    def _():
        pair_refs = (one_ref, two_ref)
        edge_ref[0:1], edge_ref[1:2] = edge_rows(
            grad_ref, pair_refs, [], gpre_ref, temporal_ref, spatial_ref, views_ref
        )
        edge_ref[2:3], edge_ref[3:4] = beside_band(pair_refs, 0)


def inner_kernel(later, *refs):
    inputs, wholes, kernels = refs[:2], refs[2 : 2 + later], refs[2 + later : 4 + later]
    known, outs = refs[4 + later : -3], refs[-3:]
    if not known:
        interior(*inputs, wholes, *kernels, *outs)
        return

    @pl.when(is_last())
    def _():
        outs[0][...] = known[0][...]
        outs[1][...] = known[1][...]

    @pl.when(jnp.logical_not(is_last()))
    def _():
        interior(*inputs, wholes, *kernels, *outs)


def mid_kernel(later, *refs):
    grad_ref, inner_ref, gpre_ref = refs[0], refs[3], refs[4]
    afters, (temporal_ref, spatial_ref, mid_ref, views_ref) = refs[5 : 5 + later], refs[5 + later :]
    rows = grad_ref.shape[0]
    first, last = edge_rows(
        grad_ref, refs[1:3], afters, gpre_ref, temporal_ref, spatial_ref, views_ref
    )
    mid_ref[0:1], mid_ref[rows - 1 : rows] = first, last
    mid_ref[1 : rows - 1] = inner_ref[...]


def two_kernel(later, *refs):
    saved_ref, preact_ref, gpre_ref = refs[:3]
    pair_refs, grad_ref = refs[3:5], refs[5]
    wholes, outs = refs[6 : 6 + later], refs[6 + later : 9 + later]
    views_ref, sides_ref, sums_ref = refs[9 + later :]
    rows, cols, ch = saved_ref.shape
    step = 4

    for n in range(rows // step):
        here = pl.ds(n * step, step)
        beside(gpre_ref[here].astype(jnp.float32), views_ref, n * step)

    views = views_ref[...].reshape(rows * cols, 3 * ch)
    grads = [ref[...] for ref in (grad_ref, *wholes)]
    left_sides(saved_ref, preact_ref, *beside_band(pair_refs, 2), sides_ref)
    kernel_sums(sides_ref, grads, views, sums_ref)
    hand_out(sums_ref, *outs)


def sides_kernel(saved_ref, preact_ref, one_ref, two_ref, sides_ref):
    left_sides(saved_ref, preact_ref, *beside_band((one_ref, two_ref), 3), sides_ref)


def pre_rows(preact, mids, temporal_ref, gpre_ref, views_ref, start):
    gpre = pre_gradient(mids, preact, temporal_ref)
    gpre_ref[start : start + preact.shape[0]] = gpre.astype(jnp.bfloat16)
    beside(gpre, views_ref, start)


def block_sums(gpre_ref, sides_ref, mids, views_ref, sums_ref, keep_ref, send_ref):
    rows, cols, ch = gpre_ref.shape
    odd = lax.rem(lax.axis_index("section"), 2)
    size = send_ref.shape[0] - 2 * cols
    send_ref[size : size + cols] = gpre_ref[(1 - odd) * (rows - 1)]
    send_ref[size + cols : size + 2 * cols] = gpre_ref[odd * (rows - 1)]
    views = views_ref[...].reshape(rows * cols, 3 * ch)
    kernel_sums(sides_ref, [ref[...] for ref in mids], views, sums_ref)
    height = sums_ref.shape[1]
    hand_out(sums_ref, keep_ref, send_ref.at[:height], send_ref.at[height : 2 * height])


def one_kernel(later, *refs):
    sides_ref, preact_ref, mids = refs[0], refs[1], refs[2 : 3 + later]
    temporal_ref, outs, scratch = refs[3 + later], refs[4 + later : 7 + later], refs[7 + later :]
    gpre_ref, keep_ref, send_ref = outs
    views_ref, sums_ref = scratch
    for n in range(preact_ref.shape[0] // 4):
        here = slice(4 * n, 4 * n + 4)
        grads = [ref[here] for ref in mids]
        pre_rows(preact_ref[here], grads, temporal_ref, gpre_ref, views_ref, 4 * n)
    block_sums(gpre_ref, sides_ref, mids, views_ref, sums_ref, keep_ref, send_ref)


def one_inner_kernel(preact_ref, inner_ref, after_ref, temporal_ref, gpre_ref, views_ref):
    rows = inner_ref.shape[0]
    for n in range(rows // 7):
        here = slice(7 * n, 7 * n + 7)
        after = after_ref[here]
        after = jnp.where(is_last(), jnp.zeros_like(after), after)
        preact = preact_ref[7 * n + 1 : 7 * n + 8]
        pre_rows(preact, [inner_ref[here], after], temporal_ref, gpre_ref, views_ref, 7 * n)


def mid_one_kernel(*refs):
    after_inner_ref, after_edge_ref = refs[5:7]
    temporal_two_ref, spatial_two_ref, sides_ref, preact_ref, temporal_ref = refs[7:12]
    inner_gpre_ref, inner_views_ref = refs[12:14]
    mid_ref, gpre_ref, keep_ref, send_ref = refs[14:18]
    views_ref, sums_ref, next_ref, edge_ref, edge_views_ref = refs[18:]
    rows = next_ref.shape[0]

    @pl.when(is_last())
    def _():
        edge_ref[...] = jnp.zeros(edge_ref.shape, edge_ref.dtype)
        next_ref[...] = jnp.zeros(next_ref.shape, next_ref.dtype)

    @pl.when(jnp.logical_not(is_last()))
    def _():
        edge_ref[...] = after_edge_ref[2:4]
        next_ref[0:1] = after_edge_ref[0:1]
        next_ref[1 : rows - 1] = after_inner_ref[...]
        next_ref[rows - 1 : rows] = after_edge_ref[1:2]

    mid_kernel(
        1, *refs[:5], edge_ref, temporal_two_ref, spatial_two_ref, mid_ref, edge_views_ref
    )
    gpre_ref[1 : rows - 1] = inner_gpre_ref[...]
    views_ref[1 : rows - 1] = inner_views_ref[...]
    for row in (0, rows - 1):
        here = slice(row, row + 1)
        grads = [mid_ref[here], next_ref[here]]
        pre_rows(preact_ref[here], grads, temporal_ref, gpre_ref, views_ref, row)
    block_sums(gpre_ref, sides_ref, [mid_ref, next_ref], views_ref, sums_ref, keep_ref, send_ref)


def input_kernel(mid_ref, gpre_ref, pair_ref, across_ref, spatial_ref, out_ref, token_ref, views_ref):
    rows, cols, ch = out_ref.shape
    pair = pair_ref[pair_ref.shape[0] - 2 * cols : pair_ref.shape[0] - cols]
    above, below = beside_band((pair[None], across_ref[across_ref.shape[0] - cols :][None]), 0)
    token_ref[...] = jnp.zeros(token_ref.shape, token_ref.dtype)
    step = 4
    beside(above.astype(jnp.float32), views_ref, 0)
    beside(below.astype(jnp.float32), views_ref, rows + 1)

    for n in range(rows // step):
        gpre = gpre_ref[pl.ds(n * step, step)].astype(jnp.float32)
        beside(gpre, views_ref, n * step + 1)

    for n in range(rows // step):
        here = pl.ds(n * step, step)
        out_ref[here] = convolved(views_ref, spatial_ref, n * step, mid_ref[here])


def halves(count, index):
    return [pl.ds(pl.multiple_of(n * count, count), count) for n in (index, 1 - index)]


def pair_kernel(keep_ref, low_ref, high_ref, own_ref, send_ref):
    across = lax.axis_index("section") // 2
    parts = [ref[...].astype(jnp.float32) for ref in (low_ref, high_ref)]
    own_ref[...] = keep_ref[across] + jnp.where(across == 0, *parts)
    total = keep_ref[1 - across] + jnp.where(across == 0, *parts[::-1])
    send_ref[...] = total.astype(jnp.bfloat16)


def band_kernel(own_ref, part_ref, keep_ref, send_ref):
    mine, other = halves(keep_ref.shape[0], lax.axis_index("video"))
    half = keep_ref.shape[0]
    keep_ref[...] = own_ref[mine] + part_ref[mine].astype(jnp.float32)
    send_ref[:half] = (own_ref[other] + part_ref[other].astype(jnp.float32)).astype(jnp.bfloat16)


def pair_quarter_kernel(keep_ref, part_ref, own_ref, across_ref, frame_ref, both_ref):
    _, height, _ = keep_ref.shape
    half = own_ref.shape[0]
    band = lax.axis_index("section") // 2
    frames = halves(half, lax.axis_index("video"))

    def quarter(band, rows):
        start = pl.multiple_of(band * height, height)
        part = part_ref.at[pl.ds(start, height)][rows]
        return keep_ref[band, rows] + part.astype(jnp.float32)

    own_ref[...] = quarter(band, frames[0])
    across_ref[:half] = quarter(1 - band, frames[0]).astype(jnp.bfloat16)
    rest = across_ref.shape[0] - half
    across_ref[half:] = part_ref[2 * height + rest :]
    frame_ref[...] = quarter(band, frames[1]).astype(jnp.bfloat16)
    both_ref[:half] = quarter(1 - band, frames[1]).astype(jnp.bfloat16)


def plane_kernel(own_ref, *refs):
    parts, out_ref = refs[:-1], refs[-1]
    total = own_ref[...]
    for part in parts:
        total = total + part[: out_ref.shape[0]].astype(jnp.float32)
    out_ref[...] = total.astype(jnp.bfloat16)


def add_kernel(one_ref, two_ref, out_ref):
    total = one_ref[...].astype(jnp.float32) + two_ref[: one_ref.shape[0]].astype(jnp.float32)
    out_ref[...] = total.astype(jnp.bfloat16)


def scaled_kernel(factor, *refs):
    outs = refs[4:]
    height = outs[0].shape[1]
    for block in range(2):
        one, two = (ref[...].astype(jnp.float32) for ref in refs[2 * block : 2 * block + 2])
        total = ((one + two) * factor).astype(jnp.bfloat16)
        for out_ref in outs:
            out_ref[block, :height] = total


def place_kernel(places, *refs):
    shares, outs = refs[: len(places)], refs[-6:-2]
    sums_ref, sems = refs[-2:]
    band, frame = lax.axis_index("section"), lax.axis_index("video")
    height = sums_ref.shape[2]

    def copies(n, block):
        flip, other = places[n]
        place = jnp.bitwise_xor(band, flip)
        half = 0 if other is None else jnp.bitwise_xor(frame, int(other))
        here = pl.ds(pl.multiple_of(half * height, height), height)
        spatial, temporal = outs[2 * block : 2 * block + 2]
        source, sem = sums_ref.at[n, block], sems.at[n, block]
        return (
            (place < 3, lambda: pltpu.make_async_copy(source, spatial.at[place, here], sem)),
            (place == 3, lambda: pltpu.make_async_copy(source, temporal.at[here], sem)),
        )

    for n, share in enumerate(shares):
        for block in range(2):
            sums_ref[n, block] = share[block, :height].astype(jnp.float32)
            for inside, copy in copies(n, block):
                pl.when(inside)(lambda: copy().start())
    for n in range(len(shares)):
        for block in range(2):
            for inside, copy in copies(n, block):
                pl.when(inside)(lambda: copy().wait())


def placed(shares, places, given=()):
    ch = shares[0].shape[2]
    height = 3 * ch if places[0][1] is None else 3 * ch // 2
    count = len(shares)
    outs = (f32(3, 3 * ch, ch), f32(3 * ch, ch)) * 2
    vmem, spare = (pl.BlockSpec(memory_space=space) for space in (pltpu.VMEM, pl.ANY))
    return pl.pallas_call(
        functools.partial(place_kernel, places),
        out_shape=outs,
        in_specs=[vmem] * count + [spare] * len(given),
        out_specs=(spare,) * 4,
        scratch_shapes=[
            pltpu.VMEM((count, 2, height, ch), jnp.float32),
            pltpu.SemaphoreType.DMA((count, 2)),
        ],
        input_output_aliases={count + n: n for n in range(len(given))},
        compiler_params=pltpu.CompilerParams(vmem_limit_bytes=24 * MIB),
        cost_estimate=pl.CostEstimate(
            flops=0, bytes_accessed=6 * count * height * ch * 2, transcendentals=0
        ),
    )(*shares, *given)


def unpacked(sums):
    ch = sums[0].shape[-1]
    return [x.reshape(3, 3, ch, ch) if x.ndim == 3 else x.reshape(3, ch, ch) for x in sums]


def on_device(
    grad_latent,
    input_one,
    preact_one,
    input_two,
    preact_two,
    spatial_one,
    temporal_one,
    spatial_two,
    temporal_two,
):
    shape = grad_latent.shape
    rows, cols, ch = shape[2:]
    bands, frames = lax.axis_size("section"), lax.axis_size("video")
    later = min(2, frames - 1)
    pixels = lax.axis_size("dp") * frames * bands * rows * cols
    factor = 1.0 / math.sqrt(pixels)
    grad, saved_one, pre_one, saved_two, pre_two = (
        x.reshape(rows, cols, ch)
        for x in (grad_latent, input_one, preact_one, input_two, preact_two)
    )
    conv = 2 * rows * cols * 9 * ch * ch
    views = pltpu.VMEM((rows, cols, 3 * ch), jnp.bfloat16)
    edge_views = pltpu.VMEM((6, cols, 3 * ch), jnp.bfloat16)
    act = pltpu.VMEM((rows, cols, ch), jnp.bfloat16)
    sides = bf16(4, ch, rows * cols)
    sums = pltpu.VMEM((4, 3 * ch, ch), jnp.float32)
    handed = [f32(2, 3 * ch, ch)] + [bf16(3 * ch, ch)] * 2
    inner_outs = [bf16(rows - 2, cols, ch), bf16(rows, cols, ch)]
    kernels = (temporal_two, spatial_two)

    def from_later(x):
        if frames == 2:
            return [flipped(x, "video", 1)]
        return [from_ahead(x, 0, n + 1) for n in range(later)]

    wholes = from_later(grad)
    packs = call(
        pack_kernel,
        [bf16(4, cols, ch)] * 2,
        [pltpu.SemaphoreType.DMA((8,))],
        1,
        grad,
        pre_two,
        saved_two,
        saved_one,
        spare_inputs=True,
        limit=58,
    )
    second = flipped(packs[1], "section", 1)
    first = flipped(later_than(packs[0], second), "section", 1)
    pairs = [first, flipped(second, "section", 2)]

    known = ()
    if frames == 2:
        known = call(
            last_inner_kernel,
            inner_outs,
            [views],
            0,
            grad,
            pre_two,
            *kernels,
            after=(first, second),
        )
        afters = from_later(known[0])
    else:
        afters = from_later(jnp.concatenate(beside_band(pairs, 0)))
    inner, gpre_two = call(
        functools.partial(inner_kernel, later),
        inner_outs,
        [views],
        0,
        grad,
        pre_two,
        *wholes,
        *kernels,
        *known,
        early=(saved_two, saved_one, pre_one, temporal_one),
    )
    if frames == 2:
        edge = call(
            last_edge_kernel,
            [bf16(4, cols, ch)],
            [edge_views],
            0,
            grad,
            *pairs,
            known[1],
            *kernels,
            after=(gpre_two,),
        )
        afters += from_later(edge)
    parts_two = call(
        functools.partial(two_kernel, later),
        handed,
        [views, pltpu.VMEM(sides.shape, sides.dtype), sums],
        8 * conv,
        saved_two,
        pre_two,
        gpre_two,
        *pairs,
        grad,
        *wholes,
        after=(edge,) if frames == 2 else (),
    )
    sides_one = call(
        sides_kernel, [sides], [], conv // 8, saved_one, pre_one, *pairs, after=parts_two[:1]
    )
    height, half = 3 * ch, 3 * ch // 2
    keep_two, low_two, high_two = parts_two
    own_two, send_two = call(
        pair_kernel,
        [f32(height, ch), bf16(height, ch)],
        [],
        height * ch,
        keep_two,
        flipped(low_two, "section", 1),
        flipped(high_two, "section", 1),
    )
    across_two = flipped(send_two, "section", 2)
    mid_inputs = (grad, *pairs, inner, gpre_two)
    one_inputs = (sides_one, pre_one)
    mid_outs = [bf16(rows, cols, ch)]
    one_outs = [bf16(rows, cols, ch), f32(2, 3 * ch, ch), bf16(6 * ch + 2 * cols, ch)]
    if frames == 2:
        inners_one = call(
            one_inner_kernel,
            [bf16(rows - 2, cols, ch), bf16(rows - 2, cols, 3 * ch)],
            [],
            conv // 8,
            pre_one,
            inner,
            afters[0],
            temporal_one,
        )
        mid, gpre_one, *parts_one = call(
            mid_one_kernel,
            mid_outs + one_outs,
            [views, sums, act, pltpu.VMEM((2, cols, ch), jnp.bfloat16), edge_views],
            8 * conv,
            *mid_inputs,
            *afters,
            *kernels,
            *one_inputs,
            temporal_one,
            *inners_one,
            after=(own_two,),
        )
    else:
        mid = call(
            functools.partial(mid_kernel, later),
            mid_outs,
            [edge_views],
            conv // 8,
            *mid_inputs,
            *afters,
            *kernels,
        )
        gpre_one, *parts_one = call(
            functools.partial(one_kernel, later),
            one_outs,
            [views, sums],
            1.2 * conv,
            *one_inputs,
            mid,
            *from_later(mid),
            temporal_one,
        )
    keep_one, send_one = parts_one
    split = frames == 2 and lax.axis_size("dp") == 4
    if split:
        send_one = later_than(send_one, across_two)
    pair_one = flipped(send_one, "section", 1)

    def input_gradient(edge, after):
        return call(
            input_kernel,
            [bf16(rows, cols, ch), f32(8, 128)],
            [pltpu.VMEM((rows + 2, cols, 3 * ch), jnp.bfloat16)],
            conv,
            mid,
            gpre_one,
            pair_one,
            edge,
            spatial_one,
            after=after,
        )

    if split:

        def added(one, two):
            return call(add_kernel, [bf16(half, ch)], [], half * ch, one, two)

        keep_two, send_two = call(
            band_kernel,
            [f32(half, ch), bf16(half + 2 * cols, ch)],
            [],
            0,
            own_two,
            across_two,
        )
        sum_two = added(keep_two, flipped(send_two, "video", 1))
        quarters = [f32(half, ch)] + [bf16(half + more, ch) for more in (cols, 0, cols + 16)]
        own_one, *sends = call(
            pair_quarter_kernel, quarters, [], 0, keep_one, pair_one, after=(send_two,)
        )
        across = flipped(sends[0], "section", 2)
        parts = [across, flipped(sends[1], "video", 1), flipped_both(sends[2])]
        sum_one = call(plane_kernel, [bf16(half, ch)], [], 4 * half * ch, own_one, *parts)
        part_two = flipped(sum_two, "dp", 1)
        part_one = flipped(later_than(sum_one, sum_two), "dp", 1)
        sum_two = added(sum_two, part_two)
        sum_one = added(sum_one, part_one)
        last_two = flipped(sum_two, "dp", 2)
        last_one = flipped(later_than(sum_one, sum_two), "dp", 2)
        grad_in, token = input_gradient(across, (sum_one,))
        own, longer = call(
            functools.partial(scaled_kernel, factor),
            [bf16(2, half, ch), bf16(2, half + 16, ch)],
            [],
            height * ch,
            sum_one,
            last_one,
            sum_two,
            last_two,
            after=(token,),
        )
        frame, across, both = flipped(own, "video", 1), flipped(longer, "section", 2), flipped_both(own)
        shares = [own, frame, across]
        shares += [flipped(share, "section", 1) for share in shares]
        places = [(0, False), (0, True), (2, False), (1, False), (1, True), (3, False)]
        sums = placed([*shares, both], [*places, (2, True)])
        sums = unpacked(placed([flipped(both, "section", 1)], [(3, True)], sums))
    else:
        own_one, send_one = call(
            pair_kernel,
            [f32(height, ch), bf16(height, ch)],
            [],
            height * ch,
            keep_one,
            pair_one[:height],
            pair_one[height : 2 * height],
        )
        edge = flipped(pair_one[pair_one.shape[0] - cols :], "section", 2)
        grad_in, _ = input_gradient(edge, ())
        own_one = own_one + flipped(send_one, "section", 2).astype(jnp.float32)
        own_two = own_two + across_two.astype(jnp.float32)
        share = lax.psum(jnp.stack((own_one, own_two)), ("video", "dp")) * factor
        share = share.astype(jnp.bfloat16)
        shares = [share, flipped(share, "section", 2)]
        shares += [flipped(share, "section", 1) for share in shares]
        sums = unpacked(placed(shares, [(0, None), (2, None), (1, None), (3, None)]))
    return (grad_in.reshape(shape), *sums)


def solution(mesh):
    whole = P("dp", "video", "section", None, None)
    return jax.shard_map(
        on_device,
        mesh=mesh,
        in_specs=(whole,) * 5 + (P(),) * 4,
        out_specs=(whole, P(), P(), P(), P()),
        check_vma=False,
    )
```

```python
import functools
import math

import jax
import jax.numpy as jnp
from jax import lax
from jax.experimental import pallas as pl
from jax.experimental.pallas import tpu as pltpu
from jax.sharding import PartitionSpec as P

MIB = 1024 * 1024


def sigmoid(value):
    return 1.0 / (1.0 + jnp.exp(-value))


def bf16(*shape):
    return jax.ShapeDtypeStruct(shape, jnp.bfloat16)


def f32(*shape):
    return jax.ShapeDtypeStruct(shape, jnp.float32)


def call(kernel, outs, scratch, flops, *operands, after=(), early=(), spare_inputs=False, limit=24):
    single = len(outs) == 1
    moved = sum(math.prod(x.shape) * x.dtype.itemsize for x in (*operands, *outs))
    vmem = pl.BlockSpec(memory_space=pltpu.VMEM)
    spare = pl.BlockSpec(memory_space=pl.ANY)
    spec = spare if spare_inputs else vmem
    count = len(operands)
    operands = (*operands, *early, *after)

    def body(*refs):
        kernel(*refs[:count], *refs[len(operands) :])

    return pl.pallas_call(
        body,
        out_shape=outs[0] if single else tuple(outs),
        in_specs=[spec] * count + [vmem] * len(early) + [spare] * len(after),
        out_specs=vmem if single else (vmem,) * len(outs),
        scratch_shapes=scratch,
        compiler_params=pltpu.CompilerParams(vmem_limit_bytes=limit * MIB),
        cost_estimate=pl.CostEstimate(
            flops=int(flops), bytes_accessed=int(moved) if flops else 0, transcendentals=0
        ),
    )(*operands)


def from_ahead(block, band_step, frame_step):
    bands, frames = lax.axis_size("section"), lax.axis_size("video")
    pairs = [
        ((band + band_step) * frames + frame + frame_step, band * frames + frame)
        for band in range(bands)
        for frame in range(frames)
        if 0 <= band + band_step < bands and frame + frame_step < frames
    ]
    return lax.ppermute(block, ("section", "video"), pairs)


def beside_band(pair_refs, row):
    band = lax.axis_index("section")
    odd = lax.rem(band, 2) == 1
    inside = (band > 0) & (band < lax.axis_size("section") - 1)
    first, second = (ref[row : row + 1] for ref in pair_refs)
    second = jnp.where(inside, second, jnp.zeros_like(second))
    return jnp.where(odd, first, second), jnp.where(odd, second, first)


def flipped(block, axis, flip):
    count = lax.axis_size(axis)
    return lax.ppermute(block, axis, [(place ^ flip, place) for place in range(count)])


def flipped_both(block):
    bands = lax.axis_size("section")
    pairs = [
        (2 * (band ^ 2) + 1 - frame, 2 * band + frame) for band in range(bands) for frame in range(2)
    ]
    return lax.ppermute(block, ("section", "video"), pairs)


def later_than(block, *others):
    return lax.optimization_barrier((block, *others))[0]


def beside(gpre, views_ref, start):
    count, cols, ch = gpre.shape
    at = lax.broadcasted_iota(jnp.int32, gpre.shape, 1)
    right = jnp.where(at == cols - 1, 0.0, pltpu.roll(gpre, cols - 1, 1))
    left = jnp.where(at == 0, 0.0, pltpu.roll(gpre, 1, 1))
    here = pl.ds(start, count)
    views_ref[here, :, 0:ch] = right.astype(jnp.bfloat16)
    views_ref[here, :, ch : 2 * ch] = gpre.astype(jnp.bfloat16)
    views_ref[here, :, 2 * ch : 3 * ch] = left.astype(jnp.bfloat16)


def pre_gradient(grads, preact, temporal_ref):
    count, cols, ch = preact.shape
    flat = jnp.concatenate([grad.reshape(count * cols, ch) for grad in grads], axis=1)
    kernel = jnp.concatenate([temporal_ref[2 - step] for step in range(len(grads))], axis=1)
    gact = lax.dot_general(
        flat, kernel, (((1,), (1,)), ((), ())), preferred_element_type=jnp.float32
    )
    gact = gact.astype(jnp.bfloat16).astype(jnp.float32).reshape(preact.shape)
    hval = preact.astype(jnp.float32)
    sig = sigmoid(hval)
    return gact * sig * (1.0 + hval * (1.0 - sig))


def convolved(views_ref, spatial_ref, start, first):
    count, cols, ch = first.shape
    total = first.astype(jnp.float32).reshape(count * cols, ch)
    for ky in range(3):
        view = views_ref[pl.ds(start + 2 - ky, count)].reshape(count * cols, 3 * ch)
        kernel = jnp.concatenate([spatial_ref[ky, kx] for kx in range(3)], axis=1)
        total = total + lax.dot_general(
            view, kernel, (((1,), (1,)), ((), ())), preferred_element_type=jnp.float32
        )
    return total.astype(jnp.bfloat16).reshape(first.shape)


def is_last():
    return lax.axis_index("video") == lax.axis_size("video") - 1


def left_sides(saved_ref, preact_ref, above, below, sides_ref):
    rows, cols, ch = saved_ref.shape
    flat = (rows * cols, ch)
    shifts = [
        jnp.concatenate([above, saved_ref[: rows - 1]], axis=0),
        saved_ref[...],
        jnp.concatenate([saved_ref[1:], below], axis=0),
    ]
    for n, shift in enumerate(shifts):
        sides_ref[n] = shift.reshape(flat).T
    hval = preact_ref[...].astype(jnp.float32)
    sides_ref[3] = (hval * sigmoid(hval)).astype(jnp.bfloat16).reshape(flat).T


def kernel_sums(sides_ref, grads, views, sums_ref):
    _, ch, pixels = sides_ref.shape
    shifts = sides_ref[0:3].reshape(3 * ch, pixels)
    sums = jnp.dot(shifts, views, preferred_element_type=jnp.float32)
    for ky in range(3):
        for kx in range(3):
            here = slice(kx * ch, (kx + 1) * ch)
            sums_ref[ky, here] = sums[ky * ch : (ky + 1) * ch, here]
    grads = jnp.concatenate([grad.reshape(pixels, ch) for grad in grads], axis=1)
    sums = jnp.dot(sides_ref[3], grads, preferred_element_type=jnp.float32)
    zeros = jnp.zeros((ch, ch), jnp.float32)
    for k in range(3):
        step = 2 - k
        value = sums[:, step * ch : (step + 1) * ch] if step * ch < grads.shape[1] else zeros
        sums_ref[3, k * ch : (k + 1) * ch] = jnp.where(is_last(), zeros, value) if step else value


def hand_out(sums_ref, keep_ref, *send_refs):
    odd = lax.rem(lax.axis_index("section"), 2)
    for n, send_ref in enumerate(send_refs):
        keep_ref[n] = sums_ref[2 * n + odd]
        send_ref[...] = sums_ref[2 * n + 1 - odd].astype(jnp.bfloat16)


def pack_kernel(*refs):
    parts, outs, sems = refs[:4], refs[4:6], refs[6]
    last = parts[0].shape[0] - 1
    odd = lax.rem(lax.axis_index("section"), 2)
    copies = []
    for n, part in enumerate(parts):
        for out, row in zip(outs, ((1 - odd) * last, odd * last)):
            sem = sems.at[len(copies)]
            copies.append(
                pltpu.make_async_copy(part.at[pl.ds(row, 1)], out.at[pl.ds(n, 1)], sem)
            )
    for copy in copies:
        copy.start()
    for copy in copies:
        copy.wait()


def interior(grad_ref, preact_ref, wholes, temporal_ref, spatial_ref, inner_ref, gpre_ref, views_ref):
    rows, cols, ch = grad_ref.shape
    step = 4

    for n in range(rows // step):
        here = pl.ds(n * step, step)
        grads = [ref[here] for ref in (grad_ref, *wholes)]
        gpre = pre_gradient(grads, preact_ref[here], temporal_ref)
        gpre_ref[here] = gpre.astype(jnp.bfloat16)
        beside(gpre, views_ref, n * step)

    half = rows // 2 - 1

    for n in range(2):
        first = grad_ref[pl.ds(n * half + 1, half)]
        inner_ref[pl.ds(n * half, half)] = convolved(views_ref, spatial_ref, n * half, first)


def edge_rows(grad_ref, pair_refs, afters, gpre_ref, temporal_ref, spatial_ref, views_ref):
    rows, cols, ch = grad_ref.shape
    (grad_above, grad_below), (above_pre, below_pre) = (beside_band(pair_refs, n) for n in (0, 1))
    above = [grad_above] + [ref[0:1] for ref in afters]
    below = [grad_below] + [ref[1:2] for ref in afters]
    beside(pre_gradient(above, above_pre, temporal_ref), views_ref, 0)
    beside(gpre_ref[0:2].astype(jnp.float32), views_ref, 1)
    beside(gpre_ref[rows - 2 : rows].astype(jnp.float32), views_ref, 3)
    beside(pre_gradient(below, below_pre, temporal_ref), views_ref, 5)
    return (
        convolved(views_ref, spatial_ref, 0, grad_ref[0:1]),
        convolved(views_ref, spatial_ref, 3, grad_ref[rows - 1 : rows]),
    )


def last_inner_kernel(grad_ref, preact_ref, temporal_ref, spatial_ref, inner_ref, gpre_ref, views_ref):
    @pl.when(is_last())
    def _():
        interior(
            grad_ref, preact_ref, [], temporal_ref, spatial_ref, inner_ref, gpre_ref, views_ref
        )


def last_edge_kernel(grad_ref, one_ref, two_ref, gpre_ref, temporal_ref, spatial_ref, edge_ref, views_ref):
    @pl.when(is_last())
    def _():
        pair_refs = (one_ref, two_ref)
        edge_ref[0:1], edge_ref[1:2] = edge_rows(
            grad_ref, pair_refs, [], gpre_ref, temporal_ref, spatial_ref, views_ref
        )
        edge_ref[2:3], edge_ref[3:4] = beside_band(pair_refs, 0)


def inner_kernel(later, *refs):
    inputs, wholes, kernels = refs[:2], refs[2 : 2 + later], refs[2 + later : 4 + later]
    known, outs = refs[4 + later : -3], refs[-3:]
    if not known:
        interior(*inputs, wholes, *kernels, *outs)
        return

    @pl.when(is_last())
    def _():
        outs[0][...] = known[0][...]
        outs[1][...] = known[1][...]

    @pl.when(jnp.logical_not(is_last()))
    def _():
        interior(*inputs, wholes, *kernels, *outs)


def mid_kernel(later, *refs):
    grad_ref, inner_ref, gpre_ref = refs[0], refs[3], refs[4]
    afters, (temporal_ref, spatial_ref, mid_ref, views_ref) = refs[5 : 5 + later], refs[5 + later :]
    rows = grad_ref.shape[0]
    first, last = edge_rows(
        grad_ref, refs[1:3], afters, gpre_ref, temporal_ref, spatial_ref, views_ref
    )
    mid_ref[0:1], mid_ref[rows - 1 : rows] = first, last
    mid_ref[1 : rows - 1] = inner_ref[...]


def two_kernel(later, *refs):
    saved_ref, preact_ref, gpre_ref = refs[:3]
    pair_refs, grad_ref = refs[3:5], refs[5]
    wholes, outs = refs[6 : 6 + later], refs[6 + later : 9 + later]
    views_ref, sides_ref, sums_ref = refs[9 + later :]
    rows, cols, ch = saved_ref.shape
    step = 4

    for n in range(rows // step):
        here = pl.ds(n * step, step)
        beside(gpre_ref[here].astype(jnp.float32), views_ref, n * step)

    views = views_ref[...].reshape(rows * cols, 3 * ch)
    grads = [ref[...] for ref in (grad_ref, *wholes)]
    left_sides(saved_ref, preact_ref, *beside_band(pair_refs, 2), sides_ref)
    kernel_sums(sides_ref, grads, views, sums_ref)
    hand_out(sums_ref, *outs)


def sides_kernel(saved_ref, preact_ref, one_ref, two_ref, sides_ref):
    left_sides(saved_ref, preact_ref, *beside_band((one_ref, two_ref), 3), sides_ref)


def pre_rows(preact, mids, temporal_ref, gpre_ref, views_ref, start):
    gpre = pre_gradient(mids, preact, temporal_ref)
    gpre_ref[start : start + preact.shape[0]] = gpre.astype(jnp.bfloat16)
    beside(gpre, views_ref, start)


def block_sums(gpre_ref, sides_ref, mids, views_ref, sums_ref, keep_ref, send_ref):
    rows, cols, ch = gpre_ref.shape
    odd = lax.rem(lax.axis_index("section"), 2)
    size = send_ref.shape[0] - 2 * cols
    send_ref[size : size + cols] = gpre_ref[(1 - odd) * (rows - 1)]
    send_ref[size + cols : size + 2 * cols] = gpre_ref[odd * (rows - 1)]
    views = views_ref[...].reshape(rows * cols, 3 * ch)
    kernel_sums(sides_ref, [ref[...] for ref in mids], views, sums_ref)
    height = sums_ref.shape[1]
    hand_out(sums_ref, keep_ref, send_ref.at[:height], send_ref.at[height : 2 * height])


def one_kernel(later, *refs):
    sides_ref, preact_ref, mids = refs[0], refs[1], refs[2 : 3 + later]
    temporal_ref, outs, scratch = refs[3 + later], refs[4 + later : 7 + later], refs[7 + later :]
    gpre_ref, keep_ref, send_ref = outs
    views_ref, sums_ref = scratch
    for n in range(preact_ref.shape[0] // 4):
        here = slice(4 * n, 4 * n + 4)
        grads = [ref[here] for ref in mids]
        pre_rows(preact_ref[here], grads, temporal_ref, gpre_ref, views_ref, 4 * n)
    block_sums(gpre_ref, sides_ref, mids, views_ref, sums_ref, keep_ref, send_ref)


def one_inner_kernel(preact_ref, inner_ref, after_ref, temporal_ref, gpre_ref, views_ref):
    rows = inner_ref.shape[0]
    for n in range(rows // 7):
        here = slice(7 * n, 7 * n + 7)
        after = after_ref[here]
        after = jnp.where(is_last(), jnp.zeros_like(after), after)
        preact = preact_ref[7 * n + 1 : 7 * n + 8]
        pre_rows(preact, [inner_ref[here], after], temporal_ref, gpre_ref, views_ref, 7 * n)


def mid_one_kernel(*refs):
    after_inner_ref, after_edge_ref = refs[5:7]
    temporal_two_ref, spatial_two_ref, sides_ref, preact_ref, temporal_ref = refs[7:12]
    inner_gpre_ref, inner_views_ref = refs[12:14]
    mid_ref, gpre_ref, keep_ref, send_ref = refs[14:18]
    views_ref, sums_ref, next_ref, edge_ref, edge_views_ref = refs[18:]
    rows = next_ref.shape[0]

    @pl.when(is_last())
    def _():
        edge_ref[...] = jnp.zeros(edge_ref.shape, edge_ref.dtype)
        next_ref[...] = jnp.zeros(next_ref.shape, next_ref.dtype)

    @pl.when(jnp.logical_not(is_last()))
    def _():
        edge_ref[...] = after_edge_ref[2:4]
        next_ref[0:1] = after_edge_ref[0:1]
        next_ref[1 : rows - 1] = after_inner_ref[...]
        next_ref[rows - 1 : rows] = after_edge_ref[1:2]

    mid_kernel(
        1, *refs[:5], edge_ref, temporal_two_ref, spatial_two_ref, mid_ref, edge_views_ref
    )
    gpre_ref[1 : rows - 1] = inner_gpre_ref[...]
    views_ref[1 : rows - 1] = inner_views_ref[...]
    for row in (0, rows - 1):
        here = slice(row, row + 1)
        grads = [mid_ref[here], next_ref[here]]
        pre_rows(preact_ref[here], grads, temporal_ref, gpre_ref, views_ref, row)
    block_sums(gpre_ref, sides_ref, [mid_ref, next_ref], views_ref, sums_ref, keep_ref, send_ref)


def input_kernel(mid_ref, gpre_ref, pair_ref, across_ref, spatial_ref, out_ref, token_ref, views_ref):
    rows, cols, ch = out_ref.shape
    pair = pair_ref[pair_ref.shape[0] - 2 * cols : pair_ref.shape[0] - cols]
    above, below = beside_band((pair[None], across_ref[across_ref.shape[0] - cols :][None]), 0)
    token_ref[...] = jnp.zeros(token_ref.shape, token_ref.dtype)
    step = 4
    beside(above.astype(jnp.float32), views_ref, 0)
    beside(below.astype(jnp.float32), views_ref, rows + 1)

    for n in range(rows // step):
        gpre = gpre_ref[pl.ds(n * step, step)].astype(jnp.float32)
        beside(gpre, views_ref, n * step + 1)

    for n in range(rows // step):
        here = pl.ds(n * step, step)
        out_ref[here] = convolved(views_ref, spatial_ref, n * step, mid_ref[here])


def halves(count, index):
    return [pl.ds(pl.multiple_of(n * count, count), count) for n in (index, 1 - index)]


def pair_kernel(keep_ref, low_ref, high_ref, own_ref, send_ref):
    across = lax.axis_index("section") // 2
    parts = [ref[...].astype(jnp.float32) for ref in (low_ref, high_ref)]
    own_ref[...] = keep_ref[across] + jnp.where(across == 0, *parts)
    total = keep_ref[1 - across] + jnp.where(across == 0, *parts[::-1])
    send_ref[...] = total.astype(jnp.bfloat16)


def band_kernel(own_ref, part_ref, keep_ref, send_ref):
    mine, other = halves(keep_ref.shape[0], lax.axis_index("video"))
    half = keep_ref.shape[0]
    keep_ref[...] = own_ref[mine] + part_ref[mine].astype(jnp.float32)
    send_ref[:half] = (own_ref[other] + part_ref[other].astype(jnp.float32)).astype(jnp.bfloat16)


def pair_quarter_kernel(keep_ref, part_ref, own_ref, across_ref, frame_ref, both_ref):
    _, height, _ = keep_ref.shape
    half = own_ref.shape[0]
    band = lax.axis_index("section") // 2
    frames = halves(half, lax.axis_index("video"))

    def quarter(band, rows):
        start = pl.multiple_of(band * height, height)
        part = part_ref.at[pl.ds(start, height)][rows]
        return keep_ref[band, rows] + part.astype(jnp.float32)

    own_ref[...] = quarter(band, frames[0])
    across_ref[:half] = quarter(1 - band, frames[0]).astype(jnp.bfloat16)
    rest = across_ref.shape[0] - half
    across_ref[half:] = part_ref[2 * height + rest :]
    frame_ref[...] = quarter(band, frames[1]).astype(jnp.bfloat16)
    both_ref[:half] = quarter(1 - band, frames[1]).astype(jnp.bfloat16)


def plane_kernel(own_ref, *refs):
    parts, out_ref = refs[:-1], refs[-1]
    total = own_ref[...]
    for part in parts:
        total = total + part[: out_ref.shape[0]].astype(jnp.float32)
    out_ref[...] = total.astype(jnp.bfloat16)


def add_kernel(one_ref, two_ref, out_ref):
    total = one_ref[...].astype(jnp.float32) + two_ref[: one_ref.shape[0]].astype(jnp.float32)
    out_ref[...] = total.astype(jnp.bfloat16)


def scaled_kernel(factor, *refs):
    out_ref = refs[-1]
    for block in range(2):
        one, two = (ref[...].astype(jnp.float32) for ref in refs[2 * block : 2 * block + 2])
        out_ref[block] = ((one + two) * factor).astype(jnp.bfloat16)


def place_kernel(places, *refs):
    shares, outs = refs[: len(places)], refs[-6:-2]
    sums_ref, sems = refs[-2:]
    band, frame = lax.axis_index("section"), lax.axis_index("video")
    height = shares[0].shape[1]

    def copies(n, block):
        flip, other = places[n]
        place = jnp.bitwise_xor(band, flip)
        half = 0 if other is None else jnp.bitwise_xor(frame, int(other))
        here = pl.ds(pl.multiple_of(half * height, height), height)
        spatial, temporal = outs[2 * block : 2 * block + 2]
        source, sem = sums_ref.at[n, block], sems.at[n, block]
        return (
            (place < 3, lambda: pltpu.make_async_copy(source, spatial.at[place, here], sem)),
            (place == 3, lambda: pltpu.make_async_copy(source, temporal.at[here], sem)),
        )

    for n, share in enumerate(shares):
        for block in range(2):
            sums_ref[n, block] = share[block].astype(jnp.float32)
            for inside, copy in copies(n, block):
                pl.when(inside)(lambda: copy().start())
    for n in range(len(shares)):
        for block in range(2):
            for inside, copy in copies(n, block):
                pl.when(inside)(lambda: copy().wait())


def placed(shares, places, given=()):
    _, height, ch = shares[0].shape
    count = len(shares)
    outs = (f32(3, 3 * ch, ch), f32(3 * ch, ch)) * 2
    vmem, spare = (pl.BlockSpec(memory_space=space) for space in (pltpu.VMEM, pl.ANY))
    return pl.pallas_call(
        functools.partial(place_kernel, places),
        out_shape=outs,
        in_specs=[vmem] * count + [spare] * len(given),
        out_specs=(spare,) * 4,
        scratch_shapes=[
            pltpu.VMEM((count, 2, height, ch), jnp.float32),
            pltpu.SemaphoreType.DMA((count, 2)),
        ],
        input_output_aliases={count + n: n for n in range(len(given))},
        compiler_params=pltpu.CompilerParams(vmem_limit_bytes=24 * MIB),
        cost_estimate=pl.CostEstimate(
            flops=0, bytes_accessed=6 * count * height * ch * 2, transcendentals=0
        ),
    )(*shares, *given)


def unpacked(sums):
    ch = sums[0].shape[-1]
    return [x.reshape(3, 3, ch, ch) if x.ndim == 3 else x.reshape(3, ch, ch) for x in sums]


def on_device(
    grad_latent,
    input_one,
    preact_one,
    input_two,
    preact_two,
    spatial_one,
    temporal_one,
    spatial_two,
    temporal_two,
):
    shape = grad_latent.shape
    rows, cols, ch = shape[2:]
    bands, frames = lax.axis_size("section"), lax.axis_size("video")
    later = min(2, frames - 1)
    pixels = lax.axis_size("dp") * frames * bands * rows * cols
    factor = 1.0 / math.sqrt(pixels)
    grad, saved_one, pre_one, saved_two, pre_two = (
        x.reshape(rows, cols, ch)
        for x in (grad_latent, input_one, preact_one, input_two, preact_two)
    )
    conv = 2 * rows * cols * 9 * ch * ch
    views = pltpu.VMEM((rows, cols, 3 * ch), jnp.bfloat16)
    edge_views = pltpu.VMEM((6, cols, 3 * ch), jnp.bfloat16)
    act = pltpu.VMEM((rows, cols, ch), jnp.bfloat16)
    sides = bf16(4, ch, rows * cols)
    sums = pltpu.VMEM((4, 3 * ch, ch), jnp.float32)
    handed = [f32(2, 3 * ch, ch)] + [bf16(3 * ch, ch)] * 2
    inner_outs = [bf16(rows - 2, cols, ch), bf16(rows, cols, ch)]
    kernels = (temporal_two, spatial_two)

    def from_later(x):
        if frames == 2:
            return [flipped(x, "video", 1)]
        return [from_ahead(x, 0, n + 1) for n in range(later)]

    wholes = from_later(grad)
    packs = call(
        pack_kernel,
        [bf16(4, cols, ch)] * 2,
        [pltpu.SemaphoreType.DMA((8,))],
        1,
        grad,
        pre_two,
        saved_two,
        saved_one,
        spare_inputs=True,
        limit=58,
    )
    second = flipped(packs[1], "section", 1)
    first = flipped(later_than(packs[0], second), "section", 1)
    pairs = [first, flipped(second, "section", 2)]

    known = ()
    if frames == 2:
        known = call(
            last_inner_kernel,
            inner_outs,
            [views],
            0,
            grad,
            pre_two,
            *kernels,
            after=(first, second),
        )
        afters = from_later(known[0])
    else:
        afters = from_later(jnp.concatenate(beside_band(pairs, 0)))
    inner, gpre_two = call(
        functools.partial(inner_kernel, later),
        inner_outs,
        [views],
        0,
        grad,
        pre_two,
        *wholes,
        *kernels,
        *known,
        early=(saved_two, saved_one, pre_one, temporal_one),
    )
    if frames == 2:
        edge = call(
            last_edge_kernel,
            [bf16(4, cols, ch)],
            [edge_views],
            0,
            grad,
            *pairs,
            known[1],
            *kernels,
            after=(gpre_two,),
        )
        afters += from_later(edge)
    parts_two = call(
        functools.partial(two_kernel, later),
        handed,
        [views, pltpu.VMEM(sides.shape, sides.dtype), sums],
        8 * conv,
        saved_two,
        pre_two,
        gpre_two,
        *pairs,
        grad,
        *wholes,
        after=(edge,) if frames == 2 else (),
    )
    sides_one = call(
        sides_kernel, [sides], [], conv // 8, saved_one, pre_one, *pairs, after=parts_two[:1]
    )
    height, half = 3 * ch, 3 * ch // 2
    keep_two, low_two, high_two = parts_two
    own_two, send_two = call(
        pair_kernel,
        [f32(height, ch), bf16(height, ch)],
        [],
        height * ch,
        keep_two,
        flipped(low_two, "section", 1),
        flipped(high_two, "section", 1),
    )
    across_two = flipped(send_two, "section", 2)
    mid_inputs = (grad, *pairs, inner, gpre_two)
    one_inputs = (sides_one, pre_one)
    mid_outs = [bf16(rows, cols, ch)]
    one_outs = [bf16(rows, cols, ch), f32(2, 3 * ch, ch), bf16(6 * ch + 2 * cols, ch)]
    if frames == 2:
        inners_one = call(
            one_inner_kernel,
            [bf16(rows - 2, cols, ch), bf16(rows - 2, cols, 3 * ch)],
            [],
            conv // 8,
            pre_one,
            inner,
            afters[0],
            temporal_one,
        )
        mid, gpre_one, *parts_one = call(
            mid_one_kernel,
            mid_outs + one_outs,
            [views, sums, act, pltpu.VMEM((2, cols, ch), jnp.bfloat16), edge_views],
            8 * conv,
            *mid_inputs,
            *afters,
            *kernels,
            *one_inputs,
            temporal_one,
            *inners_one,
            after=(own_two,),
        )
    else:
        mid = call(
            functools.partial(mid_kernel, later),
            mid_outs,
            [edge_views],
            conv // 8,
            *mid_inputs,
            *afters,
            *kernels,
        )
        gpre_one, *parts_one = call(
            functools.partial(one_kernel, later),
            one_outs,
            [views, sums],
            1.2 * conv,
            *one_inputs,
            mid,
            *from_later(mid),
            temporal_one,
        )
    keep_one, send_one = parts_one
    split = frames == 2 and lax.axis_size("dp") == 4
    if split:
        send_one = later_than(send_one, across_two)
    pair_one = flipped(send_one, "section", 1)

    def input_gradient(edge, after):
        return call(
            input_kernel,
            [bf16(rows, cols, ch), f32(8, 128)],
            [pltpu.VMEM((rows + 2, cols, 3 * ch), jnp.bfloat16)],
            conv,
            mid,
            gpre_one,
            pair_one,
            edge,
            spatial_one,
            after=after,
        )

    if split:

        def added(one, two):
            return call(add_kernel, [bf16(half, ch)], [], half * ch, one, two)

        keep_two, send_two = call(
            band_kernel,
            [f32(half, ch), bf16(half + cols + 32, ch)],
            [],
            0,
            own_two,
            across_two,
        )
        sum_two = added(keep_two, flipped(send_two, "video", 1))
        quarters = [f32(half, ch)] + [bf16(half + more, ch) for more in (cols, 0, cols + 16)]
        own_one, *sends = call(
            pair_quarter_kernel, quarters, [], 0, keep_one, pair_one, after=(send_two,)
        )
        across = flipped(sends[0], "section", 2)
        parts = [across, flipped(sends[1], "video", 1), flipped_both(sends[2])]
        sum_one = call(plane_kernel, [bf16(half, ch)], [], 4 * half * ch, own_one, *parts)
        part_two = flipped(sum_two, "dp", 1)
        part_one = flipped(later_than(sum_one, sum_two), "dp", 1)
        sum_two = added(sum_two, part_two)
        sum_one = added(sum_one, part_one)
        last_two = flipped(sum_two, "dp", 2)
        last_one = flipped(later_than(sum_one, sum_two), "dp", 2)
        grad_in, token = input_gradient(across, (sum_one,))
        own = call(
            functools.partial(scaled_kernel, factor),
            [bf16(2, half, ch)],
            [],
            height * ch,
            sum_one,
            last_one,
            sum_two,
            last_two,
            after=(token,),
        )
        frame, across, both = flipped(own, "video", 1), flipped(own, "section", 2), flipped_both(own)
        shares = [own, frame, across]
        shares += [flipped(share, "section", 1) for share in shares]
        places = [(0, False), (0, True), (2, False), (1, False), (1, True), (3, False)]
        sums = placed([*shares, both], [*places, (2, True)])
        sums = unpacked(placed([flipped(both, "section", 1)], [(3, True)], sums))
    else:
        own_one, send_one = call(
            pair_kernel,
            [f32(height, ch), bf16(height, ch)],
            [],
            height * ch,
            keep_one,
            pair_one[:height],
            pair_one[height : 2 * height],
        )
        edge = flipped(pair_one[pair_one.shape[0] - cols :], "section", 2)
        grad_in, _ = input_gradient(edge, ())
        own_one = own_one + flipped(send_one, "section", 2).astype(jnp.float32)
        own_two = own_two + across_two.astype(jnp.float32)
        share = lax.psum(jnp.stack((own_one, own_two)), ("video", "dp")) * factor
        share = share.astype(jnp.bfloat16)
        shares = [share, flipped(share, "section", 2)]
        shares += [flipped(share, "section", 1) for share in shares]
        sums = unpacked(placed(shares, [(0, None), (2, None), (1, None), (3, None)]))
    return (grad_in.reshape(shape), *sums)


def solution(mesh):
    whole = P("dp", "video", "section", None, None)
    return jax.shard_map(
        on_device,
        mesh=mesh,
        in_specs=(whole,) * 5 + (P(),) * 4,
        out_specs=(whole, P(), P(), P(), P()),
        check_vma=False,
    )
```
